32 devices in a mesh: seq: 2 (over core), mp: 4 (over y, x), row: 4 (over z).
Axes of the slice: x: 2, y: 2, z: 4, core: 2. Of those that a mesh axis runs over, the one named last changes fastest.
Arguments:
- block_in: bfloat16 [4, 2048, 2048], P('row', 'seq'), may hold values from -6 to 6
- doc_lengths: int32 [4, 3], P('row'), may hold values from 1 to 1856, as said below
- attn_gain: float32 [2048], replicated, may hold values from 0.5 to 1.5
- qkv_weight: bfloat16 [3, 2048, 2048], P(None, ('seq', 'row'), 'mp'), may hold values from -0.125 to 0.125
- conv_weight: float32 [3, 4, 2048], P(None, None, 'mp'), may hold values from -3 to 3
- beta_weight: bfloat16 [16, 2048], P('mp', ('seq', 'row')), may hold values from -0.125 to 0.125
- out_gain: float32 [128], replicated, may hold values from 0.5 to 1.5
- out_weight: bfloat16 [2048, 2048], P('mp', ('seq', 'row')), may hold values from -0.125 to 0.125
- ffn_gain: float32 [2048], replicated, may hold values from 0.5 to 1.5
- gateup_weight: bfloat16 [2, 2048, 5632], P(None, ('seq', 'row'), 'mp'), may hold values from -0.125 to 0.125
- down_weight: bfloat16 [5632, 2048], P('mp', ('seq', 'row')), may hold values from -0.078125 to 0.078125
- cotangent: bfloat16 [4, 2048, 2048], P('row', 'seq'), may hold values from -6 to 6
Outputs:
- block_out: bfloat16 [4, 2048, 2048], P('row', 'seq')
- grad_in: float32 [4, 2048, 2048], P('row', 'seq')
- grad_attn_gain: float32 [2048], replicated
- grad_qkv: float32 [3, 2048, 2048], P(None, ('seq', 'row'), 'mp')
- grad_conv: float32 [3, 4, 2048], P(None, None, 'mp')
- grad_beta: float32 [16, 2048], P('mp', ('seq', 'row'))
- grad_out_gain: float32 [128], replicated
- grad_out_weight: float32 [2048, 2048], P('mp', ('seq', 'row'))
- grad_ffn_gain: float32 [2048], replicated
- grad_gateup: float32 [2, 2048, 5632], P(None, ('seq', 'row'), 'mp')
- grad_down: float32 [5632, 2048], P('mp', ('seq', 'row'))
The draws below stay inside these ranges and needn't reach their ends.
Inputs may be any that keep to these rules, and one draw needn't show every extreme that they name: `doc_lengths`: in each row one document, which one drawn from the seed, has exactly 1856 tokens; the others have at most 64. Each document's region is its length rounded up to a multiple of 64, the regions lie in order from position 0, and positions past a document's length or past the last region are padding.
All inputs are finite; a program needn't handle non-finite values.
Results may differ from the reference program's by a relative error of at most 0.018.
Values may be sent and summed in bfloat16 or wider, within the bound.
A program may use at most 320 MiB of HBM per device.

```python
import jax
import jax.numpy as jnp
from jax import lax

D = 2048
HEADS = 16
HDIM = 128
FF = 5632
KERNEL = 4
BLOCK = 64
NDOC = 3
NPOS = 2048
ROWS = 4


def draw_doc_lengths(key, part):
    key = jax.random.fold_in(key, 7)
    short_key, place_key = jax.random.split(key)
    shorts = jax.random.randint(short_key, (ROWS, NDOC), 1, BLOCK + 1)
    longest = jax.random.randint(place_key, (ROWS, 1), 0, NDOC)
    columns = jnp.arange(NDOC)[None, :]
    return jnp.where(columns == longest, NPOS - NDOC * BLOCK, shorts).astype(jnp.int32)


def level_of(own_key, extent, cuts, least, largest):
    gain = 1.0
    for dim, parts in cuts:
        draws = jax.random.uniform(jax.random.fold_in(jax.random.fold_in(own_key, 6), dim), (parts,), jnp.float32, least / len(cuts), largest / len(cuts))
        gain = gain * jnp.repeat(jnp.exp(draws), extent[dim] // parts).reshape((-1,) + (1,) * (len(extent) - 1 - dim))
    return gain


def scatter_about(stream_key, shape, spread, most, cuts=(), kind=jnp.bfloat16):
    drawn = spread * jax.random.normal(stream_key, shape, jnp.float32)
    if cuts:
        drawn = drawn * level_of(stream_key, shape, cuts, -0.22, 0.18)
    return jnp.clip(drawn, -most, most).astype(kind)


def setup_inputs(seed: int = 0) -> dict:
    keys = jax.random.split(jax.random.key(seed), 13)
    block_in = scatter_about(keys[0], (ROWS, NPOS, D), 1.0, 6.0, ((0, 4), (1, 2)))
    doc_lengths = draw_doc_lengths(jax.random.fold_in(keys[12], 71), 0)
    attn_gain = jnp.clip(1.0 + 0.1 * jax.random.normal(keys[2], (D,), jnp.float32), 0.5, 1.5)
    qkv_weight = scatter_about(keys[3], (3, D, HEADS * HDIM), D ** -0.5, 0.125, ((1, 8), (2, 4)))
    conv_weight = scatter_about(keys[4], (3, KERNEL, HEADS * HDIM), KERNEL ** -0.5, 3.0, ((2, 4),), jnp.float32)
    beta_weight = scatter_about(keys[5], (HEADS, D), D ** -0.5, 0.125, ((0, 4), (1, 8)))
    out_gain = jnp.clip(1.0 + 0.1 * jax.random.normal(keys[6], (HDIM,), jnp.float32), 0.5, 1.5)
    out_weight = scatter_about(keys[7], (HEADS * HDIM, D), (HEADS * HDIM) ** -0.5, 0.125, ((0, 4), (1, 8)))
    ffn_gain = jnp.clip(1.0 + 0.1 * jax.random.normal(keys[8], (D,), jnp.float32), 0.5, 1.5)
    gateup_weight = scatter_about(keys[9], (2, D, FF), D ** -0.5, 0.125, ((1, 8), (2, 4)))
    down_weight = scatter_about(keys[10], (FF, D), FF ** -0.5, 0.078125, ((0, 4), (1, 8)))
    cotangent = scatter_about(keys[11], (ROWS, NPOS, D), 1.0, 6.0, ((0, 4), (1, 2)))
    return {"block_in": block_in, "doc_lengths": doc_lengths, "attn_gain": attn_gain, "qkv_weight": qkv_weight, "conv_weight": conv_weight, "beta_weight": beta_weight, "out_gain": out_gain, "out_weight": out_weight, "ffn_gain": ffn_gain, "gateup_weight": gateup_weight, "down_weight": down_weight, "cotangent": cotangent}


EPSILON = 1e-06
PRECISE = lax.Precision.HIGHEST

@jax.custom_vjp
def low(v):
    return lax.optimization_barrier(v.astype(jnp.bfloat16)).astype(jnp.float32)

@jax.custom_vjp
def low_back(v):
    return v

def low_keep(v):
    return (low(v), None)

def low_pass(kept, grad):
    return (grad,)

def back_keep(v):
    return (v, None)

def back_low(kept, grad):
    return (low(grad),)
low.defvjp(low_keep, low_pass)
low_back.defvjp(back_keep, back_low)

def row_layout(lengths, positions):
    span_len = (lengths + BLOCK - 1) // BLOCK * BLOCK
    closing = jnp.cumsum(span_len).astype(jnp.int32)
    opening = (closing - span_len).astype(jnp.int32)
    bounds = jnp.concatenate([opening, closing[-1:]])
    reached = bounds[None, :] <= positions[:, None]
    doc_start = lax.optimization_barrier(jnp.max(jnp.where(reached, bounds[None, :], 0), axis=1)).astype(jnp.int32)
    inside = (positions[:, None] >= opening[None, :]) & (positions[:, None] < (opening + lengths)[None, :])
    real_mask = jnp.any(inside, axis=1).astype(jnp.float32)
    return (doc_start, real_mask)

def block_step(memory, block_in):
    q_blk, k_blk, v_blk, s_blk, carry_flag = block_in
    memory = memory * carry_flag[:, None, None, None]
    blk_len = k_blk.shape[2]
    head_width = k_blk.shape[3]
    strict_lower = jnp.tril(jnp.ones((blk_len, blk_len), jnp.float32), -1)
    causal = jnp.tril(jnp.ones((blk_len, blk_len), jnp.float32))
    key_gram = jnp.einsum('bhcp,bhdp->bhcd', k_blk, k_blk, precision=PRECISE)
    system = jnp.eye(blk_len, dtype=jnp.float32) + strict_lower * (s_blk[..., :, None] * key_gram)
    right_side = jnp.concatenate([s_blk[..., None] * k_blk, s_blk[..., None] * v_blk], axis=-1)
    solved = lax.linalg.triangular_solve(system, right_side, left_side=True, lower=True, unit_diagonal=True)
    w_mat = solved[..., :head_width]
    u_mat = solved[..., head_width:]
    corrected = u_mat - jnp.einsum('bhcp,bhpv->bhcv', w_mat, memory, precision=PRECISE)
    scores = causal * jnp.einsum('bhcp,bhdp->bhcd', q_blk, k_blk, precision=PRECISE)
    outputs = jnp.einsum('bhcp,bhpv->bhcv', q_blk, memory, precision=PRECISE)
    outputs = outputs + jnp.einsum('bhcd,bhdv->bhcv', scores, corrected, precision=PRECISE)
    memory = memory + jnp.einsum('bhcp,bhcv->bhpv', k_blk, corrected, precision=PRECISE)
    return (memory, outputs)

def delta_rule(queries, keys_in, values, strength, carry_on):

    def to_blocks(tensor):
        return tensor.reshape(ROWS, NPOS // BLOCK, BLOCK, HEADS, -1).transpose(1, 0, 3, 2, 4)
    blocks = (to_blocks(queries), to_blocks(keys_in), to_blocks(values), to_blocks(strength[..., None])[..., 0], carry_on.T)
    initial = jnp.zeros((ROWS, HEADS, HDIM, HDIM), jnp.float32)
    final_state, outputs = lax.scan(jax.checkpoint(block_step), initial, blocks)
    return outputs.transpose(1, 0, 3, 2, 4).reshape(ROWS, NPOS, HEADS, HDIM)

def forward(residual_in, attn_gain, qkv_weight, conv_weight, beta_weight, out_gain, out_weight, ffn_gain, gateup_weight, down_weight, taps, real_mask, carry_on):
    stat_in = lax.rsqrt(lax.optimization_barrier(jnp.mean(residual_in * residual_in, axis=-1, keepdims=True)) + EPSILON)
    normed = low(residual_in * stat_in * attn_gain)
    raw = low(low_back(jnp.einsum('btd,sdc->sbtc', normed, qkv_weight, precision=PRECISE)))
    padded = jnp.pad(raw, ((0, 0), (0, 0), (KERNEL - 1, 0), (0, 0)))
    conv_sum = jnp.zeros_like(raw)
    for shift_no in range(KERNEL):
        window = padded[:, :, KERNEL - 1 - shift_no:KERNEL - 1 - shift_no + NPOS]
        conv_sum = conv_sum + conv_weight[:, shift_no][:, None, None, :] * window * taps[shift_no][None, :, :, None]
    activated = jax.nn.silu(conv_sum).reshape(3, ROWS, NPOS, HEADS, HDIM)
    queries = activated[0]
    queries = queries * lax.rsqrt(lax.optimization_barrier(jnp.sum(queries * queries, axis=-1, keepdims=True)) + EPSILON) * HDIM ** (-0.5)
    keys_in = activated[1]
    keys_in = keys_in * lax.rsqrt(lax.optimization_barrier(jnp.sum(keys_in * keys_in, axis=-1, keepdims=True)) + EPSILON)
    values = activated[2]
    logits = low_back(jnp.einsum('btd,hd->bth', normed, beta_weight, precision=PRECISE))
    strength = jax.nn.sigmoid(logits) * real_mask[:, :, None]
    mixer = delta_rule(queries, keys_in, values, strength, carry_on)
    stat_out = lax.rsqrt(lax.optimization_barrier(jnp.mean(mixer * mixer, axis=-1, keepdims=True)) + EPSILON)
    normed_out = low((mixer * stat_out * out_gain).reshape(ROWS, NPOS, HEADS * HDIM))
    branch = low_back(jnp.einsum('btc,cd->btd', normed_out, out_weight, precision=PRECISE))
    hidden = residual_in + branch
    stat_mid = lax.rsqrt(lax.optimization_barrier(jnp.mean(hidden * hidden, axis=-1, keepdims=True)) + EPSILON)
    normed_mid = low(hidden * stat_mid * ffn_gain)
    gate_up = low_back(jnp.einsum('btd,sdf->sbtf', normed_mid, gateup_weight, precision=PRECISE))
    product = low(jax.nn.silu(gate_up[0]) * gate_up[1])
    return hidden + jnp.einsum('btf,fd->btd', product, down_weight, precision=PRECISE)

def reference(block_in, doc_lengths, attn_gain, qkv_weight, conv_weight, beta_weight, out_gain, out_weight, ffn_gain, gateup_weight, down_weight, cotangent):
    positions = jnp.arange(NPOS, dtype=jnp.int32)
    doc_start, real_mask = jax.vmap(row_layout, in_axes=(0, None))(doc_lengths, positions)
    taps = jnp.stack([(positions[None, :] - shift_no >= doc_start).astype(jnp.float32) for shift_no in range(KERNEL)])
    carry_on = (doc_start[:, ::BLOCK] != positions[::BLOCK][None, :]).astype(jnp.float32)
    floats = (block_in.astype(jnp.float32), attn_gain, qkv_weight.astype(jnp.float32), conv_weight, beta_weight.astype(jnp.float32), out_gain, out_weight.astype(jnp.float32), ffn_gain, gateup_weight.astype(jnp.float32), down_weight.astype(jnp.float32))

    def wrapped(*params):
        return forward(*params, taps, real_mask, carry_on)
    result, pullback = jax.vjp(wrapped, *floats)
    grads = pullback(cotangent.astype(jnp.float32))
    return (result.astype(jnp.bfloat16), grads[0], grads[1], grads[2], grads[3], grads[4], grads[5], grads[6], grads[7], grads[8], grads[9])
```

```python
import functools
from functools import partial

import jax
import jax.numpy as jnp
from jax import lax
from jax.experimental import pallas as pl
from jax.experimental.pallas import tpu as pltpu
from jax.sharding import PartitionSpec as P

HDIM = 128
KERNEL = 4
BLOCK = 64
CHUNK = 128
EPSILON = 1e-06
PRECISE = lax.Precision.HIGHEST
F32 = jnp.float32
BF16 = jnp.bfloat16

NT=(((1,),(1,)),((),())); NN=(((1,),(0,)),((),())); TN=(((0,),(0,)),((),()))

def mm(a,b,dims=NN):
    return lax.dot_general(a.astype(BF16), b.astype(BF16), dims, preferred_element_type=F32)

def iotas():
    return lax.broadcasted_iota(jnp.int32,(CHUNK,CHUNK),0), lax.broadcasted_iota(jnp.int32,(CHUNK,CHUNK),1)

def inverse(a):
    r,c=iotas()
    t=jnp.where(r==c,1.0,0.0)-jnp.where(r//2==c//2,a,0.0)
    size=2
    while size<CHUNK:
        off=jnp.where((r//(2*size)==c//(2*size))&(r//size!=c//size),a,0.0)
        t=t-mm(t,mm(off,t))
        size*=2
    return t

def conv_act(ext_ref, s, base, lanes, cw, taps):
    total=cw[0:1]*ext_ref[s,pl.ds(base+8,CHUNK),lanes]
    for j in range(1,KERNEL):
        total=total+(cw[j:j+1]*taps[j-1])*ext_ref[s,pl.ds(base+8-j,CHUNK),lanes]
    sig=jax.nn.sigmoid(total)
    return total,sig

def fwd_kernel(heads, group, raw_ref, cw_ref, gain_ref, cols_ref, normed_ref, o_ref, s_ref, t_ref, w_ref, r_ref, ext, state):
    rows=group*CHUNK
    step=pl.program_id(0)
    @pl.when(step==0)
    def _():
        ext[:,0:8,:]=jnp.zeros((3,8,heads*HDIM),F32)
        state[...]=jnp.zeros(state.shape,F32)
    @pl.when(step>0)
    def _():
        ext[:,0:8,:]=ext[:,rows:rows+8,:]
    ext[:,8:,:]=raw_ref[...].astype(F32)
    r,c=iotas()
    width=heads*HDIM
    units=[]
    for g in range(group):
        base=g*CHUNK
        cols=cols_ref[pl.ds(base,CHUNK),:]
        taps=[cols[:,j:j+1] for j in range(3)]
        m=cols[:,6:7]
        for h in range(heads):
            act=[]
            for s in range(3):
                lanes=pl.ds(h*HDIM,HDIM)
                total,sig=conv_act(ext,s,base,lanes,cw_ref[s,:,lanes],taps)
                act.append(total*sig)
            q=act[0]*(lax.rsqrt(jnp.sum(act[0]*act[0],axis=1,keepdims=True)+EPSILON)*HDIM**-0.5)
            k=act[1]*lax.rsqrt(jnp.sum(act[1]*act[1],axis=1,keepdims=True)+EPSILON)
            v=act[2]
            b=cols[:,9+h:10+h]
            gram=mm(k,k,NT)
            score=mm(q,k,NT)
            mask=jnp.where(c<BLOCK,m,1.0)
            a=jnp.where(r>c,b*gram*mask,0.0)
            l=jnp.where(r>=c,score*mask,0.0)
            t=inverse(a)
            w=mm(t,b*k)*m
            u=mm(t,b*v)
            t_ref[g,h]=t.astype(BF16)
            w_ref[pl.ds(base,CHUNK),pl.ds(h*HDIM,HDIM)]=w.astype(BF16)
            units.append((g,h,q*m,k*cols[:,7:8],l,w,u,cols[0:1,8:9],m[CHUNK-1:CHUNK]))
    for g,h,q,k,l,w,u,keep0,keep1 in units:
        base=g*CHUNK
        out=(pl.ds(base,CHUNK),pl.ds(h*HDIM,HDIM))
        s=state[h]*keep0
        s_ref[g,h]=s.astype(BF16)
        rr=u-mm(w,s)
        o=mm(q,s)+mm(l,rr)
        state[h]=s*keep1+mm(k,rr,TN)
        r_ref[out]=rr.astype(BF16)
        o_ref[out]=o
        stat=lax.rsqrt(jnp.mean(o*o,axis=1,keepdims=True)+EPSILON)
        normed_ref[out]=(o*stat*gain_ref[...]).astype(BF16)

def forward(raw, cw, gain, cols, group):
    n=raw.shape[1]; heads=raw.shape[2]//HDIM; rows=group*CHUNK; width=heads*HDIM
    nc=n//CHUNK
    row=lambda w: pl.BlockSpec((rows,w),lambda i:(i,0))
    mat=pl.BlockSpec((group,heads,HDIM,HDIM),lambda i:(i,0,0,0))
    full=lambda a: pl.BlockSpec(a.shape,lambda i:(0,0))
    return pl.pallas_call(functools.partial(fwd_kernel,heads,group),
        grid=(n//rows,),
        in_specs=[pl.BlockSpec((3,rows,width),lambda i:(0,i,0)),pl.BlockSpec(cw.shape,lambda i:(0,0,0)),full(gain),row(16)],
        out_specs=[row(width),row(width),mat,mat,row(width),row(width)],
        out_shape=[jax.ShapeDtypeStruct((n,width),BF16),jax.ShapeDtypeStruct((n,width),F32),
            jax.ShapeDtypeStruct((nc,heads,HDIM,HDIM),BF16),jax.ShapeDtypeStruct((nc,heads,HDIM,HDIM),BF16),
            jax.ShapeDtypeStruct((n,width),BF16),jax.ShapeDtypeStruct((n,width),BF16)],
        scratch_shapes=[pltpu.VMEM((3,rows+8,width),F32),pltpu.VMEM((heads,HDIM,HDIM),F32)],
        compiler_params=pltpu.CompilerParams(vmem_limit_bytes=48<<20),
    )(raw,cw,gain,cols)

def bwd_kernel(heads, group, raw_ref, prev_ref, cw_ref, gain_ref, cols_ref, gno_ref, o_ref, s_ref, t_ref, w_ref, r_ref,
               graw_ref, gb_ref, gcw_ref, ggain_ref, ext, gext, grad_state):
    rows=group*CHUNK
    step=pl.program_id(0); steps=pl.num_programs(0)
    width=heads*HDIM
    @pl.when(step==0)
    def _():
        gext[:,rows:rows+8,:]=jnp.zeros((3,8,heads*HDIM),F32)
        grad_state[...]=jnp.zeros(grad_state.shape,F32)
        gcw_ref[...]=jnp.zeros(gcw_ref.shape,F32)
        ggain_ref[...]=jnp.zeros(ggain_ref.shape,F32)
    @pl.when(step>0)
    def _():
        gext[:,rows:rows+8,:]=gext[:,0:8,:]
    first=jnp.where(step==steps-1,0.0,1.0)
    ext[:,0:8,:]=prev_ref[...].astype(F32)[:,8:16]*first
    ext[:,8:,:]=raw_ref[...].astype(F32)
    r,c=iotas()
    for g in range(group-1,-1,-1):
        base=g*CHUNK
        cols=cols_ref[pl.ds(base,CHUNK),:]
        taps=[cols[:,j:j+1] for j in range(3)]
        m=cols[:,6:7]; m2=cols[:,7:8]; keep0=cols[0:1,8:9]; keep1=m[CHUNK-1:CHUNK]
        gbs=[]
        for h in range(heads):
            out=(pl.ds(base,CHUNK),pl.ds(h*HDIM,HDIM))
            act=[];tot=[];sigs=[]
            for s in range(3):
                lanes=pl.ds(h*HDIM,HDIM)
                total,sig=conv_act(ext,s,base,lanes,cw_ref[s,:,lanes],taps)
                act.append(total*sig);tot.append(total);sigs.append(sig)
            rq=lax.rsqrt(jnp.sum(act[0]*act[0],axis=1,keepdims=True)+EPSILON)
            rk=lax.rsqrt(jnp.sum(act[1]*act[1],axis=1,keepdims=True)+EPSILON)
            qu=act[0]*rq; q=qu*HDIM**-0.5
            k=act[1]*rk; v=act[2]
            b=cols[:,9+h:10+h]
            mask=jnp.where(c<BLOCK,m,1.0)
            gram=mm(k,k,NT)*mask
            l=jnp.where(r>=c,mm(q,k,NT)*mask,0.0)
            s=s_ref[g,h]; t=t_ref[g,h]; w=w_ref[out]; rr=r_ref[out]
            o=o_ref[out]
            stat=lax.rsqrt(jnp.mean(o*o,axis=1,keepdims=True)+EPSILON)
            uo=o*stat
            gno=gno_ref[out].astype(F32)
            ggain_ref[...]+=jnp.sum(gno*uo,axis=0,keepdims=True)
            gu=gno*gain_ref[...]
            do=stat*(gu-uo*jnp.mean(gu*uo,axis=1,keepdims=True))
            dsn=grad_state[h]
            dr=mm(l,do,TN)+m2*mm(k,dsn)
            ds=keep1*dsn+mm(q*m,do,TN)-mm(w,dr,TN)
            grad_state[h]=keep0*ds
            df=mm(t,dr,TN)
            dl=jnp.where(r>=c,mm(do,rr,NT)*mask,0.0)
            da=jnp.where(r>c,-mm(df,rr,NT),0.0)
            de=b*df
            e=v-m*mm(k,s)
            gbs.append(jnp.sum(df*e,axis=1,keepdims=True)+jnp.sum(da*gram,axis=1,keepdims=True))
            dkk=b*da*mask
            dq=m*mm(do,s,NT)+mm(dl,k)
            dk=mm(dl,q,TN)+m2*mm(rr,dsn,NT)-m*mm(de,s,NT)+mm(dkk,k)+mm(dkk,k,TN)
            dv=de
            gq=dq*HDIM**-0.5
            gq=rq*(gq-qu*jnp.sum(gq*qu,axis=1,keepdims=True))
            gk=rk*(dk-k*jnp.sum(dk*k,axis=1,keepdims=True))
            for i,ga in enumerate((gq,gk,dv)):
                lanes=pl.ds(h*HDIM,HDIM)
                gc=ga*sigs[i]*(1.0+tot[i]*(1.0-sigs[i]))
                gext[i,pl.ds(base,CHUNK),lanes]=gc
                for j in range(KERNEL):
                    win=ext[i,pl.ds(base+8-j,CHUNK),lanes]
                    prod=gc*win if j==0 else gc*win*taps[j-1]
                    gcw_ref[i,j:j+1,lanes]+=jnp.sum(prod,axis=0,keepdims=True)
        gb_ref[pl.ds(base,CHUNK),:]=jnp.concatenate(gbs,axis=1)
        for h in range(heads):
            for i in range(3):
                lanes=pl.ds(h*HDIM,HDIM)
                cw=cw_ref[i,:,lanes]
                total=cw[0:1]*gext[i,pl.ds(base,CHUNK),lanes]
                for j in range(1,KERNEL):
                    total=total+(cw[j:j+1]*cols[:,2+j:3+j])*gext[i,pl.ds(base+j,CHUNK),lanes]
                graw_ref[i,pl.ds(base,CHUNK),lanes]=total.astype(BF16)

def backward(raw, cw, gain, cols, gno, o, s, t, w, r, group):
    n=raw.shape[1]; heads=raw.shape[2]//HDIM; rows=group*CHUNK; width=heads*HDIM
    steps=n//rows
    row=lambda w: pl.BlockSpec((rows,w),lambda i:(steps-1-i,0))
    mat=pl.BlockSpec((group,heads,HDIM,HDIM),lambda i:(steps-1-i,0,0,0))
    full=lambda a: pl.BlockSpec(a.shape,lambda i:(0,0))
    prev=pl.BlockSpec((3,16,width),lambda i:(0,jnp.maximum((steps-1-i)*(rows//16)-1,0),0))
    return pl.pallas_call(functools.partial(bwd_kernel,heads,group),
        grid=(steps,),
        in_specs=[pl.BlockSpec((3,rows,width),lambda i:(0,steps-1-i,0)),prev,pl.BlockSpec(cw.shape,lambda i:(0,0,0)),full(gain),row(16),row(width),row(width),mat,mat,row(width),row(width)],
        out_specs=[pl.BlockSpec((3,rows,width),lambda i:(0,steps-1-i,0)),row(heads),pl.BlockSpec((3,KERNEL,width),lambda i:(0,0,0)),pl.BlockSpec((1,HDIM),lambda i:(0,0))],
        out_shape=[jax.ShapeDtypeStruct((3,n,width),BF16),jax.ShapeDtypeStruct((n,heads),F32),
            jax.ShapeDtypeStruct((3,KERNEL,width),F32),jax.ShapeDtypeStruct((1,HDIM),F32)],
        scratch_shapes=[pltpu.VMEM((3,rows+8,width),F32),pltpu.VMEM((3,rows+8,width),F32),pltpu.VMEM((heads,HDIM,HDIM),F32)],
        compiler_params=pltpu.CompilerParams(vmem_limit_bytes=48<<20),
    )(raw,raw,cw,gain,cols,gno,o,s,t,w,r)

def make_cols(starts, strength):
    n,heads=strength.shape
    blocks=n//BLOCK
    keep=starts[:blocks]; nxt=jnp.concatenate([starts[1:blocks],jnp.ones((1,),F32)])
    inside=jnp.arange(BLOCK)
    cols=[]
    for j in range(1,KERNEL):
        cols.append(jnp.where(inside[None,:]<j,keep[:,None],1.0).reshape(n))
    for j in range(1,KERNEL):
        cols.append(jnp.where(inside[None,:]>=BLOCK-j,nxt[:,None],1.0).reshape(n))
    pair=keep.reshape(-1,2)
    one=jnp.ones_like(pair[:,0])
    per=CHUNK//BLOCK
    cols.append(jnp.repeat(jnp.stack([one,pair[:,1]],axis=1).reshape(-1),BLOCK))
    cols.append(jnp.repeat(jnp.stack([pair[:,1],one],axis=1).reshape(-1),BLOCK))
    cols.append(jnp.repeat(pair[:,0],CHUNK))
    cols=jnp.stack(cols,axis=1)
    return jnp.concatenate([cols,strength,jnp.zeros((n,16-9-heads),F32)],axis=1)


def passed_along(block, axis, distance):
    devices = range(lax.axis_size(axis))
    route = [(i - distance, i) for i in devices if i - distance in devices]
    return lax.ppermute(block, axis, route)


def row_layout(lengths, positions):
    span_len = (lengths + BLOCK - 1) // BLOCK * BLOCK
    closing = jnp.cumsum(span_len)
    opening = closing - span_len
    bounds = jnp.concatenate([opening, closing[-1:]])
    reached = bounds[None, :] <= positions[:, None]
    doc_start = jnp.max(jnp.where(reached, bounds[None, :], 0), axis=1)
    inside = (positions[:, None] >= opening[None, :]) & (
        positions[:, None] < (opening + lengths)[None, :]
    )
    real_mask = jnp.any(inside, axis=1).astype(jnp.float32)
    return (doc_start, real_mask)


def local_span(carry_on, queries, keys_in, values, strength):
    head_count, token_count, head_width = queries.shape
    block_count = token_count // BLOCK

    def to_blocks(tensor):
        return tensor.reshape(head_count, block_count, BLOCK, -1).transpose(1, 0, 2, 3)

    def from_blocks(tensor):
        return tensor.transpose(1, 0, 2, 3).reshape(head_count, token_count, -1)

    strict_lower = jnp.tril(jnp.ones((BLOCK, BLOCK), jnp.float32), -1)
    causal = jnp.tril(jnp.ones((BLOCK, BLOCK), jnp.float32))
    identity = jnp.broadcast_to(
        jnp.eye(head_width, dtype=jnp.float32), (head_count, head_width, head_width)
    )

    def block_step(carried, block_in):
        memory, mapping = carried
        q_blk, k_blk, v_blk, s_blk, carry_flag = block_in
        write_rate = s_blk[..., 0]
        memory = memory * carry_flag
        mapping = mapping * carry_flag
        key_gram = jnp.einsum("hcp,hdp->hcd", k_blk, k_blk, precision=PRECISE)
        system = jnp.eye(BLOCK, dtype=jnp.float32) + strict_lower * (
            write_rate[:, :, None] * key_gram
        )
        right_side = jnp.concatenate(
            [write_rate[..., None] * k_blk, write_rate[..., None] * v_blk], axis=-1
        )
        solved = lax.linalg.triangular_solve(
            system, right_side, left_side=True, lower=True, unit_diagonal=True
        )
        w_mat = solved[..., :head_width]
        u_mat = solved[..., head_width:]
        corrected = u_mat - jnp.einsum("hcp,hpv->hcv", w_mat, memory, precision=PRECISE)
        scores = causal * jnp.einsum("hcp,hdp->hcd", q_blk, k_blk, precision=PRECISE)
        out_zero = jnp.einsum("hcp,hpv->hcv", q_blk, memory, precision=PRECISE)
        out_zero = out_zero + jnp.einsum("hcd,hdv->hcv", scores, corrected, precision=PRECISE)
        w_map = jnp.einsum("hcp,hpq->hcq", w_mat, mapping, precision=PRECISE)
        q_prop = jnp.einsum("hcp,hpq->hcq", q_blk, mapping, precision=PRECISE)
        q_prop = q_prop - jnp.einsum("hcd,hdq->hcq", scores, w_map, precision=PRECISE)
        memory = memory + jnp.einsum("hcp,hcv->hpv", k_blk, corrected, precision=PRECISE)
        mapping = mapping - jnp.einsum("hcp,hcq->hpq", k_blk, w_map, precision=PRECISE)
        return ((memory, mapping), (out_zero, q_prop))

    initial = (jnp.zeros((head_count, head_width, head_width), jnp.float32), identity)
    blocks = (
        to_blocks(queries),
        to_blocks(keys_in),
        to_blocks(values),
        to_blocks(strength[..., None]),
        carry_on,
    )
    (memory, mapping), (out_zero, q_prop) = lax.scan(block_step, initial, blocks)
    return (from_blocks(out_zero), from_blocks(q_prop), mapping, memory)


def span_forward(raw, conv_weight, out_gain, strength, taps, carry_on):
    tok_count = raw.shape[1]
    seq_count = lax.axis_size("seq")
    own_index = lax.axis_index("seq")
    head_count = conv_weight.shape[2] // HDIM
    rims = passed_along(raw[:, tok_count - KERNEL + 1 :, :], "seq", 1)
    extended = jnp.concatenate([rims, raw], axis=1).astype(jnp.float32)
    conv_sum = jnp.zeros(raw.shape, jnp.float32)
    for shift_no in range(KERNEL):
        window = extended[:, KERNEL - 1 - shift_no : KERNEL - 1 - shift_no + tok_count]
        conv_sum = (
            conv_sum
            + conv_weight[:, shift_no][:, None, :]
            * window
            * taps[shift_no][:tok_count][None, :, None]
        )
    conv_sig = jax.nn.sigmoid(conv_sum)
    split_heads = (
        (conv_sum * conv_sig).reshape(3, tok_count, head_count, HDIM).transpose(0, 2, 1, 3)
    )
    q_scale = lax.rsqrt(jnp.sum(split_heads[0] * split_heads[0], axis=-1, keepdims=True) + EPSILON)
    q_unit = split_heads[0] * q_scale
    queries = q_unit * HDIM ** (-0.5)
    k_scale = lax.rsqrt(jnp.sum(split_heads[1] * split_heads[1], axis=-1, keepdims=True) + EPSILON)
    keys_in = split_heads[1] * k_scale
    values = split_heads[2]
    (out_zero, q_prop, span_map, span_state), span_pullback = jax.vjp(
        partial(local_span, carry_on), queries, keys_in, values, strength.T
    )
    empty_state = jnp.zeros_like(span_state)
    all_maps, all_states = (
        lax.all_gather(span_map[None].astype(jnp.bfloat16), "seq", axis=0, tiled=True).astype(
            jnp.float32
        ),
        lax.all_gather(span_state[None].astype(jnp.bfloat16), "seq", axis=0, tiled=True).astype(
            jnp.float32
        ),
    )

    def fold_forward(counter, incoming):
        moved = (
            jnp.einsum("hpq,hqv->hpv", all_maps[counter], incoming, precision=PRECISE)
            + all_states[counter]
        )
        return jnp.where(counter < own_index, moved, incoming)

    state_in = lax.fori_loop(0, seq_count, fold_forward, empty_state)
    mixer = out_zero + jnp.einsum("htp,hpv->htv", q_prop, state_in, precision=PRECISE)
    stat_out = lax.rsqrt(jnp.mean(mixer * mixer, axis=-1, keepdims=True) + EPSILON)
    unit_out = mixer * stat_out
    normed_out = (
        (unit_out * out_gain).transpose(1, 0, 2).reshape(tok_count, -1).astype(jnp.bfloat16)
    )

    def pullback(grad_normed_out):
        grad_normed_out = grad_normed_out.astype(jnp.float32)
        grad_normed_out = grad_normed_out.reshape(tok_count, head_count, HDIM).transpose(1, 0, 2)
        out_gain_part = jnp.sum(grad_normed_out * unit_out, axis=(0, 1))
        grad_unit_out = grad_normed_out * out_gain
        grad_mixer = stat_out * (
            grad_unit_out - unit_out * jnp.mean(grad_unit_out * unit_out, axis=-1, keepdims=True)
        )
        local_grad = jnp.einsum("htp,htv->hpv", q_prop, grad_mixer, precision=PRECISE)
        grad_q_prop = jnp.einsum("htv,hpv->htp", grad_mixer, state_in, precision=PRECISE)
        all_grads = lax.all_gather(
            local_grad[None].astype(jnp.bfloat16), "seq", axis=0, tiled=True
        ).astype(jnp.float32)

        def fold_backward(counter, later_grad):
            source = seq_count - 1 - counter
            moved = (
                jnp.einsum("hqp,hqv->hpv", all_maps[source], later_grad, precision=PRECISE)
                + all_grads[source]
            )
            return jnp.where(source > own_index, moved, later_grad)

        grad_end = lax.fori_loop(0, seq_count, fold_backward, empty_state)
        grad_map = jnp.einsum("hpv,hqv->hpq", grad_end, state_in, precision=PRECISE)
        grad_queries, grad_keys, grad_values, grad_strength = span_pullback(
            (grad_mixer, grad_q_prop, grad_map, grad_end)
        )
        grad_q_unit = grad_queries * HDIM ** (-0.5)
        grad_q_raw = q_scale * (
            grad_q_unit - q_unit * jnp.sum(grad_q_unit * q_unit, axis=-1, keepdims=True)
        )
        grad_k_raw = k_scale * (
            grad_keys - keys_in * jnp.sum(grad_keys * keys_in, axis=-1, keepdims=True)
        )
        grad_act = (
            jnp.stack([grad_q_raw, grad_k_raw, grad_values])
            .transpose(0, 2, 1, 3)
            .reshape(3, tok_count, -1)
        )
        grad_conv_sum = grad_act * conv_sig * (1.0 + conv_sum * (1.0 - conv_sig))
        rims_back = passed_along(grad_conv_sum[:, : KERNEL - 1, :], "seq", -1)
        grad_ext = jnp.concatenate([grad_conv_sum, rims_back], axis=1)
        grad_raw = jnp.zeros(grad_conv_sum.shape, jnp.float32)
        conv_terms = []
        for shift_no in range(KERNEL):
            grad_raw = (
                grad_raw
                + conv_weight[:, shift_no][:, None, :]
                * grad_ext[:, shift_no : shift_no + tok_count]
                * taps[shift_no][shift_no : shift_no + tok_count][None, :, None]
            )
            window = extended[:, KERNEL - 1 - shift_no : KERNEL - 1 - shift_no + tok_count]
            conv_terms.append(
                jnp.sum(grad_conv_sum * window * taps[shift_no][:tok_count][None, :, None], axis=1)
            )
        grad_conv_part = jnp.stack(conv_terms, axis=1)
        return grad_raw.astype(jnp.bfloat16), grad_strength.T, grad_conv_part, out_gain_part

    return normed_out, pullback


def head_forward(raw, conv_weight, out_gain, strength, starts):
    width = conv_weight.shape[2] // lax.axis_size("seq")
    own_index = lax.axis_index("seq")

    def to_heads(block, axis, concat):
        return lax.all_to_all(block, "seq", split_axis=axis, concat_axis=concat, tiled=True)

    raw = to_heads(raw, 2, 1)
    own_conv = lax.dynamic_slice_in_dim(conv_weight, own_index * width, width, axis=2)
    cols = make_cols(starts, to_heads(strength, 1, 0))
    gain = out_gain[None, :]
    normed_out, *saved = forward(raw, own_conv, gain, cols, 2)

    def pullback(grad_normed_out):
        grad_raw, grad_strength, grad_conv, grad_gain = backward(
            raw, own_conv, gain, cols, to_heads(grad_normed_out, 1, 0), *saved, 2
        )
        grad_conv_part = lax.dynamic_update_slice_in_dim(
            jnp.zeros_like(conv_weight), grad_conv, own_index * width, axis=2
        )
        return to_heads(grad_raw, 1, 2), to_heads(grad_strength, 0, 1), grad_conv_part, grad_gain[0]

    return to_heads(normed_out, 0, 1), pullback


def shards(
    block_in,
    doc_lengths,
    attn_gain,
    qkv_weight,
    conv_weight,
    beta_weight,
    out_gain,
    out_weight,
    ffn_gain,
    gateup_weight,
    down_weight,
    cotangent,
):
    tok_count = block_in.shape[1]
    seq_count = lax.axis_size("seq")
    own_index = lax.axis_index("seq")
    head_count = conv_weight.shape[2] // HDIM
    residual_in = block_in[0].astype(jnp.float32)
    stat_in = lax.rsqrt(jnp.mean(residual_in * residual_in, axis=-1, keepdims=True) + EPSILON)
    unit_in = residual_in * stat_in
    normed = (unit_in * attn_gain).astype(jnp.bfloat16)
    gather = lambda weight: lax.all_gather(weight, ("seq", "row"), axis=1, tiled=True)
    qkv_full, beta_full, out_full, gateup_full, down_full = (
        gather(qkv_weight),
        gather(beta_weight),
        gather(out_weight),
        gather(gateup_weight),
        gather(down_weight),
    )
    raw = jnp.einsum("td,sdc->stc", normed, qkv_full, preferred_element_type=jnp.float32).astype(
        jnp.bfloat16
    )
    logits = jnp.einsum("td,hd->th", normed, beta_full, preferred_element_type=jnp.float32)
    beta_sig = jax.nn.sigmoid(logits)
    if head_count % seq_count == 0 and seq_count * tok_count % (2 * CHUNK) == 0:
        positions = jnp.arange(seq_count * tok_count, dtype=jnp.int32)
        doc_start, real_row = row_layout(doc_lengths[0], positions)
        real_mask = lax.dynamic_slice_in_dim(real_row, own_index * tok_count, tok_count)[:, None]
        starts = (doc_start[::BLOCK] != positions[::BLOCK]).astype(jnp.float32)
        normed_out, mixer_pullback = head_forward(
            raw, conv_weight, out_gain, beta_sig * real_mask, starts
        )
    else:
        positions = own_index * tok_count + jnp.arange(tok_count + KERNEL - 1, dtype=jnp.int32)
        doc_start, real_ext = row_layout(doc_lengths[0], positions)
        real_mask = real_ext[:tok_count, None]
        taps = [(positions - shift_no >= doc_start).astype(jnp.float32) for shift_no in range(KERNEL)]
        carry_on = (doc_start[:tok_count:BLOCK] != positions[:tok_count:BLOCK]).astype(jnp.float32)
        normed_out, mixer_pullback = span_forward(
            raw, conv_weight, out_gain, beta_sig * real_mask, taps, carry_on
        )
    branch_part = jnp.dot(normed_out, out_full, preferred_element_type=jnp.float32)
    hidden = residual_in + lax.psum(branch_part.astype(jnp.bfloat16), "mp").astype(jnp.float32)
    stat_mid = lax.rsqrt(jnp.mean(hidden * hidden, axis=-1, keepdims=True) + EPSILON)
    unit_mid = hidden * stat_mid
    normed_mid = (unit_mid * ffn_gain).astype(jnp.bfloat16)
    gate_up = jnp.einsum("td,sdf->stf", normed_mid, gateup_full, preferred_element_type=jnp.float32)
    gate_sig = jax.nn.sigmoid(gate_up[0])
    product = (gate_up[0] * gate_sig * gate_up[1]).astype(jnp.bfloat16)
    ffn_part = jnp.dot(product, down_full, preferred_element_type=jnp.float32)
    block_out = hidden + lax.psum(ffn_part.astype(jnp.bfloat16), "mp").astype(jnp.float32)
    grad_top = cotangent[0]
    grad_down_part = jnp.dot(product.T, grad_top, preferred_element_type=jnp.float32)
    grad_product = jnp.dot(grad_top, down_full.T, preferred_element_type=jnp.float32)
    grad_gate = grad_product * gate_up[1] * gate_sig * (1.0 + gate_up[0] * (1.0 - gate_sig))
    grad_up = grad_product * gate_up[0] * gate_sig
    grad_gate_up = jnp.stack([grad_gate, grad_up]).astype(jnp.bfloat16)
    grad_gateup_part = jnp.einsum(
        "td,stf->sdf", normed_mid, grad_gate_up, preferred_element_type=jnp.float32
    )
    grad_mid_part = jnp.einsum(
        "stf,sdf->td", grad_gate_up, gateup_full, preferred_element_type=jnp.float32
    )
    grad_mid = lax.psum(grad_mid_part.astype(jnp.bfloat16), "mp").astype(jnp.float32)
    ffn_gain_part = jnp.sum(grad_mid * unit_mid, axis=0)
    grad_unit_mid = grad_mid * ffn_gain
    grad_hidden = grad_top.astype(jnp.float32) + stat_mid * (
        grad_unit_mid - unit_mid * jnp.mean(grad_unit_mid * unit_mid, axis=-1, keepdims=True)
    )
    grad_branch = grad_hidden.astype(jnp.bfloat16)
    grad_out_part = jnp.dot(normed_out.T, grad_branch, preferred_element_type=jnp.float32)
    grad_normed_out = jnp.dot(grad_branch, out_full.T, preferred_element_type=jnp.float32)
    grad_raw_low, grad_strength, grad_conv_part, out_gain_part = mixer_pullback(
        grad_normed_out.astype(jnp.bfloat16)
    )
    grad_logits = (grad_strength * real_mask * beta_sig * (1.0 - beta_sig)).astype(jnp.bfloat16)
    grad_beta_part = jnp.einsum(
        "th,td->hd", grad_logits, normed, preferred_element_type=jnp.float32
    )
    grad_qkv_part = jnp.einsum(
        "td,stc->sdc", normed, grad_raw_low, preferred_element_type=jnp.float32
    )
    grad_normed = jnp.einsum(
        "stc,sdc->td", grad_raw_low, qkv_full, preferred_element_type=jnp.float32
    )
    grad_normed = grad_normed + jnp.einsum(
        "th,hd->td", grad_logits, beta_full, preferred_element_type=jnp.float32
    )
    grad_normed, out_gain_sum = (
        lax.psum(grad_normed.astype(jnp.bfloat16), "mp").astype(jnp.float32),
        lax.psum(out_gain_part, "mp"),
    )
    attn_gain_part = jnp.sum(grad_normed * unit_in, axis=0)
    grad_unit_in = grad_normed * attn_gain
    grad_input = grad_hidden + stat_in * (
        grad_unit_in - unit_in * jnp.mean(grad_unit_in * unit_in, axis=-1, keepdims=True)
    )

    def scatter(part):
        part = part.astype(jnp.bfloat16)
        part = lax.psum_scatter(part, ("seq", "row"), scatter_dimension=1, tiled=True)
        return part.astype(jnp.float32)

    weight_sums = (
        scatter(grad_qkv_part),
        scatter(grad_beta_part),
        scatter(grad_out_part),
        scatter(grad_gateup_part),
        scatter(grad_down_part),
    )
    small_sums = lax.psum(
        (attn_gain_part, grad_conv_part, out_gain_sum, ffn_gain_part), ("seq", "row")
    )
    return (
        block_out.astype(jnp.bfloat16)[None],
        grad_input[None],
        small_sums[0],
        weight_sums[0],
        small_sums[1],
        weight_sums[1],
        small_sums[2],
        weight_sums[2],
        small_sums[3],
        weight_sums[3],
        weight_sums[4],
    )


def solution(mesh):
    return jax.shard_map(
        shards,
        mesh=mesh,
        in_specs=(
            P("row", "seq", None),
            P("row", None),
            P(),
            P(None, ("seq", "row"), "mp"),
            P(None, None, "mp"),
            P("mp", ("seq", "row")),
            P(),
            P("mp", ("seq", "row")),
            P(),
            P(None, ("seq", "row"), "mp"),
            P("mp", ("seq", "row")),
            P("row", "seq", None),
        ),
        out_specs=(
            P("row", "seq", None),
            P("row", "seq", None),
            P(),
            P(None, ("seq", "row"), "mp"),
            P(None, None, "mp"),
            P("mp", ("seq", "row")),
            P(),
            P("mp", ("seq", "row")),
            P(),
            P(None, ("seq", "row"), "mp"),
            P("mp", ("seq", "row")),
        ),
        check_vma=False,
    )
```

```python
import functools
from functools import partial

import jax
import jax.numpy as jnp
from jax import lax
from jax.experimental import pallas as pl
from jax.experimental.pallas import tpu as pltpu
from jax.sharding import PartitionSpec as P

HDIM = 128
KERNEL = 4
BLOCK = 64
CHUNK = 128
EPSILON = 1e-06
PRECISE = lax.Precision.HIGHEST
F32 = jnp.float32
BF16 = jnp.bfloat16

NT=(((1,),(1,)),((),())); NN=(((1,),(0,)),((),())); TN=(((0,),(0,)),((),()))

def mm(a,b,dims=NN):
    return lax.dot_general(a.astype(BF16), b.astype(BF16), dims, preferred_element_type=F32)

def iotas():
    return lax.broadcasted_iota(jnp.int32,(CHUNK,CHUNK),0), lax.broadcasted_iota(jnp.int32,(CHUNK,CHUNK),1)

def inverses(below):
    r,c=iotas()
    done=[jnp.where(r==c,1.0,0.0)-jnp.where(r//2==c//2,a,0.0) for a in below]
    size=2
    while size<CHUNK:
        pairs=(r//(2*size)==c//(2*size))&(r//size!=c//size)
        half=[mm(jnp.where(pairs,a,0.0),t) for a,t in zip(below,done)]
        done=[t-mm(t,x) for t,x in zip(done,half)]
        size*=2
    return done

def conv_act(ext_ref, base, lanes, cw, taps):
    total=cw[0:1]*ext_ref[pl.ds(base+8,CHUNK),lanes]
    for j in range(1,KERNEL):
        total=total+(cw[j:j+1]*taps[j-1])*ext_ref[pl.ds(base+8-j,CHUNK),lanes]
    sig=jax.nn.sigmoid(total)
    return total,sig

def layout(keep_ref, count_ref, block):
    r,_=iotas()
    inside=r%BLOCK
    first=r<BLOCK
    keep0,keep1,after=keep_ref[block],keep_ref[block+1],keep_ref[block+2]
    here=jnp.where(first,keep0,keep1)
    later=jnp.where(first,keep1,after)
    taps=[jnp.where(inside<j,here,1.0) for j in range(1,KERNEL)]
    taps_later=[jnp.where(inside>=BLOCK-j,later,1.0) for j in range(1,KERNEL)]
    real=jnp.where(inside<jnp.where(first,count_ref[block],count_ref[block+1]),1.0,0.0)
    return taps,taps_later,jnp.where(first,1.0,keep1),jnp.where(first,keep1,1.0),real,keep0,keep1

def fwd_kernel(heads, group, keep_ref, count_ref, raw_ref, cw_ref, gain_ref, normed_ref, o_ref, s_ref, t_ref, w_ref, r_ref, ext, state):
    rows=group*CHUNK
    step=pl.program_id(0)
    @pl.when(step==0)
    def _():
        ext[0:8,:]=jnp.zeros((8,3*heads*HDIM),F32)
        state[...]=jnp.zeros(state.shape,F32)
    @pl.when(step>0)
    def _():
        ext[0:8,:]=ext[rows:rows+8,:]
    ext[8:,:]=raw_ref[:,0:3*heads*HDIM].astype(F32)
    r,c=iotas()
    width=heads*HDIM
    units=[]
    below=[]
    for g in range(group):
        base=g*CHUNK
        taps,_,m,m2,real,keep0,keep1=layout(keep_ref,count_ref,2*(step*group+g))
        sig_b=jax.nn.sigmoid(raw_ref[pl.ds(base,CHUNK),pl.ds(3*width,HDIM)].astype(F32))*real
        for h in range(heads):
            act=[]
            for s in range(3):
                lanes=pl.ds(s*width+h*HDIM,HDIM)
                total,sig=conv_act(ext,base,lanes,cw_ref[:,lanes],taps)
                act.append(total*sig)
            q=act[0]*(lax.rsqrt(jnp.sum(act[0]*act[0],axis=1,keepdims=True)+EPSILON)*HDIM**-0.5)
            k=act[1]*lax.rsqrt(jnp.sum(act[1]*act[1],axis=1,keepdims=True)+EPSILON)
            v=act[2]
            b=sig_b[:,h:h+1]
            gram=mm(k,k,NT)
            score=mm(q,k,NT)
            mask=jnp.where(c<BLOCK,m,1.0)
            a=jnp.where(r>c,b*gram*mask,0.0)
            l=jnp.where(r>=c,score*mask,0.0)
            below.append(a)
            units.append((g,h,q*m,k*m2,l,b*k,b*v,m,keep0,keep1))
    done=inverses(below)
    wus=[(mm(t,u[5])*u[7],mm(t,u[6])) for t,u in zip(done,units)]
    for t,(w,u),(g,h,q,k,l,_,_,_,keep0,keep1) in zip(done,wus,units):
        base=g*CHUNK
        out=(pl.ds(base,CHUNK),pl.ds(h*HDIM,HDIM))
        t_ref[g,h]=t.astype(BF16)
        w_ref[out]=w.astype(BF16)
        s=state[h]*keep0
        s_ref[g,h]=s.astype(BF16)
        rr=u-mm(w,s)
        o=mm(q,s)+mm(l,rr)
        state[h]=s*keep1+mm(k,rr,TN)
        r_ref[out]=rr.astype(BF16)
        o_ref[out]=o
        stat=lax.rsqrt(jnp.mean(o*o,axis=1,keepdims=True)+EPSILON)
        normed_ref[out]=(o*stat*gain_ref[...]).astype(BF16)

def forward(keep, count, raw, cw, gain, group):
    n=raw.shape[0]; width=cw.shape[1]//3; heads=width//HDIM; rows=group*CHUNK
    nc=n//CHUNK
    row=lambda w: pl.BlockSpec((rows,w),lambda i:(i,0))
    mat=pl.BlockSpec((group,heads,HDIM,HDIM),lambda i:(i,0,0,0))
    full=lambda a: pl.BlockSpec(a.shape,lambda i:(0,0))
    return pl.pallas_call(functools.partial(fwd_kernel,heads,group),
        grid=(n//rows,),
        in_specs=[pl.BlockSpec(memory_space=pltpu.SMEM)]*2+[row(raw.shape[1]),full(cw),full(gain)],
        out_specs=[row(width),row(width),mat,mat,row(width),row(width)],
        out_shape=[jax.ShapeDtypeStruct((n,width),BF16),jax.ShapeDtypeStruct((n,width),F32),
            jax.ShapeDtypeStruct((nc,heads,HDIM,HDIM),BF16),jax.ShapeDtypeStruct((nc,heads,HDIM,HDIM),BF16),
            jax.ShapeDtypeStruct((n,width),BF16),jax.ShapeDtypeStruct((n,width),BF16)],
        scratch_shapes=[pltpu.VMEM((rows+8,3*width),F32),pltpu.VMEM((heads,HDIM,HDIM),F32)],
        compiler_params=pltpu.CompilerParams(vmem_limit_bytes=48<<20),
    )(keep,count,raw,cw,gain)

def bwd_kernel(heads, group, keep_ref, count_ref, raw_ref, prev_ref, cw_ref, gain_ref, gno_ref, o_ref, s_ref, t_ref, w_ref, r_ref,
               graw_ref, gcw_ref, ggain_ref, ext, gext, grad_state):
    rows=group*CHUNK
    step=pl.program_id(0); steps=pl.num_programs(0)
    width=heads*HDIM
    @pl.when(step==0)
    def _():
        gext[rows:rows+8,:]=jnp.zeros((8,3*heads*HDIM),F32)
        grad_state[...]=jnp.zeros(grad_state.shape,F32)
        gcw_ref[...]=jnp.zeros(gcw_ref.shape,F32)
        ggain_ref[...]=jnp.zeros(ggain_ref.shape,F32)
    @pl.when(step>0)
    def _():
        gext[rows:rows+8,:]=gext[0:8,:]
    first=jnp.where(step==steps-1,0.0,1.0)
    ext[0:8,:]=prev_ref[:,0:3*width].astype(F32)[8:16]*first
    ext[8:,:]=raw_ref[:,0:3*heads*HDIM].astype(F32)
    r,c=iotas()
    units=[]
    for g in range(group-1,-1,-1):
        base=g*CHUNK
        taps,taps_later,m,m2,real,keep0,keep1=layout(keep_ref,count_ref,2*((steps-1-step)*group+g))
        beta=jax.nn.sigmoid(raw_ref[pl.ds(base,CHUNK),pl.ds(3*width,HDIM)].astype(F32))
        sig_b=beta*real
        for h in range(heads):
            out=(pl.ds(base,CHUNK),pl.ds(h*HDIM,HDIM))
            act=[];tot=[];sigs=[]
            for s in range(3):
                lanes=pl.ds(s*width+h*HDIM,HDIM)
                total,sig=conv_act(ext,base,lanes,cw_ref[:,lanes],taps)
                act.append(total*sig);tot.append(total);sigs.append(sig)
            rq=lax.rsqrt(jnp.sum(act[0]*act[0],axis=1,keepdims=True)+EPSILON)
            rk=lax.rsqrt(jnp.sum(act[1]*act[1],axis=1,keepdims=True)+EPSILON)
            qu=act[0]*rq
            o=o_ref[out]
            stat=lax.rsqrt(jnp.mean(o*o,axis=1,keepdims=True)+EPSILON)
            uo=o*stat
            gno=gno_ref[out].astype(F32)
            ggain_ref[...]+=jnp.sum(gno*uo,axis=0,keepdims=True)
            gu=gno*gain_ref[...]
            do=stat*(gu-uo*jnp.mean(gu*uo,axis=1,keepdims=True))
            units.append(dict(g=g,h=h,base=base,out=out,taps=taps,m=m,m2=m2,keep0=keep0,keep1=keep1,tot=tot,sigs=sigs,
                rq=rq,rk=rk,qu=qu,q=qu*HDIM**-0.5,k=act[1]*rk,v=act[2],b=sig_b[:,h:h+1],do=do,
                mask=jnp.where(c<BLOCK,m,1.0)))
        for u in units[-heads:]: u.update(taps_later=taps_later,beta=beta,sig_b=sig_b)
    for u in units: u['gram']=mm(u['k'],u['k'],NT)*u['mask']
    for u in units: u['l']=jnp.where(r>=c,mm(u['q'],u['k'],NT)*u['mask'],0.0)
    for u in units: u['dr0']=mm(u['l'],u['do'],TN)
    for u in units: u['ds0']=mm(u['q']*u['m'],u['do'],TN)
    for u in units:
        dsn=grad_state[u['h']]
        u['dsn']=dsn
        u['dr']=u['dr0']+u['m2']*mm(u['k'],dsn)
        ds=u['keep1']*dsn+u['ds0']-mm(w_ref[u['out']],u['dr'],TN)
        grad_state[u['h']]=u['keep0']*ds
    for u in units: u['df']=mm(t_ref[u['g'],u['h']],u['dr'],TN)
    for u in units: u['dl']=jnp.where(r>=c,mm(u['do'],r_ref[u['out']],NT)*u['mask'],0.0)
    for u in units: u['da']=jnp.where(r>c,-mm(u['df'],r_ref[u['out']],NT),0.0)
    for u in units:
        u['de']=u['b']*u['df']
        u['e']=u['v']-u['m']*mm(u['k'],s_ref[u['g'],u['h']])
        u['gb']=jnp.sum(u['df']*u['e']+u['da']*u['gram'],axis=1,keepdims=True)
        u['dkk']=u['b']*u['da']*u['mask']
    for u in units: u['dq']=u['m']*mm(u['do'],s_ref[u['g'],u['h']],NT)+mm(u['dl'],u['k'])
    for u in units:
        u['dk']=(mm(u['dl'],u['q'],TN)+u['m2']*mm(r_ref[u['out']],u['dsn'],NT)-u['m']*mm(u['de'],s_ref[u['g'],u['h']],NT)
            +mm(u['dkk'],u['k'])+mm(u['dkk'],u['k'],TN))
    for u in units:
        gq=u['dq']*HDIM**-0.5
        gq=u['rq']*(gq-u['qu']*jnp.sum(gq*u['qu'],axis=1,keepdims=True))
        gk=u['rk']*(u['dk']-u['k']*jnp.sum(u['dk']*u['k'],axis=1,keepdims=True))
        for i,ga in enumerate((gq,gk,u['de'])):
            lanes=pl.ds(i*width+u['h']*HDIM,HDIM)
            sig,tot=u['sigs'][i],u['tot'][i]
            gc=ga*sig*(1.0+tot*(1.0-sig))
            gext[pl.ds(u['base'],CHUNK),lanes]=gc
            for j in range(KERNEL):
                win=ext[pl.ds(u['base']+8-j,CHUNK),lanes]
                prod=gc*win if j==0 else gc*win*u['taps'][j-1]
                gcw_ref[j:j+1,lanes]+=jnp.sum(prod,axis=0,keepdims=True)
    for at in range(0,len(units),heads):
        glog=jnp.zeros((CHUNK,HDIM),F32)
        for u in units[at:at+heads]:
            glog=jnp.where(c==u['h'],u['gb'],glog)
            for i in range(3):
                lanes=pl.ds(i*width+u['h']*HDIM,HDIM)
                cw=cw_ref[:,lanes]
                total=cw[0:1]*gext[pl.ds(u['base'],CHUNK),lanes]
                for j in range(1,KERNEL):
                    total=total+(cw[j:j+1]*u['taps_later'][j-1])*gext[pl.ds(u['base']+j,CHUNK),lanes]
                graw_ref[pl.ds(u['base'],CHUNK),lanes]=total.astype(BF16)
        graw_ref[pl.ds(u['base'],CHUNK),pl.ds(3*width,HDIM)]=(glog*u['sig_b']*(1.0-u['beta'])).astype(BF16)

def backward(keep, count, raw, cw, gain, gno, o, s, t, w, r, group):
    n=raw.shape[0]; width=cw.shape[1]//3; heads=width//HDIM; rows=group*CHUNK
    steps=n//rows
    row=lambda w: pl.BlockSpec((rows,w),lambda i:(steps-1-i,0))
    mat=pl.BlockSpec((group,heads,HDIM,HDIM),lambda i:(steps-1-i,0,0,0))
    full=lambda a: pl.BlockSpec(a.shape,lambda i:(0,0))
    prev=pl.BlockSpec((16,raw.shape[1]),lambda i:(jnp.maximum((steps-1-i)*(rows//16)-1,0),0))
    return pl.pallas_call(functools.partial(bwd_kernel,heads,group),
        grid=(steps,),
        in_specs=[pl.BlockSpec(memory_space=pltpu.SMEM)]*2+[row(raw.shape[1]),prev,full(cw),full(gain),row(width),row(width),mat,mat,row(width),row(width)],
        out_specs=[row(raw.shape[1]),pl.BlockSpec((KERNEL,3*width),lambda i:(0,0)),pl.BlockSpec((1,HDIM),lambda i:(0,0))],
        out_shape=[jax.ShapeDtypeStruct(raw.shape,BF16),
            jax.ShapeDtypeStruct((KERNEL,3*width),F32),jax.ShapeDtypeStruct((1,HDIM),F32)],
        scratch_shapes=[pltpu.VMEM((rows+8,3*width),F32),pltpu.VMEM((rows+8,3*width),F32),pltpu.VMEM((heads,HDIM,HDIM),F32)],
        compiler_params=pltpu.CompilerParams(vmem_limit_bytes=48<<20),
    )(keep,count,raw,raw,cw,gain,gno,o,s,t,w,r)


def passed_along(block, axis, distance):
    devices = range(lax.axis_size(axis))
    route = [(i - distance, i) for i in devices if i - distance in devices]
    return lax.ppermute(block, axis, route)


def row_layout(lengths, positions):
    span_len = (lengths + BLOCK - 1) // BLOCK * BLOCK
    closing = jnp.cumsum(span_len)
    opening = closing - span_len
    bounds = jnp.concatenate([opening, closing[-1:]])
    reached = bounds[None, :] <= positions[:, None]
    doc_start = jnp.max(jnp.where(reached, bounds[None, :], 0), axis=1)
    inside = (positions[:, None] >= opening[None, :]) & (
        positions[:, None] < (opening + lengths)[None, :]
    )
    real_mask = jnp.any(inside, axis=1).astype(jnp.float32)
    return (doc_start, real_mask)


def local_span(carry_on, queries, keys_in, values, strength):
    head_count, token_count, head_width = queries.shape
    block_count = token_count // BLOCK

    def to_blocks(tensor):
        return tensor.reshape(head_count, block_count, BLOCK, -1).transpose(1, 0, 2, 3)

    def from_blocks(tensor):
        return tensor.transpose(1, 0, 2, 3).reshape(head_count, token_count, -1)

    strict_lower = jnp.tril(jnp.ones((BLOCK, BLOCK), jnp.float32), -1)
    causal = jnp.tril(jnp.ones((BLOCK, BLOCK), jnp.float32))
    identity = jnp.broadcast_to(
        jnp.eye(head_width, dtype=jnp.float32), (head_count, head_width, head_width)
    )

    def block_step(carried, block_in):
        memory, mapping = carried
        q_blk, k_blk, v_blk, s_blk, carry_flag = block_in
        write_rate = s_blk[..., 0]
        memory = memory * carry_flag
        mapping = mapping * carry_flag
        key_gram = jnp.einsum("hcp,hdp->hcd", k_blk, k_blk, precision=PRECISE)
        system = jnp.eye(BLOCK, dtype=jnp.float32) + strict_lower * (
            write_rate[:, :, None] * key_gram
        )
        right_side = jnp.concatenate(
            [write_rate[..., None] * k_blk, write_rate[..., None] * v_blk], axis=-1
        )
        solved = lax.linalg.triangular_solve(
            system, right_side, left_side=True, lower=True, unit_diagonal=True
        )
        w_mat = solved[..., :head_width]
        u_mat = solved[..., head_width:]
        corrected = u_mat - jnp.einsum("hcp,hpv->hcv", w_mat, memory, precision=PRECISE)
        scores = causal * jnp.einsum("hcp,hdp->hcd", q_blk, k_blk, precision=PRECISE)
        out_zero = jnp.einsum("hcp,hpv->hcv", q_blk, memory, precision=PRECISE)
        out_zero = out_zero + jnp.einsum("hcd,hdv->hcv", scores, corrected, precision=PRECISE)
        w_map = jnp.einsum("hcp,hpq->hcq", w_mat, mapping, precision=PRECISE)
        q_prop = jnp.einsum("hcp,hpq->hcq", q_blk, mapping, precision=PRECISE)
        q_prop = q_prop - jnp.einsum("hcd,hdq->hcq", scores, w_map, precision=PRECISE)
        memory = memory + jnp.einsum("hcp,hcv->hpv", k_blk, corrected, precision=PRECISE)
        mapping = mapping - jnp.einsum("hcp,hcq->hpq", k_blk, w_map, precision=PRECISE)
        return ((memory, mapping), (out_zero, q_prop))

    initial = (jnp.zeros((head_count, head_width, head_width), jnp.float32), identity)
    blocks = (
        to_blocks(queries),
        to_blocks(keys_in),
        to_blocks(values),
        to_blocks(strength[..., None]),
        carry_on,
    )
    (memory, mapping), (out_zero, q_prop) = lax.scan(block_step, initial, blocks)
    return (from_blocks(out_zero), from_blocks(q_prop), mapping, memory)


def spread_shards(
    block_in,
    doc_lengths,
    attn_gain,
    qkv_weight,
    conv_weight,
    beta_weight,
    out_gain,
    out_weight,
    ffn_gain,
    gateup_weight,
    down_weight,
    cotangent,
):
    tok_count = block_in.shape[1]
    seq_count = lax.axis_size("seq")
    own_index = lax.axis_index("seq")
    positions = own_index * tok_count + jnp.arange(tok_count + KERNEL - 1, dtype=jnp.int32)
    doc_start, real_ext = row_layout(doc_lengths[0], positions)
    real_mask = real_ext[:tok_count]
    taps = [(positions - shift_no >= doc_start).astype(jnp.float32) for shift_no in range(KERNEL)]
    carry_on = (doc_start[:tok_count:BLOCK] != positions[:tok_count:BLOCK]).astype(jnp.float32)
    residual_in = block_in[0].astype(jnp.float32)
    stat_in = lax.rsqrt(jnp.mean(residual_in * residual_in, axis=-1, keepdims=True) + EPSILON)
    unit_in = residual_in * stat_in
    normed = (unit_in * attn_gain).astype(jnp.bfloat16)
    qkv_full, beta_full, out_full, gateup_full, down_full = (
        lax.all_gather(qkv_weight, ("seq", "row"), axis=1, tiled=True),
        lax.all_gather(beta_weight, ("seq", "row"), axis=1, tiled=True),
        lax.all_gather(out_weight, ("seq", "row"), axis=1, tiled=True),
        lax.all_gather(gateup_weight, ("seq", "row"), axis=1, tiled=True),
        lax.all_gather(down_weight, ("seq", "row"), axis=1, tiled=True),
    )
    raw = jnp.einsum("td,sdc->stc", normed, qkv_full, preferred_element_type=jnp.float32).astype(
        jnp.bfloat16
    )
    rims = passed_along(raw[:, tok_count - KERNEL + 1 :, :], "seq", 1)
    extended = jnp.concatenate([rims, raw], axis=1).astype(jnp.float32)
    conv_sum = jnp.zeros(raw.shape, jnp.float32)
    for shift_no in range(KERNEL):
        window = extended[:, KERNEL - 1 - shift_no : KERNEL - 1 - shift_no + tok_count]
        conv_sum = (
            conv_sum
            + conv_weight[:, shift_no][:, None, :]
            * window
            * taps[shift_no][:tok_count][None, :, None]
        )
    conv_sig = jax.nn.sigmoid(conv_sum)
    head_count = conv_weight.shape[2] // HDIM
    split_heads = (
        (conv_sum * conv_sig).reshape(3, tok_count, head_count, HDIM).transpose(0, 2, 1, 3)
    )
    q_scale = lax.rsqrt(jnp.sum(split_heads[0] * split_heads[0], axis=-1, keepdims=True) + EPSILON)
    q_unit = split_heads[0] * q_scale
    queries = q_unit * HDIM ** (-0.5)
    k_scale = lax.rsqrt(jnp.sum(split_heads[1] * split_heads[1], axis=-1, keepdims=True) + EPSILON)
    keys_in = split_heads[1] * k_scale
    values = split_heads[2]
    logits = jnp.einsum("td,hd->ht", normed, beta_full, preferred_element_type=jnp.float32)
    beta_sig = jax.nn.sigmoid(logits)
    strength = beta_sig * real_mask[None, :]
    (out_zero, q_prop, span_map, span_state), span_pullback = jax.vjp(
        partial(local_span, carry_on), queries, keys_in, values, strength
    )
    empty_state = jnp.zeros_like(span_state)
    all_maps, all_states = (
        lax.all_gather(span_map[None].astype(jnp.bfloat16), "seq", axis=0, tiled=True).astype(
            jnp.float32
        ),
        lax.all_gather(span_state[None].astype(jnp.bfloat16), "seq", axis=0, tiled=True).astype(
            jnp.float32
        ),
    )

    def fold_forward(counter, incoming):
        moved = (
            jnp.einsum("hpq,hqv->hpv", all_maps[counter], incoming, precision=PRECISE)
            + all_states[counter]
        )
        return jnp.where(counter < own_index, moved, incoming)

    state_in = lax.fori_loop(0, seq_count, fold_forward, empty_state)
    mixer = out_zero + jnp.einsum("htp,hpv->htv", q_prop, state_in, precision=PRECISE)
    stat_out = lax.rsqrt(jnp.mean(mixer * mixer, axis=-1, keepdims=True) + EPSILON)
    unit_out = mixer * stat_out
    normed_out = (
        (unit_out * out_gain).transpose(1, 0, 2).reshape(tok_count, -1).astype(jnp.bfloat16)
    )
    branch_part = jnp.dot(normed_out, out_full, preferred_element_type=jnp.float32)
    hidden = residual_in + lax.psum(branch_part.astype(jnp.bfloat16), "mp").astype(jnp.float32)
    stat_mid = lax.rsqrt(jnp.mean(hidden * hidden, axis=-1, keepdims=True) + EPSILON)
    unit_mid = hidden * stat_mid
    normed_mid = (unit_mid * ffn_gain).astype(jnp.bfloat16)
    gate_up = jnp.einsum("td,sdf->stf", normed_mid, gateup_full, preferred_element_type=jnp.float32)
    gate_sig = jax.nn.sigmoid(gate_up[0])
    product = (gate_up[0] * gate_sig * gate_up[1]).astype(jnp.bfloat16)
    ffn_part = jnp.dot(product, down_full, preferred_element_type=jnp.float32)
    block_out = hidden + lax.psum(ffn_part.astype(jnp.bfloat16), "mp").astype(jnp.float32)
    qkv_full, beta_full, out_full, gateup_full, down_full = (
        lax.all_gather(qkv_weight, ("seq", "row"), axis=1, tiled=True),
        lax.all_gather(beta_weight, ("seq", "row"), axis=1, tiled=True),
        lax.all_gather(out_weight, ("seq", "row"), axis=1, tiled=True),
        lax.all_gather(gateup_weight, ("seq", "row"), axis=1, tiled=True),
        lax.all_gather(down_weight, ("seq", "row"), axis=1, tiled=True),
    )
    grad_top = cotangent[0]
    grad_down_part = jnp.dot(product.T, grad_top, preferred_element_type=jnp.float32)
    grad_product = jnp.dot(grad_top, down_full.T, preferred_element_type=jnp.float32)
    grad_gate = grad_product * gate_up[1] * gate_sig * (1.0 + gate_up[0] * (1.0 - gate_sig))
    grad_up = grad_product * gate_up[0] * gate_sig
    grad_gate_up = jnp.stack([grad_gate, grad_up]).astype(jnp.bfloat16)
    grad_gateup_part = jnp.einsum(
        "td,stf->sdf", normed_mid, grad_gate_up, preferred_element_type=jnp.float32
    )
    grad_mid_part = jnp.einsum(
        "stf,sdf->td", grad_gate_up, gateup_full, preferred_element_type=jnp.float32
    )
    grad_mid = lax.psum(grad_mid_part.astype(jnp.bfloat16), "mp").astype(jnp.float32)
    ffn_gain_part = jnp.sum(grad_mid * unit_mid, axis=0)
    grad_unit_mid = grad_mid * ffn_gain
    grad_hidden = grad_top.astype(jnp.float32) + stat_mid * (
        grad_unit_mid - unit_mid * jnp.mean(grad_unit_mid * unit_mid, axis=-1, keepdims=True)
    )
    grad_branch = grad_hidden.astype(jnp.bfloat16)
    grad_out_part = jnp.dot(normed_out.T, grad_branch, preferred_element_type=jnp.float32)
    grad_normed_out = jnp.dot(grad_branch, out_full.T, preferred_element_type=jnp.float32)
    grad_normed_out = grad_normed_out.reshape(tok_count, head_count, HDIM).transpose(1, 0, 2)
    out_gain_part = jnp.sum(grad_normed_out * unit_out, axis=(0, 1))
    grad_unit_out = grad_normed_out * out_gain
    grad_mixer = stat_out * (
        grad_unit_out - unit_out * jnp.mean(grad_unit_out * unit_out, axis=-1, keepdims=True)
    )
    local_grad = jnp.einsum("htp,htv->hpv", q_prop, grad_mixer, precision=PRECISE)
    grad_q_prop = jnp.einsum("htv,hpv->htp", grad_mixer, state_in, precision=PRECISE)
    all_grads = lax.all_gather(
        local_grad[None].astype(jnp.bfloat16), "seq", axis=0, tiled=True
    ).astype(jnp.float32)

    def fold_backward(counter, later_grad):
        source = seq_count - 1 - counter
        moved = (
            jnp.einsum("hqp,hqv->hpv", all_maps[source], later_grad, precision=PRECISE)
            + all_grads[source]
        )
        return jnp.where(source > own_index, moved, later_grad)

    grad_end = lax.fori_loop(0, seq_count, fold_backward, empty_state)
    grad_map = jnp.einsum("hpv,hqv->hpq", grad_end, state_in, precision=PRECISE)
    grad_queries, grad_keys, grad_values, grad_strength = span_pullback(
        (grad_mixer, grad_q_prop, grad_map, grad_end)
    )
    grad_logits = (grad_strength * real_mask[None, :] * beta_sig * (1.0 - beta_sig)).astype(
        jnp.bfloat16
    )
    grad_beta_part = jnp.einsum(
        "ht,td->hd", grad_logits, normed, preferred_element_type=jnp.float32
    )
    grad_q_unit = grad_queries * HDIM ** (-0.5)
    grad_q_raw = q_scale * (
        grad_q_unit - q_unit * jnp.sum(grad_q_unit * q_unit, axis=-1, keepdims=True)
    )
    grad_k_raw = k_scale * (
        grad_keys - keys_in * jnp.sum(grad_keys * keys_in, axis=-1, keepdims=True)
    )
    grad_act = (
        jnp.stack([grad_q_raw, grad_k_raw, grad_values])
        .transpose(0, 2, 1, 3)
        .reshape(3, tok_count, -1)
    )
    grad_conv_sum = grad_act * conv_sig * (1.0 + conv_sum * (1.0 - conv_sig))
    rims_back = passed_along(grad_conv_sum[:, : KERNEL - 1, :], "seq", -1)
    grad_ext = jnp.concatenate([grad_conv_sum, rims_back], axis=1)
    grad_raw = jnp.zeros(grad_conv_sum.shape, jnp.float32)
    conv_terms = []
    for shift_no in range(KERNEL):
        grad_raw = (
            grad_raw
            + conv_weight[:, shift_no][:, None, :]
            * grad_ext[:, shift_no : shift_no + tok_count]
            * taps[shift_no][shift_no : shift_no + tok_count][None, :, None]
        )
        window = extended[:, KERNEL - 1 - shift_no : KERNEL - 1 - shift_no + tok_count]
        conv_terms.append(
            jnp.sum(grad_conv_sum * window * taps[shift_no][:tok_count][None, :, None], axis=1)
        )
    grad_conv_part = jnp.stack(conv_terms, axis=1)
    grad_raw_low = grad_raw.astype(jnp.bfloat16)
    grad_qkv_part = jnp.einsum(
        "td,stc->sdc", normed, grad_raw_low, preferred_element_type=jnp.float32
    )
    grad_normed = jnp.einsum(
        "stc,sdc->td", grad_raw_low, qkv_full, preferred_element_type=jnp.float32
    )
    grad_normed = grad_normed + jnp.einsum(
        "ht,hd->td", grad_logits, beta_full, preferred_element_type=jnp.float32
    )
    grad_normed, out_gain_sum = (
        lax.psum(grad_normed.astype(jnp.bfloat16), "mp").astype(jnp.float32),
        lax.psum(out_gain_part.astype(jnp.bfloat16), "mp").astype(jnp.float32),
    )
    attn_gain_part = jnp.sum(grad_normed * unit_in, axis=0)
    grad_unit_in = grad_normed * attn_gain
    grad_input = grad_hidden + stat_in * (
        grad_unit_in - unit_in * jnp.mean(grad_unit_in * unit_in, axis=-1, keepdims=True)
    )
    weight_sums = (
        lax.psum_scatter(grad_qkv_part, ("seq", "row"), scatter_dimension=1, tiled=True),
        lax.psum_scatter(grad_beta_part, ("seq", "row"), scatter_dimension=1, tiled=True),
        lax.psum_scatter(grad_out_part, ("seq", "row"), scatter_dimension=1, tiled=True),
        lax.psum_scatter(grad_gateup_part, ("seq", "row"), scatter_dimension=1, tiled=True),
        lax.psum_scatter(grad_down_part, ("seq", "row"), scatter_dimension=1, tiled=True),
    )
    small_sums = lax.psum(
        (attn_gain_part, grad_conv_part, out_gain_sum, ffn_gain_part), ("seq", "row")
    )
    return (
        block_out.astype(jnp.bfloat16)[None],
        grad_input[None],
        small_sums[0],
        weight_sums[0],
        small_sums[1],
        weight_sums[1],
        small_sums[2],
        weight_sums[2],
        small_sums[3],
        weight_sums[3],
        weight_sums[4],
    )


def swapped(block):
    return lax.ppermute(block, "seq", [(0, 1), (1, 0)])


def across(block, bit):
    return lax.ppermute(block, "mp", [(i, i ^ bit) for i in range(4)])


def total_over(part, axis):
    size = lax.axis_size(axis)
    bit = 1
    while bit < size:
        part = part + lax.ppermute(part, axis, [(i, i ^ bit) for i in range(size)])
        bit *= 2
    return part


def sum_over_mp(parts):
    upper, lower = parts[0], parts[1]
    upper_in = [across(upper[1], 1), across(upper[3], 1)]
    lower_in = [across(lower[2], 2), across(lower[3], 2)]
    later = lambda mine, other: (mine.astype(F32) + other.astype(F32)).astype(BF16)
    upper_last = across(later(upper[2], upper_in[1]), 2)
    lower_last = across(later(lower[1], lower_in[1]), 1)
    add = lambda *terms: sum(term.astype(F32) for term in terms)
    return jnp.stack(
        [add(upper[0], upper_in[0], upper_last), add(lower[0], lower_in[0], lower_last)]
    )


def gather_over_mp(own):
    upper, lower = own[0], own[1]
    upper_one, lower_two = across(upper, 1), across(lower, 2)
    upper_two, lower_one = across(upper, 2), across(lower, 1)
    upper_three, lower_three = across(upper_one, 2), across(lower_two, 1)
    return jnp.stack(
        [
            jnp.stack([upper, upper_one, upper_two, upper_three]),
            jnp.stack([lower, lower_one, lower_two, lower_three]),
        ]
    )


def reordered(block, own):
    quarters = block.reshape(4, 2, -1, block.shape[-1])
    picked = [lax.dynamic_index_in_dim(quarters, own ^ j, 0, keepdims=False) for j in range(4)]
    return jnp.stack(picked, axis=1)


def restored(block, own):
    picked = [lax.dynamic_index_in_dim(block, own ^ j, 1, keepdims=False) for j in range(4)]
    return jnp.stack(picked).reshape(-1, block.shape[-1])


def in_order(mine, other, core, axis):
    first = jnp.where(core == 0, mine, other)
    second = jnp.where(core == 0, other, mine)
    return jnp.concatenate([first, second], axis=axis)


def halves(block, core, axis):
    size = block.shape[axis] // 2
    pick = lambda i: lax.dynamic_slice_in_dim(block, i * size, size, axis=axis)
    return pick(core), pick(1 - core)


def joined_shards(
    block_in,
    doc_lengths,
    attn_gain,
    qkv_weight,
    conv_weight,
    beta_weight,
    out_gain,
    out_weight,
    ffn_gain,
    gateup_weight,
    down_weight,
    cotangent,
):
    tok_count, model = block_in.shape[1:]
    core, own = lax.axis_index("seq"), lax.axis_index("mp")
    width = conv_weight.shape[2] // 2
    own_heads = width // HDIM
    quarter = tok_count // 4

    gather = lambda weight: lax.all_gather(weight, ("seq", "row"), axis=1, tiled=True)
    qkv_full, beta_full = gather(qkv_weight), gather(beta_weight)
    out_full, gateup_full, down_full = (
        gather(out_weight),
        gather(gateup_weight),
        gather(down_weight),
    )
    qkv_own = lax.dynamic_slice_in_dim(qkv_full, core * width, width, axis=2)
    beta_own = lax.dynamic_slice_in_dim(beta_full, core * own_heads, own_heads, axis=0)
    mix_weight = jnp.concatenate(
        [qkv_own[0], qkv_own[1], qkv_own[2], jnp.pad(beta_own.T, ((0, 0), (0, HDIM - own_heads)))],
        axis=1,
    )
    conv_own = lax.dynamic_slice_in_dim(conv_weight, core * width, width, axis=2)
    conv_own = conv_own.transpose(1, 0, 2).reshape(KERNEL, 3 * width)

    residual_in = block_in[0].astype(F32)
    stat_in = lax.rsqrt(jnp.mean(residual_in * residual_in, axis=-1, keepdims=True) + EPSILON)
    normed_mine = (residual_in * stat_in * attn_gain).astype(BF16)
    normed = in_order(normed_mine, swapped(normed_mine), core, 0)

    positions = jnp.arange(2 * tok_count, dtype=jnp.int32)
    doc_start, real_row = row_layout(doc_lengths[0], positions)
    keep = jnp.pad((doc_start[::BLOCK] != positions[::BLOCK]).astype(F32), (0, 1))
    count = jnp.sum(real_row.reshape(-1, BLOCK), axis=1).astype(jnp.int32)
    raw = jnp.dot(normed, mix_weight, preferred_element_type=F32).astype(BF16)
    gain = out_gain[None, :]
    group = 4 if raw.shape[0] % (4 * CHUNK) == 0 else 1
    heads_out, *saved = forward(keep, count, raw, conv_own, gain, group)

    mine, other = halves(heads_out, core, 0)
    normed_out = reordered(in_order(mine, swapped(other), core, 1), own)
    branch_part = jnp.einsum("hqtc,cd->hqtd", normed_out, out_full, preferred_element_type=F32)
    branch = sum_over_mp(branch_part.astype(BF16))
    own_rows = lambda block: lax.dynamic_slice_in_dim(
        block[0], own * quarter, quarter, axis=0
    ).reshape(2, -1, model)
    residual_own = own_rows(block_in).astype(F32)
    hidden = residual_own + branch
    stat_mid = lax.rsqrt(jnp.mean(hidden * hidden, axis=-1, keepdims=True) + EPSILON)
    unit_mid = hidden * stat_mid
    normed_mid = gather_over_mp((unit_mid * ffn_gain).astype(BF16)).reshape(tok_count, model)

    grad_top = reordered(cotangent[0], own).reshape(tok_count, model)
    gate_up = jnp.einsum("td,sdf->stf", normed_mid, gateup_full, preferred_element_type=F32)
    gate_sig = jax.nn.sigmoid(gate_up[0])
    product = (gate_up[0] * gate_sig * gate_up[1]).astype(BF16)
    grad_product = jnp.dot(grad_top, down_full.T, preferred_element_type=F32)
    grad_gate = grad_product * gate_up[1] * gate_sig * (1.0 + gate_up[0] * (1.0 - gate_sig))
    grad_up = grad_product * gate_up[0] * gate_sig
    grad_gate_up = jnp.stack([grad_gate, grad_up]).astype(BF16)
    grad_mid_part = jnp.einsum("stf,sdf->td", grad_gate_up, gateup_full, preferred_element_type=F32)
    local = lambda part: part.astype(BF16).reshape(2, 4, -1, model)
    grad_mid = sum_over_mp(local(grad_mid_part))
    ffn_gain_part = jnp.sum(grad_mid * unit_mid, axis=(0, 1))
    grad_unit_mid = grad_mid * ffn_gain
    grad_hidden = own_rows(cotangent).astype(F32) + stat_mid * (
        grad_unit_mid - unit_mid * jnp.mean(grad_unit_mid * unit_mid, axis=-1, keepdims=True)
    )
    grad_branch = gather_over_mp(grad_hidden.astype(BF16))
    grad_normed_out = jnp.einsum(
        "hqtd,cd->hqtc", grad_branch, out_full, preferred_element_type=F32
    ).astype(BF16)

    mine, other = halves(restored(grad_normed_out, own), core, 1)
    grad_heads = in_order(mine, swapped(other), core, 0)
    grad_raw, grad_conv_own, out_gain_part = backward(
        keep, count, raw, conv_own, gain, grad_heads, *saved, group
    )
    grad_normed = lax.dot_general(
        grad_raw, mix_weight, (((1,), (1,)), ((), ())), preferred_element_type=F32
    )
    mine, other = halves(grad_normed.astype(BF16), core, 0)
    grad_normed_sum = (mine.astype(F32) + swapped(other).astype(F32)).astype(BF16)
    grad_normed = sum_over_mp(reordered(grad_normed_sum, own))
    stat_own = lax.rsqrt(jnp.mean(residual_own * residual_own, axis=-1, keepdims=True) + EPSILON)
    unit_in = residual_own * stat_own
    attn_gain_part = jnp.sum(grad_normed * unit_in, axis=(0, 1))
    grad_unit_in = grad_normed * attn_gain
    grad_input = grad_hidden + stat_own * (
        grad_unit_in - unit_in * jnp.mean(grad_unit_in * unit_in, axis=-1, keepdims=True)
    )
    grad_input = restored(gather_over_mp(grad_input.astype(BF16)), own).astype(F32)

    ffn_part = jnp.dot(product, down_full, preferred_element_type=F32)
    block_out = (hidden + sum_over_mp(local(ffn_part))).astype(BF16)
    block_out = restored(gather_over_mp(block_out), own)

    def summed(part, axis):
        mine, other = halves(part.astype(BF16), core, axis)
        pair = (mine.astype(F32) + swapped(other).astype(F32)).astype(BF16)
        return lax.psum_scatter(pair, "row", scatter_dimension=axis, tiled=True).astype(F32)

    grad_down = summed(jnp.dot(product.T, grad_top, preferred_element_type=F32), 1)
    grad_gateup = summed(
        jnp.einsum("td,stf->sdf", normed_mid, grad_gate_up, preferred_element_type=F32), 1
    )
    grad_out = summed(
        jnp.einsum("hqtc,hqtd->cd", normed_out, grad_branch, preferred_element_type=F32), 1
    )
    grad_qkv = lax.dot_general(
        normed, grad_raw[:, : 3 * width], (((0,), (0,)), ((), ())), preferred_element_type=F32
    ).astype(BF16)
    grad_qkv = lax.psum_scatter(
        grad_qkv.reshape(2, -1, 3 * width), "row", scatter_dimension=1, tiled=True
    )
    mine, other = halves(grad_qkv, core, 0)
    by_kind = lambda part: part[0].reshape(-1, 3, width).transpose(1, 0, 2)
    grad_qkv = in_order(by_kind(mine), by_kind(swapped(other)), core, 2).astype(F32)
    grad_beta = lax.dot_general(
        grad_raw[:, 3 * width :], normed, (((0,), (0,)), ((), ())), preferred_element_type=F32
    )[:own_heads]

    per_head = jnp.concatenate([grad_conv_own.ravel(), grad_beta.ravel()]).reshape(-1, HDIM)
    per_head = total_over(per_head, "row")
    conv_size = grad_conv_own.size // HDIM

    def unpacked(flat):
        conv = flat[:conv_size].reshape(KERNEL, 3, width).transpose(1, 0, 2)
        return conv, flat[conv_size:].reshape(own_heads, model)

    conv_mine, beta_mine = unpacked(per_head)
    conv_other, beta_other = unpacked(swapped(per_head))
    grad_conv = in_order(conv_mine, conv_other, core, 2)
    grad_beta = in_order(beta_mine, beta_other, core, 0)
    span = beta_weight.shape[1]
    place_no = core * lax.axis_size("row") + lax.axis_index("row")
    grad_beta = lax.dynamic_slice_in_dim(grad_beta, place_no * span, span, axis=1)

    gains = jnp.concatenate([attn_gain_part, ffn_gain_part, out_gain_part[0]]).reshape(-1, HDIM)
    for axis in ("mp", "seq", "row"):
        gains = total_over(gains, axis)
    gains = gains.ravel()
    grad_attn_gain, grad_ffn_gain = gains[:model], gains[model : 2 * model]
    grad_out_gain = gains[2 * model :]
    return (
        block_out[None],
        grad_input[None],
        grad_attn_gain,
        grad_qkv,
        grad_conv,
        grad_beta,
        grad_out_gain,
        grad_out,
        grad_ffn_gain,
        grad_gateup,
        grad_down,
    )


def solution(mesh):
    rows = mesh.shape["row"]
    joined = mesh.shape["seq"] == 2 and mesh.shape["mp"] == 4 and rows & (rows - 1) == 0
    return jax.shard_map(
        joined_shards if joined else spread_shards,
        mesh=mesh,
        in_specs=(
            P("row", "seq", None),
            P("row", None),
            P(),
            P(None, ("seq", "row"), "mp"),
            P(None, None, "mp"),
            P("mp", ("seq", "row")),
            P(),
            P("mp", ("seq", "row")),
            P(),
            P(None, ("seq", "row"), "mp"),
            P("mp", ("seq", "row")),
            P("row", "seq", None),
        ),
        out_specs=(
            P("row", "seq", None),
            P("row", "seq", None),
            P(),
            P(None, ("seq", "row"), "mp"),
            P(None, None, "mp"),
            P("mp", ("seq", "row")),
            P(),
            P("mp", ("seq", "row")),
            P(),
            P(None, ("seq", "row"), "mp"),
            P("mp", ("seq", "row")),
        ),
        check_vma=False,
    )
```

```python
import functools
from functools import partial

import jax
import jax.numpy as jnp
from jax import lax
from jax.experimental import pallas as pl
from jax.experimental.pallas import tpu as pltpu
from jax.sharding import PartitionSpec as P

HDIM = 128
KERNEL = 4
BLOCK = 64
CHUNK = 128
EPSILON = 1e-06
PRECISE = lax.Precision.HIGHEST
F32 = jnp.float32
BF16 = jnp.bfloat16

NT=(((1,),(1,)),((),())); NN=(((1,),(0,)),((),())); TN=(((0,),(0,)),((),()))

def mm(a,b,dims=NN):
    return lax.dot_general(a.astype(BF16), b.astype(BF16), dims, preferred_element_type=F32)

def iotas():
    return lax.broadcasted_iota(jnp.int32,(CHUNK,CHUNK),0), lax.broadcasted_iota(jnp.int32,(CHUNK,CHUNK),1)

def inverses(below):
    r,c=iotas()
    done=[jnp.where(r==c,1.0,0.0)-jnp.where(r//2==c//2,a,0.0) for a in below]
    size=2
    while size<CHUNK:
        pairs=(r//(2*size)==c//(2*size))&(r//size!=c//size)
        half=[mm(jnp.where(pairs,a,0.0),t) for a,t in zip(below,done)]
        done=[t-mm(t,x) for t,x in zip(done,half)]
        size*=2
    return done

def conv_act(ext_ref, base, lanes, cw, taps):
    total=cw[0:1]*ext_ref[pl.ds(base+8,CHUNK),lanes]
    for j in range(1,KERNEL):
        total=total+(cw[j:j+1]*taps[j-1])*ext_ref[pl.ds(base+8-j,CHUNK),lanes]
    sig=jax.nn.sigmoid(total)
    return total,sig

def layout(keep_ref, count_ref, block):
    r,_=iotas()
    inside=r%BLOCK
    first=r<BLOCK
    keep0,keep1,after=keep_ref[block],keep_ref[block+1],keep_ref[block+2]
    here=jnp.where(first,keep0,keep1)
    later=jnp.where(first,keep1,after)
    taps=[jnp.where(inside<j,here,1.0) for j in range(1,KERNEL)]
    taps_later=[jnp.where(inside>=BLOCK-j,later,1.0) for j in range(1,KERNEL)]
    real=jnp.where(inside<jnp.where(first,count_ref[block],count_ref[block+1]),1.0,0.0)
    return taps,taps_later,jnp.where(first,1.0,keep1),jnp.where(first,keep1,1.0),real,keep0,keep1

def fwd_kernel(heads, group, keep_ref, count_ref, raw_ref, cw_ref, gain_ref, normed_ref, o_ref, s_ref, t_ref, w_ref, r_ref, ext, state):
    rows=group*CHUNK
    step=pl.program_id(0)
    @pl.when(step==0)
    def _():
        ext[0:8,:]=jnp.zeros((8,3*heads*HDIM),F32)
        state[...]=jnp.zeros(state.shape,F32)
    @pl.when(step>0)
    def _():
        ext[0:8,:]=ext[rows:rows+8,:]
    ext[8:,:]=raw_ref[:,0:3*heads*HDIM].astype(F32)
    r,c=iotas()
    width=heads*HDIM
    units=[]
    below=[]
    for g in range(group):
        base=g*CHUNK
        taps,_,m,m2,real,keep0,keep1=layout(keep_ref,count_ref,2*(step*group+g))
        sig_b=jax.nn.sigmoid(raw_ref[pl.ds(base,CHUNK),pl.ds(3*width,HDIM)].astype(F32))*real
        for h in range(heads):
            act=[]
            for s in range(3):
                lanes=pl.ds(s*width+h*HDIM,HDIM)
                total,sig=conv_act(ext,base,lanes,cw_ref[:,lanes],taps)
                act.append(total*sig)
            q=act[0]*(lax.rsqrt(jnp.sum(act[0]*act[0],axis=1,keepdims=True)+EPSILON)*HDIM**-0.5)
            k=act[1]*lax.rsqrt(jnp.sum(act[1]*act[1],axis=1,keepdims=True)+EPSILON)
            v=act[2]
            b=sig_b[:,h:h+1]
            gram=mm(k,k,NT)
            score=mm(q,k,NT)
            mask=jnp.where(c<BLOCK,m,1.0)
            a=jnp.where(r>c,b*gram*mask,0.0)
            l=jnp.where(r>=c,score*mask,0.0)
            below.append(a)
            units.append((g,h,q*m,k*m2,l,b*k,b*v,m,keep0,keep1))
    done=inverses(below)
    wus=[(mm(t,u[5])*u[7],mm(t,u[6])) for t,u in zip(done,units)]
    for t,(w,u),(g,h,q,k,l,_,_,_,keep0,keep1) in zip(done,wus,units):
        base=g*CHUNK
        out=(pl.ds(base,CHUNK),pl.ds(h*HDIM,HDIM))
        t_ref[g,h]=t.astype(BF16)
        w_ref[out]=w.astype(BF16)
        s=state[h]*keep0
        s_ref[g,h]=s.astype(BF16)
        rr=u-mm(w,s)
        o=mm(q,s)+mm(l,rr)
        state[h]=s*keep1+mm(k,rr,TN)
        r_ref[out]=rr.astype(BF16)
        o_ref[out]=o
        stat=lax.rsqrt(jnp.mean(o*o,axis=1,keepdims=True)+EPSILON)
        normed_ref[out]=(o*stat*gain_ref[...]).astype(BF16)

def forward(keep, count, raw, cw, gain, group):
    n=raw.shape[0]; width=cw.shape[1]//3; heads=width//HDIM; rows=group*CHUNK
    nc=n//CHUNK
    row=lambda w: pl.BlockSpec((rows,w),lambda i:(i,0))
    mat=pl.BlockSpec((group,heads,HDIM,HDIM),lambda i:(i,0,0,0))
    full=lambda a: pl.BlockSpec(a.shape,lambda i:(0,0))
    return pl.pallas_call(functools.partial(fwd_kernel,heads,group),
        grid=(n//rows,),
        in_specs=[pl.BlockSpec(memory_space=pltpu.SMEM)]*2+[row(raw.shape[1]),full(cw),full(gain)],
        out_specs=[row(width),row(width),mat,mat,row(width),row(width)],
        out_shape=[jax.ShapeDtypeStruct((n,width),BF16),jax.ShapeDtypeStruct((n,width),F32),
            jax.ShapeDtypeStruct((nc,heads,HDIM,HDIM),BF16),jax.ShapeDtypeStruct((nc,heads,HDIM,HDIM),BF16),
            jax.ShapeDtypeStruct((n,width),BF16),jax.ShapeDtypeStruct((n,width),BF16)],
        scratch_shapes=[pltpu.VMEM((rows+8,3*width),F32),pltpu.VMEM((heads,HDIM,HDIM),F32)],
        compiler_params=pltpu.CompilerParams(vmem_limit_bytes=48<<20),
        cost_estimate=pl.CostEstimate(flops=0,bytes_accessed=120<<20,transcendentals=0),
    )(keep,count,raw,cw,gain)

def bwd_kernel(heads, group, keep_ref, count_ref, raw_ref, prev_ref, cw_ref, gain_ref, gno_ref, o_ref, s_ref, t_ref, w_ref, r_ref, *rest):
    graw_ref, gcw_ref, ggain_ref, ext, gext, grad_state = rest[-6:]
    rows=group*CHUNK
    step=pl.program_id(0); steps=pl.num_programs(0)
    width=heads*HDIM
    @pl.when(step==0)
    def _():
        gext[rows:rows+8,:]=jnp.zeros((8,3*heads*HDIM),F32)
        grad_state[...]=jnp.zeros(grad_state.shape,F32)
        gcw_ref[...]=jnp.zeros(gcw_ref.shape,F32)
        ggain_ref[...]=jnp.zeros(ggain_ref.shape,F32)
    @pl.when(step>0)
    def _():
        gext[rows:rows+8,:]=gext[0:8,:]
    first=jnp.where(step==steps-1,0.0,1.0)
    ext[0:8,:]=prev_ref[:,0:3*width].astype(F32)[8:16]*first
    ext[8:,:]=raw_ref[:,0:3*heads*HDIM].astype(F32)
    r,c=iotas()
    units=[]
    for g in range(group-1,-1,-1):
        base=g*CHUNK
        taps,taps_later,m,m2,real,keep0,keep1=layout(keep_ref,count_ref,2*((steps-1-step)*group+g))
        beta=jax.nn.sigmoid(raw_ref[pl.ds(base,CHUNK),pl.ds(3*width,HDIM)].astype(F32))
        sig_b=beta*real
        for h in range(heads):
            out=(pl.ds(base,CHUNK),pl.ds(h*HDIM,HDIM))
            act=[];tot=[];sigs=[]
            for s in range(3):
                lanes=pl.ds(s*width+h*HDIM,HDIM)
                total,sig=conv_act(ext,base,lanes,cw_ref[:,lanes],taps)
                act.append(total*sig);tot.append(total);sigs.append(sig)
            rq=lax.rsqrt(jnp.sum(act[0]*act[0],axis=1,keepdims=True)+EPSILON)
            rk=lax.rsqrt(jnp.sum(act[1]*act[1],axis=1,keepdims=True)+EPSILON)
            qu=act[0]*rq
            o=o_ref[out]
            stat=lax.rsqrt(jnp.mean(o*o,axis=1,keepdims=True)+EPSILON)
            uo=o*stat
            gno=gno_ref[out].astype(F32)
            ggain_ref[...]+=jnp.sum(gno*uo,axis=0,keepdims=True)
            gu=gno*gain_ref[...]
            do=stat*(gu-uo*jnp.mean(gu*uo,axis=1,keepdims=True))
            units.append(dict(g=g,h=h,base=base,out=out,taps=taps,m=m,m2=m2,keep0=keep0,keep1=keep1,tot=tot,sigs=sigs,
                rq=rq,rk=rk,qu=qu,q=qu*HDIM**-0.5,k=act[1]*rk,v=act[2],b=sig_b[:,h:h+1],do=do,
                mask=jnp.where(c<BLOCK,m,1.0)))
        for u in units[-heads:]: u.update(taps_later=taps_later,beta=beta,sig_b=sig_b)
    for u in units: u['gram']=mm(u['k'],u['k'],NT)*u['mask']
    for u in units: u['l']=jnp.where(r>=c,mm(u['q'],u['k'],NT)*u['mask'],0.0)
    for u in units: u['dr0']=mm(u['l'],u['do'],TN)
    for u in units: u['ds0']=mm(u['q']*u['m'],u['do'],TN)
    for u in units:
        dsn=grad_state[u['h']]
        u['dsn']=dsn
        u['dr']=u['dr0']+u['m2']*mm(u['k'],dsn)
        ds=u['keep1']*dsn+u['ds0']-mm(w_ref[u['out']],u['dr'],TN)
        grad_state[u['h']]=u['keep0']*ds
    for u in units: u['df']=mm(t_ref[u['g'],u['h']],u['dr'],TN)
    for u in units: u['dl']=jnp.where(r>=c,mm(u['do'],r_ref[u['out']],NT)*u['mask'],0.0)
    for u in units: u['da']=jnp.where(r>c,-mm(u['df'],r_ref[u['out']],NT),0.0)
    for u in units:
        u['de']=u['b']*u['df']
        u['e']=u['v']-u['m']*mm(u['k'],s_ref[u['g'],u['h']])
        u['gb']=jnp.sum(u['df']*u['e']+u['da']*u['gram'],axis=1,keepdims=True)
        u['dkk']=u['b']*u['da']*u['mask']
    for u in units: u['dq']=u['m']*mm(u['do'],s_ref[u['g'],u['h']],NT)+mm(u['dl'],u['k'])
    for u in units:
        u['dk']=(mm(u['dl'],u['q'],TN)+u['m2']*mm(r_ref[u['out']],u['dsn'],NT)-u['m']*mm(u['de'],s_ref[u['g'],u['h']],NT)
            +mm(u['dkk'],u['k'])+mm(u['dkk'],u['k'],TN))
    for u in units:
        gq=u['dq']*HDIM**-0.5
        gq=u['rq']*(gq-u['qu']*jnp.sum(gq*u['qu'],axis=1,keepdims=True))
        gk=u['rk']*(u['dk']-u['k']*jnp.sum(u['dk']*u['k'],axis=1,keepdims=True))
        for i,ga in enumerate((gq,gk,u['de'])):
            lanes=pl.ds(i*width+u['h']*HDIM,HDIM)
            sig,tot=u['sigs'][i],u['tot'][i]
            gc=ga*sig*(1.0+tot*(1.0-sig))
            gext[pl.ds(u['base'],CHUNK),lanes]=gc
            for j in range(KERNEL):
                win=ext[pl.ds(u['base']+8-j,CHUNK),lanes]
                prod=gc*win if j==0 else gc*win*u['taps'][j-1]
                gcw_ref[j:j+1,lanes]+=jnp.sum(prod,axis=0,keepdims=True)
    for at in range(0,len(units),heads):
        glog=jnp.zeros((CHUNK,HDIM),F32)
        for u in units[at:at+heads]:
            glog=jnp.where(c==u['h'],u['gb'],glog)
            for i in range(3):
                lanes=pl.ds(i*width+u['h']*HDIM,HDIM)
                cw=cw_ref[:,lanes]
                total=cw[0:1]*gext[pl.ds(u['base'],CHUNK),lanes]
                for j in range(1,KERNEL):
                    total=total+(cw[j:j+1]*u['taps_later'][j-1])*gext[pl.ds(u['base']+j,CHUNK),lanes]
                graw_ref[pl.ds(u['base'],CHUNK),lanes]=total.astype(BF16)
        graw_ref[pl.ds(u['base'],CHUNK),pl.ds(3*width,HDIM)]=(glog*u['sig_b']*(1.0-u['beta'])).astype(BF16)

def backward(keep, count, raw, cw, gain, gno, o, s, t, w, r, group, dummies=()):
    n=raw.shape[0]; width=cw.shape[1]//3; heads=width//HDIM; rows=group*CHUNK
    steps=n//rows
    row=lambda w: pl.BlockSpec((rows,w),lambda i:(steps-1-i,0))
    mat=pl.BlockSpec((group,heads,HDIM,HDIM),lambda i:(steps-1-i,0,0,0))
    full=lambda a: pl.BlockSpec(a.shape,lambda i:(0,0))
    prev=pl.BlockSpec((16,raw.shape[1]),lambda i:(jnp.maximum((steps-1-i)*(rows//16)-1,0),0))
    return pl.pallas_call(functools.partial(bwd_kernel,heads,group),
        grid=(steps,),
        in_specs=[pl.BlockSpec(memory_space=pltpu.SMEM)]*2+[row(raw.shape[1]),prev,full(cw),full(gain),row(width),row(width),mat,mat,row(width),row(width)]+[pl.BlockSpec(memory_space=pl.ANY)]*len(dummies),
        out_specs=[row(raw.shape[1]),pl.BlockSpec((KERNEL,3*width),lambda i:(0,0)),pl.BlockSpec((1,HDIM),lambda i:(0,0))],
        out_shape=[jax.ShapeDtypeStruct(raw.shape,BF16),
            jax.ShapeDtypeStruct((KERNEL,3*width),F32),jax.ShapeDtypeStruct((1,HDIM),F32)],
        scratch_shapes=[pltpu.VMEM((rows+8,3*width),F32),pltpu.VMEM((rows+8,3*width),F32),pltpu.VMEM((heads,HDIM,HDIM),F32)],
        compiler_params=pltpu.CompilerParams(vmem_limit_bytes=48<<20),
        cost_estimate=pl.CostEstimate(flops=0,bytes_accessed=120<<20,transcendentals=0),
    )(keep,count,raw,raw,cw,gain,gno,o,s,t,w,r,*dummies)


def passed_along(block, axis, distance):
    devices = range(lax.axis_size(axis))
    route = [(i - distance, i) for i in devices if i - distance in devices]
    return lax.ppermute(block, axis, route)


def row_layout(lengths, positions):
    span_len = (lengths + BLOCK - 1) // BLOCK * BLOCK
    closing = jnp.cumsum(span_len)
    opening = closing - span_len
    bounds = jnp.concatenate([opening, closing[-1:]])
    reached = bounds[None, :] <= positions[:, None]
    doc_start = jnp.max(jnp.where(reached, bounds[None, :], 0), axis=1)
    inside = (positions[:, None] >= opening[None, :]) & (
        positions[:, None] < (opening + lengths)[None, :]
    )
    real_mask = jnp.any(inside, axis=1).astype(jnp.float32)
    return (doc_start, real_mask)


def local_span(carry_on, queries, keys_in, values, strength):
    head_count, token_count, head_width = queries.shape
    block_count = token_count // BLOCK

    def to_blocks(tensor):
        return tensor.reshape(head_count, block_count, BLOCK, -1).transpose(1, 0, 2, 3)

    def from_blocks(tensor):
        return tensor.transpose(1, 0, 2, 3).reshape(head_count, token_count, -1)

    strict_lower = jnp.tril(jnp.ones((BLOCK, BLOCK), jnp.float32), -1)
    causal = jnp.tril(jnp.ones((BLOCK, BLOCK), jnp.float32))
    identity = jnp.broadcast_to(
        jnp.eye(head_width, dtype=jnp.float32), (head_count, head_width, head_width)
    )

    def block_step(carried, block_in):
        memory, mapping = carried
        q_blk, k_blk, v_blk, s_blk, carry_flag = block_in
        write_rate = s_blk[..., 0]
        memory = memory * carry_flag
        mapping = mapping * carry_flag
        key_gram = jnp.einsum("hcp,hdp->hcd", k_blk, k_blk, precision=PRECISE)
        system = jnp.eye(BLOCK, dtype=jnp.float32) + strict_lower * (
            write_rate[:, :, None] * key_gram
        )
        right_side = jnp.concatenate(
            [write_rate[..., None] * k_blk, write_rate[..., None] * v_blk], axis=-1
        )
        solved = lax.linalg.triangular_solve(
            system, right_side, left_side=True, lower=True, unit_diagonal=True
        )
        w_mat = solved[..., :head_width]
        u_mat = solved[..., head_width:]
        corrected = u_mat - jnp.einsum("hcp,hpv->hcv", w_mat, memory, precision=PRECISE)
        scores = causal * jnp.einsum("hcp,hdp->hcd", q_blk, k_blk, precision=PRECISE)
        out_zero = jnp.einsum("hcp,hpv->hcv", q_blk, memory, precision=PRECISE)
        out_zero = out_zero + jnp.einsum("hcd,hdv->hcv", scores, corrected, precision=PRECISE)
        w_map = jnp.einsum("hcp,hpq->hcq", w_mat, mapping, precision=PRECISE)
        q_prop = jnp.einsum("hcp,hpq->hcq", q_blk, mapping, precision=PRECISE)
        q_prop = q_prop - jnp.einsum("hcd,hdq->hcq", scores, w_map, precision=PRECISE)
        memory = memory + jnp.einsum("hcp,hcv->hpv", k_blk, corrected, precision=PRECISE)
        mapping = mapping - jnp.einsum("hcp,hcq->hpq", k_blk, w_map, precision=PRECISE)
        return ((memory, mapping), (out_zero, q_prop))

    initial = (jnp.zeros((head_count, head_width, head_width), jnp.float32), identity)
    blocks = (
        to_blocks(queries),
        to_blocks(keys_in),
        to_blocks(values),
        to_blocks(strength[..., None]),
        carry_on,
    )
    (memory, mapping), (out_zero, q_prop) = lax.scan(block_step, initial, blocks)
    return (from_blocks(out_zero), from_blocks(q_prop), mapping, memory)


def spread_shards(
    block_in,
    doc_lengths,
    attn_gain,
    qkv_weight,
    conv_weight,
    beta_weight,
    out_gain,
    out_weight,
    ffn_gain,
    gateup_weight,
    down_weight,
    cotangent,
):
    tok_count = block_in.shape[1]
    seq_count = lax.axis_size("seq")
    own_index = lax.axis_index("seq")
    positions = own_index * tok_count + jnp.arange(tok_count + KERNEL - 1, dtype=jnp.int32)
    doc_start, real_ext = row_layout(doc_lengths[0], positions)
    real_mask = real_ext[:tok_count]
    taps = [(positions - shift_no >= doc_start).astype(jnp.float32) for shift_no in range(KERNEL)]
    carry_on = (doc_start[:tok_count:BLOCK] != positions[:tok_count:BLOCK]).astype(jnp.float32)
    residual_in = block_in[0].astype(jnp.float32)
    stat_in = lax.rsqrt(jnp.mean(residual_in * residual_in, axis=-1, keepdims=True) + EPSILON)
    unit_in = residual_in * stat_in
    normed = (unit_in * attn_gain).astype(jnp.bfloat16)
    qkv_full, beta_full, out_full, gateup_full, down_full = (
        lax.all_gather(qkv_weight, ("seq", "row"), axis=1, tiled=True),
        lax.all_gather(beta_weight, ("seq", "row"), axis=1, tiled=True),
        lax.all_gather(out_weight, ("seq", "row"), axis=1, tiled=True),
        lax.all_gather(gateup_weight, ("seq", "row"), axis=1, tiled=True),
        lax.all_gather(down_weight, ("seq", "row"), axis=1, tiled=True),
    )
    raw = jnp.einsum("td,sdc->stc", normed, qkv_full, preferred_element_type=jnp.float32).astype(
        jnp.bfloat16
    )
    rims = passed_along(raw[:, tok_count - KERNEL + 1 :, :], "seq", 1)
    extended = jnp.concatenate([rims, raw], axis=1).astype(jnp.float32)
    conv_sum = jnp.zeros(raw.shape, jnp.float32)
    for shift_no in range(KERNEL):
        window = extended[:, KERNEL - 1 - shift_no : KERNEL - 1 - shift_no + tok_count]
        conv_sum = (
            conv_sum
            + conv_weight[:, shift_no][:, None, :]
            * window
            * taps[shift_no][:tok_count][None, :, None]
        )
    conv_sig = jax.nn.sigmoid(conv_sum)
    head_count = conv_weight.shape[2] // HDIM
    split_heads = (
        (conv_sum * conv_sig).reshape(3, tok_count, head_count, HDIM).transpose(0, 2, 1, 3)
    )
    q_scale = lax.rsqrt(jnp.sum(split_heads[0] * split_heads[0], axis=-1, keepdims=True) + EPSILON)
    q_unit = split_heads[0] * q_scale
    queries = q_unit * HDIM ** (-0.5)
    k_scale = lax.rsqrt(jnp.sum(split_heads[1] * split_heads[1], axis=-1, keepdims=True) + EPSILON)
    keys_in = split_heads[1] * k_scale
    values = split_heads[2]
    logits = jnp.einsum("td,hd->ht", normed, beta_full, preferred_element_type=jnp.float32)
    beta_sig = jax.nn.sigmoid(logits)
    strength = beta_sig * real_mask[None, :]
    (out_zero, q_prop, span_map, span_state), span_pullback = jax.vjp(
        partial(local_span, carry_on), queries, keys_in, values, strength
    )
    empty_state = jnp.zeros_like(span_state)
    all_maps, all_states = (
        lax.all_gather(span_map[None].astype(jnp.bfloat16), "seq", axis=0, tiled=True).astype(
            jnp.float32
        ),
        lax.all_gather(span_state[None].astype(jnp.bfloat16), "seq", axis=0, tiled=True).astype(
            jnp.float32
        ),
    )

    def fold_forward(counter, incoming):
        moved = (
            jnp.einsum("hpq,hqv->hpv", all_maps[counter], incoming, precision=PRECISE)
            + all_states[counter]
        )
        return jnp.where(counter < own_index, moved, incoming)

    state_in = lax.fori_loop(0, seq_count, fold_forward, empty_state)
    mixer = out_zero + jnp.einsum("htp,hpv->htv", q_prop, state_in, precision=PRECISE)
    stat_out = lax.rsqrt(jnp.mean(mixer * mixer, axis=-1, keepdims=True) + EPSILON)
    unit_out = mixer * stat_out
    normed_out = (
        (unit_out * out_gain).transpose(1, 0, 2).reshape(tok_count, -1).astype(jnp.bfloat16)
    )
    branch_part = jnp.dot(normed_out, out_full, preferred_element_type=jnp.float32)
    hidden = residual_in + lax.psum(branch_part.astype(jnp.bfloat16), "mp").astype(jnp.float32)
    stat_mid = lax.rsqrt(jnp.mean(hidden * hidden, axis=-1, keepdims=True) + EPSILON)
    unit_mid = hidden * stat_mid
    normed_mid = (unit_mid * ffn_gain).astype(jnp.bfloat16)
    gate_up = jnp.einsum("td,sdf->stf", normed_mid, gateup_full, preferred_element_type=jnp.float32)
    gate_sig = jax.nn.sigmoid(gate_up[0])
    product = (gate_up[0] * gate_sig * gate_up[1]).astype(jnp.bfloat16)
    ffn_part = jnp.dot(product, down_full, preferred_element_type=jnp.float32)
    block_out = hidden + lax.psum(ffn_part.astype(jnp.bfloat16), "mp").astype(jnp.float32)
    qkv_full, beta_full, out_full, gateup_full, down_full = (
        lax.all_gather(qkv_weight, ("seq", "row"), axis=1, tiled=True),
        lax.all_gather(beta_weight, ("seq", "row"), axis=1, tiled=True),
        lax.all_gather(out_weight, ("seq", "row"), axis=1, tiled=True),
        lax.all_gather(gateup_weight, ("seq", "row"), axis=1, tiled=True),
        lax.all_gather(down_weight, ("seq", "row"), axis=1, tiled=True),
    )
    grad_top = cotangent[0]
    grad_down_part = jnp.dot(product.T, grad_top, preferred_element_type=jnp.float32)
    grad_product = jnp.dot(grad_top, down_full.T, preferred_element_type=jnp.float32)
    grad_gate = grad_product * gate_up[1] * gate_sig * (1.0 + gate_up[0] * (1.0 - gate_sig))
    grad_up = grad_product * gate_up[0] * gate_sig
    grad_gate_up = jnp.stack([grad_gate, grad_up]).astype(jnp.bfloat16)
    grad_gateup_part = jnp.einsum(
        "td,stf->sdf", normed_mid, grad_gate_up, preferred_element_type=jnp.float32
    )
    grad_mid_part = jnp.einsum(
        "stf,sdf->td", grad_gate_up, gateup_full, preferred_element_type=jnp.float32
    )
    grad_mid = lax.psum(grad_mid_part.astype(jnp.bfloat16), "mp").astype(jnp.float32)
    ffn_gain_part = jnp.sum(grad_mid * unit_mid, axis=0)
    grad_unit_mid = grad_mid * ffn_gain
    grad_hidden = grad_top.astype(jnp.float32) + stat_mid * (
        grad_unit_mid - unit_mid * jnp.mean(grad_unit_mid * unit_mid, axis=-1, keepdims=True)
    )
    grad_branch = grad_hidden.astype(jnp.bfloat16)
    grad_out_part = jnp.dot(normed_out.T, grad_branch, preferred_element_type=jnp.float32)
    grad_normed_out = jnp.dot(grad_branch, out_full.T, preferred_element_type=jnp.float32)
    grad_normed_out = grad_normed_out.reshape(tok_count, head_count, HDIM).transpose(1, 0, 2)
    out_gain_part = jnp.sum(grad_normed_out * unit_out, axis=(0, 1))
    grad_unit_out = grad_normed_out * out_gain
    grad_mixer = stat_out * (
        grad_unit_out - unit_out * jnp.mean(grad_unit_out * unit_out, axis=-1, keepdims=True)
    )
    local_grad = jnp.einsum("htp,htv->hpv", q_prop, grad_mixer, precision=PRECISE)
    grad_q_prop = jnp.einsum("htv,hpv->htp", grad_mixer, state_in, precision=PRECISE)
    all_grads = lax.all_gather(
        local_grad[None].astype(jnp.bfloat16), "seq", axis=0, tiled=True
    ).astype(jnp.float32)

    def fold_backward(counter, later_grad):
        source = seq_count - 1 - counter
        moved = (
            jnp.einsum("hqp,hqv->hpv", all_maps[source], later_grad, precision=PRECISE)
            + all_grads[source]
        )
        return jnp.where(source > own_index, moved, later_grad)

    grad_end = lax.fori_loop(0, seq_count, fold_backward, empty_state)
    grad_map = jnp.einsum("hpv,hqv->hpq", grad_end, state_in, precision=PRECISE)
    grad_queries, grad_keys, grad_values, grad_strength = span_pullback(
        (grad_mixer, grad_q_prop, grad_map, grad_end)
    )
    grad_logits = (grad_strength * real_mask[None, :] * beta_sig * (1.0 - beta_sig)).astype(
        jnp.bfloat16
    )
    grad_beta_part = jnp.einsum(
        "ht,td->hd", grad_logits, normed, preferred_element_type=jnp.float32
    )
    grad_q_unit = grad_queries * HDIM ** (-0.5)
    grad_q_raw = q_scale * (
        grad_q_unit - q_unit * jnp.sum(grad_q_unit * q_unit, axis=-1, keepdims=True)
    )
    grad_k_raw = k_scale * (
        grad_keys - keys_in * jnp.sum(grad_keys * keys_in, axis=-1, keepdims=True)
    )
    grad_act = (
        jnp.stack([grad_q_raw, grad_k_raw, grad_values])
        .transpose(0, 2, 1, 3)
        .reshape(3, tok_count, -1)
    )
    grad_conv_sum = grad_act * conv_sig * (1.0 + conv_sum * (1.0 - conv_sig))
    rims_back = passed_along(grad_conv_sum[:, : KERNEL - 1, :], "seq", -1)
    grad_ext = jnp.concatenate([grad_conv_sum, rims_back], axis=1)
    grad_raw = jnp.zeros(grad_conv_sum.shape, jnp.float32)
    conv_terms = []
    for shift_no in range(KERNEL):
        grad_raw = (
            grad_raw
            + conv_weight[:, shift_no][:, None, :]
            * grad_ext[:, shift_no : shift_no + tok_count]
            * taps[shift_no][shift_no : shift_no + tok_count][None, :, None]
        )
        window = extended[:, KERNEL - 1 - shift_no : KERNEL - 1 - shift_no + tok_count]
        conv_terms.append(
            jnp.sum(grad_conv_sum * window * taps[shift_no][:tok_count][None, :, None], axis=1)
        )
    grad_conv_part = jnp.stack(conv_terms, axis=1)
    grad_raw_low = grad_raw.astype(jnp.bfloat16)
    grad_qkv_part = jnp.einsum(
        "td,stc->sdc", normed, grad_raw_low, preferred_element_type=jnp.float32
    )
    grad_normed = jnp.einsum(
        "stc,sdc->td", grad_raw_low, qkv_full, preferred_element_type=jnp.float32
    )
    grad_normed = grad_normed + jnp.einsum(
        "ht,hd->td", grad_logits, beta_full, preferred_element_type=jnp.float32
    )
    grad_normed, out_gain_sum = (
        lax.psum(grad_normed.astype(jnp.bfloat16), "mp").astype(jnp.float32),
        lax.psum(out_gain_part.astype(jnp.bfloat16), "mp").astype(jnp.float32),
    )
    attn_gain_part = jnp.sum(grad_normed * unit_in, axis=0)
    grad_unit_in = grad_normed * attn_gain
    grad_input = grad_hidden + stat_in * (
        grad_unit_in - unit_in * jnp.mean(grad_unit_in * unit_in, axis=-1, keepdims=True)
    )
    weight_sums = (
        lax.psum_scatter(grad_qkv_part, ("seq", "row"), scatter_dimension=1, tiled=True),
        lax.psum_scatter(grad_beta_part, ("seq", "row"), scatter_dimension=1, tiled=True),
        lax.psum_scatter(grad_out_part, ("seq", "row"), scatter_dimension=1, tiled=True),
        lax.psum_scatter(grad_gateup_part, ("seq", "row"), scatter_dimension=1, tiled=True),
        lax.psum_scatter(grad_down_part, ("seq", "row"), scatter_dimension=1, tiled=True),
    )
    small_sums = lax.psum(
        (attn_gain_part, grad_conv_part, out_gain_sum, ffn_gain_part), ("seq", "row")
    )
    return (
        block_out.astype(jnp.bfloat16)[None],
        grad_input[None],
        small_sums[0],
        weight_sums[0],
        small_sums[1],
        weight_sums[1],
        small_sums[2],
        weight_sums[2],
        small_sums[3],
        weight_sums[3],
        weight_sums[4],
    )


MESH = pl.DeviceIdType.MESH
STRIP = 16


def phase_kernel(middle, both_cores, small_sum, n_in, n_out, part_ref, *refs):
    inputs, all_ref = refs[:n_in], refs[n_in]
    outs, scratch = refs[n_in + 1 : n_in + n_out], refs[n_in + n_out :]
    got, sums, gain_sum, send_sem, recv_sem = scratch[:5]
    count = all_ref.shape[0]
    rows = count // 8
    place, core, row = lax.axis_index("mp"), lax.axis_index("seq"), lax.axis_index("row")
    across_x = place + 1 - 2 * (place % 2)
    across_y = (place + 2) % 4
    across_both = 3 - place
    ways = {"x": {"mp": across_x}, "y": {"mp": across_y}}
    if both_cores or small_sum:
        ways["core"] = {"seq": 1 - core}
    steps = []
    if small_sum:
        bit = 1
        while bit < lax.axis_size("row"):
            steps.append(f"row{bit}")
            ways[steps[-1]] = {"row": row + bit - 2 * bit * ((row // bit) % 2)}
            bit *= 2
        steps += ["core", "x", "y"]
    barrier = pltpu.get_barrier_semaphore()
    for other in ways.values():
        pl.semaphore_signal(barrier, inc=1, device_id=other, device_id_type=MESH)
    pl.semaphore_wait(barrier, len(ways))

    def copy(index, source, target, way):
        return pltpu.make_async_remote_copy(
            src_ref=source,
            dst_ref=target,
            send_sem=send_sem.at[index],
            recv_sem=recv_sem.at[index],
            device_id=ways[way],
            device_id_type=MESH,
        )

    def block(of, half):
        return pl.ds(pl.multiple_of((2 * of + half) * rows, rows), rows)

    def strips(body):
        @pl.loop(0, rows // STRIP)
        def _(i):
            body(pl.multiple_of(i * STRIP, STRIP))

    order = [(across_both, 0), (across_both, 1), (across_x, 0), (across_y, 1)]
    order += [(across_y, 0), (across_x, 1), (place, 0), (place, 1)]
    if both_cores:
        part, incoming, local_sem = scratch[5:8]
        mine = pltpu.make_async_copy(part_ref.at[pl.ds(core * count, count)], part, local_sem)
        mine.start()
        shared = []
        for i, (of, half) in enumerate(order):
            start = pl.multiple_of((1 - core) * count + (2 * of + half) * rows, rows)
            shared.append(
                copy(12 + i, part_ref.at[pl.ds(start, rows)], incoming.at[block(of, half)], "core")
            )
            shared[-1].start()
        mine.wait()
    else:
        part = part_ref

    def ready(index):
        if both_cores:
            of, half = order[index]
            shared[index].wait_recv()

            def add(at):
                strip = pl.ds((2 * of + half) * rows + at, STRIP)
                part[strip, :] = (
                    part[strip, :].astype(F32) + incoming[strip, :].astype(F32)
                ).astype(BF16)

            strips(add)

    far = [
        copy(0, part.at[block(across_both, 0)], got.at[0], "x"),
        copy(1, part.at[block(across_both, 1)], got.at[1], "y"),
    ]
    near = [
        copy(2, part.at[block(across_x, 0)], got.at[2], "x"),
        copy(3, part.at[block(across_y, 1)], got.at[3], "y"),
    ]
    last = [copy(4, sums.at[0], got.at[4], "y"), copy(5, sums.at[1], got.at[5], "x")]
    own = [all_ref.at[block(place, 0)], all_ref.at[block(place, 1)]]
    passed = [all_ref.at[block(across_x, 0)], all_ref.at[block(across_y, 1)]]
    out_first = [copy(6, own[0], own[0], "x"), copy(7, own[1], own[1], "y")]
    out_second = [copy(8, own[0], own[0], "y"), copy(9, own[1], own[1], "x")]
    out_third = [copy(10, passed[0], passed[0], "y"), copy(11, passed[1], passed[1], "x")]

    for index, step in enumerate((*far, *near)):
        ready(index)
        step.start()
    gain_sum[...] = jnp.zeros_like(gain_sum)
    for half, onward in ((0, across_y), (1, across_x)):
        ready(4 + half)
        far[half].wait_recv()

        def add(at):
            strip = pl.ds(at, STRIP)
            mine = part[pl.ds((2 * onward + half) * rows + at, STRIP), :]
            sums[half, strip, :] = (mine.astype(F32) + got[half, strip, :].astype(F32)).astype(BF16)

        strips(add)
        last[half].start()
    for half in (0, 1):
        ready(6 + half)
        near[half].wait_recv()
        last[half].wait_recv()

        def finish(at):
            strip = pl.ds(at, STRIP)
            total = part[pl.ds((2 * place + half) * rows + at, STRIP), :].astype(F32)
            total = total + got[2 + half, strip, :].astype(F32)
            total = total + got[4 + half, strip, :].astype(F32)
            result = middle(total, half, strip, inputs, outs, gain_sum)
            all_ref[pl.ds((2 * place + half) * rows + at, STRIP), :] = result.astype(BF16)

        strips(finish)
        out_first[half].start()
        out_second[half].start()

    gain = jnp.sum(gain_sum[...], axis=0, keepdims=True)
    small = []
    if small_sum:
        values, arrived = outs[-1], scratch[-1]
        values[...] = inputs[-1 - small_sum["dummies"]][...]
        values[0:1, :] = gain
    elif n_out > 2:
        outs[-1][...] = gain

    def small_step(number):
        height = 8 if steps[number] in ("x", "y") else values.shape[0]
        step = copy(
            20 + number,
            arrived.at[number, 1, pl.ds(0, height)],
            arrived.at[number, 0, pl.ds(0, height)],
            steps[number],
        )
        arrived[number, 1, 0:height, :] = values[0:height, :]
        step.start()
        step.wait_recv()
        values[0:height, :] = values[0:height, :] + arrived[number, 0, 0:height, :]
        small.append(step)

    for half in (0, 1):
        out_first[half].wait_recv()
        out_third[half].start()
    if small_sum:
        for number in range(len(steps)):
            small_step(number)
    for step in (*out_second, *out_third):
        step.wait_recv()
    for step in (*far, *near, *last, *out_first, *out_second, *out_third, *small):
        step.wait_send()
    if both_cores:
        for step in shared:
            step.wait_send()


def normed_forward(total, half, strip, inputs, outs, gain_sum):
    residual, gain = inputs[:2]
    hidden = residual[half, strip, :].astype(F32) + total
    outs[0][half, strip, :] = hidden
    stat = lax.rsqrt(jnp.mean(hidden * hidden, axis=1, keepdims=True) + EPSILON)
    return hidden * stat * gain[...]


def normed_backward(keep, total, half, strip, inputs, outs, gain_sum):
    value, base, gain = inputs[:3]
    value = value[half, strip, :].astype(F32)
    stat = lax.rsqrt(jnp.mean(value * value, axis=1, keepdims=True) + EPSILON)
    unit = value * stat
    gain_sum[...] += jnp.sum((total * unit).reshape(2, 8, -1), axis=0)
    scaled = total * gain[...]
    grad = base[half, strip, :].astype(F32) + stat * (
        scaled - unit * jnp.mean(scaled * unit, axis=1, keepdims=True)
    )
    if keep:
        outs[0][half, strip, :] = grad
    return grad


def mp_phase(number, middle, part, inputs, dummies, outs, both_cores=False, small=None):
    here, there = pl.BlockSpec(memory_space=pltpu.VMEM), pl.BlockSpec(memory_space=pl.ANY)
    count, model = part.shape[0] // (2 if both_cores else 1), part.shape[1]
    block = (count // 8, model)
    copies, scratch, small_sum = 12, [], None
    if both_cores:
        copies = 20
        scratch += [pltpu.VMEM((count, model), BF16)] * 2 + [pltpu.SemaphoreType.DMA(())]
    if small is not None:
        stages = lax.axis_size("row").bit_length() - 1 + 3
        copies = 20 + stages
        scratch += [pltpu.VMEM((stages, 2, *small.shape), F32)]
        small_sum = {"dummies": len(dummies)}
        inputs = [*inputs, small]
        outs = [*outs, jax.ShapeDtypeStruct(small.shape, F32)]
    kernel = functools.partial(
        phase_kernel, middle, both_cores, small_sum, len(inputs) + len(dummies), 1 + len(outs)
    )
    return pl.pallas_call(
        kernel,
        in_specs=[there if both_cores else here] + [here] * len(inputs) + [there] * len(dummies),
        out_specs=[here] * (1 + len(outs)),
        out_shape=[jax.ShapeDtypeStruct((count, model), BF16), *outs],
        scratch_shapes=[
            pltpu.VMEM((6, *block), BF16),
            pltpu.VMEM((2, *block), BF16),
            pltpu.VMEM((8, model), F32),
            pltpu.SemaphoreType.DMA((copies,)),
            pltpu.SemaphoreType.DMA((copies,)),
            *scratch,
        ],
        compiler_params=pltpu.CompilerParams(
            collective_id=number, has_side_effects=True, vmem_limit_bytes=48 << 20
        ),
        cost_estimate=pl.CostEstimate(flops=0, bytes_accessed=250 << 20, transcendentals=0),
    )(part, *inputs, *dummies)


def swapped(block):
    return lax.ppermute(block, "seq", [(0, 1), (1, 0)])


def across(block, bit):
    return lax.ppermute(block, "mp", [(i, i ^ bit) for i in range(4)])


def in_order(mine, other, core, axis):
    first = jnp.where(core == 0, mine, other)
    second = jnp.where(core == 0, other, mine)
    return jnp.concatenate([first, second], axis=axis)


def after(block, *done):
    nothing = sum(part[(0,) * part.ndim].astype(F32) for part in done) * 0.0
    return block + nothing.astype(block.dtype)


def halves(block, core, axis):
    size = block.shape[axis] // 2
    pick = lambda i: lax.dynamic_slice_in_dim(block, i * size, size, axis=axis)
    return pick(core), pick(1 - core)


def both_tokens(left, right):
    product = lambda a, b: lax.dot_general(
        a, b, (((0,), (0,)), ((), ())), preferred_element_type=F32
    )
    return (product(left[0], right[0]) + product(left[1], right[1])).astype(BF16)


def own_columns(block, core):
    mine, other = halves(block, core, 1)
    return mine, swapped(other)


def product_pair(left, right, core):
    mine, other = halves(right, core, 1)
    product = lambda part: lax.dot_general(
        left, part, (((0,), (0,)), ((), ())), preferred_element_type=F32
    )
    incoming = swapped(product(other).astype(BF16))
    return (product(mine) + incoming.astype(F32)).astype(BF16)


def over_row(pair, axis):
    return lax.psum_scatter(pair, "row", scatter_dimension=axis, tiled=True)


def joined_shards(
    block_in,
    doc_lengths,
    attn_gain,
    qkv_weight,
    conv_weight,
    beta_weight,
    out_gain,
    out_weight,
    ffn_gain,
    gateup_weight,
    down_weight,
    cotangent,
):
    tok_count, model = block_in.shape[1:]
    core, own = lax.axis_index("seq"), lax.axis_index("mp")
    width = conv_weight.shape[2] // 2
    own_heads = width // HDIM
    quarter = tok_count // 4

    gather = lambda weight: lax.all_gather(weight, ("seq", "row"), axis=1, tiled=True)
    mixer_full = gather(jnp.concatenate([qkv_weight, out_weight.T[None]]))
    qkv_full, out_full = mixer_full[:3], mixer_full[3]
    beta_full, gateup_full, down_full = (
        gather(beta_weight),
        gather(gateup_weight),
        gather(down_weight),
    )
    qkv_own = lax.dynamic_slice_in_dim(qkv_full, core * width, width, axis=2)
    beta_own = lax.dynamic_slice_in_dim(beta_full, core * own_heads, own_heads, axis=0)
    mix_weight = jnp.concatenate(
        [qkv_own[0], qkv_own[1], qkv_own[2], jnp.pad(beta_own.T, ((0, 0), (0, HDIM - own_heads)))],
        axis=1,
    )
    conv_own = lax.dynamic_slice_in_dim(conv_weight, core * width, width, axis=2)
    conv_own = conv_own.transpose(1, 0, 2).reshape(KERNEL, 3 * width)

    residual_in = block_in[0].astype(F32)
    stat_in = lax.rsqrt(jnp.mean(residual_in * residual_in, axis=-1, keepdims=True) + EPSILON)
    normed_mine = (residual_in * stat_in * attn_gain).astype(BF16)
    normed = in_order(normed_mine, swapped(normed_mine), core, 0)

    positions = jnp.arange(2 * tok_count, dtype=jnp.int32)
    doc_start, real_row = row_layout(doc_lengths[0], positions)
    keep = jnp.pad((doc_start[::BLOCK] != positions[::BLOCK]).astype(F32), (0, 1))
    count = jnp.sum(real_row.reshape(-1, BLOCK), axis=1).astype(jnp.int32)
    raw = jnp.dot(normed, mix_weight, preferred_element_type=F32).astype(BF16)
    gain = out_gain[None, :]
    group = 4 if raw.shape[0] % (4 * CHUNK) == 0 else 1
    heads_out, *saved = forward(keep, count, raw, conv_own, gain, group)

    mine, other = halves(heads_out, core, 0)
    normed_out = in_order(mine, swapped(other), core, 1)
    branch_part = lax.dot_general(
        normed_out, out_full, (((1,), (1,)), ((), ())), preferred_element_type=F32
    )
    own_rows = lambda block: lax.dynamic_slice_in_dim(
        block[0], own * quarter, quarter, axis=0
    ).reshape(2, -1, model)
    residual_own = own_rows(block_in)
    rows_own = jax.ShapeDtypeStruct(residual_own.shape, F32)
    normed_mid, hidden = mp_phase(
        0,
        normed_forward,
        branch_part.astype(BF16),
        [residual_own, ffn_gain[None, :]],
        [],
        [rows_own],
    )

    grad_top = cotangent[0]
    gate_up = jnp.einsum("td,sdf->stf", normed_mid, gateup_full, preferred_element_type=F32)
    gate_sig = jax.nn.sigmoid(gate_up[0])
    product = (gate_up[0] * gate_sig * gate_up[1]).astype(BF16)
    down_pair = product_pair(product, grad_top, core)
    ffn_part = jnp.dot(
        after(product, down_pair), down_full, preferred_element_type=F32
    ).astype(BF16)
    ffn_parts = lax.all_to_all(ffn_part, "mp", split_axis=0, concat_axis=0, tiled=True)
    ffn_own = jnp.sum(ffn_parts.astype(F32).reshape(4, quarter, model), axis=0)
    block_out = (hidden.reshape(quarter, model) + ffn_own).astype(BF16)
    grad_product = jnp.dot(grad_top, down_full.T, preferred_element_type=F32)
    grad_product = after(grad_product, ffn_part)
    grad_gate = grad_product * gate_up[1] * gate_sig * (1.0 + gate_up[0] * (1.0 - gate_sig))
    grad_up = grad_product * gate_up[0] * gate_sig
    grad_gate, grad_up = grad_gate.astype(BF16), grad_up.astype(BF16)
    grad_mid_part = jnp.einsum(
        "stf,sdf->td",
        jnp.stack([grad_gate, grad_up]),
        gateup_full,
        preferred_element_type=F32,
    ).astype(BF16)
    normed_halves = own_columns(normed_mid, core)
    gate_pair = both_tokens(normed_halves, (grad_gate, swapped(grad_gate)))
    up_pair = both_tokens(normed_halves, (grad_up, swapped(grad_up)))
    down_sum, gate_sum, up_sum = over_row(down_pair, 1), over_row(gate_pair, 0), over_row(up_pair, 0)
    grad_branch, grad_hidden, ffn_gain_part = mp_phase(
        1,
        partial(normed_backward, True),
        grad_mid_part,
        [hidden, own_rows(cotangent), ffn_gain[None, :]],
        [block_out, down_pair, gate_pair, up_pair],
        [rows_own, jax.ShapeDtypeStruct((1, model), F32)],
    )
    grad_normed_out = jnp.dot(grad_branch, out_full, preferred_element_type=F32).astype(BF16)

    mine, other = halves(grad_normed_out, core, 1)
    grad_heads = in_order(mine, swapped(other), core, 0)
    grad_raw, grad_conv_own, out_gain_part = backward(
        keep, count, raw, conv_own, gain, grad_heads, *saved, group, [down_sum, gate_sum]
    )
    block_outs = [block_out] + [
        lax.ppermute(after(block_out, grad_branch), "mp", [(i, i ^ k) for i in range(4)])
        for k in (1, 2, 3)
    ]
    out_pair = product_pair(after(normed_out, up_sum), grad_branch, core)
    grad_raw = after(grad_raw, *block_outs[1:])
    grad_normed = lax.dot_general(
        grad_raw, mix_weight, (((1,), (1,)), ((), ())), preferred_element_type=F32
    )
    grad_normed_part = grad_normed.astype(BF16)
    grad_qkv = lax.dot_general(
        normed,
        grad_raw[:, : 3 * width],
        (((0,), (0,)), ((), ())),
        preferred_element_type=F32,
    ).astype(BF16)
    grad_beta = lax.dot_general(
        grad_raw[:, 3 * width :], normed, (((0,), (0,)), ((), ())), preferred_element_type=F32
    )[:own_heads]

    line = lambda part: jnp.pad(part.reshape(1, -1), ((0, 0), (0, model - part.size)))
    place = lambda part, lines: lax.dynamic_update_slice_in_dim(
        jnp.zeros((2 * lines, model), F32), part, core * lines, axis=0
    )
    conv_lines = -(-grad_conv_own.size // model)
    conv_part = jnp.pad(grad_conv_own.ravel(), (0, conv_lines * model - grad_conv_own.size))
    small = jnp.concatenate(
        [
            jnp.zeros((1, model), F32),
            ffn_gain_part,
            line(out_gain_part[0]),
            jnp.zeros((5, model), F32),
            place(grad_beta, own_heads),
            place(conv_part.reshape(conv_lines, model), conv_lines),
        ]
    )
    small = jnp.pad(small, ((0, -small.shape[0] % 8), (0, 0)))
    grad_input, small = mp_phase(
        2,
        partial(normed_backward, False),
        grad_normed_part,
        [residual_own, grad_hidden, attn_gain[None, :]],
        [*block_outs, up_sum, out_pair, grad_qkv],
        [],
        both_cores=True,
        small=small,
    )
    grad_input = grad_input.astype(F32)
    block_outs = jnp.stack(block_outs)
    block_out = jnp.concatenate(
        [lax.dynamic_index_in_dim(block_outs, own ^ k, 0, keepdims=False) for k in range(4)]
    )
    grad_attn_gain, grad_ffn_gain = small[0], small[1]
    grad_out_gain = small[2, : out_gain.shape[0]]
    span = beta_weight.shape[1]
    place_no = core * lax.axis_size("row") + lax.axis_index("row")
    grad_beta = lax.dynamic_slice_in_dim(small[8 : 8 + 2 * own_heads], place_no * span, span, axis=1)
    conv_at = 8 + 2 * own_heads
    conv_of = lambda i: (
        small[conv_at + i * conv_lines : conv_at + (i + 1) * conv_lines]
        .ravel()[: grad_conv_own.size]
        .reshape(KERNEL, 3, width)
        .transpose(1, 0, 2)
    )
    grad_conv = jnp.concatenate([conv_of(0), conv_of(1)], axis=2)
    grad_down, grad_out = down_sum.astype(F32), over_row(out_pair, 1).astype(F32)
    grad_gateup = jnp.stack([gate_sum, up_sum]).astype(F32)
    grad_qkv = lax.psum_scatter(
        grad_qkv.reshape(2, -1, 3 * width), "row", scatter_dimension=1, tiled=True
    )
    mine, other = halves(grad_qkv, core, 0)
    by_kind = lambda part: part[0].reshape(-1, 3, width).transpose(1, 0, 2)
    grad_qkv = in_order(by_kind(mine), by_kind(swapped(other)), core, 2).astype(F32)
    return (
        block_out[None],
        grad_input[None],
        grad_attn_gain,
        grad_qkv,
        grad_conv,
        grad_beta,
        grad_out_gain,
        grad_out,
        grad_ffn_gain,
        grad_gateup,
        grad_down,
    )


def solution(mesh):
    rows = mesh.shape["row"]
    joined = mesh.shape["seq"] == 2 and mesh.shape["mp"] == 4 and rows & (rows - 1) == 0
    return jax.shard_map(
        joined_shards if joined else spread_shards,
        mesh=mesh,
        in_specs=(
            P("row", "seq", None),
            P("row", None),
            P(),
            P(None, ("seq", "row"), "mp"),
            P(None, None, "mp"),
            P("mp", ("seq", "row")),
            P(),
            P("mp", ("seq", "row")),
            P(),
            P(None, ("seq", "row"), "mp"),
            P("mp", ("seq", "row")),
            P("row", "seq", None),
        ),
        out_specs=(
            P("row", "seq", None),
            P("row", "seq", None),
            P(),
            P(None, ("seq", "row"), "mp"),
            P(None, None, "mp"),
            P("mp", ("seq", "row")),
            P(),
            P("mp", ("seq", "row")),
            P(),
            P(None, ("seq", "row"), "mp"),
            P("mp", ("seq", "row")),
        ),
        check_vma=False,
    )
```

```python
import functools
from functools import partial

import jax
import jax.numpy as jnp
from jax import lax
from jax.experimental import pallas as pl
from jax.experimental.pallas import tpu as pltpu
from jax.sharding import PartitionSpec as P

HDIM = 128
KERNEL = 4
BLOCK = 64
CHUNK = 128
EPSILON = 1e-06
PRECISE = lax.Precision.HIGHEST
F32 = jnp.float32
BF16 = jnp.bfloat16

NT=(((1,),(1,)),((),())); NN=(((1,),(0,)),((),())); TN=(((0,),(0,)),((),()))

def mm(a,b,dims=NN):
    return lax.dot_general(a.astype(BF16), b.astype(BF16), dims, preferred_element_type=F32)

def iotas():
    return lax.broadcasted_iota(jnp.int32,(CHUNK,CHUNK),0), lax.broadcasted_iota(jnp.int32,(CHUNK,CHUNK),1)

def inverses(below):
    r,c=iotas()
    done=[jnp.where(r==c,1.0,0.0)-jnp.where(r//2==c//2,a,0.0) for a in below]
    size=2
    while size<CHUNK:
        pairs=(r//(2*size)==c//(2*size))&(r//size!=c//size)
        half=[mm(jnp.where(pairs,a,0.0),t) for a,t in zip(below,done)]
        done=[t-mm(t,x) for t,x in zip(done,half)]
        size*=2
    return done

def conv_act(ext_ref, base, lanes, cw, taps):
    total=cw[0:1]*ext_ref[pl.ds(base+8,CHUNK),lanes]
    for j in range(1,KERNEL):
        total=total+(cw[j:j+1]*taps[j-1])*ext_ref[pl.ds(base+8-j,CHUNK),lanes]
    sig=jax.nn.sigmoid(total)
    return total,sig

def layout(keep_ref, count_ref, block):
    r,_=iotas()
    inside=r%BLOCK
    first=r<BLOCK
    keep0,keep1,after=keep_ref[block],keep_ref[block+1],keep_ref[block+2]
    here=jnp.where(first,keep0,keep1)
    later=jnp.where(first,keep1,after)
    taps=[jnp.where(inside<j,here,1.0) for j in range(1,KERNEL)]
    taps_later=[jnp.where(inside>=BLOCK-j,later,1.0) for j in range(1,KERNEL)]
    real=jnp.where(inside<jnp.where(first,count_ref[block],count_ref[block+1]),1.0,0.0)
    return taps,taps_later,jnp.where(first,1.0,keep1),jnp.where(first,keep1,1.0),real,keep0,keep1

def fwd_kernel(heads, group, keep_ref, count_ref, raw_ref, cw_ref, gain_ref, normed_ref, o_ref, s_ref, t_ref, w_ref, r_ref, ext, state):
    rows=group*CHUNK
    step=pl.program_id(0)
    @pl.when(step==0)
    def _():
        ext[0:8,:]=jnp.zeros((8,3*heads*HDIM),F32)
        state[...]=jnp.zeros(state.shape,F32)
    @pl.when(step>0)
    def _():
        ext[0:8,:]=ext[rows:rows+8,:]
    ext[8:,:]=raw_ref[:,0:3*heads*HDIM].astype(F32)
    r,c=iotas()
    width=heads*HDIM
    units=[]
    below=[]
    for g in range(group):
        base=g*CHUNK
        taps,_,m,m2,real,keep0,keep1=layout(keep_ref,count_ref,2*(step*group+g))
        sig_b=jax.nn.sigmoid(raw_ref[pl.ds(base,CHUNK),pl.ds(3*width,HDIM)].astype(F32))*real
        for h in range(heads):
            act=[]
            for s in range(3):
                lanes=pl.ds(s*width+h*HDIM,HDIM)
                total,sig=conv_act(ext,base,lanes,cw_ref[:,lanes],taps)
                act.append(total*sig)
            q=act[0]*(lax.rsqrt(jnp.sum(act[0]*act[0],axis=1,keepdims=True)+EPSILON)*HDIM**-0.5)
            k=act[1]*lax.rsqrt(jnp.sum(act[1]*act[1],axis=1,keepdims=True)+EPSILON)
            v=act[2]
            b=sig_b[:,h:h+1]
            gram=mm(k,k,NT)
            score=mm(q,k,NT)
            mask=jnp.where(c<BLOCK,m,1.0)
            a=jnp.where(r>c,b*gram*mask,0.0)
            l=jnp.where(r>=c,score*mask,0.0)
            below.append(a)
            units.append((g,h,q*m,k*m2,l,b*k,b*v,m,keep0,keep1))
    done=inverses(below)
    wus=[(mm(t,u[5])*u[7],mm(t,u[6])) for t,u in zip(done,units)]
    for t,(w,u),(g,h,q,k,l,_,_,_,keep0,keep1) in zip(done,wus,units):
        base=g*CHUNK
        out=(pl.ds(base,CHUNK),pl.ds(h*HDIM,HDIM))
        t_ref[g,h]=t.astype(BF16)
        w_ref[out]=w.astype(BF16)
        s=state[h]*keep0
        s_ref[g,h]=s.astype(BF16)
        rr=u-mm(w,s)
        o=mm(q,s)+mm(l,rr)
        state[h]=s*keep1+mm(k,rr,TN)
        r_ref[out]=rr.astype(BF16)
        o_ref[out]=o
        stat=lax.rsqrt(jnp.mean(o*o,axis=1,keepdims=True)+EPSILON)
        normed_ref[out]=(o*stat*gain_ref[...]).astype(BF16)

def forward(keep, count, raw, cw, gain, group):
    n=raw.shape[0]; width=cw.shape[1]//3; heads=width//HDIM; rows=group*CHUNK
    nc=n//CHUNK
    row=lambda w: pl.BlockSpec((rows,w),lambda i:(i,0))
    mat=pl.BlockSpec((group,heads,HDIM,HDIM),lambda i:(i,0,0,0))
    full=lambda a: pl.BlockSpec(a.shape,lambda i:(0,0))
    return pl.pallas_call(functools.partial(fwd_kernel,heads,group),
        grid=(n//rows,),
        in_specs=[pl.BlockSpec(memory_space=pltpu.SMEM)]*2+[row(raw.shape[1]),full(cw),full(gain)],
        out_specs=[row(width),row(width),mat,mat,row(width),row(width)],
        out_shape=[jax.ShapeDtypeStruct((n,width),BF16),jax.ShapeDtypeStruct((n,width),F32),
            jax.ShapeDtypeStruct((nc,heads,HDIM,HDIM),BF16),jax.ShapeDtypeStruct((nc,heads,HDIM,HDIM),BF16),
            jax.ShapeDtypeStruct((n,width),BF16),jax.ShapeDtypeStruct((n,width),BF16)],
        scratch_shapes=[pltpu.VMEM((rows+8,3*width),F32),pltpu.VMEM((heads,HDIM,HDIM),F32)],
        compiler_params=pltpu.CompilerParams(vmem_limit_bytes=56<<20),
        cost_estimate=pl.CostEstimate(flops=0,bytes_accessed=120<<20,transcendentals=0),
    )(keep,count,raw,cw,gain)

def bwd_kernel(heads, group, keep_ref, count_ref, raw_ref, prev_ref, cw_ref, gain_ref, gno_ref, o_ref, s_ref, t_ref, w_ref, r_ref, *rest):
    block_ref=rest[0]
    graw_ref, gcw_ref, ggain_ref, all_ref, ext, gext, grad_state, local_sem, send_sem, recv_sem = rest[-10:]
    rows=group*CHUNK
    step=pl.program_id(0); steps=pl.num_programs(0)
    width=heads*HDIM
    @pl.when(step==0)
    def _():
        gext[rows:rows+8,:]=jnp.zeros((8,3*heads*HDIM),F32)
        grad_state[...]=jnp.zeros(grad_state.shape,F32)
        gcw_ref[...]=jnp.zeros(gcw_ref.shape,F32)
        ggain_ref[...]=jnp.zeros(ggain_ref.shape,F32)
    @pl.when(step>0)
    def _():
        gext[rows:rows+8,:]=gext[0:8,:]
    first=jnp.where(step==steps-1,0.0,1.0)
    place=lax.axis_index("mp")
    across_x=place+1-2*(place%2)
    across_y=(place+2)%4
    part=block_ref.shape[0]//2
    at=lambda of,half: all_ref.at[pl.ds(pl.multiple_of((2*of+half)*part,part),part)]
    def copy(index,source,target,other):
        return pltpu.make_async_remote_copy(src_ref=source,dst_ref=target,send_sem=send_sem.at[index],recv_sem=recv_sem.at[index],
            device_id={"mp":other},device_id_type=pl.DeviceIdType.MESH)
    top,low=block_ref.at[pl.ds(0,part)],block_ref.at[pl.ds(part,part)]
    keep_own=pltpu.make_async_copy(block_ref,all_ref.at[pl.ds(pl.multiple_of(2*place*part,2*part),2*part)],local_sem)
    sends=[copy(0,top,at(place,0),across_x),copy(1,low,at(place,1),across_y),copy(2,top,at(place,0),across_y),copy(3,low,at(place,1),across_x)]
    onward=[copy(4,at(across_x,0),at(across_x,0),across_y),copy(5,at(across_y,1),at(across_y,1),across_x)]
    @pl.when(step==0)
    def _():
        barrier=pltpu.get_barrier_semaphore()
        for other in (across_x,across_y):
            pl.semaphore_signal(barrier,inc=1,device_id={"mp":other},device_id_type=pl.DeviceIdType.MESH)
        pl.semaphore_wait(barrier,2)
        keep_own.start()
        for send in sends: send.start()
    @pl.when(step==steps//2)
    def _():
        for send,follow in zip(sends[:2],onward):
            send.wait_recv()
            follow.start()
    ext[0:8,:]=prev_ref[:,0:3*width].astype(F32)[8:16]*first
    ext[8:,:]=raw_ref[:,0:3*heads*HDIM].astype(F32)
    r,c=iotas()
    units=[]
    for g in range(group-1,-1,-1):
        base=g*CHUNK
        taps,taps_later,m,m2,real,keep0,keep1=layout(keep_ref,count_ref,2*((steps-1-step)*group+g))
        beta=jax.nn.sigmoid(raw_ref[pl.ds(base,CHUNK),pl.ds(3*width,HDIM)].astype(F32))
        sig_b=beta*real
        for h in range(heads):
            out=(pl.ds(base,CHUNK),pl.ds(h*HDIM,HDIM))
            act=[];tot=[];sigs=[]
            for s in range(3):
                lanes=pl.ds(s*width+h*HDIM,HDIM)
                total,sig=conv_act(ext,base,lanes,cw_ref[:,lanes],taps)
                act.append(total*sig);tot.append(total);sigs.append(sig)
            rq=lax.rsqrt(jnp.sum(act[0]*act[0],axis=1,keepdims=True)+EPSILON)
            rk=lax.rsqrt(jnp.sum(act[1]*act[1],axis=1,keepdims=True)+EPSILON)
            qu=act[0]*rq
            o=o_ref[out]
            stat=lax.rsqrt(jnp.mean(o*o,axis=1,keepdims=True)+EPSILON)
            uo=o*stat
            gno=gno_ref[out].astype(F32)
            ggain_ref[...]+=jnp.sum(gno*uo,axis=0,keepdims=True)
            gu=gno*gain_ref[...]
            do=stat*(gu-uo*jnp.mean(gu*uo,axis=1,keepdims=True))
            units.append(dict(g=g,h=h,base=base,out=out,taps=taps,m=m,m2=m2,keep0=keep0,keep1=keep1,tot=tot,sigs=sigs,
                rq=rq,rk=rk,qu=qu,q=qu*HDIM**-0.5,k=act[1]*rk,v=act[2],b=sig_b[:,h:h+1],do=do,
                mask=jnp.where(c<BLOCK,m,1.0)))
        for u in units[-heads:]: u.update(taps_later=taps_later,beta=beta,sig_b=sig_b)
    for u in units: u['gram']=mm(u['k'],u['k'],NT)*u['mask']
    for u in units: u['l']=jnp.where(r>=c,mm(u['q'],u['k'],NT)*u['mask'],0.0)
    for u in units: u['dr0']=mm(u['l'],u['do'],TN)
    for u in units: u['ds0']=mm(u['q']*u['m'],u['do'],TN)
    for u in units:
        dsn=grad_state[u['h']]
        u['dsn']=dsn
        u['dr']=u['dr0']+u['m2']*mm(u['k'],dsn)
        ds=u['keep1']*dsn+u['ds0']-mm(w_ref[u['out']],u['dr'],TN)
        grad_state[u['h']]=u['keep0']*ds
    for u in units: u['df']=mm(t_ref[u['g'],u['h']],u['dr'],TN)
    for u in units: u['dl']=jnp.where(r>=c,mm(u['do'],r_ref[u['out']],NT)*u['mask'],0.0)
    for u in units: u['da']=jnp.where(r>c,-mm(u['df'],r_ref[u['out']],NT),0.0)
    for u in units:
        u['de']=u['b']*u['df']
        u['e']=u['v']-u['m']*mm(u['k'],s_ref[u['g'],u['h']])
        u['gb']=jnp.sum(u['df']*u['e']+u['da']*u['gram'],axis=1,keepdims=True)
        u['dkk']=u['b']*u['da']*u['mask']
    for u in units: u['dq']=u['m']*mm(u['do'],s_ref[u['g'],u['h']],NT)+mm(u['dl'],u['k'])
    for u in units:
        u['dk']=(mm(u['dl'],u['q'],TN)+u['m2']*mm(r_ref[u['out']],u['dsn'],NT)-u['m']*mm(u['de'],s_ref[u['g'],u['h']],NT)
            +mm(u['dkk'],u['k'])+mm(u['dkk'],u['k'],TN))
    for u in units:
        gq=u['dq']*HDIM**-0.5
        gq=u['rq']*(gq-u['qu']*jnp.sum(gq*u['qu'],axis=1,keepdims=True))
        gk=u['rk']*(u['dk']-u['k']*jnp.sum(u['dk']*u['k'],axis=1,keepdims=True))
        for i,ga in enumerate((gq,gk,u['de'])):
            lanes=pl.ds(i*width+u['h']*HDIM,HDIM)
            sig,tot=u['sigs'][i],u['tot'][i]
            gc=ga*sig*(1.0+tot*(1.0-sig))
            gext[pl.ds(u['base'],CHUNK),lanes]=gc
            for j in range(KERNEL):
                win=ext[pl.ds(u['base']+8-j,CHUNK),lanes]
                prod=gc*win if j==0 else gc*win*u['taps'][j-1]
                gcw_ref[j:j+1,lanes]+=jnp.sum(prod,axis=0,keepdims=True)
    for at in range(0,len(units),heads):
        glog=jnp.zeros((CHUNK,HDIM),F32)
        for u in units[at:at+heads]:
            glog=jnp.where(c==u['h'],u['gb'],glog)
            for i in range(3):
                lanes=pl.ds(i*width+u['h']*HDIM,HDIM)
                cw=cw_ref[:,lanes]
                total=cw[0:1]*gext[pl.ds(u['base'],CHUNK),lanes]
                for j in range(1,KERNEL):
                    total=total+(cw[j:j+1]*u['taps_later'][j-1])*gext[pl.ds(u['base']+j,CHUNK),lanes]
                graw_ref[pl.ds(u['base'],CHUNK),lanes]=total.astype(BF16)
        graw_ref[pl.ds(u['base'],CHUNK),pl.ds(3*width,HDIM)]=(glog*u['sig_b']*(1.0-u['beta'])).astype(BF16)
    @pl.when(step==steps-1)
    def _():
        keep_own.wait()
        for send in (*sends[2:],*onward): send.wait_recv()
        for send in (*sends,*onward): send.wait_send()

def backward(keep, count, raw, cw, gain, gno, o, s, t, w, r, group, block, dummies=()):
    n=raw.shape[0]; width=cw.shape[1]//3; heads=width//HDIM; rows=group*CHUNK
    steps=n//rows
    row=lambda w: pl.BlockSpec((rows,w),lambda i:(steps-1-i,0))
    mat=pl.BlockSpec((group,heads,HDIM,HDIM),lambda i:(steps-1-i,0,0,0))
    full=lambda a: pl.BlockSpec(a.shape,lambda i:(0,0))
    prev=pl.BlockSpec((16,raw.shape[1]),lambda i:(jnp.maximum((steps-1-i)*(rows//16)-1,0),0))
    return pl.pallas_call(functools.partial(bwd_kernel,heads,group),
        grid=(steps,),
        in_specs=[pl.BlockSpec(memory_space=pltpu.SMEM)]*2+[row(raw.shape[1]),prev,full(cw),full(gain),row(width),row(width),mat,mat,row(width),row(width)]+[pl.BlockSpec(memory_space=pl.ANY)]*(1+len(dummies)),
        out_specs=[row(raw.shape[1]),pl.BlockSpec((KERNEL,3*width),lambda i:(0,0)),pl.BlockSpec((1,HDIM),lambda i:(0,0)),pl.BlockSpec(memory_space=pl.ANY)],
        out_shape=[jax.ShapeDtypeStruct(raw.shape,BF16),
            jax.ShapeDtypeStruct((KERNEL,3*width),F32),jax.ShapeDtypeStruct((1,HDIM),F32),jax.ShapeDtypeStruct((4*block.shape[0],block.shape[1]),BF16)],
        scratch_shapes=[pltpu.VMEM((rows+8,3*width),F32),pltpu.VMEM((rows+8,3*width),F32),pltpu.VMEM((heads,HDIM,HDIM),F32),
            pltpu.SemaphoreType.DMA(()),pltpu.SemaphoreType.DMA((6,)),pltpu.SemaphoreType.DMA((6,))],
        compiler_params=pltpu.CompilerParams(collective_id=3,has_side_effects=True,vmem_limit_bytes=56<<20),
        cost_estimate=pl.CostEstimate(flops=0,bytes_accessed=120<<20,transcendentals=0),
    )(keep,count,raw,raw,cw,gain,gno,o,s,t,w,r,block,*dummies)


def passed_along(block, axis, distance):
    devices = range(lax.axis_size(axis))
    route = [(i - distance, i) for i in devices if i - distance in devices]
    return lax.ppermute(block, axis, route)


def row_layout(lengths, positions):
    span_len = (lengths + BLOCK - 1) // BLOCK * BLOCK
    closing = jnp.cumsum(span_len)
    opening = closing - span_len
    bounds = jnp.concatenate([opening, closing[-1:]])
    reached = bounds[None, :] <= positions[:, None]
    doc_start = jnp.max(jnp.where(reached, bounds[None, :], 0), axis=1)
    inside = (positions[:, None] >= opening[None, :]) & (
        positions[:, None] < (opening + lengths)[None, :]
    )
    real_mask = jnp.any(inside, axis=1).astype(jnp.float32)
    return (doc_start, real_mask)


def local_span(carry_on, queries, keys_in, values, strength):
    head_count, token_count, head_width = queries.shape
    block_count = token_count // BLOCK

    def to_blocks(tensor):
        return tensor.reshape(head_count, block_count, BLOCK, -1).transpose(1, 0, 2, 3)

    def from_blocks(tensor):
        return tensor.transpose(1, 0, 2, 3).reshape(head_count, token_count, -1)

    strict_lower = jnp.tril(jnp.ones((BLOCK, BLOCK), jnp.float32), -1)
    causal = jnp.tril(jnp.ones((BLOCK, BLOCK), jnp.float32))
    identity = jnp.broadcast_to(
        jnp.eye(head_width, dtype=jnp.float32), (head_count, head_width, head_width)
    )

    def block_step(carried, block_in):
        memory, mapping = carried
        q_blk, k_blk, v_blk, s_blk, carry_flag = block_in
        write_rate = s_blk[..., 0]
        memory = memory * carry_flag
        mapping = mapping * carry_flag
        key_gram = jnp.einsum("hcp,hdp->hcd", k_blk, k_blk, precision=PRECISE)
        system = jnp.eye(BLOCK, dtype=jnp.float32) + strict_lower * (
            write_rate[:, :, None] * key_gram
        )
        right_side = jnp.concatenate(
            [write_rate[..., None] * k_blk, write_rate[..., None] * v_blk], axis=-1
        )
        solved = lax.linalg.triangular_solve(
            system, right_side, left_side=True, lower=True, unit_diagonal=True
        )
        w_mat = solved[..., :head_width]
        u_mat = solved[..., head_width:]
        corrected = u_mat - jnp.einsum("hcp,hpv->hcv", w_mat, memory, precision=PRECISE)
        scores = causal * jnp.einsum("hcp,hdp->hcd", q_blk, k_blk, precision=PRECISE)
        out_zero = jnp.einsum("hcp,hpv->hcv", q_blk, memory, precision=PRECISE)
        out_zero = out_zero + jnp.einsum("hcd,hdv->hcv", scores, corrected, precision=PRECISE)
        w_map = jnp.einsum("hcp,hpq->hcq", w_mat, mapping, precision=PRECISE)
        q_prop = jnp.einsum("hcp,hpq->hcq", q_blk, mapping, precision=PRECISE)
        q_prop = q_prop - jnp.einsum("hcd,hdq->hcq", scores, w_map, precision=PRECISE)
        memory = memory + jnp.einsum("hcp,hcv->hpv", k_blk, corrected, precision=PRECISE)
        mapping = mapping - jnp.einsum("hcp,hcq->hpq", k_blk, w_map, precision=PRECISE)
        return ((memory, mapping), (out_zero, q_prop))

    initial = (jnp.zeros((head_count, head_width, head_width), jnp.float32), identity)
    blocks = (
        to_blocks(queries),
        to_blocks(keys_in),
        to_blocks(values),
        to_blocks(strength[..., None]),
        carry_on,
    )
    (memory, mapping), (out_zero, q_prop) = lax.scan(block_step, initial, blocks)
    return (from_blocks(out_zero), from_blocks(q_prop), mapping, memory)


def spread_shards(
    block_in,
    doc_lengths,
    attn_gain,
    qkv_weight,
    conv_weight,
    beta_weight,
    out_gain,
    out_weight,
    ffn_gain,
    gateup_weight,
    down_weight,
    cotangent,
):
    tok_count = block_in.shape[1]
    seq_count = lax.axis_size("seq")
    own_index = lax.axis_index("seq")
    positions = own_index * tok_count + jnp.arange(tok_count + KERNEL - 1, dtype=jnp.int32)
    doc_start, real_ext = row_layout(doc_lengths[0], positions)
    real_mask = real_ext[:tok_count]
    taps = [(positions - shift_no >= doc_start).astype(jnp.float32) for shift_no in range(KERNEL)]
    carry_on = (doc_start[:tok_count:BLOCK] != positions[:tok_count:BLOCK]).astype(jnp.float32)
    residual_in = block_in[0].astype(jnp.float32)
    stat_in = lax.rsqrt(jnp.mean(residual_in * residual_in, axis=-1, keepdims=True) + EPSILON)
    unit_in = residual_in * stat_in
    normed = (unit_in * attn_gain).astype(jnp.bfloat16)
    qkv_full, beta_full, out_full, gateup_full, down_full = (
        lax.all_gather(qkv_weight, ("seq", "row"), axis=1, tiled=True),
        lax.all_gather(beta_weight, ("seq", "row"), axis=1, tiled=True),
        lax.all_gather(out_weight, ("seq", "row"), axis=1, tiled=True),
        lax.all_gather(gateup_weight, ("seq", "row"), axis=1, tiled=True),
        lax.all_gather(down_weight, ("seq", "row"), axis=1, tiled=True),
    )
    raw = jnp.einsum("td,sdc->stc", normed, qkv_full, preferred_element_type=jnp.float32).astype(
        jnp.bfloat16
    )
    rims = passed_along(raw[:, tok_count - KERNEL + 1 :, :], "seq", 1)
    extended = jnp.concatenate([rims, raw], axis=1).astype(jnp.float32)
    conv_sum = jnp.zeros(raw.shape, jnp.float32)
    for shift_no in range(KERNEL):
        window = extended[:, KERNEL - 1 - shift_no : KERNEL - 1 - shift_no + tok_count]
        conv_sum = (
            conv_sum
            + conv_weight[:, shift_no][:, None, :]
            * window
            * taps[shift_no][:tok_count][None, :, None]
        )
    conv_sig = jax.nn.sigmoid(conv_sum)
    head_count = conv_weight.shape[2] // HDIM
    split_heads = (
        (conv_sum * conv_sig).reshape(3, tok_count, head_count, HDIM).transpose(0, 2, 1, 3)
    )
    q_scale = lax.rsqrt(jnp.sum(split_heads[0] * split_heads[0], axis=-1, keepdims=True) + EPSILON)
    q_unit = split_heads[0] * q_scale
    queries = q_unit * HDIM ** (-0.5)
    k_scale = lax.rsqrt(jnp.sum(split_heads[1] * split_heads[1], axis=-1, keepdims=True) + EPSILON)
    keys_in = split_heads[1] * k_scale
    values = split_heads[2]
    logits = jnp.einsum("td,hd->ht", normed, beta_full, preferred_element_type=jnp.float32)
    beta_sig = jax.nn.sigmoid(logits)
    strength = beta_sig * real_mask[None, :]
    (out_zero, q_prop, span_map, span_state), span_pullback = jax.vjp(
        partial(local_span, carry_on), queries, keys_in, values, strength
    )
    empty_state = jnp.zeros_like(span_state)
    all_maps, all_states = (
        lax.all_gather(span_map[None].astype(jnp.bfloat16), "seq", axis=0, tiled=True).astype(
            jnp.float32
        ),
        lax.all_gather(span_state[None].astype(jnp.bfloat16), "seq", axis=0, tiled=True).astype(
            jnp.float32
        ),
    )

    def fold_forward(counter, incoming):
        moved = (
            jnp.einsum("hpq,hqv->hpv", all_maps[counter], incoming, precision=PRECISE)
            + all_states[counter]
        )
        return jnp.where(counter < own_index, moved, incoming)

    state_in = lax.fori_loop(0, seq_count, fold_forward, empty_state)
    mixer = out_zero + jnp.einsum("htp,hpv->htv", q_prop, state_in, precision=PRECISE)
    stat_out = lax.rsqrt(jnp.mean(mixer * mixer, axis=-1, keepdims=True) + EPSILON)
    unit_out = mixer * stat_out
    normed_out = (
        (unit_out * out_gain).transpose(1, 0, 2).reshape(tok_count, -1).astype(jnp.bfloat16)
    )
    branch_part = jnp.dot(normed_out, out_full, preferred_element_type=jnp.float32)
    hidden = residual_in + lax.psum(branch_part.astype(jnp.bfloat16), "mp").astype(jnp.float32)
    stat_mid = lax.rsqrt(jnp.mean(hidden * hidden, axis=-1, keepdims=True) + EPSILON)
    unit_mid = hidden * stat_mid
    normed_mid = (unit_mid * ffn_gain).astype(jnp.bfloat16)
    gate_up = jnp.einsum("td,sdf->stf", normed_mid, gateup_full, preferred_element_type=jnp.float32)
    gate_sig = jax.nn.sigmoid(gate_up[0])
    product = (gate_up[0] * gate_sig * gate_up[1]).astype(jnp.bfloat16)
    ffn_part = jnp.dot(product, down_full, preferred_element_type=jnp.float32)
    block_out = hidden + lax.psum(ffn_part.astype(jnp.bfloat16), "mp").astype(jnp.float32)
    qkv_full, beta_full, out_full, gateup_full, down_full = (
        lax.all_gather(qkv_weight, ("seq", "row"), axis=1, tiled=True),
        lax.all_gather(beta_weight, ("seq", "row"), axis=1, tiled=True),
        lax.all_gather(out_weight, ("seq", "row"), axis=1, tiled=True),
        lax.all_gather(gateup_weight, ("seq", "row"), axis=1, tiled=True),
        lax.all_gather(down_weight, ("seq", "row"), axis=1, tiled=True),
    )
    grad_top = cotangent[0]
    grad_down_part = jnp.dot(product.T, grad_top, preferred_element_type=jnp.float32)
    grad_product = jnp.dot(grad_top, down_full.T, preferred_element_type=jnp.float32)
    grad_gate = grad_product * gate_up[1] * gate_sig * (1.0 + gate_up[0] * (1.0 - gate_sig))
    grad_up = grad_product * gate_up[0] * gate_sig
    grad_gate_up = jnp.stack([grad_gate, grad_up]).astype(jnp.bfloat16)
    grad_gateup_part = jnp.einsum(
        "td,stf->sdf", normed_mid, grad_gate_up, preferred_element_type=jnp.float32
    )
    grad_mid_part = jnp.einsum(
        "stf,sdf->td", grad_gate_up, gateup_full, preferred_element_type=jnp.float32
    )
    grad_mid = lax.psum(grad_mid_part.astype(jnp.bfloat16), "mp").astype(jnp.float32)
    ffn_gain_part = jnp.sum(grad_mid * unit_mid, axis=0)
    grad_unit_mid = grad_mid * ffn_gain
    grad_hidden = grad_top.astype(jnp.float32) + stat_mid * (
        grad_unit_mid - unit_mid * jnp.mean(grad_unit_mid * unit_mid, axis=-1, keepdims=True)
    )
    grad_branch = grad_hidden.astype(jnp.bfloat16)
    grad_out_part = jnp.dot(normed_out.T, grad_branch, preferred_element_type=jnp.float32)
    grad_normed_out = jnp.dot(grad_branch, out_full.T, preferred_element_type=jnp.float32)
    grad_normed_out = grad_normed_out.reshape(tok_count, head_count, HDIM).transpose(1, 0, 2)
    out_gain_part = jnp.sum(grad_normed_out * unit_out, axis=(0, 1))
    grad_unit_out = grad_normed_out * out_gain
    grad_mixer = stat_out * (
        grad_unit_out - unit_out * jnp.mean(grad_unit_out * unit_out, axis=-1, keepdims=True)
    )
    local_grad = jnp.einsum("htp,htv->hpv", q_prop, grad_mixer, precision=PRECISE)
    grad_q_prop = jnp.einsum("htv,hpv->htp", grad_mixer, state_in, precision=PRECISE)
    all_grads = lax.all_gather(
        local_grad[None].astype(jnp.bfloat16), "seq", axis=0, tiled=True
    ).astype(jnp.float32)

    def fold_backward(counter, later_grad):
        source = seq_count - 1 - counter
        moved = (
            jnp.einsum("hqp,hqv->hpv", all_maps[source], later_grad, precision=PRECISE)
            + all_grads[source]
        )
        return jnp.where(source > own_index, moved, later_grad)

    grad_end = lax.fori_loop(0, seq_count, fold_backward, empty_state)
    grad_map = jnp.einsum("hpv,hqv->hpq", grad_end, state_in, precision=PRECISE)
    grad_queries, grad_keys, grad_values, grad_strength = span_pullback(
        (grad_mixer, grad_q_prop, grad_map, grad_end)
    )
    grad_logits = (grad_strength * real_mask[None, :] * beta_sig * (1.0 - beta_sig)).astype(
        jnp.bfloat16
    )
    grad_beta_part = jnp.einsum(
        "ht,td->hd", grad_logits, normed, preferred_element_type=jnp.float32
    )
    grad_q_unit = grad_queries * HDIM ** (-0.5)
    grad_q_raw = q_scale * (
        grad_q_unit - q_unit * jnp.sum(grad_q_unit * q_unit, axis=-1, keepdims=True)
    )
    grad_k_raw = k_scale * (
        grad_keys - keys_in * jnp.sum(grad_keys * keys_in, axis=-1, keepdims=True)
    )
    grad_act = (
        jnp.stack([grad_q_raw, grad_k_raw, grad_values])
        .transpose(0, 2, 1, 3)
        .reshape(3, tok_count, -1)
    )
    grad_conv_sum = grad_act * conv_sig * (1.0 + conv_sum * (1.0 - conv_sig))
    rims_back = passed_along(grad_conv_sum[:, : KERNEL - 1, :], "seq", -1)
    grad_ext = jnp.concatenate([grad_conv_sum, rims_back], axis=1)
    grad_raw = jnp.zeros(grad_conv_sum.shape, jnp.float32)
    conv_terms = []
    for shift_no in range(KERNEL):
        grad_raw = (
            grad_raw
            + conv_weight[:, shift_no][:, None, :]
            * grad_ext[:, shift_no : shift_no + tok_count]
            * taps[shift_no][shift_no : shift_no + tok_count][None, :, None]
        )
        window = extended[:, KERNEL - 1 - shift_no : KERNEL - 1 - shift_no + tok_count]
        conv_terms.append(
            jnp.sum(grad_conv_sum * window * taps[shift_no][:tok_count][None, :, None], axis=1)
        )
    grad_conv_part = jnp.stack(conv_terms, axis=1)
    grad_raw_low = grad_raw.astype(jnp.bfloat16)
    grad_qkv_part = jnp.einsum(
        "td,stc->sdc", normed, grad_raw_low, preferred_element_type=jnp.float32
    )
    grad_normed = jnp.einsum(
        "stc,sdc->td", grad_raw_low, qkv_full, preferred_element_type=jnp.float32
    )
    grad_normed = grad_normed + jnp.einsum(
        "ht,hd->td", grad_logits, beta_full, preferred_element_type=jnp.float32
    )
    grad_normed, out_gain_sum = (
        lax.psum(grad_normed.astype(jnp.bfloat16), "mp").astype(jnp.float32),
        lax.psum(out_gain_part.astype(jnp.bfloat16), "mp").astype(jnp.float32),
    )
    attn_gain_part = jnp.sum(grad_normed * unit_in, axis=0)
    grad_unit_in = grad_normed * attn_gain
    grad_input = grad_hidden + stat_in * (
        grad_unit_in - unit_in * jnp.mean(grad_unit_in * unit_in, axis=-1, keepdims=True)
    )
    weight_sums = (
        lax.psum_scatter(grad_qkv_part, ("seq", "row"), scatter_dimension=1, tiled=True),
        lax.psum_scatter(grad_beta_part, ("seq", "row"), scatter_dimension=1, tiled=True),
        lax.psum_scatter(grad_out_part, ("seq", "row"), scatter_dimension=1, tiled=True),
        lax.psum_scatter(grad_gateup_part, ("seq", "row"), scatter_dimension=1, tiled=True),
        lax.psum_scatter(grad_down_part, ("seq", "row"), scatter_dimension=1, tiled=True),
    )
    small_sums = lax.psum(
        (attn_gain_part, grad_conv_part, out_gain_sum, ffn_gain_part), ("seq", "row")
    )
    return (
        block_out.astype(jnp.bfloat16)[None],
        grad_input[None],
        small_sums[0],
        weight_sums[0],
        small_sums[1],
        weight_sums[1],
        small_sums[2],
        weight_sums[2],
        small_sums[3],
        weight_sums[3],
        weight_sums[4],
    )


MESH = pl.DeviceIdType.MESH
STRIP = 16


def phase_kernel(middle, both_cores, small_sum, n_in, n_out, part_ref, *refs):
    inputs, all_ref = refs[:n_in], refs[n_in]
    outs, scratch = refs[n_in + 1 : n_in + n_out], refs[n_in + n_out :]
    got, sums, gain_sum, send_sem, recv_sem = scratch[:5]
    count = all_ref.shape[0]
    rows = count // 8
    place, core, row = lax.axis_index("mp"), lax.axis_index("seq"), lax.axis_index("row")
    across_x = place + 1 - 2 * (place % 2)
    across_y = (place + 2) % 4
    across_both = 3 - place
    ways = {"x": {"mp": across_x}, "y": {"mp": across_y}}
    if both_cores or small_sum:
        ways["core"] = {"seq": 1 - core}
    steps = []
    if small_sum:
        bit = 1
        while bit < lax.axis_size("row"):
            steps.append(f"row{bit}")
            ways[steps[-1]] = {"row": row + bit - 2 * bit * ((row // bit) % 2)}
            bit *= 2
        steps += ["core", "x", "y"]
    barrier = pltpu.get_barrier_semaphore()
    for other in ways.values():
        pl.semaphore_signal(barrier, inc=1, device_id=other, device_id_type=MESH)
    pl.semaphore_wait(barrier, len(ways))

    def copy(index, source, target, way):
        return pltpu.make_async_remote_copy(
            src_ref=source,
            dst_ref=target,
            send_sem=send_sem.at[index],
            recv_sem=recv_sem.at[index],
            device_id=ways[way],
            device_id_type=MESH,
        )

    def block(of, half):
        return pl.ds(pl.multiple_of((2 * of + half) * rows, rows), rows)

    def strips(body):
        @pl.loop(0, rows // STRIP)
        def _(i):
            body(pl.multiple_of(i * STRIP, STRIP))

    order = [(across_both, 0), (across_both, 1), (across_x, 0), (across_y, 1)]
    order += [(across_y, 0), (across_x, 1), (place, 0), (place, 1)]
    if both_cores:
        part, incoming, local_sem = scratch[5:8]
        mine = pltpu.make_async_copy(part_ref.at[pl.ds(core * count, count)], part, local_sem)
        mine.start()
        shared = []
        for i, (of, half) in enumerate(order):
            start = pl.multiple_of((1 - core) * count + (2 * of + half) * rows, rows)
            shared.append(
                copy(12 + i, part_ref.at[pl.ds(start, rows)], incoming.at[block(of, half)], "core")
            )
            shared[-1].start()
        mine.wait()
    else:
        part = part_ref

    def ready(index):
        if both_cores:
            of, half = order[index]
            shared[index].wait_recv()

            def add(at):
                strip = pl.ds((2 * of + half) * rows + at, STRIP)
                part[strip, :] = (
                    part[strip, :].astype(F32) + incoming[strip, :].astype(F32)
                ).astype(BF16)

            strips(add)

    far = [
        copy(0, part.at[block(across_both, 0)], got.at[0], "x"),
        copy(1, part.at[block(across_both, 1)], got.at[1], "y"),
    ]
    near = [
        copy(2, part.at[block(across_x, 0)], got.at[2], "x"),
        copy(3, part.at[block(across_y, 1)], got.at[3], "y"),
    ]
    last = [copy(4, sums.at[0], got.at[4], "y"), copy(5, sums.at[1], got.at[5], "x")]
    own = [all_ref.at[block(place, 0)], all_ref.at[block(place, 1)]]
    passed = [all_ref.at[block(across_x, 0)], all_ref.at[block(across_y, 1)]]
    out_first = [copy(6, own[0], own[0], "x"), copy(7, own[1], own[1], "y")]
    out_second = [copy(8, own[0], own[0], "y"), copy(9, own[1], own[1], "x")]
    out_third = [copy(10, passed[0], passed[0], "y"), copy(11, passed[1], passed[1], "x")]

    for index, step in enumerate((*far, *near)):
        ready(index)
        step.start()
    gain_sum[...] = jnp.zeros_like(gain_sum)
    for half, onward in ((0, across_y), (1, across_x)):
        ready(4 + half)
        far[half].wait_recv()

        def add(at):
            strip = pl.ds(at, STRIP)
            mine = part[pl.ds((2 * onward + half) * rows + at, STRIP), :]
            sums[half, strip, :] = (mine.astype(F32) + got[half, strip, :].astype(F32)).astype(BF16)

        strips(add)
        last[half].start()
    for half in (0, 1):
        ready(6 + half)
        near[half].wait_recv()
        last[half].wait_recv()

        def finish(at):
            strip = pl.ds(at, STRIP)
            total = part[pl.ds((2 * place + half) * rows + at, STRIP), :].astype(F32)
            total = total + got[2 + half, strip, :].astype(F32)
            total = total + got[4 + half, strip, :].astype(F32)
            result = middle(total, half, strip, inputs, outs, gain_sum)
            all_ref[pl.ds((2 * place + half) * rows + at, STRIP), :] = result.astype(BF16)

        strips(finish)
        out_first[half].start()
        out_second[half].start()

    gain = jnp.sum(gain_sum[...], axis=0, keepdims=True)
    small = []
    if small_sum:
        values, arrived = outs[-1], scratch[-1]
        first = n_in - small_sum["dummies"] - 4
        ffn_gain, out_gain, beta, conv = inputs[first : first + 4]
        heads, taps, width = beta.shape[0], conv.shape[0], conv.shape[1]
        middle_lane = values.shape[1] // 2
        values[...] = jnp.zeros_like(values)
        values[0:1, :] = gain
        values[1:2, :] = ffn_gain[...]
        values[2:3, 0 : out_gain.shape[1]] = out_gain[...]
        for i in (0, 1):
            share = jnp.where(core == i, 1.0, 0.0)
            values[8 + i * heads : 8 + (i + 1) * heads, :] = beta[...] * share
            at = 8 + 2 * heads
            lane = i * middle_lane
            values[at : at + taps, lane : lane + width] = conv[...] * share
    elif n_out > 2:
        outs[-1][...] = gain

    def small_step(number):
        height = 8 if steps[number] in ("x", "y") else values.shape[0]
        step = copy(
            20 + number,
            arrived.at[number, 1, pl.ds(0, height)],
            arrived.at[number, 0, pl.ds(0, height)],
            steps[number],
        )
        arrived[number, 1, 0:height, :] = values[0:height, :]
        step.start()
        step.wait_recv()
        values[0:height, :] = values[0:height, :] + arrived[number, 0, 0:height, :]
        small.append(step)

    for half in (0, 1):
        out_first[half].wait_recv()
        out_third[half].start()
    if small_sum:
        for number in range(len(steps)):
            small_step(number)
    for step in (*out_second, *out_third):
        step.wait_recv()
    for step in (*far, *near, *last, *out_first, *out_second, *out_third, *small):
        step.wait_send()
    if both_cores:
        for step in shared:
            step.wait_send()


def normed_forward(total, half, strip, inputs, outs, gain_sum):
    residual, gain = inputs[:2]
    hidden = residual[half, strip, :].astype(F32) + total
    outs[0][half, strip, :] = hidden
    stat = lax.rsqrt(jnp.mean(hidden * hidden, axis=1, keepdims=True) + EPSILON)
    return hidden * stat * gain[...]


def normed_backward(keep, total, half, strip, inputs, outs, gain_sum):
    value, base, gain = inputs[:3]
    value = value[half, strip, :].astype(F32)
    stat = lax.rsqrt(jnp.mean(value * value, axis=1, keepdims=True) + EPSILON)
    unit = value * stat
    gain_sum[...] += jnp.sum((total * unit).reshape(2, 8, -1), axis=0)
    scaled = total * gain[...]
    grad = base[half, strip, :].astype(F32) + stat * (
        scaled - unit * jnp.mean(scaled * unit, axis=1, keepdims=True)
    )
    if keep:
        outs[0][half, strip, :] = grad
    return grad


def mp_phase(number, middle, part, inputs, dummies, outs, both_cores=False, small=None):
    here, there = pl.BlockSpec(memory_space=pltpu.VMEM), pl.BlockSpec(memory_space=pl.ANY)
    count, model = part.shape[0] // (2 if both_cores else 1), part.shape[1]
    block = (count // 8, model)
    copies, scratch, small_sum = 12, [], None
    if both_cores:
        copies = 20
        scratch += [pltpu.VMEM((count, model), BF16)] * 2 + [pltpu.SemaphoreType.DMA(())]
    if small is not None:
        stages = lax.axis_size("row").bit_length() - 1 + 3
        copies = 20 + stages
        height = 8 + 2 * small[2].shape[0] + small[3].shape[0]
        shape = (height + -height % 8, model)
        scratch += [pltpu.VMEM((stages, 2, *shape), F32)]
        small_sum = {"dummies": len(dummies)}
        inputs = [*inputs, *small]
        outs = [*outs, jax.ShapeDtypeStruct(shape, F32)]
    kernel = functools.partial(
        phase_kernel, middle, both_cores, small_sum, len(inputs) + len(dummies), 1 + len(outs)
    )
    return pl.pallas_call(
        kernel,
        in_specs=[there if both_cores else here] + [here] * len(inputs) + [there] * len(dummies),
        out_specs=[here] * (1 + len(outs)),
        out_shape=[jax.ShapeDtypeStruct((count, model), BF16), *outs],
        scratch_shapes=[
            pltpu.VMEM((6, *block), BF16),
            pltpu.VMEM((2, *block), BF16),
            pltpu.VMEM((8, model), F32),
            pltpu.SemaphoreType.DMA((copies,)),
            pltpu.SemaphoreType.DMA((copies,)),
            *scratch,
        ],
        compiler_params=pltpu.CompilerParams(
            collective_id=number, has_side_effects=True, vmem_limit_bytes=48 << 20
        ),
        cost_estimate=pl.CostEstimate(flops=0, bytes_accessed=250 << 20, transcendentals=0),
    )(part, *inputs, *dummies)


def swapped(block):
    return lax.ppermute(block, "seq", [(0, 1), (1, 0)])


def in_order(mine, other, core, axis):
    first = jnp.where(core == 0, mine, other)
    second = jnp.where(core == 0, other, mine)
    return jnp.concatenate([first, second], axis=axis)


def after(block, *done):
    nothing = sum(part[(0,) * part.ndim].astype(F32) for part in done) * 0.0
    return block + nothing.astype(block.dtype)


def halves(block, core, axis):
    size = block.shape[axis] // 2
    pick = lambda i: lax.dynamic_slice_in_dim(block, i * size, size, axis=axis)
    return pick(core), pick(1 - core)


def both_tokens(left, right):
    product = lambda a, b: lax.dot_general(
        a, b, (((0,), (0,)), ((), ())), preferred_element_type=F32
    )
    return (product(left[0], right[0]) + product(left[1], right[1])).astype(BF16)


def own_columns(block, core):
    mine, other = halves(block, core, 1)
    return mine, swapped(other)


def over_row(pair, axis):
    return lax.psum_scatter(pair, "row", scatter_dimension=axis, tiled=True)


def joined_shards(
    block_in,
    doc_lengths,
    attn_gain,
    qkv_weight,
    conv_weight,
    beta_weight,
    out_gain,
    out_weight,
    ffn_gain,
    gateup_weight,
    down_weight,
    cotangent,
):
    tok_count, model = block_in.shape[1:]
    core, own = lax.axis_index("seq"), lax.axis_index("mp")
    width = conv_weight.shape[2] // 2
    own_heads = width // HDIM
    quarter = tok_count // 4

    gather = lambda weight: lax.all_gather(weight, ("seq", "row"), axis=1, tiled=True)
    mixer_full = gather(jnp.concatenate([qkv_weight, out_weight.T[None]]))
    qkv_full, out_full = mixer_full[:3], mixer_full[3]
    beta_full, gateup_full, down_full = (
        gather(beta_weight),
        gather(gateup_weight),
        gather(down_weight),
    )
    qkv_own = lax.dynamic_slice_in_dim(qkv_full, core * width, width, axis=2)
    beta_own = lax.dynamic_slice_in_dim(beta_full, core * own_heads, own_heads, axis=0)
    mix_weight = jnp.concatenate(
        [qkv_own[0], qkv_own[1], qkv_own[2], jnp.pad(beta_own.T, ((0, 0), (0, HDIM - own_heads)))],
        axis=1,
    )
    conv_own = lax.dynamic_slice_in_dim(conv_weight, core * width, width, axis=2)
    conv_own = conv_own.transpose(1, 0, 2).reshape(KERNEL, 3 * width)

    residual_in = block_in[0].astype(F32)
    stat_in = lax.rsqrt(jnp.mean(residual_in * residual_in, axis=-1, keepdims=True) + EPSILON)
    normed_mine = (residual_in * stat_in * attn_gain).astype(BF16)
    normed = in_order(normed_mine, swapped(normed_mine), core, 0)

    positions = jnp.arange(2 * tok_count, dtype=jnp.int32)
    doc_start, real_row = row_layout(doc_lengths[0], positions)
    keep = jnp.pad((doc_start[::BLOCK] != positions[::BLOCK]).astype(F32), (0, 1))
    count = jnp.sum(real_row.reshape(-1, BLOCK), axis=1).astype(jnp.int32)
    raw = jnp.dot(normed, mix_weight, preferred_element_type=F32).astype(BF16)
    gain = out_gain[None, :]
    group = 4 if raw.shape[0] % (4 * CHUNK) == 0 else 1
    heads_out, *saved = forward(keep, count, raw, conv_own, gain, group)

    mine, other = halves(heads_out, core, 0)
    normed_out = in_order(mine, swapped(other), core, 1)
    branch_part = lax.dot_general(
        normed_out, out_full, (((1,), (1,)), ((), ())), preferred_element_type=F32
    )
    own_rows = lambda block: lax.dynamic_slice_in_dim(
        block[0], own * quarter, quarter, axis=0
    ).reshape(2, -1, model)
    residual_own = own_rows(block_in)
    rows_own = jax.ShapeDtypeStruct(residual_own.shape, F32)
    normed_mid, hidden = mp_phase(
        0,
        normed_forward,
        branch_part.astype(BF16),
        [residual_own, ffn_gain[None, :]],
        [],
        [rows_own],
    )

    grad_top = cotangent[0]
    gate_up = jnp.einsum("td,sdf->stf", normed_mid, gateup_full, preferred_element_type=F32)
    gate_sig = jax.nn.sigmoid(gate_up[0])
    product = (gate_up[0] * gate_sig * gate_up[1]).astype(BF16)
    down_pair = both_tokens((product, swapped(product)), own_columns(grad_top, core))
    ffn_part = jnp.dot(
        after(product, down_pair), down_full, preferred_element_type=F32
    ).astype(BF16)
    ffn_parts = lax.all_to_all(ffn_part, "mp", split_axis=0, concat_axis=0, tiled=True)
    ffn_own = jnp.sum(ffn_parts.astype(F32).reshape(4, quarter, model), axis=0)
    block_out = (hidden.reshape(quarter, model) + ffn_own).astype(BF16)
    grad_product = jnp.dot(grad_top, down_full.T, preferred_element_type=F32)
    grad_product = after(grad_product, ffn_part)
    grad_gate = grad_product * gate_up[1] * gate_sig * (1.0 + gate_up[0] * (1.0 - gate_sig))
    grad_up = grad_product * gate_up[0] * gate_sig
    grad_gate, grad_up = grad_gate.astype(BF16), grad_up.astype(BF16)
    grad_mid_part = jnp.einsum(
        "stf,sdf->td",
        jnp.stack([grad_gate, grad_up]),
        gateup_full,
        preferred_element_type=F32,
    ).astype(BF16)
    normed_halves = own_columns(normed_mid, core)
    gate_pair = both_tokens(normed_halves, (grad_gate, swapped(grad_gate)))
    up_pair = both_tokens(normed_halves, (grad_up, swapped(grad_up)))
    down_sum, gate_sum, up_sum = over_row(down_pair, 1), over_row(gate_pair, 0), over_row(up_pair, 0)
    grad_branch, grad_hidden, ffn_gain_part = mp_phase(
        1,
        partial(normed_backward, True),
        grad_mid_part,
        [hidden, own_rows(cotangent), ffn_gain[None, :]],
        [block_out, down_pair, gate_pair, up_pair],
        [rows_own, jax.ShapeDtypeStruct((1, model), F32)],
    )
    grad_normed_out = jnp.dot(grad_branch, out_full, preferred_element_type=F32).astype(BF16)

    mine, other = halves(grad_normed_out, core, 1)
    grad_heads = in_order(mine, swapped(other), core, 0)
    out_pair = both_tokens(
        (normed_out, swapped(after(normed_out, up_sum))), own_columns(grad_branch, core)
    )
    grad_raw, grad_conv_own, out_gain_part, block_out = backward(
        keep,
        count,
        raw,
        conv_own,
        gain,
        grad_heads,
        *saved,
        group,
        block_out,
        [down_sum, gate_sum],
    )
    grad_normed = lax.dot_general(
        grad_raw, mix_weight, (((1,), (1,)), ((), ())), preferred_element_type=F32
    )
    grad_normed_part = grad_normed.astype(BF16)
    normed_mine, normed_other = halves(normed, core, 1)
    by_columns = lambda part: lax.dot_general(
        part, grad_raw[:, : 3 * width], (((0,), (0,)), ((), ())), preferred_element_type=F32
    ).astype(BF16)
    qkv_other = swapped(by_columns(normed_other))
    qkv_mine = by_columns(normed_mine)
    grad_beta = lax.dot_general(
        grad_raw[:, 3 * width :], normed, (((0,), (0,)), ((), ())), preferred_element_type=F32
    )[:own_heads]
    grad_input, small = mp_phase(
        2,
        partial(normed_backward, False),
        grad_normed_part,
        [residual_own, grad_hidden, attn_gain[None, :]],
        [up_sum, out_pair, qkv_mine, qkv_other],
        [],
        both_cores=True,
        small=[ffn_gain_part, out_gain_part, grad_beta, grad_conv_own],
    )
    grad_input = grad_input.astype(F32)
    grad_attn_gain, grad_ffn_gain = small[0], small[1]
    grad_out_gain = small[2, : out_gain.shape[0]]
    span = beta_weight.shape[1]
    place_no = core * lax.axis_size("row") + lax.axis_index("row")
    grad_beta = lax.dynamic_slice_in_dim(small[8 : 8 + 2 * own_heads], place_no * span, span, axis=1)
    conv_at = 8 + 2 * own_heads
    conv_of = lambda i: (
        small[conv_at : conv_at + KERNEL, i * (model // 2) : i * (model // 2) + 3 * width]
        .reshape(KERNEL, 3, width)
        .transpose(1, 0, 2)
    )
    grad_conv = jnp.concatenate([conv_of(0), conv_of(1)], axis=2)
    grad_down, grad_out = down_sum.astype(F32), over_row(out_pair, 1).astype(F32)
    grad_gateup = jnp.stack([gate_sum, up_sum]).astype(F32)
    by_kind = lambda part: over_row(part, 0).reshape(-1, 3, width).transpose(1, 0, 2)
    grad_qkv = in_order(by_kind(qkv_mine), by_kind(qkv_other), core, 2).astype(F32)
    return (
        block_out[None],
        grad_input[None],
        grad_attn_gain,
        grad_qkv,
        grad_conv,
        grad_beta,
        grad_out_gain,
        grad_out,
        grad_ffn_gain,
        grad_gateup,
        grad_down,
    )


def solution(mesh):
    rows = mesh.shape["row"]
    joined = mesh.shape["seq"] == 2 and mesh.shape["mp"] == 4 and rows & (rows - 1) == 0
    return jax.shard_map(
        joined_shards if joined else spread_shards,
        mesh=mesh,
        in_specs=(
            P("row", "seq", None),
            P("row", None),
            P(),
            P(None, ("seq", "row"), "mp"),
            P(None, None, "mp"),
            P("mp", ("seq", "row")),
            P(),
            P("mp", ("seq", "row")),
            P(),
            P(None, ("seq", "row"), "mp"),
            P("mp", ("seq", "row")),
            P("row", "seq", None),
        ),
        out_specs=(
            P("row", "seq", None),
            P("row", "seq", None),
            P(),
            P(None, ("seq", "row"), "mp"),
            P(None, None, "mp"),
            P("mp", ("seq", "row")),
            P(),
            P("mp", ("seq", "row")),
            P(),
            P(None, ("seq", "row"), "mp"),
            P("mp", ("seq", "row")),
        ),
        check_vma=False,
    )
```

```python
import functools
from functools import partial

import jax
import jax.numpy as jnp
from jax import lax
from jax.experimental import pallas as pl
from jax.experimental.pallas import tpu as pltpu
from jax.sharding import PartitionSpec as P

HDIM = 128
KERNEL = 4
BLOCK = 64
CHUNK = 128
EPSILON = 1e-06
PRECISE = lax.Precision.HIGHEST
F32 = jnp.float32
BF16 = jnp.bfloat16

NT=(((1,),(1,)),((),())); NN=(((1,),(0,)),((),())); TN=(((0,),(0,)),((),()))

def mm(a,b,dims=NN):
    return lax.dot_general(a.astype(BF16), b.astype(BF16), dims, preferred_element_type=F32)

def iotas():
    return lax.broadcasted_iota(jnp.int32,(CHUNK,CHUNK),0), lax.broadcasted_iota(jnp.int32,(CHUNK,CHUNK),1)

def inverses(below):
    r,c=iotas()
    done=[jnp.where(r==c,1.0,0.0)-jnp.where(r//2==c//2,a,0.0) for a in below]
    size=2
    while size<CHUNK:
        pairs=(r//(2*size)==c//(2*size))&(r//size!=c//size)
        half=[mm(jnp.where(pairs,a,0.0),t) for a,t in zip(below,done)]
        done=[t-mm(t,x) for t,x in zip(done,half)]
        size*=2
    return done

def conv_act(ext_ref, base, lanes, cw, taps):
    total=cw[0:1]*ext_ref[pl.ds(base+8,CHUNK),lanes]
    for j in range(1,KERNEL):
        total=total+(cw[j:j+1]*taps[j-1])*ext_ref[pl.ds(base+8-j,CHUNK),lanes]
    sig=jax.nn.sigmoid(total)
    return total,sig

def layout(keep_ref, count_ref, block):
    r,_=iotas()
    inside=r%BLOCK
    first=r<BLOCK
    keep0,keep1,after=keep_ref[block],keep_ref[block+1],keep_ref[block+2]
    here=jnp.where(first,keep0,keep1)
    later=jnp.where(first,keep1,after)
    taps=[jnp.where(inside<j,here,1.0) for j in range(1,KERNEL)]
    taps_later=[jnp.where(inside>=BLOCK-j,later,1.0) for j in range(1,KERNEL)]
    real=jnp.where(inside<jnp.where(first,count_ref[block],count_ref[block+1]),1.0,0.0)
    return taps,taps_later,jnp.where(first,1.0,keep1),jnp.where(first,keep1,1.0),real,keep0,keep1

def fwd_kernel(heads, group, keep_ref, count_ref, raw_ref, cw_ref, gain_ref, normed_ref, o_ref, s_ref, t_ref, w_ref, r_ref, ext, state):
    rows=group*CHUNK
    step=pl.program_id(0)
    @pl.when(step==0)
    def _():
        ext[0:8,:]=jnp.zeros((8,3*heads*HDIM),F32)
        state[...]=jnp.zeros(state.shape,F32)
    @pl.when(step>0)
    def _():
        ext[0:8,:]=ext[rows:rows+8,:]
    ext[8:,:]=raw_ref[:,0:3*heads*HDIM].astype(F32)
    r,c=iotas()
    width=heads*HDIM
    units=[]
    below=[]
    for g in range(group):
        base=g*CHUNK
        taps,_,m,m2,real,keep0,keep1=layout(keep_ref,count_ref,2*(step*group+g))
        sig_b=jax.nn.sigmoid(raw_ref[pl.ds(base,CHUNK),pl.ds(3*width,HDIM)].astype(F32))*real
        for h in range(heads):
            act=[]
            for s in range(3):
                lanes=pl.ds(s*width+h*HDIM,HDIM)
                total,sig=conv_act(ext,base,lanes,cw_ref[:,lanes],taps)
                act.append(total*sig)
            q=act[0]*(lax.rsqrt(jnp.sum(act[0]*act[0],axis=1,keepdims=True)+EPSILON)*HDIM**-0.5)
            k=act[1]*lax.rsqrt(jnp.sum(act[1]*act[1],axis=1,keepdims=True)+EPSILON)
            v=act[2]
            b=sig_b[:,h:h+1]
            gram=mm(k,k,NT)
            score=mm(q,k,NT)
            mask=jnp.where(c<BLOCK,m,1.0)
            a=jnp.where(r>c,b*gram*mask,0.0)
            l=jnp.where(r>=c,score*mask,0.0)
            below.append(a)
            units.append((g,h,q*m,k*m2,l,b*k,b*v,m,keep0,keep1))
    done=inverses(below)
    wus=[(mm(t,u[5])*u[7],mm(t,u[6])) for t,u in zip(done,units)]
    for t,(w,u),(g,h,q,k,l,_,_,_,keep0,keep1) in zip(done,wus,units):
        base=g*CHUNK
        out=(pl.ds(base,CHUNK),pl.ds(h*HDIM,HDIM))
        t_ref[g,h]=t.astype(BF16)
        w_ref[out]=w.astype(BF16)
        s=state[h]*keep0
        s_ref[g,h]=s.astype(BF16)
        rr=u-mm(w,s)
        o=mm(q,s)+mm(l,rr)
        state[h]=s*keep1+mm(k,rr,TN)
        r_ref[out]=rr.astype(BF16)
        o_ref[out]=o
        stat=lax.rsqrt(jnp.mean(o*o,axis=1,keepdims=True)+EPSILON)
        normed_ref[out]=(o*stat*gain_ref[...]).astype(BF16)

def forward(keep, count, raw, cw, gain, group):
    n=raw.shape[0]; width=cw.shape[1]//3; heads=width//HDIM; rows=group*CHUNK
    nc=n//CHUNK
    row=lambda w: pl.BlockSpec((rows,w),lambda i:(i,0))
    mat=pl.BlockSpec((group,heads,HDIM,HDIM),lambda i:(i,0,0,0))
    full=lambda a: pl.BlockSpec(a.shape,lambda i:(0,0))
    return pl.pallas_call(functools.partial(fwd_kernel,heads,group),
        grid=(n//rows,),
        in_specs=[pl.BlockSpec(memory_space=pltpu.SMEM)]*2+[row(raw.shape[1]),full(cw),full(gain)],
        out_specs=[row(width),row(width),mat,mat,row(width),row(width)],
        out_shape=[jax.ShapeDtypeStruct((n,width),BF16),jax.ShapeDtypeStruct((n,width),F32),
            jax.ShapeDtypeStruct((nc,heads,HDIM,HDIM),BF16),jax.ShapeDtypeStruct((nc,heads,HDIM,HDIM),BF16),
            jax.ShapeDtypeStruct((n,width),BF16),jax.ShapeDtypeStruct((n,width),BF16)],
        scratch_shapes=[pltpu.VMEM((rows+8,3*width),F32),pltpu.VMEM((heads,HDIM,HDIM),F32)],
        compiler_params=pltpu.CompilerParams(vmem_limit_bytes=24<<20),
        cost_estimate=pl.CostEstimate(flops=0,bytes_accessed=120<<20,transcendentals=0),
    )(keep,count,raw,cw,gain)

def bwd_kernel(heads, group, keep_ref, count_ref, raw_ref, prev_ref, cw_ref, gain_ref, gno_ref, o_ref, s_ref, t_ref, w_ref, r_ref, *rest):
    block_ref=rest[0]
    graw_ref, gcw_ref, ggain_ref, all_ref, ext, gext, grad_state, local_sem, send_sem, recv_sem = rest[-10:]
    rows=group*CHUNK
    step=pl.program_id(0); steps=pl.num_programs(0)
    width=heads*HDIM
    @pl.when(step==0)
    def _():
        gext[rows:rows+8,:]=jnp.zeros((8,3*heads*HDIM),F32)
        grad_state[...]=jnp.zeros(grad_state.shape,F32)
        gcw_ref[...]=jnp.zeros(gcw_ref.shape,F32)
        ggain_ref[...]=jnp.zeros(ggain_ref.shape,F32)
    @pl.when(step>0)
    def _():
        gext[rows:rows+8,:]=gext[0:8,:]
    first=jnp.where(step==steps-1,0.0,1.0)
    place=lax.axis_index("mp")
    across_x=place+1-2*(place%2)
    across_y=(place+2)%4
    part=block_ref.shape[0]//2
    at=lambda of,half: all_ref.at[pl.ds(pl.multiple_of((2*of+half)*part,part),part)]
    def copy(index,source,target,other):
        return pltpu.make_async_remote_copy(src_ref=source,dst_ref=target,send_sem=send_sem.at[index],recv_sem=recv_sem.at[index],
            device_id={"mp":other},device_id_type=pl.DeviceIdType.MESH)
    top,low=block_ref.at[pl.ds(0,part)],block_ref.at[pl.ds(part,part)]
    keep_own=pltpu.make_async_copy(block_ref,all_ref.at[pl.ds(pl.multiple_of(2*place*part,2*part),2*part)],local_sem)
    sends=[copy(0,top,at(place,0),across_x),copy(1,low,at(place,1),across_y),copy(2,top,at(place,0),across_y),copy(3,low,at(place,1),across_x)]
    @pl.when(step==0)
    def _():
        barrier=pltpu.get_barrier_semaphore()
        for other in (across_x,across_y):
            pl.semaphore_signal(barrier,inc=1,device_id={"mp":other},device_id_type=pl.DeviceIdType.MESH)
        pl.semaphore_wait(barrier,2)
        keep_own.start()
        for send in sends: send.start()
    ext[0:8,:]=prev_ref[:,0:3*width].astype(F32)[8:16]*first
    ext[8:,:]=raw_ref[:,0:3*heads*HDIM].astype(F32)
    r,c=iotas()
    units=[]
    for g in range(group-1,-1,-1):
        base=g*CHUNK
        taps,taps_later,m,m2,real,keep0,keep1=layout(keep_ref,count_ref,2*((steps-1-step)*group+g))
        beta=jax.nn.sigmoid(raw_ref[pl.ds(base,CHUNK),pl.ds(3*width,HDIM)].astype(F32))
        sig_b=beta*real
        for h in range(heads):
            out=(pl.ds(base,CHUNK),pl.ds(h*HDIM,HDIM))
            act=[];tot=[];sigs=[]
            for s in range(3):
                lanes=pl.ds(s*width+h*HDIM,HDIM)
                total,sig=conv_act(ext,base,lanes,cw_ref[:,lanes],taps)
                act.append(total*sig);tot.append(total);sigs.append(sig)
            rq=lax.rsqrt(jnp.sum(act[0]*act[0],axis=1,keepdims=True)+EPSILON)
            rk=lax.rsqrt(jnp.sum(act[1]*act[1],axis=1,keepdims=True)+EPSILON)
            qu=act[0]*rq
            o=o_ref[out]
            stat=lax.rsqrt(jnp.mean(o*o,axis=1,keepdims=True)+EPSILON)
            uo=o*stat
            gno=gno_ref[out].astype(F32)
            ggain_ref[...]+=jnp.sum(gno*uo,axis=0,keepdims=True)
            gu=gno*gain_ref[...]
            do=stat*(gu-uo*jnp.mean(gu*uo,axis=1,keepdims=True))
            units.append(dict(g=g,h=h,base=base,out=out,taps=taps,m=m,m2=m2,keep0=keep0,keep1=keep1,tot=tot,sigs=sigs,
                rq=rq,rk=rk,qu=qu,q=qu*HDIM**-0.5,k=act[1]*rk,v=act[2],b=sig_b[:,h:h+1],do=do,
                mask=jnp.where(c<BLOCK,m,1.0)))
        for u in units[-heads:]: u.update(taps_later=taps_later,beta=beta,sig_b=sig_b)
    for u in units: u['gram']=mm(u['k'],u['k'],NT)*u['mask']
    for u in units: u['l']=jnp.where(r>=c,mm(u['q'],u['k'],NT)*u['mask'],0.0)
    for u in units: u['dr0']=mm(u['l'],u['do'],TN)
    for u in units: u['ds0']=mm(u['q']*u['m'],u['do'],TN)
    for u in units:
        dsn=grad_state[u['h']]
        u['dsn']=dsn
        u['dr']=u['dr0']+u['m2']*mm(u['k'],dsn)
        ds=u['keep1']*dsn+u['ds0']-mm(w_ref[u['out']],u['dr'],TN)
        grad_state[u['h']]=u['keep0']*ds
    for u in units: u['df']=mm(t_ref[u['g'],u['h']],u['dr'],TN)
    for u in units: u['dl']=jnp.where(r>=c,mm(u['do'],r_ref[u['out']],NT)*u['mask'],0.0)
    for u in units: u['da']=jnp.where(r>c,-mm(u['df'],r_ref[u['out']],NT),0.0)
    for u in units:
        u['de']=u['b']*u['df']
        u['e']=u['v']-u['m']*mm(u['k'],s_ref[u['g'],u['h']])
        u['gb']=jnp.sum(u['df']*u['e']+u['da']*u['gram'],axis=1,keepdims=True)
        u['dkk']=u['b']*u['da']*u['mask']
    for u in units: u['dq']=u['m']*mm(u['do'],s_ref[u['g'],u['h']],NT)+mm(u['dl'],u['k'])
    for u in units:
        u['dk']=(mm(u['dl'],u['q'],TN)+u['m2']*mm(r_ref[u['out']],u['dsn'],NT)-u['m']*mm(u['de'],s_ref[u['g'],u['h']],NT)
            +mm(u['dkk'],u['k'])+mm(u['dkk'],u['k'],TN))
    for u in units:
        gq=u['dq']*HDIM**-0.5
        gq=u['rq']*(gq-u['qu']*jnp.sum(gq*u['qu'],axis=1,keepdims=True))
        gk=u['rk']*(u['dk']-u['k']*jnp.sum(u['dk']*u['k'],axis=1,keepdims=True))
        for i,ga in enumerate((gq,gk,u['de'])):
            lanes=pl.ds(i*width+u['h']*HDIM,HDIM)
            sig,tot=u['sigs'][i],u['tot'][i]
            gc=ga*sig*(1.0+tot*(1.0-sig))
            gext[pl.ds(u['base'],CHUNK),lanes]=gc
            for j in range(KERNEL):
                win=ext[pl.ds(u['base']+8-j,CHUNK),lanes]
                prod=gc*win if j==0 else gc*win*u['taps'][j-1]
                gcw_ref[j:j+1,lanes]+=jnp.sum(prod,axis=0,keepdims=True)
    for at in range(0,len(units),heads):
        glog=jnp.zeros((CHUNK,HDIM),F32)
        for u in units[at:at+heads]:
            glog=jnp.where(c==u['h'],u['gb'],glog)
            for i in range(3):
                lanes=pl.ds(i*width+u['h']*HDIM,HDIM)
                cw=cw_ref[:,lanes]
                total=cw[0:1]*gext[pl.ds(u['base'],CHUNK),lanes]
                for j in range(1,KERNEL):
                    total=total+(cw[j:j+1]*u['taps_later'][j-1])*gext[pl.ds(u['base']+j,CHUNK),lanes]
                graw_ref[pl.ds(u['base'],CHUNK),lanes]=total.astype(BF16)
        graw_ref[pl.ds(u['base'],CHUNK),pl.ds(3*width,HDIM)]=(glog*u['sig_b']*(1.0-u['beta'])).astype(BF16)
    @pl.when(step==steps-1)
    def _():
        keep_own.wait()
        for send in sends: send.wait_recv()
        for send in sends: send.wait_send()

def backward(keep, count, raw, cw, gain, gno, o, s, t, w, r, group, block, dummies=()):
    n=raw.shape[0]; width=cw.shape[1]//3; heads=width//HDIM; rows=group*CHUNK
    steps=n//rows
    row=lambda w: pl.BlockSpec((rows,w),lambda i:(steps-1-i,0))
    mat=pl.BlockSpec((group,heads,HDIM,HDIM),lambda i:(steps-1-i,0,0,0))
    full=lambda a: pl.BlockSpec(a.shape,lambda i:(0,0))
    prev=pl.BlockSpec((16,raw.shape[1]),lambda i:(jnp.maximum((steps-1-i)*(rows//16)-1,0),0))
    return pl.pallas_call(functools.partial(bwd_kernel,heads,group),
        grid=(steps,),
        in_specs=[pl.BlockSpec(memory_space=pltpu.SMEM)]*2+[row(raw.shape[1]),prev,full(cw),full(gain),row(width),row(width),mat,mat,row(width),row(width)]+[pl.BlockSpec(memory_space=pl.ANY)]*(1+len(dummies)),
        out_specs=[row(raw.shape[1]),pl.BlockSpec((KERNEL,3*width),lambda i:(0,0)),pl.BlockSpec((1,HDIM),lambda i:(0,0)),pl.BlockSpec(memory_space=pl.ANY)],
        out_shape=[jax.ShapeDtypeStruct(raw.shape,BF16),
            jax.ShapeDtypeStruct((KERNEL,3*width),F32),jax.ShapeDtypeStruct((1,HDIM),F32),jax.ShapeDtypeStruct((4*block.shape[0],block.shape[1]),BF16)],
        scratch_shapes=[pltpu.VMEM((rows+8,3*width),F32),pltpu.VMEM((rows+8,3*width),F32),pltpu.VMEM((heads,HDIM,HDIM),F32),
            pltpu.SemaphoreType.DMA(()),pltpu.SemaphoreType.DMA((4,)),pltpu.SemaphoreType.DMA((4,))],
        compiler_params=pltpu.CompilerParams(collective_id=3,has_side_effects=True,vmem_limit_bytes=24<<20),
        cost_estimate=pl.CostEstimate(flops=0,bytes_accessed=120<<20,transcendentals=0),
    )(keep,count,raw,raw,cw,gain,gno,o,s,t,w,r,block,*dummies)


def passed_along(block, axis, distance):
    devices = range(lax.axis_size(axis))
    route = [(i - distance, i) for i in devices if i - distance in devices]
    return lax.ppermute(block, axis, route)


def row_layout(lengths, positions):
    span_len = (lengths + BLOCK - 1) // BLOCK * BLOCK
    closing = jnp.cumsum(span_len)
    opening = closing - span_len
    bounds = jnp.concatenate([opening, closing[-1:]])
    reached = bounds[None, :] <= positions[:, None]
    doc_start = jnp.max(jnp.where(reached, bounds[None, :], 0), axis=1)
    inside = (positions[:, None] >= opening[None, :]) & (
        positions[:, None] < (opening + lengths)[None, :]
    )
    real_mask = jnp.any(inside, axis=1).astype(jnp.float32)
    return (doc_start, real_mask)


def local_span(carry_on, queries, keys_in, values, strength):
    head_count, token_count, head_width = queries.shape
    block_count = token_count // BLOCK

    def to_blocks(tensor):
        return tensor.reshape(head_count, block_count, BLOCK, -1).transpose(1, 0, 2, 3)

    def from_blocks(tensor):
        return tensor.transpose(1, 0, 2, 3).reshape(head_count, token_count, -1)

    strict_lower = jnp.tril(jnp.ones((BLOCK, BLOCK), jnp.float32), -1)
    causal = jnp.tril(jnp.ones((BLOCK, BLOCK), jnp.float32))
    identity = jnp.broadcast_to(
        jnp.eye(head_width, dtype=jnp.float32), (head_count, head_width, head_width)
    )

    def block_step(carried, block_in):
        memory, mapping = carried
        q_blk, k_blk, v_blk, s_blk, carry_flag = block_in
        write_rate = s_blk[..., 0]
        memory = memory * carry_flag
        mapping = mapping * carry_flag
        key_gram = jnp.einsum("hcp,hdp->hcd", k_blk, k_blk, precision=PRECISE)
        system = jnp.eye(BLOCK, dtype=jnp.float32) + strict_lower * (
            write_rate[:, :, None] * key_gram
        )
        right_side = jnp.concatenate(
            [write_rate[..., None] * k_blk, write_rate[..., None] * v_blk], axis=-1
        )
        solved = lax.linalg.triangular_solve(
            system, right_side, left_side=True, lower=True, unit_diagonal=True
        )
        w_mat = solved[..., :head_width]
        u_mat = solved[..., head_width:]
        corrected = u_mat - jnp.einsum("hcp,hpv->hcv", w_mat, memory, precision=PRECISE)
        scores = causal * jnp.einsum("hcp,hdp->hcd", q_blk, k_blk, precision=PRECISE)
        out_zero = jnp.einsum("hcp,hpv->hcv", q_blk, memory, precision=PRECISE)
        out_zero = out_zero + jnp.einsum("hcd,hdv->hcv", scores, corrected, precision=PRECISE)
        w_map = jnp.einsum("hcp,hpq->hcq", w_mat, mapping, precision=PRECISE)
        q_prop = jnp.einsum("hcp,hpq->hcq", q_blk, mapping, precision=PRECISE)
        q_prop = q_prop - jnp.einsum("hcd,hdq->hcq", scores, w_map, precision=PRECISE)
        memory = memory + jnp.einsum("hcp,hcv->hpv", k_blk, corrected, precision=PRECISE)
        mapping = mapping - jnp.einsum("hcp,hcq->hpq", k_blk, w_map, precision=PRECISE)
        return ((memory, mapping), (out_zero, q_prop))

    initial = (jnp.zeros((head_count, head_width, head_width), jnp.float32), identity)
    blocks = (
        to_blocks(queries),
        to_blocks(keys_in),
        to_blocks(values),
        to_blocks(strength[..., None]),
        carry_on,
    )
    (memory, mapping), (out_zero, q_prop) = lax.scan(block_step, initial, blocks)
    return (from_blocks(out_zero), from_blocks(q_prop), mapping, memory)


def spread_shards(
    block_in,
    doc_lengths,
    attn_gain,
    qkv_weight,
    conv_weight,
    beta_weight,
    out_gain,
    out_weight,
    ffn_gain,
    gateup_weight,
    down_weight,
    cotangent,
):
    tok_count = block_in.shape[1]
    seq_count = lax.axis_size("seq")
    own_index = lax.axis_index("seq")
    positions = own_index * tok_count + jnp.arange(tok_count + KERNEL - 1, dtype=jnp.int32)
    doc_start, real_ext = row_layout(doc_lengths[0], positions)
    real_mask = real_ext[:tok_count]
    taps = [(positions - shift_no >= doc_start).astype(jnp.float32) for shift_no in range(KERNEL)]
    carry_on = (doc_start[:tok_count:BLOCK] != positions[:tok_count:BLOCK]).astype(jnp.float32)
    residual_in = block_in[0].astype(jnp.float32)
    stat_in = lax.rsqrt(jnp.mean(residual_in * residual_in, axis=-1, keepdims=True) + EPSILON)
    unit_in = residual_in * stat_in
    normed = (unit_in * attn_gain).astype(jnp.bfloat16)
    qkv_full, beta_full, out_full, gateup_full, down_full = (
        lax.all_gather(qkv_weight, ("seq", "row"), axis=1, tiled=True),
        lax.all_gather(beta_weight, ("seq", "row"), axis=1, tiled=True),
        lax.all_gather(out_weight, ("seq", "row"), axis=1, tiled=True),
        lax.all_gather(gateup_weight, ("seq", "row"), axis=1, tiled=True),
        lax.all_gather(down_weight, ("seq", "row"), axis=1, tiled=True),
    )
    raw = jnp.einsum("td,sdc->stc", normed, qkv_full, preferred_element_type=jnp.float32).astype(
        jnp.bfloat16
    )
    rims = passed_along(raw[:, tok_count - KERNEL + 1 :, :], "seq", 1)
    extended = jnp.concatenate([rims, raw], axis=1).astype(jnp.float32)
    conv_sum = jnp.zeros(raw.shape, jnp.float32)
    for shift_no in range(KERNEL):
        window = extended[:, KERNEL - 1 - shift_no : KERNEL - 1 - shift_no + tok_count]
        conv_sum = (
            conv_sum
            + conv_weight[:, shift_no][:, None, :]
            * window
            * taps[shift_no][:tok_count][None, :, None]
        )
    conv_sig = jax.nn.sigmoid(conv_sum)
    head_count = conv_weight.shape[2] // HDIM
    split_heads = (
        (conv_sum * conv_sig).reshape(3, tok_count, head_count, HDIM).transpose(0, 2, 1, 3)
    )
    q_scale = lax.rsqrt(jnp.sum(split_heads[0] * split_heads[0], axis=-1, keepdims=True) + EPSILON)
    q_unit = split_heads[0] * q_scale
    queries = q_unit * HDIM ** (-0.5)
    k_scale = lax.rsqrt(jnp.sum(split_heads[1] * split_heads[1], axis=-1, keepdims=True) + EPSILON)
    keys_in = split_heads[1] * k_scale
    values = split_heads[2]
    logits = jnp.einsum("td,hd->ht", normed, beta_full, preferred_element_type=jnp.float32)
    beta_sig = jax.nn.sigmoid(logits)
    strength = beta_sig * real_mask[None, :]
    (out_zero, q_prop, span_map, span_state), span_pullback = jax.vjp(
        partial(local_span, carry_on), queries, keys_in, values, strength
    )
    empty_state = jnp.zeros_like(span_state)
    all_maps, all_states = (
        lax.all_gather(span_map[None].astype(jnp.bfloat16), "seq", axis=0, tiled=True).astype(
            jnp.float32
        ),
        lax.all_gather(span_state[None].astype(jnp.bfloat16), "seq", axis=0, tiled=True).astype(
            jnp.float32
        ),
    )

    def fold_forward(counter, incoming):
        moved = (
            jnp.einsum("hpq,hqv->hpv", all_maps[counter], incoming, precision=PRECISE)
            + all_states[counter]
        )
        return jnp.where(counter < own_index, moved, incoming)

    state_in = lax.fori_loop(0, seq_count, fold_forward, empty_state)
    mixer = out_zero + jnp.einsum("htp,hpv->htv", q_prop, state_in, precision=PRECISE)
    stat_out = lax.rsqrt(jnp.mean(mixer * mixer, axis=-1, keepdims=True) + EPSILON)
    unit_out = mixer * stat_out
    normed_out = (
        (unit_out * out_gain).transpose(1, 0, 2).reshape(tok_count, -1).astype(jnp.bfloat16)
    )
    branch_part = jnp.dot(normed_out, out_full, preferred_element_type=jnp.float32)
    hidden = residual_in + lax.psum(branch_part.astype(jnp.bfloat16), "mp").astype(jnp.float32)
    stat_mid = lax.rsqrt(jnp.mean(hidden * hidden, axis=-1, keepdims=True) + EPSILON)
    unit_mid = hidden * stat_mid
    normed_mid = (unit_mid * ffn_gain).astype(jnp.bfloat16)
    gate_up = jnp.einsum("td,sdf->stf", normed_mid, gateup_full, preferred_element_type=jnp.float32)
    gate_sig = jax.nn.sigmoid(gate_up[0])
    product = (gate_up[0] * gate_sig * gate_up[1]).astype(jnp.bfloat16)
    ffn_part = jnp.dot(product, down_full, preferred_element_type=jnp.float32)
    block_out = hidden + lax.psum(ffn_part.astype(jnp.bfloat16), "mp").astype(jnp.float32)
    qkv_full, beta_full, out_full, gateup_full, down_full = (
        lax.all_gather(qkv_weight, ("seq", "row"), axis=1, tiled=True),
        lax.all_gather(beta_weight, ("seq", "row"), axis=1, tiled=True),
        lax.all_gather(out_weight, ("seq", "row"), axis=1, tiled=True),
        lax.all_gather(gateup_weight, ("seq", "row"), axis=1, tiled=True),
        lax.all_gather(down_weight, ("seq", "row"), axis=1, tiled=True),
    )
    grad_top = cotangent[0]
    grad_down_part = jnp.dot(product.T, grad_top, preferred_element_type=jnp.float32)
    grad_product = jnp.dot(grad_top, down_full.T, preferred_element_type=jnp.float32)
    grad_gate = grad_product * gate_up[1] * gate_sig * (1.0 + gate_up[0] * (1.0 - gate_sig))
    grad_up = grad_product * gate_up[0] * gate_sig
    grad_gate_up = jnp.stack([grad_gate, grad_up]).astype(jnp.bfloat16)
    grad_gateup_part = jnp.einsum(
        "td,stf->sdf", normed_mid, grad_gate_up, preferred_element_type=jnp.float32
    )
    grad_mid_part = jnp.einsum(
        "stf,sdf->td", grad_gate_up, gateup_full, preferred_element_type=jnp.float32
    )
    grad_mid = lax.psum(grad_mid_part.astype(jnp.bfloat16), "mp").astype(jnp.float32)
    ffn_gain_part = jnp.sum(grad_mid * unit_mid, axis=0)
    grad_unit_mid = grad_mid * ffn_gain
    grad_hidden = grad_top.astype(jnp.float32) + stat_mid * (
        grad_unit_mid - unit_mid * jnp.mean(grad_unit_mid * unit_mid, axis=-1, keepdims=True)
    )
    grad_branch = grad_hidden.astype(jnp.bfloat16)
    grad_out_part = jnp.dot(normed_out.T, grad_branch, preferred_element_type=jnp.float32)
    grad_normed_out = jnp.dot(grad_branch, out_full.T, preferred_element_type=jnp.float32)
    grad_normed_out = grad_normed_out.reshape(tok_count, head_count, HDIM).transpose(1, 0, 2)
    out_gain_part = jnp.sum(grad_normed_out * unit_out, axis=(0, 1))
    grad_unit_out = grad_normed_out * out_gain
    grad_mixer = stat_out * (
        grad_unit_out - unit_out * jnp.mean(grad_unit_out * unit_out, axis=-1, keepdims=True)
    )
    local_grad = jnp.einsum("htp,htv->hpv", q_prop, grad_mixer, precision=PRECISE)
    grad_q_prop = jnp.einsum("htv,hpv->htp", grad_mixer, state_in, precision=PRECISE)
    all_grads = lax.all_gather(
        local_grad[None].astype(jnp.bfloat16), "seq", axis=0, tiled=True
    ).astype(jnp.float32)

    def fold_backward(counter, later_grad):
        source = seq_count - 1 - counter
        moved = (
            jnp.einsum("hqp,hqv->hpv", all_maps[source], later_grad, precision=PRECISE)
            + all_grads[source]
        )
        return jnp.where(source > own_index, moved, later_grad)

    grad_end = lax.fori_loop(0, seq_count, fold_backward, empty_state)
    grad_map = jnp.einsum("hpv,hqv->hpq", grad_end, state_in, precision=PRECISE)
    grad_queries, grad_keys, grad_values, grad_strength = span_pullback(
        (grad_mixer, grad_q_prop, grad_map, grad_end)
    )
    grad_logits = (grad_strength * real_mask[None, :] * beta_sig * (1.0 - beta_sig)).astype(
        jnp.bfloat16
    )
    grad_beta_part = jnp.einsum(
        "ht,td->hd", grad_logits, normed, preferred_element_type=jnp.float32
    )
    grad_q_unit = grad_queries * HDIM ** (-0.5)
    grad_q_raw = q_scale * (
        grad_q_unit - q_unit * jnp.sum(grad_q_unit * q_unit, axis=-1, keepdims=True)
    )
    grad_k_raw = k_scale * (
        grad_keys - keys_in * jnp.sum(grad_keys * keys_in, axis=-1, keepdims=True)
    )
    grad_act = (
        jnp.stack([grad_q_raw, grad_k_raw, grad_values])
        .transpose(0, 2, 1, 3)
        .reshape(3, tok_count, -1)
    )
    grad_conv_sum = grad_act * conv_sig * (1.0 + conv_sum * (1.0 - conv_sig))
    rims_back = passed_along(grad_conv_sum[:, : KERNEL - 1, :], "seq", -1)
    grad_ext = jnp.concatenate([grad_conv_sum, rims_back], axis=1)
    grad_raw = jnp.zeros(grad_conv_sum.shape, jnp.float32)
    conv_terms = []
    for shift_no in range(KERNEL):
        grad_raw = (
            grad_raw
            + conv_weight[:, shift_no][:, None, :]
            * grad_ext[:, shift_no : shift_no + tok_count]
            * taps[shift_no][shift_no : shift_no + tok_count][None, :, None]
        )
        window = extended[:, KERNEL - 1 - shift_no : KERNEL - 1 - shift_no + tok_count]
        conv_terms.append(
            jnp.sum(grad_conv_sum * window * taps[shift_no][:tok_count][None, :, None], axis=1)
        )
    grad_conv_part = jnp.stack(conv_terms, axis=1)
    grad_raw_low = grad_raw.astype(jnp.bfloat16)
    grad_qkv_part = jnp.einsum(
        "td,stc->sdc", normed, grad_raw_low, preferred_element_type=jnp.float32
    )
    grad_normed = jnp.einsum(
        "stc,sdc->td", grad_raw_low, qkv_full, preferred_element_type=jnp.float32
    )
    grad_normed = grad_normed + jnp.einsum(
        "ht,hd->td", grad_logits, beta_full, preferred_element_type=jnp.float32
    )
    grad_normed, out_gain_sum = (
        lax.psum(grad_normed.astype(jnp.bfloat16), "mp").astype(jnp.float32),
        lax.psum(out_gain_part.astype(jnp.bfloat16), "mp").astype(jnp.float32),
    )
    attn_gain_part = jnp.sum(grad_normed * unit_in, axis=0)
    grad_unit_in = grad_normed * attn_gain
    grad_input = grad_hidden + stat_in * (
        grad_unit_in - unit_in * jnp.mean(grad_unit_in * unit_in, axis=-1, keepdims=True)
    )
    weight_sums = (
        lax.psum_scatter(grad_qkv_part, ("seq", "row"), scatter_dimension=1, tiled=True),
        lax.psum_scatter(grad_beta_part, ("seq", "row"), scatter_dimension=1, tiled=True),
        lax.psum_scatter(grad_out_part, ("seq", "row"), scatter_dimension=1, tiled=True),
        lax.psum_scatter(grad_gateup_part, ("seq", "row"), scatter_dimension=1, tiled=True),
        lax.psum_scatter(grad_down_part, ("seq", "row"), scatter_dimension=1, tiled=True),
    )
    small_sums = lax.psum(
        (attn_gain_part, grad_conv_part, out_gain_sum, ffn_gain_part), ("seq", "row")
    )
    return (
        block_out.astype(jnp.bfloat16)[None],
        grad_input[None],
        small_sums[0],
        weight_sums[0],
        small_sums[1],
        weight_sums[1],
        small_sums[2],
        weight_sums[2],
        small_sums[3],
        weight_sums[3],
        weight_sums[4],
    )


MESH = pl.DeviceIdType.MESH
STRIP = 16


def phase_kernel(middle, both_cores, small_sum, n_in, n_out, part_ref, *refs):
    inputs, all_ref = refs[:n_in], refs[n_in]
    outs, scratch = refs[n_in + 1 : n_in + n_out], refs[n_in + n_out :]
    got, sums, gain_sum, send_sem, recv_sem = scratch[:5]
    count = all_ref.shape[0]
    rows = count // 8
    place, core, row = lax.axis_index("mp"), lax.axis_index("seq"), lax.axis_index("row")
    across_x = place + 1 - 2 * (place % 2)
    across_y = (place + 2) % 4
    across_both = 3 - place
    ways = {"x": {"mp": across_x}, "y": {"mp": across_y}}
    if both_cores or small_sum:
        ways["core"] = {"seq": 1 - core}
    steps = []
    if small_sum:
        bit = 1
        while bit < lax.axis_size("row"):
            steps.append(f"row{bit}")
            ways[steps[-1]] = {"row": row + bit - 2 * bit * ((row // bit) % 2)}
            bit *= 2
        steps += ["core", "x", "y"]
    barrier = pltpu.get_barrier_semaphore()
    for other in ways.values():
        pl.semaphore_signal(barrier, inc=1, device_id=other, device_id_type=MESH)
    pl.semaphore_wait(barrier, len(ways))

    def copy(index, source, target, way):
        return pltpu.make_async_remote_copy(
            src_ref=source,
            dst_ref=target,
            send_sem=send_sem.at[index],
            recv_sem=recv_sem.at[index],
            device_id=ways[way],
            device_id_type=MESH,
        )

    def block(of, half):
        return pl.ds(pl.multiple_of((2 * of + half) * rows, rows), rows)

    def strips(body):
        @pl.loop(0, rows // STRIP)
        def _(i):
            body(pl.multiple_of(i * STRIP, STRIP))

    order = [(across_both, 0), (across_both, 1), (across_x, 0), (across_y, 1)]
    order += [(across_y, 0), (across_x, 1), (place, 0), (place, 1)]
    if both_cores:
        part, incoming, local_sem = scratch[5:8]
        mine = pltpu.make_async_copy(part_ref.at[pl.ds(core * count, count)], part, local_sem)
        mine.start()
        shared = []
        for i, (of, half) in enumerate(order):
            start = pl.multiple_of((1 - core) * count + (2 * of + half) * rows, rows)
            shared.append(
                copy(12 + i, part_ref.at[pl.ds(start, rows)], incoming.at[block(of, half)], "core")
            )
            shared[-1].start()
        mine.wait()
    else:
        part = part_ref

    def ready(index):
        if both_cores:
            of, half = order[index]
            shared[index].wait_recv()

            def add(at):
                strip = pl.ds((2 * of + half) * rows + at, STRIP)
                part[strip, :] = (
                    part[strip, :].astype(F32) + incoming[strip, :].astype(F32)
                ).astype(BF16)

            strips(add)

    far = [
        copy(0, part.at[block(across_both, 0)], got.at[0], "x"),
        copy(1, part.at[block(across_both, 1)], got.at[1], "y"),
    ]
    near = [
        copy(2, part.at[block(across_x, 0)], got.at[2], "x"),
        copy(3, part.at[block(across_y, 1)], got.at[3], "y"),
    ]
    last = [copy(4, sums.at[0], got.at[4], "y"), copy(5, sums.at[1], got.at[5], "x")]
    own = [all_ref.at[block(place, 0)], all_ref.at[block(place, 1)]]
    passed = [all_ref.at[block(across_x, 0)], all_ref.at[block(across_y, 1)]]
    out_first = [copy(6, own[0], own[0], "x"), copy(7, own[1], own[1], "y")]
    out_second = [copy(8, own[0], own[0], "y"), copy(9, own[1], own[1], "x")]
    out_third = [copy(10, passed[0], passed[0], "y"), copy(11, passed[1], passed[1], "x")]

    for index, step in enumerate((*far, *near)):
        ready(index)
        step.start()
    gain_sum[...] = jnp.zeros_like(gain_sum)
    for half, onward in ((0, across_y), (1, across_x)):
        ready(4 + half)
        far[half].wait_recv()

        def add(at):
            strip = pl.ds(at, STRIP)
            mine = part[pl.ds((2 * onward + half) * rows + at, STRIP), :]
            sums[half, strip, :] = (mine.astype(F32) + got[half, strip, :].astype(F32)).astype(BF16)

        strips(add)
        last[half].start()
    for half in (0, 1):
        ready(6 + half)
        near[half].wait_recv()
        last[half].wait_recv()

        def finish(at):
            strip = pl.ds(at, STRIP)
            total = part[pl.ds((2 * place + half) * rows + at, STRIP), :].astype(F32)
            total = total + got[2 + half, strip, :].astype(F32)
            total = total + got[4 + half, strip, :].astype(F32)
            result = middle(total, half, strip, inputs, outs, gain_sum)
            all_ref[pl.ds((2 * place + half) * rows + at, STRIP), :] = result.astype(BF16)

        strips(finish)
        out_first[half].start()
        out_second[half].start()

    gain = jnp.sum(gain_sum[...], axis=0, keepdims=True)
    small = []
    if small_sum:
        values, arrived = outs[-1], scratch[-1]
        first = n_in - small_sum["dummies"] - 3
        ffn_gain, out_gain, conv = inputs[first : first + 3]
        taps, width = conv.shape
        middle_lane = values.shape[1] // 2
        values[...] = jnp.zeros_like(values)
        values[0:1, :] = gain
        values[1:2, :] = ffn_gain[...]
        values[2:3, 0 : out_gain.shape[1]] = out_gain[...]
        for i in (0, 1):
            share = jnp.where(core == i, 1.0, 0.0)
            lane = i * middle_lane
            values[8 : 8 + taps, lane : lane + width] = conv[...] * share
    elif n_out > 2:
        outs[-1][...] = gain

    def small_step(number):
        height = 8 if steps[number] in ("x", "y") else values.shape[0]
        step = copy(
            20 + number,
            arrived.at[number, 1, pl.ds(0, height)],
            arrived.at[number, 0, pl.ds(0, height)],
            steps[number],
        )
        arrived[number, 1, 0:height, :] = values[0:height, :]
        step.start()
        step.wait_recv()
        values[0:height, :] = values[0:height, :] + arrived[number, 0, 0:height, :]
        small.append(step)

    for half in (0, 1):
        out_first[half].wait_recv()
        out_third[half].start()
    if small_sum:
        for number in range(len(steps)):
            small_step(number)
    for step in (*out_second, *out_third):
        step.wait_recv()
    for step in (*far, *near, *last, *out_first, *out_second, *out_third, *small):
        step.wait_send()
    if both_cores:
        for step in shared:
            step.wait_send()


def normed_forward(total, half, strip, inputs, outs, gain_sum):
    residual, gain = inputs[:2]
    hidden = residual[half, strip, :].astype(F32) + total
    outs[0][half, strip, :] = hidden
    stat = lax.rsqrt(jnp.mean(hidden * hidden, axis=1, keepdims=True) + EPSILON)
    return hidden * stat * gain[...]


def normed_backward(keep, total, half, strip, inputs, outs, gain_sum):
    value, base, gain = inputs[:3]
    value = value[half, strip, :].astype(F32)
    stat = lax.rsqrt(jnp.mean(value * value, axis=1, keepdims=True) + EPSILON)
    unit = value * stat
    gain_sum[...] += jnp.sum((total * unit).reshape(2, 8, -1), axis=0)
    scaled = total * gain[...]
    grad = base[half, strip, :].astype(F32) + stat * (
        scaled - unit * jnp.mean(scaled * unit, axis=1, keepdims=True)
    )
    if keep:
        outs[0][half, strip, :] = grad
    return grad


def mp_phase(number, middle, part, inputs, dummies, outs, both_cores=False, small=None):
    here, there = pl.BlockSpec(memory_space=pltpu.VMEM), pl.BlockSpec(memory_space=pl.ANY)
    count, model = part.shape[0] // (2 if both_cores else 1), part.shape[1]
    block = (count // 8, model)
    copies, scratch, small_sum = 12, [], None
    if both_cores:
        copies = 20
        scratch += [pltpu.VMEM((count, model), BF16)] * 2 + [pltpu.SemaphoreType.DMA(())]
    if small is not None:
        stages = lax.axis_size("row").bit_length() - 1 + 3
        copies = 20 + stages
        height = 8 + small[2].shape[0]
        shape = (height + -height % 8, model)
        scratch += [pltpu.VMEM((stages, 2, *shape), F32)]
        small_sum = {"dummies": len(dummies)}
        inputs = [*inputs, *small]
        outs = [*outs, jax.ShapeDtypeStruct(shape, F32)]
    kernel = functools.partial(
        phase_kernel, middle, both_cores, small_sum, len(inputs) + len(dummies), 1 + len(outs)
    )
    return pl.pallas_call(
        kernel,
        in_specs=[there if both_cores else here] + [here] * len(inputs) + [there] * len(dummies),
        out_specs=[here] * (1 + len(outs)),
        out_shape=[jax.ShapeDtypeStruct((count, model), BF16), *outs],
        scratch_shapes=[
            pltpu.VMEM((6, *block), BF16),
            pltpu.VMEM((2, *block), BF16),
            pltpu.VMEM((8, model), F32),
            pltpu.SemaphoreType.DMA((copies,)),
            pltpu.SemaphoreType.DMA((copies,)),
            *scratch,
        ],
        compiler_params=pltpu.CompilerParams(
            collective_id=number, has_side_effects=True, vmem_limit_bytes=48 << 20
        ),
        cost_estimate=pl.CostEstimate(flops=0, bytes_accessed=250 << 20, transcendentals=0),
    )(part, *inputs, *dummies)


def swapped(block):
    return lax.ppermute(block, "seq", [(0, 1), (1, 0)])


def across(block, bit):
    return lax.ppermute(block, "mp", [(i, i ^ bit) for i in range(4)])


def in_order(mine, other, core, axis):
    first = jnp.where(core == 0, mine, other)
    second = jnp.where(core == 0, other, mine)
    return jnp.concatenate([first, second], axis=axis)


def after(block, *done):
    nothing = sum(part[(0,) * part.ndim].astype(F32) for part in done) * 0.0
    return block + nothing.astype(block.dtype)


def halves(block, core, axis):
    size = block.shape[axis] // 2
    pick = lambda i: lax.dynamic_slice_in_dim(block, i * size, size, axis=axis)
    return pick(core), pick(1 - core)


def both_tokens(left, right):
    product = lambda a, b: lax.dot_general(
        a, b, (((0,), (0,)), ((), ())), preferred_element_type=F32
    )
    return (product(left[0], right[0]) + product(left[1], right[1])).astype(BF16)


def own_columns(block, core):
    mine, other = halves(block, core, 1)
    return mine, swapped(other)


def over_row(pair, axis):
    return lax.psum_scatter(pair, "row", scatter_dimension=axis, tiled=True)


def joined_shards(
    block_in,
    doc_lengths,
    attn_gain,
    qkv_weight,
    conv_weight,
    beta_weight,
    out_gain,
    out_weight,
    ffn_gain,
    gateup_weight,
    down_weight,
    cotangent,
):
    tok_count, model = block_in.shape[1:]
    core, own = lax.axis_index("seq"), lax.axis_index("mp")
    width = conv_weight.shape[2] // 2
    own_heads = width // HDIM
    quarter = tok_count // 4

    gather = lambda weight: lax.all_gather(weight, ("seq", "row"), axis=1, tiled=True)
    mixer_full = gather(jnp.concatenate([qkv_weight, out_weight.T[None]]))
    qkv_full, out_full = mixer_full[:3], mixer_full[3]
    beta_full, gateup_full, down_full = (
        gather(beta_weight),
        gather(gateup_weight),
        gather(down_weight),
    )
    qkv_own = lax.dynamic_slice_in_dim(qkv_full, core * width, width, axis=2)
    beta_own = lax.dynamic_slice_in_dim(beta_full, core * own_heads, own_heads, axis=0)
    mix_weight = jnp.concatenate(
        [qkv_own[0], qkv_own[1], qkv_own[2], jnp.pad(beta_own.T, ((0, 0), (0, HDIM - own_heads)))],
        axis=1,
    )
    conv_own = lax.dynamic_slice_in_dim(conv_weight, core * width, width, axis=2)
    conv_own = conv_own.transpose(1, 0, 2).reshape(KERNEL, 3 * width)

    residual_in = block_in[0].astype(F32)
    stat_in = lax.rsqrt(jnp.mean(residual_in * residual_in, axis=-1, keepdims=True) + EPSILON)
    normed_mine = (residual_in * stat_in * attn_gain).astype(BF16)
    normed = in_order(normed_mine, swapped(normed_mine), core, 0)

    positions = jnp.arange(2 * tok_count, dtype=jnp.int32)
    doc_start, real_row = row_layout(doc_lengths[0], positions)
    keep = jnp.pad((doc_start[::BLOCK] != positions[::BLOCK]).astype(F32), (0, 1))
    count = jnp.sum(real_row.reshape(-1, BLOCK), axis=1).astype(jnp.int32)
    raw = jnp.dot(normed, mix_weight, preferred_element_type=F32).astype(BF16)
    gain = out_gain[None, :]
    group = 4 if raw.shape[0] % (4 * CHUNK) == 0 else 1
    heads_out, *saved = forward(keep, count, raw, conv_own, gain, group)

    mine, other = halves(heads_out, core, 0)
    normed_out = in_order(mine, swapped(other), core, 1)
    branch_part = lax.dot_general(
        normed_out, out_full, (((1,), (1,)), ((), ())), preferred_element_type=F32
    )
    own_rows = lambda block: lax.dynamic_slice_in_dim(
        block[0], own * quarter, quarter, axis=0
    ).reshape(2, -1, model)
    residual_own = own_rows(block_in)
    rows_own = jax.ShapeDtypeStruct(residual_own.shape, F32)
    normed_mid, hidden = mp_phase(
        0,
        normed_forward,
        branch_part.astype(BF16),
        [residual_own, ffn_gain[None, :]],
        [],
        [rows_own],
    )

    grad_top = cotangent[0]
    gate_up = jnp.einsum("td,sdf->stf", normed_mid, gateup_full, preferred_element_type=F32)
    gate_sig = jax.nn.sigmoid(gate_up[0])
    product = (gate_up[0] * gate_sig * gate_up[1]).astype(BF16)
    down_pair = both_tokens((product, swapped(product)), own_columns(grad_top, core))
    ffn_part = jnp.dot(
        after(product, down_pair), down_full, preferred_element_type=F32
    ).astype(BF16)
    ffn_parts = lax.all_to_all(ffn_part, "mp", split_axis=0, concat_axis=0, tiled=True)
    ffn_own = jnp.sum(ffn_parts.astype(F32).reshape(4, quarter, model), axis=0)
    block_out = (hidden.reshape(quarter, model) + ffn_own).astype(BF16)
    grad_product = jnp.dot(grad_top, down_full.T, preferred_element_type=F32)
    grad_product = after(grad_product, ffn_part)
    grad_gate = grad_product * gate_up[1] * gate_sig * (1.0 + gate_up[0] * (1.0 - gate_sig))
    grad_up = grad_product * gate_up[0] * gate_sig
    grad_gate, grad_up = grad_gate.astype(BF16), grad_up.astype(BF16)
    grad_mid_part = jnp.einsum(
        "stf,sdf->td",
        jnp.stack([grad_gate, grad_up]),
        gateup_full,
        preferred_element_type=F32,
    ).astype(BF16)
    normed_halves = own_columns(normed_mid, core)
    gate_pair = both_tokens(normed_halves, (grad_gate, swapped(grad_gate)))
    up_pair = both_tokens(normed_halves, (grad_up, swapped(grad_up)))
    down_sum, gate_sum, up_sum = over_row(down_pair, 1), over_row(gate_pair, 0), over_row(up_pair, 0)
    grad_branch, grad_hidden, ffn_gain_part = mp_phase(
        1,
        partial(normed_backward, True),
        grad_mid_part,
        [hidden, own_rows(cotangent), ffn_gain[None, :]],
        [block_out, down_pair, gate_pair, up_pair],
        [rows_own, jax.ShapeDtypeStruct((1, model), F32)],
    )
    grad_normed_out = jnp.dot(grad_branch, out_full, preferred_element_type=F32).astype(BF16)

    mine, other = halves(grad_normed_out, core, 1)
    grad_heads = in_order(mine, swapped(other), core, 0)
    out_pair = both_tokens(
        (normed_out, swapped(after(normed_out, up_sum))), own_columns(grad_branch, core)
    )
    grad_raw, grad_conv_own, out_gain_part, block_out = backward(
        keep,
        count,
        raw,
        conv_own,
        gain,
        grad_heads,
        *saved,
        group,
        block_out,
        [down_sum, out_pair],
    )
    piece = lambda of, half: lax.dynamic_slice_in_dim(
        block_out, (2 * of + half) * (quarter // 2), quarter // 2, axis=0
    )
    far_rows = [across(piece(own ^ 1, 0), 2), across(piece(own ^ 2, 1), 1)]
    grad_normed = lax.dot_general(
        grad_raw, mix_weight, (((1,), (1,)), ((), ())), preferred_element_type=F32
    )
    grad_normed_part = grad_normed.astype(BF16)
    normed_mine, normed_other = halves(normed, core, 1)
    by_columns = lambda part: lax.dot_general(
        part, grad_raw, (((0,), (0,)), ((), ())), preferred_element_type=F32
    ).astype(BF16)
    qkv_other = swapped(by_columns(normed_other))
    qkv_mine = by_columns(normed_mine)
    grad_input, small = mp_phase(
        2,
        partial(normed_backward, False),
        grad_normed_part,
        [residual_own, grad_hidden, attn_gain[None, :]],
        [gate_sum, up_sum, qkv_mine, qkv_other, *far_rows],
        [],
        both_cores=True,
        small=[ffn_gain_part, out_gain_part, grad_conv_own],
    )
    grad_input = grad_input.astype(F32)
    places = jnp.arange(4)[:, None, None]
    block_out = jnp.where(
        places == (own ^ 3),
        jnp.concatenate(far_rows)[None],
        block_out.reshape(4, quarter, model),
    ).reshape(tok_count, model)
    grad_attn_gain, grad_ffn_gain = small[0], small[1]
    grad_out_gain = small[2, : out_gain.shape[0]]
    conv_at = 8
    conv_of = lambda i: (
        small[conv_at : conv_at + KERNEL, i * (model // 2) : i * (model // 2) + 3 * width]
        .reshape(KERNEL, 3, width)
        .transpose(1, 0, 2)
    )
    grad_conv = jnp.concatenate([conv_of(0), conv_of(1)], axis=2)
    grad_down, grad_out = down_sum.astype(F32), over_row(out_pair, 1).astype(F32)
    grad_gateup = jnp.stack([gate_sum, up_sum]).astype(F32)
    row_sums = [over_row(part, 0) for part in (qkv_mine, qkv_other)]
    by_kind = lambda part: part[:, : 3 * width].reshape(-1, 3, width).transpose(1, 0, 2)
    grad_qkv = in_order(by_kind(row_sums[0]), by_kind(row_sums[1]), core, 2).astype(F32)
    of_heads = lambda part: part[:, 3 * width : 3 * width + own_heads].T
    grad_beta = in_order(of_heads(row_sums[0]), of_heads(row_sums[1]), core, 0).astype(F32)
    return (
        block_out[None],
        grad_input[None],
        grad_attn_gain,
        grad_qkv,
        grad_conv,
        grad_beta,
        grad_out_gain,
        grad_out,
        grad_ffn_gain,
        grad_gateup,
        grad_down,
    )


def solution(mesh):
    rows = mesh.shape["row"]
    joined = mesh.shape["seq"] == 2 and mesh.shape["mp"] == 4 and rows & (rows - 1) == 0
    return jax.shard_map(
        joined_shards if joined else spread_shards,
        mesh=mesh,
        in_specs=(
            P("row", "seq", None),
            P("row", None),
            P(),
            P(None, ("seq", "row"), "mp"),
            P(None, None, "mp"),
            P("mp", ("seq", "row")),
            P(),
            P("mp", ("seq", "row")),
            P(),
            P(None, ("seq", "row"), "mp"),
            P("mp", ("seq", "row")),
            P("row", "seq", None),
        ),
        out_specs=(
            P("row", "seq", None),
            P("row", "seq", None),
            P(),
            P(None, ("seq", "row"), "mp"),
            P(None, None, "mp"),
            P("mp", ("seq", "row")),
            P(),
            P("mp", ("seq", "row")),
            P(),
            P(None, ("seq", "row"), "mp"),
            P("mp", ("seq", "row")),
        ),
        check_vma=False,
    )
```

```python
import functools
from functools import partial

import jax
import jax.numpy as jnp
from jax import lax
from jax.experimental import pallas as pl
from jax.experimental.pallas import tpu as pltpu
from jax.sharding import PartitionSpec as P

HDIM = 128
KERNEL = 4
BLOCK = 64
CHUNK = 128
EPSILON = 1e-06
PRECISE = lax.Precision.HIGHEST
F32 = jnp.float32
BF16 = jnp.bfloat16

NT=(((1,),(1,)),((),())); NN=(((1,),(0,)),((),())); TN=(((0,),(0,)),((),()))

def mm(a,b,dims=NN):
    return lax.dot_general(a.astype(BF16), b.astype(BF16), dims, preferred_element_type=F32)

def iotas():
    return lax.broadcasted_iota(jnp.int32,(CHUNK,CHUNK),0), lax.broadcasted_iota(jnp.int32,(CHUNK,CHUNK),1)

def inverses(below):
    r,c=iotas()
    done=[jnp.where(r==c,1.0,0.0)-jnp.where(r//2==c//2,a,0.0) for a in below]
    size=2
    while size<CHUNK:
        pairs=(r//(2*size)==c//(2*size))&(r//size!=c//size)
        half=[mm(jnp.where(pairs,a,0.0),t) for a,t in zip(below,done)]
        done=[t-mm(t,x) for t,x in zip(done,half)]
        size*=2
    return done

def conv_act(ext_ref, base, lanes, cw, taps):
    total=cw[0:1]*ext_ref[pl.ds(base+8,CHUNK),lanes]
    for j in range(1,KERNEL):
        total=total+(cw[j:j+1]*taps[j-1])*ext_ref[pl.ds(base+8-j,CHUNK),lanes]
    sig=jax.nn.sigmoid(total)
    return total,sig

def layout(keep_ref, count_ref, block):
    r,_=iotas()
    inside=r%BLOCK
    first=r<BLOCK
    keep0,keep1,after=keep_ref[block],keep_ref[block+1],keep_ref[block+2]
    here=jnp.where(first,keep0,keep1)
    later=jnp.where(first,keep1,after)
    taps=[jnp.where(inside<j,here,1.0) for j in range(1,KERNEL)]
    taps_later=[jnp.where(inside>=BLOCK-j,later,1.0) for j in range(1,KERNEL)]
    real=jnp.where(inside<jnp.where(first,count_ref[block],count_ref[block+1]),1.0,0.0)
    return taps,taps_later,jnp.where(first,1.0,keep1),jnp.where(first,keep1,1.0),real,keep0,keep1

def fwd_kernel(heads, group, keep_ref, count_ref, raw_ref, cw_ref, gain_ref, normed_ref, o_ref, s_ref, t_ref, w_ref, r_ref, ext, state):
    rows=group*CHUNK
    step=pl.program_id(0)
    @pl.when(step==0)
    def _():
        ext[0:8,:]=jnp.zeros((8,3*heads*HDIM),F32)
        state[...]=jnp.zeros(state.shape,F32)
    @pl.when(step>0)
    def _():
        ext[0:8,:]=ext[rows:rows+8,:]
    ext[8:,:]=raw_ref[:,0:3*heads*HDIM].astype(F32)
    r,c=iotas()
    width=heads*HDIM
    units=[]
    below=[]
    for g in range(group):
        base=g*CHUNK
        taps,_,m,m2,real,keep0,keep1=layout(keep_ref,count_ref,2*(step*group+g))
        sig_b=jax.nn.sigmoid(raw_ref[pl.ds(base,CHUNK),pl.ds(3*width,HDIM)].astype(F32))*real
        for h in range(heads):
            act=[]
            for s in range(3):
                lanes=pl.ds(s*width+h*HDIM,HDIM)
                total,sig=conv_act(ext,base,lanes,cw_ref[:,lanes],taps)
                act.append(total*sig)
            q=act[0]*(lax.rsqrt(jnp.sum(act[0]*act[0],axis=1,keepdims=True)+EPSILON)*HDIM**-0.5)
            k=act[1]*lax.rsqrt(jnp.sum(act[1]*act[1],axis=1,keepdims=True)+EPSILON)
            v=act[2]
            b=sig_b[:,h:h+1]
            gram=mm(k,k,NT)
            score=mm(q,k,NT)
            mask=jnp.where(c<BLOCK,m,1.0)
            a=jnp.where(r>c,b*gram*mask,0.0)
            l=jnp.where(r>=c,score*mask,0.0)
            below.append(a)
            units.append((g,h,q*m,k*m2,l,b*k,b*v,m,keep0,keep1))
    done=inverses(below)
    wus=[(mm(t,u[5])*u[7],mm(t,u[6])) for t,u in zip(done,units)]
    for t,(w,u),(g,h,q,k,l,_,_,_,keep0,keep1) in zip(done,wus,units):
        base=g*CHUNK
        out=(pl.ds(base,CHUNK),pl.ds(h*HDIM,HDIM))
        t_ref[g,h]=t.astype(BF16)
        w_ref[out]=w.astype(BF16)
        s=state[h]*keep0
        s_ref[g,h]=s.astype(BF16)
        rr=u-mm(w,s)
        o=mm(q,s)+mm(l,rr)
        state[h]=s*keep1+mm(k,rr,TN)
        r_ref[out]=rr.astype(BF16)
        o_ref[out]=o
        stat=lax.rsqrt(jnp.mean(o*o,axis=1,keepdims=True)+EPSILON)
        normed_ref[out]=(o*stat*gain_ref[...]).astype(BF16)

def forward(keep, count, raw, cw, gain, group):
    n=raw.shape[0]; width=cw.shape[1]//3; heads=width//HDIM; rows=group*CHUNK
    nc=n//CHUNK
    row=lambda w: pl.BlockSpec((rows,w),lambda i:(i,0))
    mat=pl.BlockSpec((group,heads,HDIM,HDIM),lambda i:(i,0,0,0))
    full=lambda a: pl.BlockSpec(a.shape,lambda i:(0,0))
    return pl.pallas_call(functools.partial(fwd_kernel,heads,group),
        grid=(n//rows,),
        in_specs=[pl.BlockSpec(memory_space=pltpu.SMEM)]*2+[row(raw.shape[1]),full(cw),full(gain)],
        out_specs=[row(width),row(width),mat,mat,row(width),row(width)],
        out_shape=[jax.ShapeDtypeStruct((n,width),BF16),jax.ShapeDtypeStruct((n,width),F32),
            jax.ShapeDtypeStruct((nc,heads,HDIM,HDIM),BF16),jax.ShapeDtypeStruct((nc,heads,HDIM,HDIM),BF16),
            jax.ShapeDtypeStruct((n,width),BF16),jax.ShapeDtypeStruct((n,width),BF16)],
        scratch_shapes=[pltpu.VMEM((rows+8,3*width),F32),pltpu.VMEM((heads,HDIM,HDIM),F32)],
        compiler_params=pltpu.CompilerParams(vmem_limit_bytes=24<<20),
        cost_estimate=pl.CostEstimate(flops=0,bytes_accessed=120<<20,transcendentals=0),
    )(keep,count,raw,cw,gain)

def bwd_kernel(heads, group, keep_ref, count_ref, raw_ref, prev_ref, cw_ref, gain_ref, gno_ref, o_ref, s_ref, t_ref, w_ref, r_ref, *rest):
    block_ref=rest[0]
    graw_ref, gcw_ref, ggain_ref, all_ref, ext, gext, grad_state, local_sem, send_sem, recv_sem = rest[-10:]
    rows=group*CHUNK
    step=pl.program_id(0); steps=pl.num_programs(0)
    width=heads*HDIM
    @pl.when(step==0)
    def _():
        gext[rows:rows+8,:]=jnp.zeros((8,3*heads*HDIM),F32)
        grad_state[...]=jnp.zeros(grad_state.shape,F32)
        gcw_ref[...]=jnp.zeros(gcw_ref.shape,F32)
        ggain_ref[...]=jnp.zeros(ggain_ref.shape,F32)
    @pl.when(step>0)
    def _():
        gext[rows:rows+8,:]=gext[0:8,:]
    first=jnp.where(step==steps-1,0.0,1.0)
    place=lax.axis_index("mp")
    across_x=place+1-2*(place%2)
    across_y=(place+2)%4
    part=block_ref.shape[0]//2
    at=lambda of,half: all_ref.at[pl.ds(pl.multiple_of((2*of+half)*part,part),part)]
    def copy(index,source,target,other):
        return pltpu.make_async_remote_copy(src_ref=source,dst_ref=target,send_sem=send_sem.at[index],recv_sem=recv_sem.at[index],
            device_id={"mp":other},device_id_type=pl.DeviceIdType.MESH)
    top,low=block_ref.at[pl.ds(0,part)],block_ref.at[pl.ds(part,part)]
    keep_own=pltpu.make_async_copy(block_ref,all_ref.at[pl.ds(pl.multiple_of(2*place*part,2*part),2*part)],local_sem)
    sends=[copy(0,top,at(place,0),across_x),copy(1,low,at(place,1),across_y),copy(2,top,at(place,0),across_y),copy(3,low,at(place,1),across_x)]
    @pl.when(step==0)
    def _():
        barrier=pltpu.get_barrier_semaphore()
        for other in (across_x,across_y):
            pl.semaphore_signal(barrier,inc=1,device_id={"mp":other},device_id_type=pl.DeviceIdType.MESH)
        pl.semaphore_wait(barrier,2)
        keep_own.start()
        for send in sends: send.start()
    ext[0:8,:]=prev_ref[:,0:3*width].astype(F32)[8:16]*first
    ext[8:,:]=raw_ref[:,0:3*heads*HDIM].astype(F32)
    r,c=iotas()
    units=[]
    for g in range(group-1,-1,-1):
        base=g*CHUNK
        taps,taps_later,m,m2,real,keep0,keep1=layout(keep_ref,count_ref,2*((steps-1-step)*group+g))
        beta=jax.nn.sigmoid(raw_ref[pl.ds(base,CHUNK),pl.ds(3*width,HDIM)].astype(F32))
        sig_b=beta*real
        for h in range(heads):
            out=(pl.ds(base,CHUNK),pl.ds(h*HDIM,HDIM))
            act=[];tot=[];sigs=[]
            for s in range(3):
                lanes=pl.ds(s*width+h*HDIM,HDIM)
                total,sig=conv_act(ext,base,lanes,cw_ref[:,lanes],taps)
                act.append(total*sig);tot.append(total);sigs.append(sig)
            rq=lax.rsqrt(jnp.sum(act[0]*act[0],axis=1,keepdims=True)+EPSILON)
            rk=lax.rsqrt(jnp.sum(act[1]*act[1],axis=1,keepdims=True)+EPSILON)
            qu=act[0]*rq
            o=o_ref[out]
            stat=lax.rsqrt(jnp.mean(o*o,axis=1,keepdims=True)+EPSILON)
            uo=o*stat
            gno=gno_ref[out].astype(F32)
            ggain_ref[...]+=jnp.sum(gno*uo,axis=0,keepdims=True)
            gu=gno*gain_ref[...]
            do=stat*(gu-uo*jnp.mean(gu*uo,axis=1,keepdims=True))
            units.append(dict(g=g,h=h,base=base,out=out,taps=taps,m=m,m2=m2,keep0=keep0,keep1=keep1,tot=tot,sigs=sigs,
                rq=rq,rk=rk,qu=qu,q=qu*HDIM**-0.5,k=act[1]*rk,v=act[2],b=sig_b[:,h:h+1],do=do,
                mask=jnp.where(c<BLOCK,m,1.0)))
        for u in units[-heads:]: u.update(taps_later=taps_later,beta=beta,sig_b=sig_b)
    for u in units: u['gram']=mm(u['k'],u['k'],NT)*u['mask']
    for u in units: u['l']=jnp.where(r>=c,mm(u['q'],u['k'],NT)*u['mask'],0.0)
    for u in units: u['dr0']=mm(u['l'],u['do'],TN)
    for u in units: u['ds0']=mm(u['q']*u['m'],u['do'],TN)
    for u in units:
        dsn=grad_state[u['h']]
        u['dsn']=dsn
        u['dr']=u['dr0']+u['m2']*mm(u['k'],dsn)
        ds=u['keep1']*dsn+u['ds0']-mm(w_ref[u['out']],u['dr'],TN)
        grad_state[u['h']]=u['keep0']*ds
    for u in units: u['df']=mm(t_ref[u['g'],u['h']],u['dr'],TN)
    for u in units: u['dl']=jnp.where(r>=c,mm(u['do'],r_ref[u['out']],NT)*u['mask'],0.0)
    for u in units: u['da']=jnp.where(r>c,-mm(u['df'],r_ref[u['out']],NT),0.0)
    for u in units:
        u['de']=u['b']*u['df']
        u['e']=u['v']-u['m']*mm(u['k'],s_ref[u['g'],u['h']])
        u['gb']=jnp.sum(u['df']*u['e']+u['da']*u['gram'],axis=1,keepdims=True)
        u['dkk']=u['b']*u['da']*u['mask']
    for u in units: u['dq']=u['m']*mm(u['do'],s_ref[u['g'],u['h']],NT)+mm(u['dl'],u['k'])
    for u in units:
        u['dk']=(mm(u['dl'],u['q'],TN)+u['m2']*mm(r_ref[u['out']],u['dsn'],NT)-u['m']*mm(u['de'],s_ref[u['g'],u['h']],NT)
            +mm(u['dkk'],u['k'])+mm(u['dkk'],u['k'],TN))
    for u in units:
        gq=u['dq']*HDIM**-0.5
        gq=u['rq']*(gq-u['qu']*jnp.sum(gq*u['qu'],axis=1,keepdims=True))
        gk=u['rk']*(u['dk']-u['k']*jnp.sum(u['dk']*u['k'],axis=1,keepdims=True))
        for i,ga in enumerate((gq,gk,u['de'])):
            lanes=pl.ds(i*width+u['h']*HDIM,HDIM)
            sig,tot=u['sigs'][i],u['tot'][i]
            gc=ga*sig*(1.0+tot*(1.0-sig))
            gext[pl.ds(u['base'],CHUNK),lanes]=gc
            for j in range(KERNEL):
                win=ext[pl.ds(u['base']+8-j,CHUNK),lanes]
                prod=gc*win if j==0 else gc*win*u['taps'][j-1]
                gcw_ref[j:j+1,lanes]+=jnp.sum(prod,axis=0,keepdims=True)
    for at in range(0,len(units),heads):
        glog=jnp.zeros((CHUNK,HDIM),F32)
        for u in units[at:at+heads]:
            glog=jnp.where(c==u['h'],u['gb'],glog)
            for i in range(3):
                lanes=pl.ds(i*width+u['h']*HDIM,HDIM)
                cw=cw_ref[:,lanes]
                total=cw[0:1]*gext[pl.ds(u['base'],CHUNK),lanes]
                for j in range(1,KERNEL):
                    total=total+(cw[j:j+1]*u['taps_later'][j-1])*gext[pl.ds(u['base']+j,CHUNK),lanes]
                graw_ref[pl.ds(u['base'],CHUNK),lanes]=total.astype(BF16)
        graw_ref[pl.ds(u['base'],CHUNK),pl.ds(3*width,HDIM)]=(glog*u['sig_b']*(1.0-u['beta'])).astype(BF16)
    @pl.when(step==steps-1)
    def _():
        keep_own.wait()
        for send in sends: send.wait_recv()
        for send in sends: send.wait_send()

def backward(keep, count, raw, cw, gain, gno, o, s, t, w, r, group, block, dummies=()):
    n=raw.shape[0]; width=cw.shape[1]//3; heads=width//HDIM; rows=group*CHUNK
    steps=n//rows
    row=lambda w: pl.BlockSpec((rows,w),lambda i:(steps-1-i,0))
    mat=pl.BlockSpec((group,heads,HDIM,HDIM),lambda i:(steps-1-i,0,0,0))
    full=lambda a: pl.BlockSpec(a.shape,lambda i:(0,0))
    prev=pl.BlockSpec((16,raw.shape[1]),lambda i:(jnp.maximum((steps-1-i)*(rows//16)-1,0),0))
    return pl.pallas_call(functools.partial(bwd_kernel,heads,group),
        grid=(steps,),
        in_specs=[pl.BlockSpec(memory_space=pltpu.SMEM)]*2+[row(raw.shape[1]),prev,full(cw),full(gain),row(width),row(width),mat,mat,row(width),row(width)]+[pl.BlockSpec(memory_space=pl.ANY)]*(1+len(dummies)),
        out_specs=[row(raw.shape[1]),pl.BlockSpec((KERNEL,3*width),lambda i:(0,0)),pl.BlockSpec((1,HDIM),lambda i:(0,0)),pl.BlockSpec(memory_space=pl.ANY)],
        out_shape=[jax.ShapeDtypeStruct(raw.shape,BF16),
            jax.ShapeDtypeStruct((KERNEL,3*width),F32),jax.ShapeDtypeStruct((1,HDIM),F32),jax.ShapeDtypeStruct((4*block.shape[0],block.shape[1]),BF16)],
        scratch_shapes=[pltpu.VMEM((rows+8,3*width),F32),pltpu.VMEM((rows+8,3*width),F32),pltpu.VMEM((heads,HDIM,HDIM),F32),
            pltpu.SemaphoreType.DMA(()),pltpu.SemaphoreType.DMA((4,)),pltpu.SemaphoreType.DMA((4,))],
        compiler_params=pltpu.CompilerParams(collective_id=3,has_side_effects=True,vmem_limit_bytes=24<<20),
        cost_estimate=pl.CostEstimate(flops=0,bytes_accessed=120<<20,transcendentals=0),
    )(keep,count,raw,raw,cw,gain,gno,o,s,t,w,r,block,*dummies)


def passed_along(block, axis, distance):
    devices = range(lax.axis_size(axis))
    route = [(i - distance, i) for i in devices if i - distance in devices]
    return lax.ppermute(block, axis, route)


def row_layout(lengths, positions):
    span_len = (lengths + BLOCK - 1) // BLOCK * BLOCK
    closing = jnp.cumsum(span_len)
    opening = closing - span_len
    bounds = jnp.concatenate([opening, closing[-1:]])
    reached = bounds[None, :] <= positions[:, None]
    doc_start = jnp.max(jnp.where(reached, bounds[None, :], 0), axis=1)
    inside = (positions[:, None] >= opening[None, :]) & (
        positions[:, None] < (opening + lengths)[None, :]
    )
    real_mask = jnp.any(inside, axis=1).astype(jnp.float32)
    return (doc_start, real_mask)


def local_span(carry_on, queries, keys_in, values, strength):
    head_count, token_count, head_width = queries.shape
    block_count = token_count // BLOCK

    def to_blocks(tensor):
        return tensor.reshape(head_count, block_count, BLOCK, -1).transpose(1, 0, 2, 3)

    def from_blocks(tensor):
        return tensor.transpose(1, 0, 2, 3).reshape(head_count, token_count, -1)

    strict_lower = jnp.tril(jnp.ones((BLOCK, BLOCK), jnp.float32), -1)
    causal = jnp.tril(jnp.ones((BLOCK, BLOCK), jnp.float32))
    identity = jnp.broadcast_to(
        jnp.eye(head_width, dtype=jnp.float32), (head_count, head_width, head_width)
    )

    def block_step(carried, block_in):
        memory, mapping = carried
        q_blk, k_blk, v_blk, s_blk, carry_flag = block_in
        write_rate = s_blk[..., 0]
        memory = memory * carry_flag
        mapping = mapping * carry_flag
        key_gram = jnp.einsum("hcp,hdp->hcd", k_blk, k_blk, precision=PRECISE)
        system = jnp.eye(BLOCK, dtype=jnp.float32) + strict_lower * (
            write_rate[:, :, None] * key_gram
        )
        right_side = jnp.concatenate(
            [write_rate[..., None] * k_blk, write_rate[..., None] * v_blk], axis=-1
        )
        solved = lax.linalg.triangular_solve(
            system, right_side, left_side=True, lower=True, unit_diagonal=True
        )
        w_mat = solved[..., :head_width]
        u_mat = solved[..., head_width:]
        corrected = u_mat - jnp.einsum("hcp,hpv->hcv", w_mat, memory, precision=PRECISE)
        scores = causal * jnp.einsum("hcp,hdp->hcd", q_blk, k_blk, precision=PRECISE)
        out_zero = jnp.einsum("hcp,hpv->hcv", q_blk, memory, precision=PRECISE)
        out_zero = out_zero + jnp.einsum("hcd,hdv->hcv", scores, corrected, precision=PRECISE)
        w_map = jnp.einsum("hcp,hpq->hcq", w_mat, mapping, precision=PRECISE)
        q_prop = jnp.einsum("hcp,hpq->hcq", q_blk, mapping, precision=PRECISE)
        q_prop = q_prop - jnp.einsum("hcd,hdq->hcq", scores, w_map, precision=PRECISE)
        memory = memory + jnp.einsum("hcp,hcv->hpv", k_blk, corrected, precision=PRECISE)
        mapping = mapping - jnp.einsum("hcp,hcq->hpq", k_blk, w_map, precision=PRECISE)
        return ((memory, mapping), (out_zero, q_prop))

    initial = (jnp.zeros((head_count, head_width, head_width), jnp.float32), identity)
    blocks = (
        to_blocks(queries),
        to_blocks(keys_in),
        to_blocks(values),
        to_blocks(strength[..., None]),
        carry_on,
    )
    (memory, mapping), (out_zero, q_prop) = lax.scan(block_step, initial, blocks)
    return (from_blocks(out_zero), from_blocks(q_prop), mapping, memory)


def spread_shards(
    block_in,
    doc_lengths,
    attn_gain,
    qkv_weight,
    conv_weight,
    beta_weight,
    out_gain,
    out_weight,
    ffn_gain,
    gateup_weight,
    down_weight,
    cotangent,
):
    tok_count = block_in.shape[1]
    seq_count = lax.axis_size("seq")
    own_index = lax.axis_index("seq")
    positions = own_index * tok_count + jnp.arange(tok_count + KERNEL - 1, dtype=jnp.int32)
    doc_start, real_ext = row_layout(doc_lengths[0], positions)
    real_mask = real_ext[:tok_count]
    taps = [(positions - shift_no >= doc_start).astype(jnp.float32) for shift_no in range(KERNEL)]
    carry_on = (doc_start[:tok_count:BLOCK] != positions[:tok_count:BLOCK]).astype(jnp.float32)
    residual_in = block_in[0].astype(jnp.float32)
    stat_in = lax.rsqrt(jnp.mean(residual_in * residual_in, axis=-1, keepdims=True) + EPSILON)
    unit_in = residual_in * stat_in
    normed = (unit_in * attn_gain).astype(jnp.bfloat16)
    qkv_full, beta_full, out_full, gateup_full, down_full = (
        lax.all_gather(qkv_weight, ("seq", "row"), axis=1, tiled=True),
        lax.all_gather(beta_weight, ("seq", "row"), axis=1, tiled=True),
        lax.all_gather(out_weight, ("seq", "row"), axis=1, tiled=True),
        lax.all_gather(gateup_weight, ("seq", "row"), axis=1, tiled=True),
        lax.all_gather(down_weight, ("seq", "row"), axis=1, tiled=True),
    )
    raw = jnp.einsum("td,sdc->stc", normed, qkv_full, preferred_element_type=jnp.float32).astype(
        jnp.bfloat16
    )
    rims = passed_along(raw[:, tok_count - KERNEL + 1 :, :], "seq", 1)
    extended = jnp.concatenate([rims, raw], axis=1).astype(jnp.float32)
    conv_sum = jnp.zeros(raw.shape, jnp.float32)
    for shift_no in range(KERNEL):
        window = extended[:, KERNEL - 1 - shift_no : KERNEL - 1 - shift_no + tok_count]
        conv_sum = (
            conv_sum
            + conv_weight[:, shift_no][:, None, :]
            * window
            * taps[shift_no][:tok_count][None, :, None]
        )
    conv_sig = jax.nn.sigmoid(conv_sum)
    head_count = conv_weight.shape[2] // HDIM
    split_heads = (
        (conv_sum * conv_sig).reshape(3, tok_count, head_count, HDIM).transpose(0, 2, 1, 3)
    )
    q_scale = lax.rsqrt(jnp.sum(split_heads[0] * split_heads[0], axis=-1, keepdims=True) + EPSILON)
    q_unit = split_heads[0] * q_scale
    queries = q_unit * HDIM ** (-0.5)
    k_scale = lax.rsqrt(jnp.sum(split_heads[1] * split_heads[1], axis=-1, keepdims=True) + EPSILON)
    keys_in = split_heads[1] * k_scale
    values = split_heads[2]
    logits = jnp.einsum("td,hd->ht", normed, beta_full, preferred_element_type=jnp.float32)
    beta_sig = jax.nn.sigmoid(logits)
    strength = beta_sig * real_mask[None, :]
    (out_zero, q_prop, span_map, span_state), span_pullback = jax.vjp(
        partial(local_span, carry_on), queries, keys_in, values, strength
    )
    empty_state = jnp.zeros_like(span_state)
    all_maps, all_states = (
        lax.all_gather(span_map[None].astype(jnp.bfloat16), "seq", axis=0, tiled=True).astype(
            jnp.float32
        ),
        lax.all_gather(span_state[None].astype(jnp.bfloat16), "seq", axis=0, tiled=True).astype(
            jnp.float32
        ),
    )

    def fold_forward(counter, incoming):
        moved = (
            jnp.einsum("hpq,hqv->hpv", all_maps[counter], incoming, precision=PRECISE)
            + all_states[counter]
        )
        return jnp.where(counter < own_index, moved, incoming)

    state_in = lax.fori_loop(0, seq_count, fold_forward, empty_state)
    mixer = out_zero + jnp.einsum("htp,hpv->htv", q_prop, state_in, precision=PRECISE)
    stat_out = lax.rsqrt(jnp.mean(mixer * mixer, axis=-1, keepdims=True) + EPSILON)
    unit_out = mixer * stat_out
    normed_out = (
        (unit_out * out_gain).transpose(1, 0, 2).reshape(tok_count, -1).astype(jnp.bfloat16)
    )
    branch_part = jnp.dot(normed_out, out_full, preferred_element_type=jnp.float32)
    hidden = residual_in + lax.psum(branch_part.astype(jnp.bfloat16), "mp").astype(jnp.float32)
    stat_mid = lax.rsqrt(jnp.mean(hidden * hidden, axis=-1, keepdims=True) + EPSILON)
    unit_mid = hidden * stat_mid
    normed_mid = (unit_mid * ffn_gain).astype(jnp.bfloat16)
    gate_up = jnp.einsum("td,sdf->stf", normed_mid, gateup_full, preferred_element_type=jnp.float32)
    gate_sig = jax.nn.sigmoid(gate_up[0])
    product = (gate_up[0] * gate_sig * gate_up[1]).astype(jnp.bfloat16)
    ffn_part = jnp.dot(product, down_full, preferred_element_type=jnp.float32)
    block_out = hidden + lax.psum(ffn_part.astype(jnp.bfloat16), "mp").astype(jnp.float32)
    qkv_full, beta_full, out_full, gateup_full, down_full = (
        lax.all_gather(qkv_weight, ("seq", "row"), axis=1, tiled=True),
        lax.all_gather(beta_weight, ("seq", "row"), axis=1, tiled=True),
        lax.all_gather(out_weight, ("seq", "row"), axis=1, tiled=True),
        lax.all_gather(gateup_weight, ("seq", "row"), axis=1, tiled=True),
        lax.all_gather(down_weight, ("seq", "row"), axis=1, tiled=True),
    )
    grad_top = cotangent[0]
    grad_down_part = jnp.dot(product.T, grad_top, preferred_element_type=jnp.float32)
    grad_product = jnp.dot(grad_top, down_full.T, preferred_element_type=jnp.float32)
    grad_gate = grad_product * gate_up[1] * gate_sig * (1.0 + gate_up[0] * (1.0 - gate_sig))
    grad_up = grad_product * gate_up[0] * gate_sig
    grad_gate_up = jnp.stack([grad_gate, grad_up]).astype(jnp.bfloat16)
    grad_gateup_part = jnp.einsum(
        "td,stf->sdf", normed_mid, grad_gate_up, preferred_element_type=jnp.float32
    )
    grad_mid_part = jnp.einsum(
        "stf,sdf->td", grad_gate_up, gateup_full, preferred_element_type=jnp.float32
    )
    grad_mid = lax.psum(grad_mid_part.astype(jnp.bfloat16), "mp").astype(jnp.float32)
    ffn_gain_part = jnp.sum(grad_mid * unit_mid, axis=0)
    grad_unit_mid = grad_mid * ffn_gain
    grad_hidden = grad_top.astype(jnp.float32) + stat_mid * (
        grad_unit_mid - unit_mid * jnp.mean(grad_unit_mid * unit_mid, axis=-1, keepdims=True)
    )
    grad_branch = grad_hidden.astype(jnp.bfloat16)
    grad_out_part = jnp.dot(normed_out.T, grad_branch, preferred_element_type=jnp.float32)
    grad_normed_out = jnp.dot(grad_branch, out_full.T, preferred_element_type=jnp.float32)
    grad_normed_out = grad_normed_out.reshape(tok_count, head_count, HDIM).transpose(1, 0, 2)
    out_gain_part = jnp.sum(grad_normed_out * unit_out, axis=(0, 1))
    grad_unit_out = grad_normed_out * out_gain
    grad_mixer = stat_out * (
        grad_unit_out - unit_out * jnp.mean(grad_unit_out * unit_out, axis=-1, keepdims=True)
    )
    local_grad = jnp.einsum("htp,htv->hpv", q_prop, grad_mixer, precision=PRECISE)
    grad_q_prop = jnp.einsum("htv,hpv->htp", grad_mixer, state_in, precision=PRECISE)
    all_grads = lax.all_gather(
        local_grad[None].astype(jnp.bfloat16), "seq", axis=0, tiled=True
    ).astype(jnp.float32)

    def fold_backward(counter, later_grad):
        source = seq_count - 1 - counter
        moved = (
            jnp.einsum("hqp,hqv->hpv", all_maps[source], later_grad, precision=PRECISE)
            + all_grads[source]
        )
        return jnp.where(source > own_index, moved, later_grad)

    grad_end = lax.fori_loop(0, seq_count, fold_backward, empty_state)
    grad_map = jnp.einsum("hpv,hqv->hpq", grad_end, state_in, precision=PRECISE)
    grad_queries, grad_keys, grad_values, grad_strength = span_pullback(
        (grad_mixer, grad_q_prop, grad_map, grad_end)
    )
    grad_logits = (grad_strength * real_mask[None, :] * beta_sig * (1.0 - beta_sig)).astype(
        jnp.bfloat16
    )
    grad_beta_part = jnp.einsum(
        "ht,td->hd", grad_logits, normed, preferred_element_type=jnp.float32
    )
    grad_q_unit = grad_queries * HDIM ** (-0.5)
    grad_q_raw = q_scale * (
        grad_q_unit - q_unit * jnp.sum(grad_q_unit * q_unit, axis=-1, keepdims=True)
    )
    grad_k_raw = k_scale * (
        grad_keys - keys_in * jnp.sum(grad_keys * keys_in, axis=-1, keepdims=True)
    )
    grad_act = (
        jnp.stack([grad_q_raw, grad_k_raw, grad_values])
        .transpose(0, 2, 1, 3)
        .reshape(3, tok_count, -1)
    )
    grad_conv_sum = grad_act * conv_sig * (1.0 + conv_sum * (1.0 - conv_sig))
    rims_back = passed_along(grad_conv_sum[:, : KERNEL - 1, :], "seq", -1)
    grad_ext = jnp.concatenate([grad_conv_sum, rims_back], axis=1)
    grad_raw = jnp.zeros(grad_conv_sum.shape, jnp.float32)
    conv_terms = []
    for shift_no in range(KERNEL):
        grad_raw = (
            grad_raw
            + conv_weight[:, shift_no][:, None, :]
            * grad_ext[:, shift_no : shift_no + tok_count]
            * taps[shift_no][shift_no : shift_no + tok_count][None, :, None]
        )
        window = extended[:, KERNEL - 1 - shift_no : KERNEL - 1 - shift_no + tok_count]
        conv_terms.append(
            jnp.sum(grad_conv_sum * window * taps[shift_no][:tok_count][None, :, None], axis=1)
        )
    grad_conv_part = jnp.stack(conv_terms, axis=1)
    grad_raw_low = grad_raw.astype(jnp.bfloat16)
    grad_qkv_part = jnp.einsum(
        "td,stc->sdc", normed, grad_raw_low, preferred_element_type=jnp.float32
    )
    grad_normed = jnp.einsum(
        "stc,sdc->td", grad_raw_low, qkv_full, preferred_element_type=jnp.float32
    )
    grad_normed = grad_normed + jnp.einsum(
        "ht,hd->td", grad_logits, beta_full, preferred_element_type=jnp.float32
    )
    grad_normed, out_gain_sum = (
        lax.psum(grad_normed.astype(jnp.bfloat16), "mp").astype(jnp.float32),
        lax.psum(out_gain_part.astype(jnp.bfloat16), "mp").astype(jnp.float32),
    )
    attn_gain_part = jnp.sum(grad_normed * unit_in, axis=0)
    grad_unit_in = grad_normed * attn_gain
    grad_input = grad_hidden + stat_in * (
        grad_unit_in - unit_in * jnp.mean(grad_unit_in * unit_in, axis=-1, keepdims=True)
    )
    weight_sums = (
        lax.psum_scatter(grad_qkv_part, ("seq", "row"), scatter_dimension=1, tiled=True),
        lax.psum_scatter(grad_beta_part, ("seq", "row"), scatter_dimension=1, tiled=True),
        lax.psum_scatter(grad_out_part, ("seq", "row"), scatter_dimension=1, tiled=True),
        lax.psum_scatter(grad_gateup_part, ("seq", "row"), scatter_dimension=1, tiled=True),
        lax.psum_scatter(grad_down_part, ("seq", "row"), scatter_dimension=1, tiled=True),
    )
    small_sums = lax.psum(
        (attn_gain_part, grad_conv_part, out_gain_sum, ffn_gain_part), ("seq", "row")
    )
    return (
        block_out.astype(jnp.bfloat16)[None],
        grad_input[None],
        small_sums[0],
        weight_sums[0],
        small_sums[1],
        weight_sums[1],
        small_sums[2],
        weight_sums[2],
        small_sums[3],
        weight_sums[3],
        weight_sums[4],
    )


MESH = pl.DeviceIdType.MESH
STRIP = 16
TILE = 512
WIDE = 256


def phase_kernel(middle, both_cores, small_sum, meanwhile, n_in, n_out, part_ref, *refs):
    inputs, all_ref = refs[:n_in], refs[n_in]
    outs, scratch = refs[n_in + 1 : n_in + n_out], refs[n_in + n_out :]
    got, sums, gain_sum, send_sem, recv_sem = scratch[:5]
    count = all_ref.shape[0]
    rows = count // 8
    place, core, row = lax.axis_index("mp"), lax.axis_index("seq"), lax.axis_index("row")
    across_x = place + 1 - 2 * (place % 2)
    across_y = (place + 2) % 4
    across_both = 3 - place
    ways = {"x": {"mp": across_x}, "y": {"mp": across_y}}
    if both_cores or small_sum:
        ways["core"] = {"seq": 1 - core}
    steps = []
    if small_sum:
        bit = 1
        while bit < lax.axis_size("row"):
            steps.append(f"row{bit}")
            ways[steps[-1]] = {"row": row + bit - 2 * bit * ((row // bit) % 2)}
            bit *= 2
        steps += ["core", "x", "y"]
    barrier = pltpu.get_barrier_semaphore()
    for other in ways.values():
        pl.semaphore_signal(barrier, inc=1, device_id=other, device_id_type=MESH)
    pl.semaphore_wait(barrier, len(ways))

    def copy(index, source, target, way):
        return pltpu.make_async_remote_copy(
            src_ref=source,
            dst_ref=target,
            send_sem=send_sem.at[index],
            recv_sem=recv_sem.at[index],
            device_id=ways[way],
            device_id_type=MESH,
        )

    def block(of, half):
        return pl.ds(pl.multiple_of((2 * of + half) * rows, rows), rows)

    def strips(body):
        @pl.loop(0, rows // STRIP)
        def _(i):
            body(pl.multiple_of(i * STRIP, STRIP))

    part = part_ref
    if meanwhile:
        fetch = pltpu.make_async_copy(inputs[3].at[3], scratch[-3], scratch[-2])
        fetch.start()
    if both_cores:
        part, outgoing, incoming = scratch[5:8]
        weight = inputs[3]
        order = [across_both, across_x, across_y, place]

        def product(whose, of, target):
            start = pl.multiple_of(whose * count + 2 * of * rows, rows)
            left = part_ref[pl.ds(start, 2 * rows), :]
            lines = pl.ds(pl.multiple_of(2 * of * rows, rows), 2 * rows)

            @pl.loop(0, weight.shape[1] // TILE)
            def _(i):
                tile = pl.ds(pl.multiple_of(i * TILE, TILE), TILE)
                target[lines, tile] = jnp.dot(
                    left, weight[:, tile], preferred_element_type=F32
                ).astype(BF16)

            return lines

        shared = []
        for number in range(4):
            lines = pl.ds(pl.multiple_of(2 * order[number] * rows, rows), 2 * rows)
            shared.append(copy(12 + number, outgoing.at[lines], incoming.at[lines], "core"))

        def give(number):
            product(1 - core, order[number], outgoing)
            shared[number].start()

        def take(number):
            of = order[number]
            product(core, of, part)
            shared[number].wait_recv()

            @pl.loop(0, 2 * rows // STRIP)
            def _(i):
                strip = pl.ds(pl.multiple_of(2 * of * rows + i * STRIP, STRIP), STRIP)
                part[strip, :] = (
                    part[strip, :].astype(F32) + incoming[strip, :].astype(F32)
                ).astype(BF16)

    far = [
        copy(0, part.at[block(across_both, 0)], got.at[0], "x"),
        copy(1, part.at[block(across_both, 1)], got.at[1], "y"),
    ]
    near = [
        copy(2, part.at[block(across_x, 0)], got.at[2], "x"),
        copy(3, part.at[block(across_y, 1)], got.at[3], "y"),
    ]
    last = [copy(4, sums.at[0], got.at[4], "y"), copy(5, sums.at[1], got.at[5], "x")]
    own = [all_ref.at[block(place, 0)], all_ref.at[block(place, 1)]]
    passed = [all_ref.at[block(across_x, 0)], all_ref.at[block(across_y, 1)]]
    out_first = [copy(6, own[0], own[0], "x"), copy(7, own[1], own[1], "y")]
    out_second = [copy(8, own[0], own[0], "y"), copy(9, own[1], own[1], "x")]
    out_third = [copy(10, passed[0], passed[0], "y"), copy(11, passed[1], passed[1], "x")]

    if both_cores:
        give(0)
        give(1)
        take(0)
    for step in far:
        step.start()
    if both_cores:
        give(2)
        take(1)
        near[0].start()
        take(2)
        near[1].start()
        give(3)
        take(3)
    else:
        for step in near:
            step.start()
    gain_sum[...] = jnp.zeros_like(gain_sum)
    for half, onward in ((0, across_y), (1, across_x)):
        far[half].wait_recv()

        def add(at):
            strip = pl.ds(at, STRIP)
            mine = part[pl.ds((2 * onward + half) * rows + at, STRIP), :]
            sums[half, strip, :] = (mine.astype(F32) + got[half, strip, :].astype(F32)).astype(BF16)

        strips(add)
        last[half].start()
    for half in (0, 1):
        near[half].wait_recv()
        last[half].wait_recv()

        def finish(at):
            strip = pl.ds(at, STRIP)
            total = part[pl.ds((2 * place + half) * rows + at, STRIP), :].astype(F32)
            total = total + got[2 + half, strip, :].astype(F32)
            total = total + got[4 + half, strip, :].astype(F32)
            result = middle(total, half, strip, inputs, outs, gain_sum)
            all_ref[pl.ds((2 * place + half) * rows + at, STRIP), :] = result.astype(BF16)

        strips(finish)
        out_first[half].start()
        out_second[half].start()

    def use(of, first=False, last=False):
        if not meanwhile:
            return
        weight, left = scratch[-3], inputs[4]
        grad_left, products = outs[2], scratch[-1]
        lines = pl.ds(pl.multiple_of(2 * of * rows, rows), 2 * rows)
        grad_left[lines, :] = lax.dot_general(
            all_ref[lines, :], weight[...], NT, preferred_element_type=F32
        ).astype(BF16)

        @pl.loop(0, products.shape[1] // TILE)
        def _(i):
            tile = pl.ds(pl.multiple_of(i * TILE, TILE), TILE)
            more = lax.dot_general(
                left[lines, :], all_ref[lines, tile], TN, preferred_element_type=F32
            )
            if first:
                products[:, tile] = more
            elif last:
                outs[3][:, tile] = (products[:, tile] + more).astype(BF16)
            else:
                products[:, tile] = products[:, tile] + more

    if meanwhile:
        fetch.wait()
    use(place, first=True)
    gain = jnp.sum(gain_sum[...], axis=0, keepdims=True)
    small = []
    if small_sum:
        values, arrived = outs[-1], scratch[-1]
        first = n_in - small_sum["dummies"] - 3
        ffn_gain, out_gain, conv = inputs[first : first + 3]
        taps, width = conv.shape
        middle_lane = values.shape[1] // 2
        values[...] = jnp.zeros_like(values)
        values[0:1, :] = gain
        values[1:2, :] = ffn_gain[...]
        values[2:3, 0 : out_gain.shape[1]] = out_gain[...]
        for i in (0, 1):
            share = jnp.where(core == i, 1.0, 0.0)
            lane = i * middle_lane
            values[8 : 8 + taps, lane : lane + width] = conv[...] * share
    elif n_out > 2:
        outs[1][...] = gain

    def small_step(number):
        height = 8 if steps[number] in ("x", "y") else values.shape[0]
        step = copy(
            16 + number,
            arrived.at[number, 1, pl.ds(0, height)],
            arrived.at[number, 0, pl.ds(0, height)],
            steps[number],
        )
        arrived[number, 1, 0:height, :] = values[0:height, :]
        step.start()
        step.wait_recv()
        values[0:height, :] = values[0:height, :] + arrived[number, 0, 0:height, :]
        small.append(step)

    for half in (0, 1):
        out_first[half].wait_recv()
        out_third[half].start()
    if small_sum:
        for number in range(len(steps)):
            small_step(number)
    for step in out_second:
        step.wait_recv()
    use(across_x)
    use(across_y)
    for step in out_third:
        step.wait_recv()
    use(across_both, last=True)
    for step in (*far, *near, *last, *out_first, *out_second, *out_third, *small):
        step.wait_send()
    if both_cores:
        for step in shared:
            step.wait_send()


def normed_forward(total, half, strip, inputs, outs, gain_sum):
    residual, gain = inputs[:2]
    hidden = residual[half, strip, :].astype(F32) + total
    outs[0][half, strip, :] = hidden
    stat = lax.rsqrt(jnp.mean(hidden * hidden, axis=1, keepdims=True) + EPSILON)
    return hidden * stat * gain[...]


def normed_backward(keep, total, half, strip, inputs, outs, gain_sum):
    value, base, gain = inputs[:3]
    value = value[half, strip, :].astype(F32)
    stat = lax.rsqrt(jnp.mean(value * value, axis=1, keepdims=True) + EPSILON)
    unit = value * stat
    gain_sum[...] += jnp.sum((total * unit).reshape(2, 8, -1), axis=0)
    scaled = total * gain[...]
    grad = base[half, strip, :].astype(F32) + stat * (
        scaled - unit * jnp.mean(scaled * unit, axis=1, keepdims=True)
    )
    if keep:
        outs[0][half, strip, :] = grad
    return grad


def mp_phase(
    number, middle, part, inputs, dummies, outs, both_cores=False, small=None, meanwhile=False
):
    here, there = pl.BlockSpec(memory_space=pltpu.VMEM), pl.BlockSpec(memory_space=pl.ANY)
    count, model = part.shape
    if both_cores:
        count, model = count // 2, inputs[3].shape[1]
    block = (count // 8, model)
    copies, scratch, small_sum = 12, [], None
    if both_cores:
        scratch += [pltpu.VMEM((count, model), BF16)] * 3
    if small is not None:
        stages = lax.axis_size("row").bit_length() - 1 + 3
        copies = 16 + stages
        height = 8 + small[2].shape[0]
        shape = (height + -height % 8, model)
        scratch += [pltpu.VMEM((stages, 2, *shape), F32)]
        small_sum = {"dummies": len(dummies)}
        inputs = [*inputs, *small]
        outs = [*outs, jax.ShapeDtypeStruct(shape, F32)]
    specs = [here] * len(inputs)
    if meanwhile:
        _, width, depth = inputs[3].shape
        specs[3] = there
        scratch += [
            pltpu.VMEM((width, depth), BF16),
            pltpu.SemaphoreType.DMA(()),
            pltpu.VMEM((width, model), F32),
        ]
    kernel = functools.partial(
        phase_kernel,
        middle,
        both_cores,
        small_sum,
        meanwhile,
        len(inputs) + len(dummies),
        1 + len(outs),
    )
    return pl.pallas_call(
        kernel,
        in_specs=[here, *specs] + [there] * len(dummies),
        out_specs=[here] * (1 + len(outs)),
        out_shape=[jax.ShapeDtypeStruct((count, model), BF16), *outs],
        scratch_shapes=[
            pltpu.VMEM((6, *block), BF16),
            pltpu.VMEM((2, *block), BF16),
            pltpu.VMEM((8, model), F32),
            pltpu.SemaphoreType.DMA((copies,)),
            pltpu.SemaphoreType.DMA((copies,)),
            *scratch,
        ],
        compiler_params=pltpu.CompilerParams(
            collective_id=number, has_side_effects=True, vmem_limit_bytes=50 << 20
        ),
        cost_estimate=pl.CostEstimate(flops=0, bytes_accessed=250 << 20, transcendentals=0),
    )(part, *inputs, *dummies)


def pair_kernel(part_ref, hidden, left_own, left_other, gate, up, *refs):
    block_ref, gate_pair, up_pair, got, sums, gate_in, up_in, send_sem, recv_sem = refs[-9:]
    rows = part_ref.shape[0] // 8
    place, core = lax.axis_index("mp"), lax.axis_index("seq")
    across_x = place + 1 - 2 * (place % 2)
    across_y = (place + 2) % 4
    across_both = 3 - place
    ways = {"x": {"mp": across_x}, "y": {"mp": across_y}, "core": {"seq": 1 - core}}
    barrier = pltpu.get_barrier_semaphore()
    for other in ways.values():
        pl.semaphore_signal(barrier, inc=1, device_id=other, device_id_type=MESH)
    pl.semaphore_wait(barrier, len(ways))

    def copy(index, source, target, way):
        return pltpu.make_async_remote_copy(
            src_ref=source,
            dst_ref=target,
            send_sem=send_sem.at[index],
            recv_sem=recv_sem.at[index],
            device_id=ways[way],
            device_id_type=MESH,
        )

    def block(of, half):
        return pl.ds(pl.multiple_of((2 * of + half) * rows, rows), rows)

    def strips(body):
        @pl.loop(0, rows // STRIP)
        def _(i):
            body(pl.multiple_of(i * STRIP, STRIP))

    far = [
        copy(0, part_ref.at[block(across_both, 0)], got.at[0], "x"),
        copy(1, part_ref.at[block(across_both, 1)], got.at[1], "y"),
    ]
    near = [
        copy(2, part_ref.at[block(across_x, 0)], got.at[2], "x"),
        copy(3, part_ref.at[block(across_y, 1)], got.at[3], "y"),
    ]
    last = [copy(4, sums.at[0], got.at[4], "y"), copy(5, sums.at[1], got.at[5], "x")]
    shared = [copy(6, gate, gate_in, "core"), copy(7, up, up_in, "core")]
    for step in (*shared, *far, *near):
        step.start()

    def products(own, other, target, first, count):
        @pl.loop(first, first + count)
        def _(i):
            tile = pl.ds(pl.multiple_of(i * WIDE, WIDE), WIDE)
            total = lax.dot_general(
                left_own[:, tile], own[...], TN, preferred_element_type=F32
            ) + lax.dot_general(left_other[:, tile], other[...], TN, preferred_element_type=F32)
            target[tile, :] = total.astype(BF16)

    tiles = left_own.shape[1] // WIDE
    shared[0].wait_recv()
    products(gate, gate_in, gate_pair, 0, tiles)
    for half, onward in ((0, across_y), (1, across_x)):
        far[half].wait_recv()

        def add(at):
            strip = pl.ds(at, STRIP)
            mine = part_ref[pl.ds((2 * onward + half) * rows + at, STRIP), :]
            sums[half, strip, :] = (mine.astype(F32) + got[half, strip, :].astype(F32)).astype(BF16)

        strips(add)
        last[half].start()
    shared[1].wait_recv()
    products(up, up_in, up_pair, 0, tiles)
    for half in (0, 1):
        near[half].wait_recv()
        last[half].wait_recv()

        def finish(at):
            strip = pl.ds(at, STRIP)
            total = part_ref[pl.ds((2 * place + half) * rows + at, STRIP), :].astype(F32)
            total = total + got[2 + half, strip, :].astype(F32)
            total = total + got[4 + half, strip, :].astype(F32)
            block_ref[pl.ds(half * rows + at, STRIP), :] = (hidden[half, strip, :] + total).astype(BF16)

        strips(finish)
    for step in (*shared, *far, *near, *last):
        step.wait_send()


def scattered_and_pairs(number, part, hidden, left, gate, up, dummies):
    here, there = pl.BlockSpec(memory_space=pltpu.VMEM), pl.BlockSpec(memory_space=pl.ANY)
    count, model = part.shape
    block = (count // 8, model)
    pair = jax.ShapeDtypeStruct((left[0].shape[1], gate.shape[1]), BF16)
    return pl.pallas_call(
        pair_kernel,
        in_specs=[here] * 6 + [there] * len(dummies),
        out_specs=[here] * 3,
        out_shape=[jax.ShapeDtypeStruct((2 * block[0], model), BF16), pair, pair],
        scratch_shapes=[
            pltpu.VMEM((6, *block), BF16),
            pltpu.VMEM((2, *block), BF16),
            pltpu.VMEM(gate.shape, BF16),
            pltpu.VMEM(up.shape, BF16),
            pltpu.SemaphoreType.DMA((8,)),
            pltpu.SemaphoreType.DMA((8,)),
        ],
        compiler_params=pltpu.CompilerParams(
            collective_id=number, has_side_effects=True, vmem_limit_bytes=50 << 20
        ),
        cost_estimate=pl.CostEstimate(flops=0, bytes_accessed=130 << 20, transcendentals=0),
    )(part, hidden, *left, gate, up, *dummies)


def swapped(block):
    return lax.ppermute(block, "seq", [(0, 1), (1, 0)])


def across(block, bit):
    return lax.ppermute(block, "mp", [(i, i ^ bit) for i in range(4)])


def in_order(mine, other, core, axis):
    first = jnp.where(core == 0, mine, other)
    second = jnp.where(core == 0, other, mine)
    return jnp.concatenate([first, second], axis=axis)


def after(block, *done):
    nothing = sum(part[(0,) * part.ndim].astype(F32) for part in done) * 0.0
    return block + nothing.astype(block.dtype)


def halves(block, core, axis):
    size = block.shape[axis] // 2
    pick = lambda i: lax.dynamic_slice_in_dim(block, i * size, size, axis=axis)
    return pick(core), pick(1 - core)


def both_tokens(left, right):
    product = lambda a, b: lax.dot_general(
        a, b, (((0,), (0,)), ((), ())), preferred_element_type=F32
    )
    return (product(left[0], right[0]) + product(left[1], right[1])).astype(BF16)


def own_columns(block, core):
    mine, other = halves(block, core, 1)
    return mine, swapped(other)


def over_row(pair, axis):
    return lax.psum_scatter(pair, "row", scatter_dimension=axis, tiled=True)


def joined_shards(
    block_in,
    doc_lengths,
    attn_gain,
    qkv_weight,
    conv_weight,
    beta_weight,
    out_gain,
    out_weight,
    ffn_gain,
    gateup_weight,
    down_weight,
    cotangent,
):
    tok_count, model = block_in.shape[1:]
    core, own = lax.axis_index("seq"), lax.axis_index("mp")
    width = conv_weight.shape[2] // 2
    own_heads = width // HDIM
    quarter = tok_count // 4

    gather = lambda weight: lax.all_gather(weight, ("seq", "row"), axis=1, tiled=True)
    mixer_full = gather(jnp.concatenate([qkv_weight, out_weight.T[None]]))
    qkv_full, out_full = mixer_full[:3], mixer_full[3]
    beta_full, gateup_full, down_full = (
        gather(beta_weight),
        gather(gateup_weight),
        gather(down_weight),
    )
    qkv_own = lax.dynamic_slice_in_dim(qkv_full, core * width, width, axis=2)
    beta_own = lax.dynamic_slice_in_dim(beta_full, core * own_heads, own_heads, axis=0)
    beta_rows = jnp.pad(beta_own, ((0, HDIM - own_heads), (0, 0)))
    mix_across = jnp.concatenate([qkv_own[0].T, qkv_own[1].T, qkv_own[2].T, beta_rows])
    conv_own = lax.dynamic_slice_in_dim(conv_weight, core * width, width, axis=2)
    conv_own = conv_own.transpose(1, 0, 2).reshape(KERNEL, 3 * width)

    residual_in = block_in[0].astype(F32)
    stat_in = lax.rsqrt(jnp.mean(residual_in * residual_in, axis=-1, keepdims=True) + EPSILON)
    normed_mine = (residual_in * stat_in * attn_gain).astype(BF16)
    normed = in_order(normed_mine, swapped(normed_mine), core, 0)

    positions = jnp.arange(2 * tok_count, dtype=jnp.int32)
    doc_start, real_row = row_layout(doc_lengths[0], positions)
    keep = jnp.pad((doc_start[::BLOCK] != positions[::BLOCK]).astype(F32), (0, 1))
    count = jnp.sum(real_row.reshape(-1, BLOCK), axis=1).astype(jnp.int32)
    raw = lax.dot_general(
        normed, mix_across, (((1,), (1,)), ((), ())), preferred_element_type=F32
    ).astype(BF16)
    gain = out_gain[None, :]
    group = 4 if raw.shape[0] % (4 * CHUNK) == 0 else 1
    heads_out, *saved = forward(keep, count, raw, conv_own, gain, group)

    mine, other = halves(heads_out, core, 0)
    normed_out = in_order(mine, swapped(other), core, 1)
    branch_part = lax.dot_general(
        normed_out, out_full, (((1,), (1,)), ((), ())), preferred_element_type=F32
    )
    own_rows = lambda block: lax.dynamic_slice_in_dim(
        block[0], own * quarter, quarter, axis=0
    ).reshape(2, -1, model)
    residual_own = own_rows(block_in)
    rows_own = jax.ShapeDtypeStruct(residual_own.shape, F32)
    normed_mid, hidden = mp_phase(
        0,
        normed_forward,
        branch_part.astype(BF16),
        [residual_own, ffn_gain[None, :]],
        [],
        [rows_own],
    )

    grad_top = cotangent[0]
    gate_up = jnp.einsum("td,sdf->stf", normed_mid, gateup_full, preferred_element_type=F32)
    gate_sig = jax.nn.sigmoid(gate_up[0])
    product = (gate_up[0] * gate_sig * gate_up[1]).astype(BF16)
    down_pair = both_tokens((product, swapped(product)), own_columns(grad_top, core))
    ffn_part = jnp.dot(
        after(product, down_pair), down_full, preferred_element_type=F32
    ).astype(BF16)
    grad_product = jnp.dot(grad_top, down_full.T, preferred_element_type=F32)
    grad_product = after(grad_product, ffn_part)
    grad_gate = grad_product * gate_up[1] * gate_sig * (1.0 + gate_up[0] * (1.0 - gate_sig))
    grad_up = grad_product * gate_up[0] * gate_sig
    grad_gate, grad_up = grad_gate.astype(BF16), grad_up.astype(BF16)
    grad_mid_part = jnp.einsum(
        "stf,sdf->td",
        jnp.stack([grad_gate, grad_up]),
        gateup_full,
        preferred_element_type=F32,
    ).astype(BF16)
    block_out, gate_pair, up_pair = scattered_and_pairs(
        4, ffn_part, hidden, own_columns(normed_mid, core), grad_gate, grad_up, []
    )
    down_sum, gate_sum, up_sum = over_row(down_pair, 1), over_row(gate_pair, 0), over_row(up_pair, 0)
    grad_branch, grad_hidden, ffn_gain_part, grad_normed_out, grad_out_part = mp_phase(
        1,
        partial(normed_backward, True),
        grad_mid_part,
        [hidden, own_rows(cotangent), ffn_gain[None, :], mixer_full.transpose(0, 2, 1), normed_out],
        [block_out, down_sum, gate_pair, up_pair],
        [
            rows_own,
            jax.ShapeDtypeStruct((1, model), F32),
            jax.ShapeDtypeStruct(normed_out.shape, BF16),
            jax.ShapeDtypeStruct((normed_out.shape[1], model), BF16),
        ],
        meanwhile=True,
    )
    mine, other = halves(grad_normed_out, core, 1)
    grad_heads = in_order(mine, swapped(other), core, 0)
    mine, other = halves(grad_out_part, core, 1)
    out_pair = after(mine.astype(F32) + swapped(other).astype(F32), up_sum).astype(BF16)
    grad_raw, grad_conv_own, out_gain_part, block_out = backward(
        keep,
        count,
        raw,
        conv_own,
        gain,
        grad_heads,
        *saved,
        group,
        block_out,
        [gate_sum],
    )
    piece = lambda of, half: lax.dynamic_slice_in_dim(
        block_out, (2 * of + half) * (quarter // 2), quarter // 2, axis=0
    )
    far_rows = [across(piece(own ^ 1, 0), 2), across(piece(own ^ 2, 1), 1)]
    normed_mine, normed_other = halves(normed, core, 1)
    by_columns = lambda part: lax.dot_general(
        part, grad_raw, (((0,), (0,)), ((), ())), preferred_element_type=F32
    ).astype(BF16)
    qkv_other = swapped(by_columns(normed_other))
    qkv_mine = by_columns(normed_mine)
    grad_input, small = mp_phase(
        2,
        partial(normed_backward, False),
        grad_raw,
        [residual_own, grad_hidden, attn_gain[None, :], mix_across],
        [up_sum, out_pair, qkv_mine, qkv_other, *far_rows],
        [],
        both_cores=True,
        small=[ffn_gain_part, out_gain_part, grad_conv_own],
    )
    grad_input = grad_input.astype(F32)
    places = jnp.arange(4)[:, None, None]
    block_out = jnp.where(
        places == (own ^ 3),
        jnp.concatenate(far_rows)[None],
        block_out.reshape(4, quarter, model),
    ).reshape(tok_count, model)
    grad_attn_gain, grad_ffn_gain = small[0], small[1]
    grad_out_gain = small[2, : out_gain.shape[0]]
    conv_at = 8
    conv_of = lambda i: (
        small[conv_at : conv_at + KERNEL, i * (model // 2) : i * (model // 2) + 3 * width]
        .reshape(KERNEL, 3, width)
        .transpose(1, 0, 2)
    )
    grad_conv = jnp.concatenate([conv_of(0), conv_of(1)], axis=2)
    grad_down, grad_out = down_sum.astype(F32), over_row(out_pair, 1).astype(F32)
    grad_gateup = jnp.stack([gate_sum, up_sum]).astype(F32)
    row_sums = [over_row(part, 0) for part in (qkv_mine, qkv_other)]
    by_kind = lambda part: part[:, : 3 * width].reshape(-1, 3, width).transpose(1, 0, 2)
    grad_qkv = in_order(by_kind(row_sums[0]), by_kind(row_sums[1]), core, 2).astype(F32)
    of_heads = lambda part: part[:, 3 * width : 3 * width + own_heads].T
    grad_beta = in_order(of_heads(row_sums[0]), of_heads(row_sums[1]), core, 0).astype(F32)
    return (
        block_out[None],
        grad_input[None],
        grad_attn_gain,
        grad_qkv,
        grad_conv,
        grad_beta,
        grad_out_gain,
        grad_out,
        grad_ffn_gain,
        grad_gateup,
        grad_down,
    )


def solution(mesh):
    rows = mesh.shape["row"]
    joined = mesh.shape["seq"] == 2 and mesh.shape["mp"] == 4 and rows & (rows - 1) == 0
    return jax.shard_map(
        joined_shards if joined else spread_shards,
        mesh=mesh,
        in_specs=(
            P("row", "seq", None),
            P("row", None),
            P(),
            P(None, ("seq", "row"), "mp"),
            P(None, None, "mp"),
            P("mp", ("seq", "row")),
            P(),
            P("mp", ("seq", "row")),
            P(),
            P(None, ("seq", "row"), "mp"),
            P("mp", ("seq", "row")),
            P("row", "seq", None),
        ),
        out_specs=(
            P("row", "seq", None),
            P("row", "seq", None),
            P(),
            P(None, ("seq", "row"), "mp"),
            P(None, None, "mp"),
            P("mp", ("seq", "row")),
            P(),
            P("mp", ("seq", "row")),
            P(),
            P(None, ("seq", "row"), "mp"),
            P("mp", ("seq", "row")),
        ),
        check_vma=False,
    )
```

```python
import functools
from functools import partial

import jax
import jax.numpy as jnp
from jax import lax
from jax.experimental import pallas as pl
from jax.experimental.pallas import tpu as pltpu
from jax.sharding import PartitionSpec as P

HDIM = 128
KERNEL = 4
BLOCK = 64
CHUNK = 128
EPSILON = 1e-06
PRECISE = lax.Precision.HIGHEST
F32 = jnp.float32
BF16 = jnp.bfloat16

NT=(((1,),(1,)),((),())); NN=(((1,),(0,)),((),())); TN=(((0,),(0,)),((),()))

def mm(a,b,dims=NN):
    return lax.dot_general(a.astype(BF16), b.astype(BF16), dims, preferred_element_type=F32)

def iotas():
    return lax.broadcasted_iota(jnp.int32,(CHUNK,CHUNK),0), lax.broadcasted_iota(jnp.int32,(CHUNK,CHUNK),1)

def inverses(below):
    r,c=iotas()
    done=[jnp.where(r==c,1.0,0.0)-jnp.where(r//2==c//2,a,0.0) for a in below]
    size=2
    while size<CHUNK:
        pairs=(r//(2*size)==c//(2*size))&(r//size!=c//size)
        half=[mm(jnp.where(pairs,a,0.0),t) for a,t in zip(below,done)]
        done=[t-mm(t,x) for t,x in zip(done,half)]
        size*=2
    return done

def conv_act(ext_ref, base, lanes, cw, taps):
    total=cw[0:1]*ext_ref[pl.ds(base+8,CHUNK),lanes]
    for j in range(1,KERNEL):
        total=total+(cw[j:j+1]*taps[j-1])*ext_ref[pl.ds(base+8-j,CHUNK),lanes]
    sig=jax.nn.sigmoid(total)
    return total,sig

def layout(keep_ref, count_ref, block):
    r,_=iotas()
    inside=r%BLOCK
    first=r<BLOCK
    keep0,keep1,after=keep_ref[block],keep_ref[block+1],keep_ref[block+2]
    here=jnp.where(first,keep0,keep1)
    later=jnp.where(first,keep1,after)
    taps=[jnp.where(inside<j,here,1.0) for j in range(1,KERNEL)]
    taps_later=[jnp.where(inside>=BLOCK-j,later,1.0) for j in range(1,KERNEL)]
    real=jnp.where(inside<jnp.where(first,count_ref[block],count_ref[block+1]),1.0,0.0)
    return taps,taps_later,jnp.where(first,1.0,keep1),jnp.where(first,keep1,1.0),real,keep0,keep1

def fwd_kernel(heads, group, keep_ref, count_ref, raw_ref, cw_ref, gain_ref, normed_ref, o_ref, s_ref, t_ref, w_ref, r_ref, ext, state):
    rows=group*CHUNK
    step=pl.program_id(0)
    @pl.when(step==0)
    def _():
        ext[0:8,:]=jnp.zeros((8,3*heads*HDIM),F32)
        state[...]=jnp.zeros(state.shape,F32)
    @pl.when(step>0)
    def _():
        ext[0:8,:]=ext[rows:rows+8,:]
    ext[8:,:]=raw_ref[:,0:3*heads*HDIM].astype(F32)
    r,c=iotas()
    width=heads*HDIM
    units=[]
    below=[]
    for g in range(group):
        base=g*CHUNK
        taps,_,m,m2,real,keep0,keep1=layout(keep_ref,count_ref,2*(step*group+g))
        sig_b=jax.nn.sigmoid(raw_ref[pl.ds(base,CHUNK),pl.ds(3*width,HDIM)].astype(F32))*real
        for h in range(heads):
            act=[]
            for s in range(3):
                lanes=pl.ds(s*width+h*HDIM,HDIM)
                total,sig=conv_act(ext,base,lanes,cw_ref[:,lanes],taps)
                act.append(total*sig)
            q=act[0]*(lax.rsqrt(jnp.sum(act[0]*act[0],axis=1,keepdims=True)+EPSILON)*HDIM**-0.5)
            k=act[1]*lax.rsqrt(jnp.sum(act[1]*act[1],axis=1,keepdims=True)+EPSILON)
            v=act[2]
            b=sig_b[:,h:h+1]
            gram=mm(k,k,NT)
            score=mm(q,k,NT)
            mask=jnp.where(c<BLOCK,m,1.0)
            a=jnp.where(r>c,b*gram*mask,0.0)
            l=jnp.where(r>=c,score*mask,0.0)
            below.append(a)
            units.append((g,h,q*m,k*m2,l,b*k,b*v,m,keep0,keep1))
    done=inverses(below)
    wus=[(mm(t,u[5])*u[7],mm(t,u[6])) for t,u in zip(done,units)]
    for t,(w,u),(g,h,q,k,l,_,_,_,keep0,keep1) in zip(done,wus,units):
        base=g*CHUNK
        out=(pl.ds(base,CHUNK),pl.ds(h*HDIM,HDIM))
        t_ref[g,h]=t.astype(BF16)
        w_ref[out]=w.astype(BF16)
        s=state[h]*keep0
        s_ref[g,h]=s.astype(BF16)
        rr=u-mm(w,s)
        o=mm(q,s)+mm(l,rr)
        state[h]=s*keep1+mm(k,rr,TN)
        r_ref[out]=rr.astype(BF16)
        o_ref[out]=o
        stat=lax.rsqrt(jnp.mean(o*o,axis=1,keepdims=True)+EPSILON)
        normed_ref[out]=(o*stat*gain_ref[...]).astype(BF16)

def forward(keep, count, raw, cw, gain, group):
    n=raw.shape[0]; width=cw.shape[1]//3; heads=width//HDIM; rows=group*CHUNK
    nc=n//CHUNK
    row=lambda w: pl.BlockSpec((rows,w),lambda i:(i,0))
    mat=pl.BlockSpec((group,heads,HDIM,HDIM),lambda i:(i,0,0,0))
    full=lambda a: pl.BlockSpec(a.shape,lambda i:(0,0))
    return pl.pallas_call(functools.partial(fwd_kernel,heads,group),
        grid=(n//rows,),
        in_specs=[pl.BlockSpec(memory_space=pltpu.SMEM)]*2+[row(raw.shape[1]),full(cw),full(gain)],
        out_specs=[row(width),row(width),mat,mat,row(width),row(width)],
        out_shape=[jax.ShapeDtypeStruct((n,width),BF16),jax.ShapeDtypeStruct((n,width),F32),
            jax.ShapeDtypeStruct((nc,heads,HDIM,HDIM),BF16),jax.ShapeDtypeStruct((nc,heads,HDIM,HDIM),BF16),
            jax.ShapeDtypeStruct((n,width),BF16),jax.ShapeDtypeStruct((n,width),BF16)],
        scratch_shapes=[pltpu.VMEM((rows+8,3*width),F32),pltpu.VMEM((heads,HDIM,HDIM),F32)],
        compiler_params=pltpu.CompilerParams(vmem_limit_bytes=24<<20),
        cost_estimate=pl.CostEstimate(flops=0,bytes_accessed=120<<20,transcendentals=0),
    )(keep,count,raw,cw,gain)

def bwd_kernel(heads, group, keep_ref, count_ref, raw_ref, prev_ref, cw_ref, gain_ref, gno_ref, o_ref, s_ref, t_ref, w_ref, r_ref, *rest):
    block_ref=rest[0]
    graw_ref, gcw_ref, ggain_ref, all_ref, ext, gext, grad_state, local_sem, send_sem, recv_sem = rest[-10:]
    rows=group*CHUNK
    step=pl.program_id(0); steps=pl.num_programs(0)
    width=heads*HDIM
    @pl.when(step==0)
    def _():
        gext[rows:rows+8,:]=jnp.zeros((8,3*heads*HDIM),F32)
        grad_state[...]=jnp.zeros(grad_state.shape,F32)
        gcw_ref[...]=jnp.zeros(gcw_ref.shape,F32)
        ggain_ref[...]=jnp.zeros(ggain_ref.shape,F32)
    @pl.when(step>0)
    def _():
        gext[rows:rows+8,:]=gext[0:8,:]
    first=jnp.where(step==steps-1,0.0,1.0)
    place=lax.axis_index("mp")
    across_x=place+1-2*(place%2)
    across_y=(place+2)%4
    part=block_ref.shape[0]//2
    at=lambda of,half: all_ref.at[pl.ds(pl.multiple_of((2*of+half)*part,part),part)]
    def copy(index,source,target,other):
        return pltpu.make_async_remote_copy(src_ref=source,dst_ref=target,send_sem=send_sem.at[index],recv_sem=recv_sem.at[index],
            device_id={"mp":other},device_id_type=pl.DeviceIdType.MESH)
    top,low=block_ref.at[pl.ds(0,part)],block_ref.at[pl.ds(part,part)]
    keep_own=pltpu.make_async_copy(block_ref,all_ref.at[pl.ds(pl.multiple_of(2*place*part,2*part),2*part)],local_sem)
    sends=[copy(0,top,at(place,0),across_x),copy(1,low,at(place,1),across_y),copy(2,top,at(place,0),across_y),copy(3,low,at(place,1),across_x)]
    @pl.when(step==0)
    def _():
        barrier=pltpu.get_barrier_semaphore()
        for other in (across_x,across_y):
            pl.semaphore_signal(barrier,inc=1,device_id={"mp":other},device_id_type=pl.DeviceIdType.MESH)
        pl.semaphore_wait(barrier,2)
        keep_own.start()
        for send in sends: send.start()
    ext[0:8,:]=prev_ref[:,0:3*width].astype(F32)[8:16]*first
    ext[8:,:]=raw_ref[:,0:3*heads*HDIM].astype(F32)
    r,c=iotas()
    units=[]
    for g in range(group-1,-1,-1):
        base=g*CHUNK
        taps,taps_later,m,m2,real,keep0,keep1=layout(keep_ref,count_ref,2*((steps-1-step)*group+g))
        beta=jax.nn.sigmoid(raw_ref[pl.ds(base,CHUNK),pl.ds(3*width,HDIM)].astype(F32))
        sig_b=beta*real
        for h in range(heads):
            out=(pl.ds(base,CHUNK),pl.ds(h*HDIM,HDIM))
            act=[];tot=[];sigs=[]
            for s in range(3):
                lanes=pl.ds(s*width+h*HDIM,HDIM)
                total,sig=conv_act(ext,base,lanes,cw_ref[:,lanes],taps)
                act.append(total*sig);tot.append(total);sigs.append(sig)
            rq=lax.rsqrt(jnp.sum(act[0]*act[0],axis=1,keepdims=True)+EPSILON)
            rk=lax.rsqrt(jnp.sum(act[1]*act[1],axis=1,keepdims=True)+EPSILON)
            qu=act[0]*rq
            o=o_ref[out]
            stat=lax.rsqrt(jnp.mean(o*o,axis=1,keepdims=True)+EPSILON)
            uo=o*stat
            gno=gno_ref[out].astype(F32)
            ggain_ref[...]+=jnp.sum(gno*uo,axis=0,keepdims=True)
            gu=gno*gain_ref[...]
            do=stat*(gu-uo*jnp.mean(gu*uo,axis=1,keepdims=True))
            units.append(dict(g=g,h=h,base=base,out=out,taps=taps,m=m,m2=m2,keep0=keep0,keep1=keep1,tot=tot,sigs=sigs,
                rq=rq,rk=rk,qu=qu,q=qu*HDIM**-0.5,k=act[1]*rk,v=act[2],b=sig_b[:,h:h+1],do=do,
                mask=jnp.where(c<BLOCK,m,1.0)))
        for u in units[-heads:]: u.update(taps_later=taps_later,beta=beta,sig_b=sig_b)
    for u in units: u['gram']=mm(u['k'],u['k'],NT)*u['mask']
    for u in units: u['l']=jnp.where(r>=c,mm(u['q'],u['k'],NT)*u['mask'],0.0)
    for u in units: u['dr0']=mm(u['l'],u['do'],TN)
    for u in units: u['ds0']=mm(u['q']*u['m'],u['do'],TN)
    for u in units:
        dsn=grad_state[u['h']]
        u['dsn']=dsn
        u['dr']=u['dr0']+u['m2']*mm(u['k'],dsn)
        ds=u['keep1']*dsn+u['ds0']-mm(w_ref[u['out']],u['dr'],TN)
        grad_state[u['h']]=u['keep0']*ds
    for u in units: u['df']=mm(t_ref[u['g'],u['h']],u['dr'],TN)
    for u in units: u['dl']=jnp.where(r>=c,mm(u['do'],r_ref[u['out']],NT)*u['mask'],0.0)
    for u in units: u['da']=jnp.where(r>c,-mm(u['df'],r_ref[u['out']],NT),0.0)
    for u in units:
        u['de']=u['b']*u['df']
        u['e']=u['v']-u['m']*mm(u['k'],s_ref[u['g'],u['h']])
        u['gb']=jnp.sum(u['df']*u['e']+u['da']*u['gram'],axis=1,keepdims=True)
        u['dkk']=u['b']*u['da']*u['mask']
    for u in units: u['dq']=u['m']*mm(u['do'],s_ref[u['g'],u['h']],NT)+mm(u['dl'],u['k'])
    for u in units:
        u['dk']=(mm(u['dl'],u['q'],TN)+u['m2']*mm(r_ref[u['out']],u['dsn'],NT)-u['m']*mm(u['de'],s_ref[u['g'],u['h']],NT)
            +mm(u['dkk'],u['k'])+mm(u['dkk'],u['k'],TN))
    for u in units:
        gq=u['dq']*HDIM**-0.5
        gq=u['rq']*(gq-u['qu']*jnp.sum(gq*u['qu'],axis=1,keepdims=True))
        gk=u['rk']*(u['dk']-u['k']*jnp.sum(u['dk']*u['k'],axis=1,keepdims=True))
        for i,ga in enumerate((gq,gk,u['de'])):
            lanes=pl.ds(i*width+u['h']*HDIM,HDIM)
            sig,tot=u['sigs'][i],u['tot'][i]
            gc=ga*sig*(1.0+tot*(1.0-sig))
            gext[pl.ds(u['base'],CHUNK),lanes]=gc
            for j in range(KERNEL):
                win=ext[pl.ds(u['base']+8-j,CHUNK),lanes]
                prod=gc*win if j==0 else gc*win*u['taps'][j-1]
                gcw_ref[j:j+1,lanes]+=jnp.sum(prod,axis=0,keepdims=True)
    for at in range(0,len(units),heads):
        glog=jnp.zeros((CHUNK,HDIM),F32)
        for u in units[at:at+heads]:
            glog=jnp.where(c==u['h'],u['gb'],glog)
            for i in range(3):
                lanes=pl.ds(i*width+u['h']*HDIM,HDIM)
                cw=cw_ref[:,lanes]
                total=cw[0:1]*gext[pl.ds(u['base'],CHUNK),lanes]
                for j in range(1,KERNEL):
                    total=total+(cw[j:j+1]*u['taps_later'][j-1])*gext[pl.ds(u['base']+j,CHUNK),lanes]
                graw_ref[pl.ds(u['base'],CHUNK),lanes]=total.astype(BF16)
        graw_ref[pl.ds(u['base'],CHUNK),pl.ds(3*width,HDIM)]=(glog*u['sig_b']*(1.0-u['beta'])).astype(BF16)
    @pl.when(step==steps-1)
    def _():
        keep_own.wait()
        for send in sends: send.wait_recv()
        for send in sends: send.wait_send()

def backward(keep, count, raw, cw, gain, gno, o, s, t, w, r, group, block, dummies=()):
    n=raw.shape[0]; width=cw.shape[1]//3; heads=width//HDIM; rows=group*CHUNK
    steps=n//rows
    row=lambda w: pl.BlockSpec((rows,w),lambda i:(steps-1-i,0))
    mat=pl.BlockSpec((group,heads,HDIM,HDIM),lambda i:(steps-1-i,0,0,0))
    full=lambda a: pl.BlockSpec(a.shape,lambda i:(0,0))
    prev=pl.BlockSpec((16,raw.shape[1]),lambda i:(jnp.maximum((steps-1-i)*(rows//16)-1,0),0))
    return pl.pallas_call(functools.partial(bwd_kernel,heads,group),
        grid=(steps,),
        in_specs=[pl.BlockSpec(memory_space=pltpu.SMEM)]*2+[row(raw.shape[1]),prev,full(cw),full(gain),row(width),row(width),mat,mat,row(width),row(width)]+[pl.BlockSpec(memory_space=pl.ANY)]*(1+len(dummies)),
        out_specs=[row(raw.shape[1]),pl.BlockSpec((KERNEL,3*width),lambda i:(0,0)),pl.BlockSpec((1,HDIM),lambda i:(0,0)),pl.BlockSpec(memory_space=pl.ANY)],
        out_shape=[jax.ShapeDtypeStruct(raw.shape,BF16),
            jax.ShapeDtypeStruct((KERNEL,3*width),F32),jax.ShapeDtypeStruct((1,HDIM),F32),jax.ShapeDtypeStruct((4*block.shape[0],block.shape[1]),BF16)],
        scratch_shapes=[pltpu.VMEM((rows+8,3*width),F32),pltpu.VMEM((rows+8,3*width),F32),pltpu.VMEM((heads,HDIM,HDIM),F32),
            pltpu.SemaphoreType.DMA(()),pltpu.SemaphoreType.DMA((4,)),pltpu.SemaphoreType.DMA((4,))],
        compiler_params=pltpu.CompilerParams(collective_id=3,has_side_effects=True,vmem_limit_bytes=24<<20),
        cost_estimate=pl.CostEstimate(flops=0,bytes_accessed=120<<20,transcendentals=0),
    )(keep,count,raw,raw,cw,gain,gno,o,s,t,w,r,block,*dummies)


def passed_along(block, axis, distance):
    devices = range(lax.axis_size(axis))
    route = [(i - distance, i) for i in devices if i - distance in devices]
    return lax.ppermute(block, axis, route)


def row_layout(lengths, positions):
    span_len = (lengths + BLOCK - 1) // BLOCK * BLOCK
    closing = jnp.cumsum(span_len)
    opening = closing - span_len
    bounds = jnp.concatenate([opening, closing[-1:]])
    reached = bounds[None, :] <= positions[:, None]
    doc_start = jnp.max(jnp.where(reached, bounds[None, :], 0), axis=1)
    inside = (positions[:, None] >= opening[None, :]) & (
        positions[:, None] < (opening + lengths)[None, :]
    )
    real_mask = jnp.any(inside, axis=1).astype(jnp.float32)
    return (doc_start, real_mask)


def local_span(carry_on, queries, keys_in, values, strength):
    head_count, token_count, head_width = queries.shape
    block_count = token_count // BLOCK

    def to_blocks(tensor):
        return tensor.reshape(head_count, block_count, BLOCK, -1).transpose(1, 0, 2, 3)

    def from_blocks(tensor):
        return tensor.transpose(1, 0, 2, 3).reshape(head_count, token_count, -1)

    strict_lower = jnp.tril(jnp.ones((BLOCK, BLOCK), jnp.float32), -1)
    causal = jnp.tril(jnp.ones((BLOCK, BLOCK), jnp.float32))
    identity = jnp.broadcast_to(
        jnp.eye(head_width, dtype=jnp.float32), (head_count, head_width, head_width)
    )

    def block_step(carried, block_in):
        memory, mapping = carried
        q_blk, k_blk, v_blk, s_blk, carry_flag = block_in
        write_rate = s_blk[..., 0]
        memory = memory * carry_flag
        mapping = mapping * carry_flag
        key_gram = jnp.einsum("hcp,hdp->hcd", k_blk, k_blk, precision=PRECISE)
        system = jnp.eye(BLOCK, dtype=jnp.float32) + strict_lower * (
            write_rate[:, :, None] * key_gram
        )
        right_side = jnp.concatenate(
            [write_rate[..., None] * k_blk, write_rate[..., None] * v_blk], axis=-1
        )
        solved = lax.linalg.triangular_solve(
            system, right_side, left_side=True, lower=True, unit_diagonal=True
        )
        w_mat = solved[..., :head_width]
        u_mat = solved[..., head_width:]
        corrected = u_mat - jnp.einsum("hcp,hpv->hcv", w_mat, memory, precision=PRECISE)
        scores = causal * jnp.einsum("hcp,hdp->hcd", q_blk, k_blk, precision=PRECISE)
        out_zero = jnp.einsum("hcp,hpv->hcv", q_blk, memory, precision=PRECISE)
        out_zero = out_zero + jnp.einsum("hcd,hdv->hcv", scores, corrected, precision=PRECISE)
        w_map = jnp.einsum("hcp,hpq->hcq", w_mat, mapping, precision=PRECISE)
        q_prop = jnp.einsum("hcp,hpq->hcq", q_blk, mapping, precision=PRECISE)
        q_prop = q_prop - jnp.einsum("hcd,hdq->hcq", scores, w_map, precision=PRECISE)
        memory = memory + jnp.einsum("hcp,hcv->hpv", k_blk, corrected, precision=PRECISE)
        mapping = mapping - jnp.einsum("hcp,hcq->hpq", k_blk, w_map, precision=PRECISE)
        return ((memory, mapping), (out_zero, q_prop))

    initial = (jnp.zeros((head_count, head_width, head_width), jnp.float32), identity)
    blocks = (
        to_blocks(queries),
        to_blocks(keys_in),
        to_blocks(values),
        to_blocks(strength[..., None]),
        carry_on,
    )
    (memory, mapping), (out_zero, q_prop) = lax.scan(block_step, initial, blocks)
    return (from_blocks(out_zero), from_blocks(q_prop), mapping, memory)


def spread_shards(
    block_in,
    doc_lengths,
    attn_gain,
    qkv_weight,
    conv_weight,
    beta_weight,
    out_gain,
    out_weight,
    ffn_gain,
    gateup_weight,
    down_weight,
    cotangent,
):
    tok_count = block_in.shape[1]
    seq_count = lax.axis_size("seq")
    own_index = lax.axis_index("seq")
    positions = own_index * tok_count + jnp.arange(tok_count + KERNEL - 1, dtype=jnp.int32)
    doc_start, real_ext = row_layout(doc_lengths[0], positions)
    real_mask = real_ext[:tok_count]
    taps = [(positions - shift_no >= doc_start).astype(jnp.float32) for shift_no in range(KERNEL)]
    carry_on = (doc_start[:tok_count:BLOCK] != positions[:tok_count:BLOCK]).astype(jnp.float32)
    residual_in = block_in[0].astype(jnp.float32)
    stat_in = lax.rsqrt(jnp.mean(residual_in * residual_in, axis=-1, keepdims=True) + EPSILON)
    unit_in = residual_in * stat_in
    normed = (unit_in * attn_gain).astype(jnp.bfloat16)
    qkv_full, beta_full, out_full, gateup_full, down_full = (
        lax.all_gather(qkv_weight, ("seq", "row"), axis=1, tiled=True),
        lax.all_gather(beta_weight, ("seq", "row"), axis=1, tiled=True),
        lax.all_gather(out_weight, ("seq", "row"), axis=1, tiled=True),
        lax.all_gather(gateup_weight, ("seq", "row"), axis=1, tiled=True),
        lax.all_gather(down_weight, ("seq", "row"), axis=1, tiled=True),
    )
    raw = jnp.einsum("td,sdc->stc", normed, qkv_full, preferred_element_type=jnp.float32).astype(
        jnp.bfloat16
    )
    rims = passed_along(raw[:, tok_count - KERNEL + 1 :, :], "seq", 1)
    extended = jnp.concatenate([rims, raw], axis=1).astype(jnp.float32)
    conv_sum = jnp.zeros(raw.shape, jnp.float32)
    for shift_no in range(KERNEL):
        window = extended[:, KERNEL - 1 - shift_no : KERNEL - 1 - shift_no + tok_count]
        conv_sum = (
            conv_sum
            + conv_weight[:, shift_no][:, None, :]
            * window
            * taps[shift_no][:tok_count][None, :, None]
        )
    conv_sig = jax.nn.sigmoid(conv_sum)
    head_count = conv_weight.shape[2] // HDIM
    split_heads = (
        (conv_sum * conv_sig).reshape(3, tok_count, head_count, HDIM).transpose(0, 2, 1, 3)
    )
    q_scale = lax.rsqrt(jnp.sum(split_heads[0] * split_heads[0], axis=-1, keepdims=True) + EPSILON)
    q_unit = split_heads[0] * q_scale
    queries = q_unit * HDIM ** (-0.5)
    k_scale = lax.rsqrt(jnp.sum(split_heads[1] * split_heads[1], axis=-1, keepdims=True) + EPSILON)
    keys_in = split_heads[1] * k_scale
    values = split_heads[2]
    logits = jnp.einsum("td,hd->ht", normed, beta_full, preferred_element_type=jnp.float32)
    beta_sig = jax.nn.sigmoid(logits)
    strength = beta_sig * real_mask[None, :]
    (out_zero, q_prop, span_map, span_state), span_pullback = jax.vjp(
        partial(local_span, carry_on), queries, keys_in, values, strength
    )
    empty_state = jnp.zeros_like(span_state)
    all_maps, all_states = (
        lax.all_gather(span_map[None].astype(jnp.bfloat16), "seq", axis=0, tiled=True).astype(
            jnp.float32
        ),
        lax.all_gather(span_state[None].astype(jnp.bfloat16), "seq", axis=0, tiled=True).astype(
            jnp.float32
        ),
    )

    def fold_forward(counter, incoming):
        moved = (
            jnp.einsum("hpq,hqv->hpv", all_maps[counter], incoming, precision=PRECISE)
            + all_states[counter]
        )
        return jnp.where(counter < own_index, moved, incoming)

    state_in = lax.fori_loop(0, seq_count, fold_forward, empty_state)
    mixer = out_zero + jnp.einsum("htp,hpv->htv", q_prop, state_in, precision=PRECISE)
    stat_out = lax.rsqrt(jnp.mean(mixer * mixer, axis=-1, keepdims=True) + EPSILON)
    unit_out = mixer * stat_out
    normed_out = (
        (unit_out * out_gain).transpose(1, 0, 2).reshape(tok_count, -1).astype(jnp.bfloat16)
    )
    branch_part = jnp.dot(normed_out, out_full, preferred_element_type=jnp.float32)
    hidden = residual_in + lax.psum(branch_part.astype(jnp.bfloat16), "mp").astype(jnp.float32)
    stat_mid = lax.rsqrt(jnp.mean(hidden * hidden, axis=-1, keepdims=True) + EPSILON)
    unit_mid = hidden * stat_mid
    normed_mid = (unit_mid * ffn_gain).astype(jnp.bfloat16)
    gate_up = jnp.einsum("td,sdf->stf", normed_mid, gateup_full, preferred_element_type=jnp.float32)
    gate_sig = jax.nn.sigmoid(gate_up[0])
    product = (gate_up[0] * gate_sig * gate_up[1]).astype(jnp.bfloat16)
    ffn_part = jnp.dot(product, down_full, preferred_element_type=jnp.float32)
    block_out = hidden + lax.psum(ffn_part.astype(jnp.bfloat16), "mp").astype(jnp.float32)
    qkv_full, beta_full, out_full, gateup_full, down_full = (
        lax.all_gather(qkv_weight, ("seq", "row"), axis=1, tiled=True),
        lax.all_gather(beta_weight, ("seq", "row"), axis=1, tiled=True),
        lax.all_gather(out_weight, ("seq", "row"), axis=1, tiled=True),
        lax.all_gather(gateup_weight, ("seq", "row"), axis=1, tiled=True),
        lax.all_gather(down_weight, ("seq", "row"), axis=1, tiled=True),
    )
    grad_top = cotangent[0]
    grad_down_part = jnp.dot(product.T, grad_top, preferred_element_type=jnp.float32)
    grad_product = jnp.dot(grad_top, down_full.T, preferred_element_type=jnp.float32)
    grad_gate = grad_product * gate_up[1] * gate_sig * (1.0 + gate_up[0] * (1.0 - gate_sig))
    grad_up = grad_product * gate_up[0] * gate_sig
    grad_gate_up = jnp.stack([grad_gate, grad_up]).astype(jnp.bfloat16)
    grad_gateup_part = jnp.einsum(
        "td,stf->sdf", normed_mid, grad_gate_up, preferred_element_type=jnp.float32
    )
    grad_mid_part = jnp.einsum(
        "stf,sdf->td", grad_gate_up, gateup_full, preferred_element_type=jnp.float32
    )
    grad_mid = lax.psum(grad_mid_part.astype(jnp.bfloat16), "mp").astype(jnp.float32)
    ffn_gain_part = jnp.sum(grad_mid * unit_mid, axis=0)
    grad_unit_mid = grad_mid * ffn_gain
    grad_hidden = grad_top.astype(jnp.float32) + stat_mid * (
        grad_unit_mid - unit_mid * jnp.mean(grad_unit_mid * unit_mid, axis=-1, keepdims=True)
    )
    grad_branch = grad_hidden.astype(jnp.bfloat16)
    grad_out_part = jnp.dot(normed_out.T, grad_branch, preferred_element_type=jnp.float32)
    grad_normed_out = jnp.dot(grad_branch, out_full.T, preferred_element_type=jnp.float32)
    grad_normed_out = grad_normed_out.reshape(tok_count, head_count, HDIM).transpose(1, 0, 2)
    out_gain_part = jnp.sum(grad_normed_out * unit_out, axis=(0, 1))
    grad_unit_out = grad_normed_out * out_gain
    grad_mixer = stat_out * (
        grad_unit_out - unit_out * jnp.mean(grad_unit_out * unit_out, axis=-1, keepdims=True)
    )
    local_grad = jnp.einsum("htp,htv->hpv", q_prop, grad_mixer, precision=PRECISE)
    grad_q_prop = jnp.einsum("htv,hpv->htp", grad_mixer, state_in, precision=PRECISE)
    all_grads = lax.all_gather(
        local_grad[None].astype(jnp.bfloat16), "seq", axis=0, tiled=True
    ).astype(jnp.float32)

    def fold_backward(counter, later_grad):
        source = seq_count - 1 - counter
        moved = (
            jnp.einsum("hqp,hqv->hpv", all_maps[source], later_grad, precision=PRECISE)
            + all_grads[source]
        )
        return jnp.where(source > own_index, moved, later_grad)

    grad_end = lax.fori_loop(0, seq_count, fold_backward, empty_state)
    grad_map = jnp.einsum("hpv,hqv->hpq", grad_end, state_in, precision=PRECISE)
    grad_queries, grad_keys, grad_values, grad_strength = span_pullback(
        (grad_mixer, grad_q_prop, grad_map, grad_end)
    )
    grad_logits = (grad_strength * real_mask[None, :] * beta_sig * (1.0 - beta_sig)).astype(
        jnp.bfloat16
    )
    grad_beta_part = jnp.einsum(
        "ht,td->hd", grad_logits, normed, preferred_element_type=jnp.float32
    )
    grad_q_unit = grad_queries * HDIM ** (-0.5)
    grad_q_raw = q_scale * (
        grad_q_unit - q_unit * jnp.sum(grad_q_unit * q_unit, axis=-1, keepdims=True)
    )
    grad_k_raw = k_scale * (
        grad_keys - keys_in * jnp.sum(grad_keys * keys_in, axis=-1, keepdims=True)
    )
    grad_act = (
        jnp.stack([grad_q_raw, grad_k_raw, grad_values])
        .transpose(0, 2, 1, 3)
        .reshape(3, tok_count, -1)
    )
    grad_conv_sum = grad_act * conv_sig * (1.0 + conv_sum * (1.0 - conv_sig))
    rims_back = passed_along(grad_conv_sum[:, : KERNEL - 1, :], "seq", -1)
    grad_ext = jnp.concatenate([grad_conv_sum, rims_back], axis=1)
    grad_raw = jnp.zeros(grad_conv_sum.shape, jnp.float32)
    conv_terms = []
    for shift_no in range(KERNEL):
        grad_raw = (
            grad_raw
            + conv_weight[:, shift_no][:, None, :]
            * grad_ext[:, shift_no : shift_no + tok_count]
            * taps[shift_no][shift_no : shift_no + tok_count][None, :, None]
        )
        window = extended[:, KERNEL - 1 - shift_no : KERNEL - 1 - shift_no + tok_count]
        conv_terms.append(
            jnp.sum(grad_conv_sum * window * taps[shift_no][:tok_count][None, :, None], axis=1)
        )
    grad_conv_part = jnp.stack(conv_terms, axis=1)
    grad_raw_low = grad_raw.astype(jnp.bfloat16)
    grad_qkv_part = jnp.einsum(
        "td,stc->sdc", normed, grad_raw_low, preferred_element_type=jnp.float32
    )
    grad_normed = jnp.einsum(
        "stc,sdc->td", grad_raw_low, qkv_full, preferred_element_type=jnp.float32
    )
    grad_normed = grad_normed + jnp.einsum(
        "ht,hd->td", grad_logits, beta_full, preferred_element_type=jnp.float32
    )
    grad_normed, out_gain_sum = (
        lax.psum(grad_normed.astype(jnp.bfloat16), "mp").astype(jnp.float32),
        lax.psum(out_gain_part.astype(jnp.bfloat16), "mp").astype(jnp.float32),
    )
    attn_gain_part = jnp.sum(grad_normed * unit_in, axis=0)
    grad_unit_in = grad_normed * attn_gain
    grad_input = grad_hidden + stat_in * (
        grad_unit_in - unit_in * jnp.mean(grad_unit_in * unit_in, axis=-1, keepdims=True)
    )
    weight_sums = (
        lax.psum_scatter(grad_qkv_part, ("seq", "row"), scatter_dimension=1, tiled=True),
        lax.psum_scatter(grad_beta_part, ("seq", "row"), scatter_dimension=1, tiled=True),
        lax.psum_scatter(grad_out_part, ("seq", "row"), scatter_dimension=1, tiled=True),
        lax.psum_scatter(grad_gateup_part, ("seq", "row"), scatter_dimension=1, tiled=True),
        lax.psum_scatter(grad_down_part, ("seq", "row"), scatter_dimension=1, tiled=True),
    )
    small_sums = lax.psum(
        (attn_gain_part, grad_conv_part, out_gain_sum, ffn_gain_part), ("seq", "row")
    )
    return (
        block_out.astype(jnp.bfloat16)[None],
        grad_input[None],
        small_sums[0],
        weight_sums[0],
        small_sums[1],
        weight_sums[1],
        small_sums[2],
        weight_sums[2],
        small_sums[3],
        weight_sums[3],
        weight_sums[4],
    )


MESH = pl.DeviceIdType.MESH
STRIP = 16
TILE = 512
WIDE = 256


def phase_kernel(middle, both_cores, small_sum, meanwhile, n_in, n_out, part_ref, *refs):
    inputs, all_ref = refs[:n_in], refs[n_in]
    outs, scratch = refs[n_in + 1 : n_in + n_out], refs[n_in + n_out :]
    got, sums, gain_sum, send_sem, recv_sem = scratch[:5]
    count = all_ref.shape[0]
    rows = count // 8
    place, core, row = lax.axis_index("mp"), lax.axis_index("seq"), lax.axis_index("row")
    across_x = place + 1 - 2 * (place % 2)
    across_y = (place + 2) % 4
    across_both = 3 - place
    ways = {"x": {"mp": across_x}, "y": {"mp": across_y}}
    if both_cores or small_sum:
        ways["core"] = {"seq": 1 - core}
    steps = []
    if small_sum:
        bit = 1
        while bit < lax.axis_size("row"):
            steps.append(f"row{bit}")
            ways[steps[-1]] = {"row": row + bit - 2 * bit * ((row // bit) % 2)}
            bit *= 2
        steps += ["core", "x", "y"]
    barrier = pltpu.get_barrier_semaphore()
    for other in ways.values():
        pl.semaphore_signal(barrier, inc=1, device_id=other, device_id_type=MESH)
    pl.semaphore_wait(barrier, len(ways))

    def copy(index, source, target, way):
        return pltpu.make_async_remote_copy(
            src_ref=source,
            dst_ref=target,
            send_sem=send_sem.at[index],
            recv_sem=recv_sem.at[index],
            device_id=ways[way],
            device_id_type=MESH,
        )

    def block(of, half):
        return pl.ds(pl.multiple_of((2 * of + half) * rows, rows), rows)

    def strips(body):
        @pl.loop(0, rows // STRIP)
        def _(i):
            body(pl.multiple_of(i * STRIP, STRIP))

    part, relayed, copies = part_ref, [], send_sem.shape[0]
    if meanwhile:
        fetch = pltpu.make_async_copy(inputs[3].at[3], scratch[-3], scratch[-2])
        fetch.start()
    if both_cores:
        part, outgoing, incoming = scratch[5:8]
        weight = inputs[3]
        order = [across_both, across_x, across_y, place]
        passed_ref, far_ref = inputs[n_in - small_sum["dummies"] - 1], outs[-2]
        relayed = [
            copy(
                copies - 2,
                passed_ref.at[block(across_x, 0)],
                far_ref.at[pl.ds(0, rows)],
                "y",
            ),
            copy(
                copies - 1,
                passed_ref.at[block(across_y, 1)],
                far_ref.at[pl.ds(rows, rows)],
                "x",
            ),
        ]
        for step in relayed:
            step.start()

        def product(whose, of, target):
            start = pl.multiple_of(whose * count + 2 * of * rows, rows)
            left = part_ref[pl.ds(start, 2 * rows), :]
            lines = pl.ds(pl.multiple_of(2 * of * rows, rows), 2 * rows)

            @pl.loop(0, weight.shape[1] // TILE)
            def _(i):
                tile = pl.ds(pl.multiple_of(i * TILE, TILE), TILE)
                target[lines, tile] = jnp.dot(
                    left, weight[:, tile], preferred_element_type=F32
                ).astype(BF16)

            return lines

        shared = []
        for number in range(4):
            lines = pl.ds(pl.multiple_of(2 * order[number] * rows, rows), 2 * rows)
            shared.append(copy(12 + number, outgoing.at[lines], incoming.at[lines], "core"))

        def give(number):
            product(1 - core, order[number], outgoing)
            shared[number].start()

        def take(number):
            of = order[number]
            product(core, of, part)
            shared[number].wait_recv()

            @pl.loop(0, 2 * rows // STRIP)
            def _(i):
                strip = pl.ds(pl.multiple_of(2 * of * rows + i * STRIP, STRIP), STRIP)
                part[strip, :] = (
                    part[strip, :].astype(F32) + incoming[strip, :].astype(F32)
                ).astype(BF16)

    far = [
        copy(0, part.at[block(across_both, 0)], got.at[0], "x"),
        copy(1, part.at[block(across_both, 1)], got.at[1], "y"),
    ]
    near = [
        copy(2, part.at[block(across_x, 0)], got.at[2], "x"),
        copy(3, part.at[block(across_y, 1)], got.at[3], "y"),
    ]
    last = [copy(4, sums.at[0], got.at[4], "y"), copy(5, sums.at[1], got.at[5], "x")]
    own = [all_ref.at[block(place, 0)], all_ref.at[block(place, 1)]]
    passed = [all_ref.at[block(across_x, 0)], all_ref.at[block(across_y, 1)]]
    out_first = [copy(6, own[0], own[0], "x"), copy(7, own[1], own[1], "y")]
    out_second = [copy(8, own[0], own[0], "y"), copy(9, own[1], own[1], "x")]
    out_third = [copy(10, passed[0], passed[0], "y"), copy(11, passed[1], passed[1], "x")]

    if both_cores:
        give(0)
        give(1)
        take(0)
    for step in far:
        step.start()
    if both_cores:
        give(2)
        take(1)
        near[0].start()
        take(2)
        near[1].start()
        give(3)
        take(3)
    else:
        for step in near:
            step.start()
    gain_sum[...] = jnp.zeros_like(gain_sum)
    for half, onward in ((0, across_y), (1, across_x)):
        far[half].wait_recv()

        def add(at):
            strip = pl.ds(at, STRIP)
            mine = part[pl.ds((2 * onward + half) * rows + at, STRIP), :]
            sums[half, strip, :] = (mine.astype(F32) + got[half, strip, :].astype(F32)).astype(BF16)

        strips(add)
        last[half].start()
    for half in (0, 1):
        near[half].wait_recv()
        last[half].wait_recv()

        def finish(at):
            strip = pl.ds(at, STRIP)
            total = part[pl.ds((2 * place + half) * rows + at, STRIP), :].astype(F32)
            total = total + got[2 + half, strip, :].astype(F32)
            total = total + got[4 + half, strip, :].astype(F32)
            result = middle(total, half, strip, inputs, outs, gain_sum)
            all_ref[pl.ds((2 * place + half) * rows + at, STRIP), :] = result.astype(BF16)

        strips(finish)
        out_first[half].start()
        out_second[half].start()

    def use(of, first=False, last=False):
        if not meanwhile:
            return
        weight, left = scratch[-3], inputs[4]
        grad_left, products = outs[2], scratch[-1]
        lines = pl.ds(pl.multiple_of(2 * of * rows, rows), 2 * rows)
        grad_left[lines, :] = lax.dot_general(
            all_ref[lines, :], weight[...], NT, preferred_element_type=F32
        ).astype(BF16)

        @pl.loop(0, products.shape[1] // TILE)
        def _(i):
            tile = pl.ds(pl.multiple_of(i * TILE, TILE), TILE)
            more = lax.dot_general(
                left[lines, :], all_ref[lines, tile], TN, preferred_element_type=F32
            )
            if first:
                products[:, tile] = more
            elif last:
                outs[3][:, tile] = (products[:, tile] + more).astype(BF16)
            else:
                products[:, tile] = products[:, tile] + more

    if meanwhile:
        fetch.wait()
    use(place, first=True)
    gain = jnp.sum(gain_sum[...], axis=0, keepdims=True)
    small = []
    if small_sum:
        values, arrived = outs[-1], scratch[-1]
        first = n_in - small_sum["dummies"] - 4
        ffn_gain, out_gain, conv = inputs[first : first + 3]
        taps, width = conv.shape
        middle_lane = values.shape[1] // 2
        values[...] = jnp.zeros_like(values)
        values[0:1, :] = gain
        values[1:2, :] = ffn_gain[...]
        values[2:3, 0 : out_gain.shape[1]] = out_gain[...]
        for i in (0, 1):
            share = jnp.where(core == i, 1.0, 0.0)
            lane = i * middle_lane
            values[8 : 8 + taps, lane : lane + width] = conv[...] * share
    elif n_out > 2:
        outs[1][...] = gain

    def small_step(number):
        height = 8 if steps[number] in ("x", "y") else values.shape[0]
        step = copy(
            16 + number,
            arrived.at[number, 1, pl.ds(0, height)],
            arrived.at[number, 0, pl.ds(0, height)],
            steps[number],
        )
        arrived[number, 1, 0:height, :] = values[0:height, :]
        step.start()
        step.wait_recv()
        values[0:height, :] = values[0:height, :] + arrived[number, 0, 0:height, :]
        small.append(step)

    for half in (0, 1):
        out_first[half].wait_recv()
        out_third[half].start()
    if small_sum:
        for number in range(len(steps)):
            small_step(number)
    for step in out_second:
        step.wait_recv()
    use(across_x)
    use(across_y)
    for step in out_third:
        step.wait_recv()
    use(across_both, last=True)
    for step in relayed:
        step.wait_recv()
    for step in (*relayed, *far, *near, *last, *out_first, *out_second, *out_third, *small):
        step.wait_send()
    if both_cores:
        for step in shared:
            step.wait_send()


def normed_forward(total, half, strip, inputs, outs, gain_sum):
    residual, gain = inputs[:2]
    hidden = residual[half, strip, :].astype(F32) + total
    outs[0][half, strip, :] = hidden
    stat = lax.rsqrt(jnp.mean(hidden * hidden, axis=1, keepdims=True) + EPSILON)
    return hidden * stat * gain[...]


def normed_backward(keep, total, half, strip, inputs, outs, gain_sum):
    value, base, gain = inputs[:3]
    value = value[half, strip, :].astype(F32)
    stat = lax.rsqrt(jnp.mean(value * value, axis=1, keepdims=True) + EPSILON)
    unit = value * stat
    gain_sum[...] += jnp.sum((total * unit).reshape(2, 8, -1), axis=0)
    scaled = total * gain[...]
    grad = base[half, strip, :].astype(F32) + stat * (
        scaled - unit * jnp.mean(scaled * unit, axis=1, keepdims=True)
    )
    if keep:
        outs[0][half, strip, :] = grad
    return grad


def mp_phase(
    number,
    middle,
    part,
    inputs,
    dummies,
    outs,
    both_cores=False,
    small=None,
    passed=None,
    meanwhile=False,
):
    here, there = pl.BlockSpec(memory_space=pltpu.VMEM), pl.BlockSpec(memory_space=pl.ANY)
    count, model = part.shape
    if both_cores:
        count, model = count // 2, inputs[3].shape[1]
    block = (count // 8, model)
    copies, scratch, small_sum = 12, [], None
    if both_cores:
        scratch += [pltpu.VMEM((count, model), BF16)] * 3
    if small is not None:
        stages = lax.axis_size("row").bit_length() - 1 + 3
        copies = 16 + stages + 2
        height = 8 + small[2].shape[0]
        shape = (height + -height % 8, model)
        scratch += [pltpu.VMEM((stages, 2, *shape), F32)]
        small_sum = {"dummies": len(dummies)}
        inputs = [*inputs, *small, passed]
        outs = [
            *outs,
            jax.ShapeDtypeStruct((2 * block[0], model), BF16),
            jax.ShapeDtypeStruct(shape, F32),
        ]
    specs = [here] * len(inputs)
    if small is not None:
        specs[-1] = there
    if meanwhile:
        _, width, depth = inputs[3].shape
        specs[3] = there
        scratch += [
            pltpu.VMEM((width, depth), BF16),
            pltpu.SemaphoreType.DMA(()),
            pltpu.VMEM((width, model), F32),
        ]
    kernel = functools.partial(
        phase_kernel,
        middle,
        both_cores,
        small_sum,
        meanwhile,
        len(inputs) + len(dummies),
        1 + len(outs),
    )
    return pl.pallas_call(
        kernel,
        in_specs=[here, *specs] + [there] * len(dummies),
        out_specs=[here] * (1 + len(outs)),
        out_shape=[jax.ShapeDtypeStruct((count, model), BF16), *outs],
        scratch_shapes=[
            pltpu.VMEM((6, *block), BF16),
            pltpu.VMEM((2, *block), BF16),
            pltpu.VMEM((8, model), F32),
            pltpu.SemaphoreType.DMA((copies,)),
            pltpu.SemaphoreType.DMA((copies,)),
            *scratch,
        ],
        compiler_params=pltpu.CompilerParams(
            collective_id=number, has_side_effects=True, vmem_limit_bytes=50 << 20
        ),
        cost_estimate=pl.CostEstimate(flops=0, bytes_accessed=250 << 20, transcendentals=0),
    )(part, *inputs, *dummies)


def pair_kernel(product_ref, weight, hidden, left_own, left_other, gate, up, *refs):
    block_ref, gate_pair, up_pair, part_ref, got, sums, gate_in, up_in, send_sem, recv_sem = refs[-10:]
    rows = part_ref.shape[0] // 8
    place, core = lax.axis_index("mp"), lax.axis_index("seq")
    across_x = place + 1 - 2 * (place % 2)
    across_y = (place + 2) % 4
    across_both = 3 - place
    ways = {"x": {"mp": across_x}, "y": {"mp": across_y}, "core": {"seq": 1 - core}}
    barrier = pltpu.get_barrier_semaphore()
    for other in ways.values():
        pl.semaphore_signal(barrier, inc=1, device_id=other, device_id_type=MESH)
    pl.semaphore_wait(barrier, len(ways))

    def copy(index, source, target, way):
        return pltpu.make_async_remote_copy(
            src_ref=source,
            dst_ref=target,
            send_sem=send_sem.at[index],
            recv_sem=recv_sem.at[index],
            device_id=ways[way],
            device_id_type=MESH,
        )

    def block(of, half):
        return pl.ds(pl.multiple_of((2 * of + half) * rows, rows), rows)

    def strips(body):
        @pl.loop(0, rows // STRIP)
        def _(i):
            body(pl.multiple_of(i * STRIP, STRIP))

    far = [
        copy(0, part_ref.at[block(across_both, 0)], got.at[0], "x"),
        copy(1, part_ref.at[block(across_both, 1)], got.at[1], "y"),
    ]
    near = [
        copy(2, part_ref.at[block(across_x, 0)], got.at[2], "x"),
        copy(3, part_ref.at[block(across_y, 1)], got.at[3], "y"),
    ]
    last = [copy(4, sums.at[0], got.at[4], "y"), copy(5, sums.at[1], got.at[5], "x")]
    shared = [copy(6, gate, gate_in, "core"), copy(7, up, up_in, "core")]

    def produce(of):
        lines = pl.ds(pl.multiple_of(2 * of * rows, rows), 2 * rows)

        @pl.loop(0, weight.shape[1] // TILE)
        def _(i):
            tile = pl.ds(pl.multiple_of(i * TILE, TILE), TILE)
            part_ref[lines, tile] = jnp.dot(
                product_ref[lines, :], weight[:, tile], preferred_element_type=F32
            ).astype(BF16)

    for step in shared:
        step.start()
    produce(across_both)
    for step in far:
        step.start()
    produce(across_x)
    near[0].start()
    produce(across_y)
    near[1].start()
    produce(place)

    def products(own, other, target, first, count):
        @pl.loop(first, first + count)
        def _(i):
            tile = pl.ds(pl.multiple_of(i * WIDE, WIDE), WIDE)
            total = lax.dot_general(
                left_own[:, tile], own[...], TN, preferred_element_type=F32
            ) + lax.dot_general(left_other[:, tile], other[...], TN, preferred_element_type=F32)
            target[tile, :] = total.astype(BF16)

    tiles = left_own.shape[1] // WIDE
    shared[0].wait_recv()
    products(gate, gate_in, gate_pair, 0, tiles)
    for half, onward in ((0, across_y), (1, across_x)):
        far[half].wait_recv()

        def add(at):
            strip = pl.ds(at, STRIP)
            mine = part_ref[pl.ds((2 * onward + half) * rows + at, STRIP), :]
            sums[half, strip, :] = (mine.astype(F32) + got[half, strip, :].astype(F32)).astype(BF16)

        strips(add)
        last[half].start()
    shared[1].wait_recv()
    products(up, up_in, up_pair, 0, tiles)
    for half in (0, 1):
        near[half].wait_recv()
        last[half].wait_recv()

        def finish(at):
            strip = pl.ds(at, STRIP)
            total = part_ref[pl.ds((2 * place + half) * rows + at, STRIP), :].astype(F32)
            total = total + got[2 + half, strip, :].astype(F32)
            total = total + got[4 + half, strip, :].astype(F32)
            block_ref[pl.ds(half * rows + at, STRIP), :] = (hidden[half, strip, :] + total).astype(BF16)

        strips(finish)
    for step in (*shared, *far, *near, *last):
        step.wait_send()


def scattered_and_pairs(number, product, weight, hidden, left, gate, up, dummies):
    here, there = pl.BlockSpec(memory_space=pltpu.VMEM), pl.BlockSpec(memory_space=pl.ANY)
    count, model = product.shape[0], weight.shape[1]
    block = (count // 8, model)
    pair = jax.ShapeDtypeStruct((left[0].shape[1], gate.shape[1]), BF16)
    return pl.pallas_call(
        pair_kernel,
        in_specs=[here] * 7 + [there] * len(dummies),
        out_specs=[here] * 3,
        out_shape=[jax.ShapeDtypeStruct((2 * block[0], model), BF16), pair, pair],
        scratch_shapes=[
            pltpu.VMEM((count, model), BF16),
            pltpu.VMEM((6, *block), BF16),
            pltpu.VMEM((2, *block), BF16),
            pltpu.VMEM(gate.shape, BF16),
            pltpu.VMEM(up.shape, BF16),
            pltpu.SemaphoreType.DMA((8,)),
            pltpu.SemaphoreType.DMA((8,)),
        ],
        compiler_params=pltpu.CompilerParams(
            collective_id=number, has_side_effects=True, vmem_limit_bytes=54 << 20
        ),
        cost_estimate=pl.CostEstimate(flops=0, bytes_accessed=130 << 20, transcendentals=0),
    )(product, weight, hidden, *left, gate, up, *dummies)


def swapped(block):
    return lax.ppermute(block, "seq", [(0, 1), (1, 0)])


def in_order(mine, other, core, axis):
    first = jnp.where(core == 0, mine, other)
    second = jnp.where(core == 0, other, mine)
    return jnp.concatenate([first, second], axis=axis)


def after(block, *done):
    nothing = sum(part[(0,) * part.ndim].astype(F32) for part in done) * 0.0
    return block + nothing.astype(block.dtype)


def halves(block, core, axis):
    size = block.shape[axis] // 2
    pick = lambda i: lax.dynamic_slice_in_dim(block, i * size, size, axis=axis)
    return pick(core), pick(1 - core)


def both_tokens(left, right, *done):
    product = lambda a, b: lax.dot_general(
        a, b, (((0,), (0,)), ((), ())), preferred_element_type=F32
    )
    total = product(left[0], right[0]) + product(left[1], right[1])
    return (after(total, *done) if done else total).astype(BF16)


def own_columns(block, core):
    mine, other = halves(block, core, 1)
    return mine, swapped(other)


def over_row(pair, axis):
    return lax.psum_scatter(pair, "row", scatter_dimension=axis, tiled=True)


def joined_shards(
    block_in,
    doc_lengths,
    attn_gain,
    qkv_weight,
    conv_weight,
    beta_weight,
    out_gain,
    out_weight,
    ffn_gain,
    gateup_weight,
    down_weight,
    cotangent,
):
    tok_count, model = block_in.shape[1:]
    core, own = lax.axis_index("seq"), lax.axis_index("mp")
    width = conv_weight.shape[2] // 2
    own_heads = width // HDIM
    quarter = tok_count // 4

    gather = lambda weight: lax.all_gather(weight, ("seq", "row"), axis=1, tiled=True)
    mixer_full = gather(jnp.concatenate([qkv_weight, out_weight.T[None]]))
    qkv_full, out_full = mixer_full[:3], mixer_full[3]
    beta_full, gateup_full, down_full = (
        gather(beta_weight),
        gather(gateup_weight),
        gather(down_weight),
    )
    qkv_own = lax.dynamic_slice_in_dim(qkv_full, core * width, width, axis=2)
    beta_own = lax.dynamic_slice_in_dim(beta_full, core * own_heads, own_heads, axis=0)
    beta_rows = jnp.pad(beta_own, ((0, HDIM - own_heads), (0, 0)))
    mix_across = jnp.concatenate([qkv_own[0].T, qkv_own[1].T, qkv_own[2].T, beta_rows])
    conv_own = lax.dynamic_slice_in_dim(conv_weight, core * width, width, axis=2)
    conv_own = conv_own.transpose(1, 0, 2).reshape(KERNEL, 3 * width)

    residual_in = block_in[0].astype(F32)
    stat_in = lax.rsqrt(jnp.mean(residual_in * residual_in, axis=-1, keepdims=True) + EPSILON)
    normed_mine = (residual_in * stat_in * attn_gain).astype(BF16)
    normed = in_order(normed_mine, swapped(normed_mine), core, 0)

    positions = jnp.arange(2 * tok_count, dtype=jnp.int32)
    doc_start, real_row = row_layout(doc_lengths[0], positions)
    keep = jnp.pad((doc_start[::BLOCK] != positions[::BLOCK]).astype(F32), (0, 1))
    count = jnp.sum(real_row.reshape(-1, BLOCK), axis=1).astype(jnp.int32)
    raw = lax.dot_general(
        normed, mix_across, (((1,), (1,)), ((), ())), preferred_element_type=F32
    ).astype(BF16)
    gain = out_gain[None, :]
    group = 4 if raw.shape[0] % (4 * CHUNK) == 0 else 1
    heads_out, *saved = forward(keep, count, raw, conv_own, gain, group)

    mine, other = halves(heads_out, core, 0)
    normed_out = in_order(mine, swapped(other), core, 1)
    branch_part = lax.dot_general(
        normed_out, out_full, (((1,), (1,)), ((), ())), preferred_element_type=F32
    )
    own_rows = lambda block: lax.dynamic_slice_in_dim(
        block[0], own * quarter, quarter, axis=0
    ).reshape(2, -1, model)
    residual_own = own_rows(block_in)
    rows_own = jax.ShapeDtypeStruct(residual_own.shape, F32)
    normed_mid, hidden = mp_phase(
        0,
        normed_forward,
        branch_part.astype(BF16),
        [residual_own, ffn_gain[None, :]],
        [],
        [rows_own],
    )

    grad_top = cotangent[0]
    gate_up = jnp.einsum("td,sdf->stf", normed_mid, gateup_full, preferred_element_type=F32)
    gate_sig = jax.nn.sigmoid(gate_up[0])
    product = (gate_up[0] * gate_sig * gate_up[1]).astype(BF16)
    normed_halves = own_columns(normed_mid, core)
    down_pair = both_tokens(
        (product, swapped(product)), own_columns(grad_top, core), normed_halves[1]
    )
    grad_product = jnp.dot(grad_top, down_full.T, preferred_element_type=F32)
    grad_product = after(grad_product, down_pair)
    grad_gate = grad_product * gate_up[1] * gate_sig * (1.0 + gate_up[0] * (1.0 - gate_sig))
    grad_up = grad_product * gate_up[0] * gate_sig
    grad_gate, grad_up = grad_gate.astype(BF16), grad_up.astype(BF16)
    grad_mid_part = jnp.einsum(
        "stf,sdf->td",
        jnp.stack([grad_gate, grad_up]),
        gateup_full,
        preferred_element_type=F32,
    ).astype(BF16)
    block_out, gate_pair, up_pair = scattered_and_pairs(
        4,
        product,
        down_full,
        hidden,
        normed_halves,
        grad_gate,
        grad_up,
        [down_pair],
    )
    down_sum, gate_sum, up_sum = over_row(down_pair, 1), over_row(gate_pair, 0), over_row(up_pair, 0)
    grad_branch, grad_hidden, ffn_gain_part, grad_normed_out, grad_out_part = mp_phase(
        1,
        partial(normed_backward, True),
        grad_mid_part,
        [hidden, own_rows(cotangent), ffn_gain[None, :], mixer_full.transpose(0, 2, 1), normed_out],
        [block_out, down_sum, gate_pair, up_pair],
        [
            rows_own,
            jax.ShapeDtypeStruct((1, model), F32),
            jax.ShapeDtypeStruct(normed_out.shape, BF16),
            jax.ShapeDtypeStruct((normed_out.shape[1], model), BF16),
        ],
        meanwhile=True,
    )
    mine, other = halves(grad_normed_out, core, 1)
    grad_heads = in_order(mine, swapped(other), core, 0)
    mine, other = halves(grad_out_part, core, 1)
    out_pair = after(mine.astype(F32) + swapped(other).astype(F32), up_sum).astype(BF16)
    grad_raw, grad_conv_own, out_gain_part, block_out = backward(
        keep,
        count,
        raw,
        conv_own,
        gain,
        grad_heads,
        *saved,
        group,
        block_out,
        [gate_sum],
    )
    normed_mine, normed_other = halves(normed, core, 1)
    by_columns = lambda part: lax.dot_general(
        part, grad_raw, (((0,), (0,)), ((), ())), preferred_element_type=F32
    ).astype(BF16)
    qkv_other = swapped(by_columns(normed_other))
    qkv_mine = by_columns(normed_mine)
    grad_input, far_rows, small = mp_phase(
        2,
        partial(normed_backward, False),
        grad_raw,
        [residual_own, grad_hidden, attn_gain[None, :], mix_across],
        [up_sum, out_pair, qkv_mine, qkv_other],
        [],
        both_cores=True,
        small=[ffn_gain_part, out_gain_part, grad_conv_own],
        passed=block_out,
    )
    grad_input = grad_input.astype(F32)
    places = jnp.arange(4)[:, None, None]
    block_out = jnp.where(
        places == (own ^ 3),
        far_rows[None],
        block_out.reshape(4, quarter, model),
    ).reshape(tok_count, model)
    grad_attn_gain, grad_ffn_gain = small[0], small[1]
    grad_out_gain = small[2, : out_gain.shape[0]]
    conv_at = 8
    conv_of = lambda i: (
        small[conv_at : conv_at + KERNEL, i * (model // 2) : i * (model // 2) + 3 * width]
        .reshape(KERNEL, 3, width)
        .transpose(1, 0, 2)
    )
    grad_conv = jnp.concatenate([conv_of(0), conv_of(1)], axis=2)
    grad_down, grad_out = down_sum.astype(F32), over_row(out_pair, 1).astype(F32)
    grad_gateup = jnp.stack([gate_sum, up_sum]).astype(F32)
    row_sums = [over_row(part, 0) for part in (qkv_mine, qkv_other)]
    by_kind = lambda part: part[:, : 3 * width].reshape(-1, 3, width).transpose(1, 0, 2)
    grad_qkv = in_order(by_kind(row_sums[0]), by_kind(row_sums[1]), core, 2).astype(F32)
    of_heads = lambda part: part[:, 3 * width : 3 * width + own_heads].T
    grad_beta = in_order(of_heads(row_sums[0]), of_heads(row_sums[1]), core, 0).astype(F32)
    return (
        block_out[None],
        grad_input[None],
        grad_attn_gain,
        grad_qkv,
        grad_conv,
        grad_beta,
        grad_out_gain,
        grad_out,
        grad_ffn_gain,
        grad_gateup,
        grad_down,
    )


def solution(mesh):
    rows = mesh.shape["row"]
    joined = mesh.shape["seq"] == 2 and mesh.shape["mp"] == 4 and rows & (rows - 1) == 0
    return jax.shard_map(
        joined_shards if joined else spread_shards,
        mesh=mesh,
        in_specs=(
            P("row", "seq", None),
            P("row", None),
            P(),
            P(None, ("seq", "row"), "mp"),
            P(None, None, "mp"),
            P("mp", ("seq", "row")),
            P(),
            P("mp", ("seq", "row")),
            P(),
            P(None, ("seq", "row"), "mp"),
            P("mp", ("seq", "row")),
            P("row", "seq", None),
        ),
        out_specs=(
            P("row", "seq", None),
            P("row", "seq", None),
            P(),
            P(None, ("seq", "row"), "mp"),
            P(None, None, "mp"),
            P("mp", ("seq", "row")),
            P(),
            P("mp", ("seq", "row")),
            P(),
            P(None, ("seq", "row"), "mp"),
            P("mp", ("seq", "row")),
        ),
        check_vma=False,
    )
```

```python
import functools
from functools import partial

import jax
import jax.numpy as jnp
from jax import lax
from jax.experimental import pallas as pl
from jax.experimental.pallas import tpu as pltpu
from jax.sharding import PartitionSpec as P

HDIM = 128
KERNEL = 4
BLOCK = 64
CHUNK = 128
EPSILON = 1e-06
PRECISE = lax.Precision.HIGHEST
F32 = jnp.float32
BF16 = jnp.bfloat16

NT=(((1,),(1,)),((),())); NN=(((1,),(0,)),((),())); TN=(((0,),(0,)),((),()))

def mm(a,b,dims=NN):
    return lax.dot_general(a.astype(BF16), b.astype(BF16), dims, preferred_element_type=F32)

def iotas():
    return lax.broadcasted_iota(jnp.int32,(CHUNK,CHUNK),0), lax.broadcasted_iota(jnp.int32,(CHUNK,CHUNK),1)

def inverses(below):
    r,c=iotas()
    done=[jnp.where(r==c,1.0,0.0)-jnp.where(r//2==c//2,a,0.0) for a in below]
    size=2
    while size<CHUNK:
        pairs=(r//(2*size)==c//(2*size))&(r//size!=c//size)
        half=[mm(jnp.where(pairs,a,0.0),t) for a,t in zip(below,done)]
        done=[t-mm(t,x) for t,x in zip(done,half)]
        size*=2
    return done

def conv_act(ext_ref, base, lanes, cw, taps):
    total=cw[0:1]*ext_ref[pl.ds(base+8,CHUNK),lanes]
    for j in range(1,KERNEL):
        total=total+(cw[j:j+1]*taps[j-1])*ext_ref[pl.ds(base+8-j,CHUNK),lanes]
    sig=jax.nn.sigmoid(total)
    return total,sig

def layout(keep_ref, count_ref, block):
    r,_=iotas()
    inside=r%BLOCK
    first=r<BLOCK
    keep0,keep1,after=keep_ref[block],keep_ref[block+1],keep_ref[block+2]
    here=jnp.where(first,keep0,keep1)
    later=jnp.where(first,keep1,after)
    taps=[jnp.where(inside<j,here,1.0) for j in range(1,KERNEL)]
    taps_later=[jnp.where(inside>=BLOCK-j,later,1.0) for j in range(1,KERNEL)]
    real=jnp.where(inside<jnp.where(first,count_ref[block],count_ref[block+1]),1.0,0.0)
    return taps,taps_later,jnp.where(first,1.0,keep1),jnp.where(first,keep1,1.0),real,keep0,keep1

def fwd_kernel(heads, group, keep_ref, count_ref, raw_ref, cw_ref, gain_ref, normed_ref, o_ref, st_ref, wr_ref, ext, state):
    rows=group*CHUNK
    step=pl.program_id(0)
    @pl.when(step==0)
    def _():
        ext[0:8,:]=jnp.zeros((8,3*heads*HDIM),F32)
        state[...]=jnp.zeros(state.shape,F32)
    @pl.when(step>0)
    def _():
        ext[0:8,:]=ext[rows:rows+8,:]
    ext[8:,:]=raw_ref[:,0:3*heads*HDIM].astype(F32)
    r,c=iotas()
    width=heads*HDIM
    units=[]
    below=[]
    for g in range(group):
        base=g*CHUNK
        taps,_,m,m2,real,keep0,keep1=layout(keep_ref,count_ref,2*(step*group+g))
        sig_b=jax.nn.sigmoid(raw_ref[pl.ds(base,CHUNK),pl.ds(3*width,HDIM)].astype(F32))*real
        for h in range(heads):
            act=[]
            for s in range(3):
                lanes=pl.ds(s*width+h*HDIM,HDIM)
                total,sig=conv_act(ext,base,lanes,cw_ref[:,lanes],taps)
                act.append(total*sig)
            q=act[0]*(lax.rsqrt(jnp.sum(act[0]*act[0],axis=1,keepdims=True)+EPSILON)*HDIM**-0.5)
            k=act[1]*lax.rsqrt(jnp.sum(act[1]*act[1],axis=1,keepdims=True)+EPSILON)
            v=act[2]
            b=sig_b[:,h:h+1]
            gram=mm(k,k,NT)
            score=mm(q,k,NT)
            mask=jnp.where(c<BLOCK,m,1.0)
            a=jnp.where(r>c,b*gram*mask,0.0)
            l=jnp.where(r>=c,score*mask,0.0)
            below.append(a)
            units.append((g,h,q*m,k*m2,l,b*k,b*v,m,keep0,keep1))
    done=inverses(below)
    wus=[(mm(t,u[5])*u[7],mm(t,u[6])) for t,u in zip(done,units)]
    for t,(w,u),(g,h,q,k,l,_,_,_,keep0,keep1) in zip(done,wus,units):
        base=g*CHUNK
        out=(pl.ds(base,CHUNK),pl.ds(h*HDIM,HDIM))
        st_ref[g,h,1]=t.astype(BF16)
        wr_ref[out]=w.astype(BF16)
        s=state[h]*keep0
        st_ref[g,h,0]=s.astype(BF16)
        rr=u-mm(w,s)
        o=mm(q,s)+mm(l,rr)
        state[h]=s*keep1+mm(k,rr,TN)
        wr_ref[pl.ds(base,CHUNK),pl.ds(width+h*HDIM,HDIM)]=rr.astype(BF16)
        o_ref[out]=o
        stat=lax.rsqrt(jnp.mean(o*o,axis=1,keepdims=True)+EPSILON)
        normed_ref[out]=(o*stat*gain_ref[...]).astype(BF16)

def forward(keep, count, raw, cw, gain, group):
    n=raw.shape[0]; width=cw.shape[1]//3; heads=width//HDIM; rows=group*CHUNK
    nc=n//CHUNK
    row=lambda w: pl.BlockSpec((rows,w),lambda i:(i,0))
    mat=pl.BlockSpec((group,heads,2,HDIM,HDIM),lambda i:(i,0,0,0,0))
    full=lambda a: pl.BlockSpec(a.shape,lambda i:(0,0))
    return pl.pallas_call(functools.partial(fwd_kernel,heads,group),
        grid=(n//rows,),
        in_specs=[pl.BlockSpec(memory_space=pltpu.SMEM)]*2+[row(raw.shape[1]),full(cw),full(gain)],
        out_specs=[row(width),row(width),mat,row(2*width)],
        out_shape=[jax.ShapeDtypeStruct((n,width),BF16),jax.ShapeDtypeStruct((n,width),F32),
            jax.ShapeDtypeStruct((nc,heads,2,HDIM,HDIM),BF16),jax.ShapeDtypeStruct((n,2*width),BF16)],
        scratch_shapes=[pltpu.VMEM((rows+8,3*width),F32),pltpu.VMEM((heads,HDIM,HDIM),F32)],
        compiler_params=pltpu.CompilerParams(vmem_limit_bytes=24<<20),
        cost_estimate=pl.CostEstimate(flops=0,bytes_accessed=120<<20,transcendentals=0),
    )(keep,count,raw,cw,gain)

def bwd_kernel(heads, group, keep_ref, count_ref, raw_ref, prev_ref, cw_ref, gain_ref, gno_ref, o_ref, st_ref, wr_ref, *rest):
    block_ref=rest[0]
    graw_ref, gcw_ref, ggain_ref, all_ref, ext, gext, grad_state, local_sem, send_sem, recv_sem = rest[-10:]
    rows=group*CHUNK
    step=pl.program_id(0); steps=pl.num_programs(0)
    width=heads*HDIM
    @pl.when(step==0)
    def _():
        gext[rows:rows+8,:]=jnp.zeros((8,3*heads*HDIM),F32)
        grad_state[...]=jnp.zeros(grad_state.shape,F32)
        gcw_ref[...]=jnp.zeros(gcw_ref.shape,F32)
        ggain_ref[...]=jnp.zeros(ggain_ref.shape,F32)
    @pl.when(step>0)
    def _():
        gext[rows:rows+8,:]=gext[0:8,:]
    first=jnp.where(step==steps-1,0.0,1.0)
    place=lax.axis_index("mp")
    across_x=place+1-2*(place%2)
    across_y=(place+2)%4
    part=block_ref.shape[0]//2
    at=lambda of,half: all_ref.at[pl.ds(pl.multiple_of((2*of+half)*part,part),part)]
    def copy(index,source,target,other):
        return pltpu.make_async_remote_copy(src_ref=source,dst_ref=target,send_sem=send_sem.at[index],recv_sem=recv_sem.at[index],
            device_id={"mp":other},device_id_type=pl.DeviceIdType.MESH)
    top,low=block_ref.at[pl.ds(0,part)],block_ref.at[pl.ds(part,part)]
    keep_own=pltpu.make_async_copy(block_ref,all_ref.at[pl.ds(pl.multiple_of(2*place*part,2*part),2*part)],local_sem)
    sends=[copy(0,top,at(place,0),across_x),copy(1,low,at(place,1),across_y),copy(2,top,at(place,0),across_y),copy(3,low,at(place,1),across_x)]
    @pl.when(step==0)
    def _():
        barrier=pltpu.get_barrier_semaphore()
        for other in (across_x,across_y):
            pl.semaphore_signal(barrier,inc=1,device_id={"mp":other},device_id_type=pl.DeviceIdType.MESH)
        pl.semaphore_wait(barrier,2)
        keep_own.start()
        for send in sends: send.start()
    ext[0:8,:]=prev_ref[:,0:3*width].astype(F32)[8:16]*first
    ext[8:,:]=raw_ref[:,0:3*heads*HDIM].astype(F32)
    r,c=iotas()
    units=[]
    for g in range(group-1,-1,-1):
        base=g*CHUNK
        taps,taps_later,m,m2,real,keep0,keep1=layout(keep_ref,count_ref,2*((steps-1-step)*group+g))
        beta=jax.nn.sigmoid(raw_ref[pl.ds(base,CHUNK),pl.ds(3*width,HDIM)].astype(F32))
        sig_b=beta*real
        for h in range(heads):
            out=(pl.ds(base,CHUNK),pl.ds(h*HDIM,HDIM))
            act=[];tot=[];sigs=[]
            for s in range(3):
                lanes=pl.ds(s*width+h*HDIM,HDIM)
                total,sig=conv_act(ext,base,lanes,cw_ref[:,lanes],taps)
                act.append(total*sig);tot.append(total);sigs.append(sig)
            rq=lax.rsqrt(jnp.sum(act[0]*act[0],axis=1,keepdims=True)+EPSILON)
            rk=lax.rsqrt(jnp.sum(act[1]*act[1],axis=1,keepdims=True)+EPSILON)
            qu=act[0]*rq
            o=o_ref[out]
            stat=lax.rsqrt(jnp.mean(o*o,axis=1,keepdims=True)+EPSILON)
            uo=o*stat
            gno=gno_ref[out].astype(F32)
            ggain_ref[...]+=jnp.sum(gno*uo,axis=0,keepdims=True)
            gu=gno*gain_ref[...]
            do=stat*(gu-uo*jnp.mean(gu*uo,axis=1,keepdims=True))
            units.append(dict(g=g,h=h,base=base,out=out,second=(pl.ds(base,CHUNK),pl.ds(width+h*HDIM,HDIM)),taps=taps,m=m,m2=m2,keep0=keep0,keep1=keep1,tot=tot,sigs=sigs,
                rq=rq,rk=rk,qu=qu,q=qu*HDIM**-0.5,k=act[1]*rk,v=act[2],b=sig_b[:,h:h+1],do=do,
                mask=jnp.where(c<BLOCK,m,1.0)))
        for u in units[-heads:]: u.update(taps_later=taps_later,beta=beta,sig_b=sig_b)
    for u in units: u['gram']=mm(u['k'],u['k'],NT)*u['mask']
    for u in units: u['l']=jnp.where(r>=c,mm(u['q'],u['k'],NT)*u['mask'],0.0)
    for u in units: u['dr0']=mm(u['l'],u['do'],TN)
    for u in units: u['ds0']=mm(u['q']*u['m'],u['do'],TN)
    for u in units:
        dsn=grad_state[u['h']]
        u['dsn']=dsn
        u['dr']=u['dr0']+u['m2']*mm(u['k'],dsn)
        ds=u['keep1']*dsn+u['ds0']-mm(wr_ref[u['out']],u['dr'],TN)
        grad_state[u['h']]=u['keep0']*ds
    for u in units: u['df']=mm(st_ref[u['g'],u['h'],1],u['dr'],TN)
    for u in units: u['dl']=jnp.where(r>=c,mm(u['do'],wr_ref[u['second']],NT)*u['mask'],0.0)
    for u in units: u['da']=jnp.where(r>c,-mm(u['df'],wr_ref[u['second']],NT),0.0)
    for u in units:
        u['de']=u['b']*u['df']
        u['e']=u['v']-u['m']*mm(u['k'],st_ref[u['g'],u['h'],0])
        u['gb']=jnp.sum(u['df']*u['e']+u['da']*u['gram'],axis=1,keepdims=True)
        u['dkk']=u['b']*u['da']*u['mask']
    for u in units: u['dq']=u['m']*mm(u['do'],st_ref[u['g'],u['h'],0],NT)+mm(u['dl'],u['k'])
    for u in units:
        u['dk']=(mm(u['dl'],u['q'],TN)+u['m2']*mm(wr_ref[u['second']],u['dsn'],NT)-u['m']*mm(u['de'],st_ref[u['g'],u['h'],0],NT)
            +mm(u['dkk'],u['k'])+mm(u['dkk'],u['k'],TN))
    for u in units:
        gq=u['dq']*HDIM**-0.5
        gq=u['rq']*(gq-u['qu']*jnp.sum(gq*u['qu'],axis=1,keepdims=True))
        gk=u['rk']*(u['dk']-u['k']*jnp.sum(u['dk']*u['k'],axis=1,keepdims=True))
        for i,ga in enumerate((gq,gk,u['de'])):
            lanes=pl.ds(i*width+u['h']*HDIM,HDIM)
            sig,tot=u['sigs'][i],u['tot'][i]
            gc=ga*sig*(1.0+tot*(1.0-sig))
            gext[pl.ds(u['base'],CHUNK),lanes]=gc
            for j in range(KERNEL):
                win=ext[pl.ds(u['base']+8-j,CHUNK),lanes]
                prod=gc*win if j==0 else gc*win*u['taps'][j-1]
                gcw_ref[j:j+1,lanes]+=jnp.sum(prod,axis=0,keepdims=True)
    for at in range(0,len(units),heads):
        glog=jnp.zeros((CHUNK,HDIM),F32)
        for u in units[at:at+heads]:
            glog=jnp.where(c==u['h'],u['gb'],glog)
            for i in range(3):
                lanes=pl.ds(i*width+u['h']*HDIM,HDIM)
                cw=cw_ref[:,lanes]
                total=cw[0:1]*gext[pl.ds(u['base'],CHUNK),lanes]
                for j in range(1,KERNEL):
                    total=total+(cw[j:j+1]*u['taps_later'][j-1])*gext[pl.ds(u['base']+j,CHUNK),lanes]
                graw_ref[pl.ds(u['base'],CHUNK),lanes]=total.astype(BF16)
        graw_ref[pl.ds(u['base'],CHUNK),pl.ds(3*width,HDIM)]=(glog*u['sig_b']*(1.0-u['beta'])).astype(BF16)
    @pl.when(step==steps-1)
    def _():
        keep_own.wait()
        for send in sends: send.wait_recv()
        for send in sends: send.wait_send()

def backward(keep, count, raw, cw, gain, gno, o, st, wr, group, block, dummies=()):
    n=raw.shape[0]; width=cw.shape[1]//3; heads=width//HDIM; rows=group*CHUNK
    steps=n//rows
    row=lambda w: pl.BlockSpec((rows,w),lambda i:(steps-1-i,0))
    mat=pl.BlockSpec((group,heads,2,HDIM,HDIM),lambda i:(steps-1-i,0,0,0,0))
    full=lambda a: pl.BlockSpec(a.shape,lambda i:(0,0))
    prev=pl.BlockSpec((16,raw.shape[1]),lambda i:(jnp.maximum((steps-1-i)*(rows//16)-1,0),0))
    return pl.pallas_call(functools.partial(bwd_kernel,heads,group),
        grid=(steps,),
        in_specs=[pl.BlockSpec(memory_space=pltpu.SMEM)]*2+[row(raw.shape[1]),prev,full(cw),full(gain),row(width),row(width),mat,row(2*width)]+[pl.BlockSpec(memory_space=pl.ANY)]*(1+len(dummies)),
        out_specs=[row(raw.shape[1]),pl.BlockSpec((KERNEL,3*width),lambda i:(0,0)),pl.BlockSpec((1,HDIM),lambda i:(0,0)),pl.BlockSpec(memory_space=pl.ANY)],
        out_shape=[jax.ShapeDtypeStruct(raw.shape,BF16),
            jax.ShapeDtypeStruct((KERNEL,3*width),F32),jax.ShapeDtypeStruct((1,HDIM),F32),jax.ShapeDtypeStruct((4*block.shape[0],block.shape[1]),BF16)],
        scratch_shapes=[pltpu.VMEM((rows+8,3*width),F32),pltpu.VMEM((rows+8,3*width),F32),pltpu.VMEM((heads,HDIM,HDIM),F32),
            pltpu.SemaphoreType.DMA(()),pltpu.SemaphoreType.DMA((4,)),pltpu.SemaphoreType.DMA((4,))],
        compiler_params=pltpu.CompilerParams(collective_id=3,has_side_effects=True,vmem_limit_bytes=24<<20),
        cost_estimate=pl.CostEstimate(flops=0,bytes_accessed=120<<20,transcendentals=0),
    )(keep,count,raw,raw,cw,gain,gno,o,st,wr,block,*dummies)


def passed_along(block, axis, distance):
    devices = range(lax.axis_size(axis))
    route = [(i - distance, i) for i in devices if i - distance in devices]
    return lax.ppermute(block, axis, route)


def row_layout(lengths, positions):
    span_len = (lengths + BLOCK - 1) // BLOCK * BLOCK
    closing = jnp.cumsum(span_len)
    opening = closing - span_len
    bounds = jnp.concatenate([opening, closing[-1:]])
    reached = bounds[None, :] <= positions[:, None]
    doc_start = jnp.max(jnp.where(reached, bounds[None, :], 0), axis=1)
    inside = (positions[:, None] >= opening[None, :]) & (
        positions[:, None] < (opening + lengths)[None, :]
    )
    real_mask = jnp.any(inside, axis=1).astype(jnp.float32)
    return (doc_start, real_mask)


def local_span(carry_on, queries, keys_in, values, strength):
    head_count, token_count, head_width = queries.shape
    block_count = token_count // BLOCK

    def to_blocks(tensor):
        return tensor.reshape(head_count, block_count, BLOCK, -1).transpose(1, 0, 2, 3)

    def from_blocks(tensor):
        return tensor.transpose(1, 0, 2, 3).reshape(head_count, token_count, -1)

    strict_lower = jnp.tril(jnp.ones((BLOCK, BLOCK), jnp.float32), -1)
    causal = jnp.tril(jnp.ones((BLOCK, BLOCK), jnp.float32))
    identity = jnp.broadcast_to(
        jnp.eye(head_width, dtype=jnp.float32), (head_count, head_width, head_width)
    )

    def block_step(carried, block_in):
        memory, mapping = carried
        q_blk, k_blk, v_blk, s_blk, carry_flag = block_in
        write_rate = s_blk[..., 0]
        memory = memory * carry_flag
        mapping = mapping * carry_flag
        key_gram = jnp.einsum("hcp,hdp->hcd", k_blk, k_blk, precision=PRECISE)
        system = jnp.eye(BLOCK, dtype=jnp.float32) + strict_lower * (
            write_rate[:, :, None] * key_gram
        )
        right_side = jnp.concatenate(
            [write_rate[..., None] * k_blk, write_rate[..., None] * v_blk], axis=-1
        )
        solved = lax.linalg.triangular_solve(
            system, right_side, left_side=True, lower=True, unit_diagonal=True
        )
        w_mat = solved[..., :head_width]
        u_mat = solved[..., head_width:]
        corrected = u_mat - jnp.einsum("hcp,hpv->hcv", w_mat, memory, precision=PRECISE)
        scores = causal * jnp.einsum("hcp,hdp->hcd", q_blk, k_blk, precision=PRECISE)
        out_zero = jnp.einsum("hcp,hpv->hcv", q_blk, memory, precision=PRECISE)
        out_zero = out_zero + jnp.einsum("hcd,hdv->hcv", scores, corrected, precision=PRECISE)
        w_map = jnp.einsum("hcp,hpq->hcq", w_mat, mapping, precision=PRECISE)
        q_prop = jnp.einsum("hcp,hpq->hcq", q_blk, mapping, precision=PRECISE)
        q_prop = q_prop - jnp.einsum("hcd,hdq->hcq", scores, w_map, precision=PRECISE)
        memory = memory + jnp.einsum("hcp,hcv->hpv", k_blk, corrected, precision=PRECISE)
        mapping = mapping - jnp.einsum("hcp,hcq->hpq", k_blk, w_map, precision=PRECISE)
        return ((memory, mapping), (out_zero, q_prop))

    initial = (jnp.zeros((head_count, head_width, head_width), jnp.float32), identity)
    blocks = (
        to_blocks(queries),
        to_blocks(keys_in),
        to_blocks(values),
        to_blocks(strength[..., None]),
        carry_on,
    )
    (memory, mapping), (out_zero, q_prop) = lax.scan(block_step, initial, blocks)
    return (from_blocks(out_zero), from_blocks(q_prop), mapping, memory)


def spread_shards(
    block_in,
    doc_lengths,
    attn_gain,
    qkv_weight,
    conv_weight,
    beta_weight,
    out_gain,
    out_weight,
    ffn_gain,
    gateup_weight,
    down_weight,
    cotangent,
):
    tok_count = block_in.shape[1]
    seq_count = lax.axis_size("seq")
    own_index = lax.axis_index("seq")
    positions = own_index * tok_count + jnp.arange(tok_count + KERNEL - 1, dtype=jnp.int32)
    doc_start, real_ext = row_layout(doc_lengths[0], positions)
    real_mask = real_ext[:tok_count]
    taps = [(positions - shift_no >= doc_start).astype(jnp.float32) for shift_no in range(KERNEL)]
    carry_on = (doc_start[:tok_count:BLOCK] != positions[:tok_count:BLOCK]).astype(jnp.float32)
    residual_in = block_in[0].astype(jnp.float32)
    stat_in = lax.rsqrt(jnp.mean(residual_in * residual_in, axis=-1, keepdims=True) + EPSILON)
    unit_in = residual_in * stat_in
    normed = (unit_in * attn_gain).astype(jnp.bfloat16)
    qkv_full, beta_full, out_full, gateup_full, down_full = (
        lax.all_gather(qkv_weight, ("seq", "row"), axis=1, tiled=True),
        lax.all_gather(beta_weight, ("seq", "row"), axis=1, tiled=True),
        lax.all_gather(out_weight, ("seq", "row"), axis=1, tiled=True),
        lax.all_gather(gateup_weight, ("seq", "row"), axis=1, tiled=True),
        lax.all_gather(down_weight, ("seq", "row"), axis=1, tiled=True),
    )
    raw = jnp.einsum("td,sdc->stc", normed, qkv_full, preferred_element_type=jnp.float32).astype(
        jnp.bfloat16
    )
    rims = passed_along(raw[:, tok_count - KERNEL + 1 :, :], "seq", 1)
    extended = jnp.concatenate([rims, raw], axis=1).astype(jnp.float32)
    conv_sum = jnp.zeros(raw.shape, jnp.float32)
    for shift_no in range(KERNEL):
        window = extended[:, KERNEL - 1 - shift_no : KERNEL - 1 - shift_no + tok_count]
        conv_sum = (
            conv_sum
            + conv_weight[:, shift_no][:, None, :]
            * window
            * taps[shift_no][:tok_count][None, :, None]
        )
    conv_sig = jax.nn.sigmoid(conv_sum)
    head_count = conv_weight.shape[2] // HDIM
    split_heads = (
        (conv_sum * conv_sig).reshape(3, tok_count, head_count, HDIM).transpose(0, 2, 1, 3)
    )
    q_scale = lax.rsqrt(jnp.sum(split_heads[0] * split_heads[0], axis=-1, keepdims=True) + EPSILON)
    q_unit = split_heads[0] * q_scale
    queries = q_unit * HDIM ** (-0.5)
    k_scale = lax.rsqrt(jnp.sum(split_heads[1] * split_heads[1], axis=-1, keepdims=True) + EPSILON)
    keys_in = split_heads[1] * k_scale
    values = split_heads[2]
    logits = jnp.einsum("td,hd->ht", normed, beta_full, preferred_element_type=jnp.float32)
    beta_sig = jax.nn.sigmoid(logits)
    strength = beta_sig * real_mask[None, :]
    (out_zero, q_prop, span_map, span_state), span_pullback = jax.vjp(
        partial(local_span, carry_on), queries, keys_in, values, strength
    )
    empty_state = jnp.zeros_like(span_state)
    all_maps, all_states = (
        lax.all_gather(span_map[None].astype(jnp.bfloat16), "seq", axis=0, tiled=True).astype(
            jnp.float32
        ),
        lax.all_gather(span_state[None].astype(jnp.bfloat16), "seq", axis=0, tiled=True).astype(
            jnp.float32
        ),
    )

    def fold_forward(counter, incoming):
        moved = (
            jnp.einsum("hpq,hqv->hpv", all_maps[counter], incoming, precision=PRECISE)
            + all_states[counter]
        )
        return jnp.where(counter < own_index, moved, incoming)

    state_in = lax.fori_loop(0, seq_count, fold_forward, empty_state)
    mixer = out_zero + jnp.einsum("htp,hpv->htv", q_prop, state_in, precision=PRECISE)
    stat_out = lax.rsqrt(jnp.mean(mixer * mixer, axis=-1, keepdims=True) + EPSILON)
    unit_out = mixer * stat_out
    normed_out = (
        (unit_out * out_gain).transpose(1, 0, 2).reshape(tok_count, -1).astype(jnp.bfloat16)
    )
    branch_part = jnp.dot(normed_out, out_full, preferred_element_type=jnp.float32)
    hidden = residual_in + lax.psum(branch_part.astype(jnp.bfloat16), "mp").astype(jnp.float32)
    stat_mid = lax.rsqrt(jnp.mean(hidden * hidden, axis=-1, keepdims=True) + EPSILON)
    unit_mid = hidden * stat_mid
    normed_mid = (unit_mid * ffn_gain).astype(jnp.bfloat16)
    gate_up = jnp.einsum("td,sdf->stf", normed_mid, gateup_full, preferred_element_type=jnp.float32)
    gate_sig = jax.nn.sigmoid(gate_up[0])
    product = (gate_up[0] * gate_sig * gate_up[1]).astype(jnp.bfloat16)
    ffn_part = jnp.dot(product, down_full, preferred_element_type=jnp.float32)
    block_out = hidden + lax.psum(ffn_part.astype(jnp.bfloat16), "mp").astype(jnp.float32)
    qkv_full, beta_full, out_full, gateup_full, down_full = (
        lax.all_gather(qkv_weight, ("seq", "row"), axis=1, tiled=True),
        lax.all_gather(beta_weight, ("seq", "row"), axis=1, tiled=True),
        lax.all_gather(out_weight, ("seq", "row"), axis=1, tiled=True),
        lax.all_gather(gateup_weight, ("seq", "row"), axis=1, tiled=True),
        lax.all_gather(down_weight, ("seq", "row"), axis=1, tiled=True),
    )
    grad_top = cotangent[0]
    grad_down_part = jnp.dot(product.T, grad_top, preferred_element_type=jnp.float32)
    grad_product = jnp.dot(grad_top, down_full.T, preferred_element_type=jnp.float32)
    grad_gate = grad_product * gate_up[1] * gate_sig * (1.0 + gate_up[0] * (1.0 - gate_sig))
    grad_up = grad_product * gate_up[0] * gate_sig
    grad_gate_up = jnp.stack([grad_gate, grad_up]).astype(jnp.bfloat16)
    grad_gateup_part = jnp.einsum(
        "td,stf->sdf", normed_mid, grad_gate_up, preferred_element_type=jnp.float32
    )
    grad_mid_part = jnp.einsum(
        "stf,sdf->td", grad_gate_up, gateup_full, preferred_element_type=jnp.float32
    )
    grad_mid = lax.psum(grad_mid_part.astype(jnp.bfloat16), "mp").astype(jnp.float32)
    ffn_gain_part = jnp.sum(grad_mid * unit_mid, axis=0)
    grad_unit_mid = grad_mid * ffn_gain
    grad_hidden = grad_top.astype(jnp.float32) + stat_mid * (
        grad_unit_mid - unit_mid * jnp.mean(grad_unit_mid * unit_mid, axis=-1, keepdims=True)
    )
    grad_branch = grad_hidden.astype(jnp.bfloat16)
    grad_out_part = jnp.dot(normed_out.T, grad_branch, preferred_element_type=jnp.float32)
    grad_normed_out = jnp.dot(grad_branch, out_full.T, preferred_element_type=jnp.float32)
    grad_normed_out = grad_normed_out.reshape(tok_count, head_count, HDIM).transpose(1, 0, 2)
    out_gain_part = jnp.sum(grad_normed_out * unit_out, axis=(0, 1))
    grad_unit_out = grad_normed_out * out_gain
    grad_mixer = stat_out * (
        grad_unit_out - unit_out * jnp.mean(grad_unit_out * unit_out, axis=-1, keepdims=True)
    )
    local_grad = jnp.einsum("htp,htv->hpv", q_prop, grad_mixer, precision=PRECISE)
    grad_q_prop = jnp.einsum("htv,hpv->htp", grad_mixer, state_in, precision=PRECISE)
    all_grads = lax.all_gather(
        local_grad[None].astype(jnp.bfloat16), "seq", axis=0, tiled=True
    ).astype(jnp.float32)

    def fold_backward(counter, later_grad):
        source = seq_count - 1 - counter
        moved = (
            jnp.einsum("hqp,hqv->hpv", all_maps[source], later_grad, precision=PRECISE)
            + all_grads[source]
        )
        return jnp.where(source > own_index, moved, later_grad)

    grad_end = lax.fori_loop(0, seq_count, fold_backward, empty_state)
    grad_map = jnp.einsum("hpv,hqv->hpq", grad_end, state_in, precision=PRECISE)
    grad_queries, grad_keys, grad_values, grad_strength = span_pullback(
        (grad_mixer, grad_q_prop, grad_map, grad_end)
    )
    grad_logits = (grad_strength * real_mask[None, :] * beta_sig * (1.0 - beta_sig)).astype(
        jnp.bfloat16
    )
    grad_beta_part = jnp.einsum(
        "ht,td->hd", grad_logits, normed, preferred_element_type=jnp.float32
    )
    grad_q_unit = grad_queries * HDIM ** (-0.5)
    grad_q_raw = q_scale * (
        grad_q_unit - q_unit * jnp.sum(grad_q_unit * q_unit, axis=-1, keepdims=True)
    )
    grad_k_raw = k_scale * (
        grad_keys - keys_in * jnp.sum(grad_keys * keys_in, axis=-1, keepdims=True)
    )
    grad_act = (
        jnp.stack([grad_q_raw, grad_k_raw, grad_values])
        .transpose(0, 2, 1, 3)
        .reshape(3, tok_count, -1)
    )
    grad_conv_sum = grad_act * conv_sig * (1.0 + conv_sum * (1.0 - conv_sig))
    rims_back = passed_along(grad_conv_sum[:, : KERNEL - 1, :], "seq", -1)
    grad_ext = jnp.concatenate([grad_conv_sum, rims_back], axis=1)
    grad_raw = jnp.zeros(grad_conv_sum.shape, jnp.float32)
    conv_terms = []
    for shift_no in range(KERNEL):
        grad_raw = (
            grad_raw
            + conv_weight[:, shift_no][:, None, :]
            * grad_ext[:, shift_no : shift_no + tok_count]
            * taps[shift_no][shift_no : shift_no + tok_count][None, :, None]
        )
        window = extended[:, KERNEL - 1 - shift_no : KERNEL - 1 - shift_no + tok_count]
        conv_terms.append(
            jnp.sum(grad_conv_sum * window * taps[shift_no][:tok_count][None, :, None], axis=1)
        )
    grad_conv_part = jnp.stack(conv_terms, axis=1)
    grad_raw_low = grad_raw.astype(jnp.bfloat16)
    grad_qkv_part = jnp.einsum(
        "td,stc->sdc", normed, grad_raw_low, preferred_element_type=jnp.float32
    )
    grad_normed = jnp.einsum(
        "stc,sdc->td", grad_raw_low, qkv_full, preferred_element_type=jnp.float32
    )
    grad_normed = grad_normed + jnp.einsum(
        "ht,hd->td", grad_logits, beta_full, preferred_element_type=jnp.float32
    )
    grad_normed, out_gain_sum = (
        lax.psum(grad_normed.astype(jnp.bfloat16), "mp").astype(jnp.float32),
        lax.psum(out_gain_part.astype(jnp.bfloat16), "mp").astype(jnp.float32),
    )
    attn_gain_part = jnp.sum(grad_normed * unit_in, axis=0)
    grad_unit_in = grad_normed * attn_gain
    grad_input = grad_hidden + stat_in * (
        grad_unit_in - unit_in * jnp.mean(grad_unit_in * unit_in, axis=-1, keepdims=True)
    )
    weight_sums = (
        lax.psum_scatter(grad_qkv_part, ("seq", "row"), scatter_dimension=1, tiled=True),
        lax.psum_scatter(grad_beta_part, ("seq", "row"), scatter_dimension=1, tiled=True),
        lax.psum_scatter(grad_out_part, ("seq", "row"), scatter_dimension=1, tiled=True),
        lax.psum_scatter(grad_gateup_part, ("seq", "row"), scatter_dimension=1, tiled=True),
        lax.psum_scatter(grad_down_part, ("seq", "row"), scatter_dimension=1, tiled=True),
    )
    small_sums = lax.psum(
        (attn_gain_part, grad_conv_part, out_gain_sum, ffn_gain_part), ("seq", "row")
    )
    return (
        block_out.astype(jnp.bfloat16)[None],
        grad_input[None],
        small_sums[0],
        weight_sums[0],
        small_sums[1],
        weight_sums[1],
        small_sums[2],
        weight_sums[2],
        small_sums[3],
        weight_sums[3],
        weight_sums[4],
    )


MESH = pl.DeviceIdType.MESH
STRIP = 16
TILE = 512
WIDE = 256


def phase_kernel(middle, both_cores, small_sum, meanwhile, n_in, n_out, part_ref, *refs):
    inputs, all_ref = refs[:n_in], refs[n_in]
    outs, scratch = refs[n_in + 1 : n_in + n_out], refs[n_in + n_out :]
    got, sums, gain_sum, send_sem, recv_sem = scratch[:5]
    count = all_ref.shape[0]
    rows = count // 8
    place, core, row = lax.axis_index("mp"), lax.axis_index("seq"), lax.axis_index("row")
    across_x = place + 1 - 2 * (place % 2)
    across_y = (place + 2) % 4
    across_both = 3 - place
    ways = {"x": {"mp": across_x}, "y": {"mp": across_y}}
    if both_cores or small_sum:
        ways["core"] = {"seq": 1 - core}
    steps = []
    if small_sum:
        bit = 1
        while bit < lax.axis_size("row"):
            steps.append(f"row{bit}")
            ways[steps[-1]] = {"row": row + bit - 2 * bit * ((row // bit) % 2)}
            bit *= 2
        steps += ["core", "x", "y"]
    barrier = pltpu.get_barrier_semaphore()
    for other in ways.values():
        pl.semaphore_signal(barrier, inc=1, device_id=other, device_id_type=MESH)
    pl.semaphore_wait(barrier, len(ways))

    def copy(index, source, target, way):
        return pltpu.make_async_remote_copy(
            src_ref=source,
            dst_ref=target,
            send_sem=send_sem.at[index],
            recv_sem=recv_sem.at[index],
            device_id=ways[way],
            device_id_type=MESH,
        )

    def block(of, half):
        return pl.ds(pl.multiple_of((2 * of + half) * rows, rows), rows)

    def strips(body):
        @pl.loop(0, rows // STRIP)
        def _(i):
            body(pl.multiple_of(i * STRIP, STRIP))

    part, relayed, copies = part_ref, [], send_sem.shape[0]
    if meanwhile:
        fetch = pltpu.make_async_copy(inputs[3].at[3], scratch[-3], scratch[-2])
        fetch.start()
    if both_cores:
        part, outgoing, incoming, weight, weight_sem = scratch[5:10]
        mixer, beta = inputs[3:5]
        width = (weight.shape[0] - beta.shape[0]) // 3
        fetches = [
            pltpu.make_async_copy(
                mixer.at[s, pl.ds(pl.multiple_of(core * width, width), width)],
                weight.at[pl.ds(s * width, width)],
                weight_sem.at[s],
            )
            for s in range(3)
        ]
        for step in fetches:
            step.start()
        weight[3 * width :, :] = beta[...]
        order = [across_both, across_x, across_y, place]
        passed_ref, far_ref = inputs[n_in - small_sum["dummies"] - 1], outs[-2]
        relayed = [
            copy(
                copies - 2,
                passed_ref.at[block(across_x, 0)],
                far_ref.at[pl.ds(0, rows)],
                "y",
            ),
            copy(
                copies - 1,
                passed_ref.at[block(across_y, 1)],
                far_ref.at[pl.ds(rows, rows)],
                "x",
            ),
        ]
        for step in relayed:
            step.start()

        def product(whose, of, target):
            start = pl.multiple_of(whose * count + 2 * of * rows, rows)
            left = part_ref[pl.ds(start, 2 * rows), :]
            lines = pl.ds(pl.multiple_of(2 * of * rows, rows), 2 * rows)

            @pl.loop(0, weight.shape[1] // TILE)
            def _(i):
                tile = pl.ds(pl.multiple_of(i * TILE, TILE), TILE)
                target[lines, tile] = jnp.dot(
                    left, weight[:, tile], preferred_element_type=F32
                ).astype(BF16)

            return lines

        shared = []
        for number in range(4):
            lines = pl.ds(pl.multiple_of(2 * order[number] * rows, rows), 2 * rows)
            shared.append(copy(12 + number, outgoing.at[lines], incoming.at[lines], "core"))

        for step in fetches:
            step.wait()

        def give(number):
            product(1 - core, order[number], outgoing)
            shared[number].start()

        def take(number):
            of = order[number]
            product(core, of, part)
            shared[number].wait_recv()

            @pl.loop(0, 2 * rows // STRIP)
            def _(i):
                strip = pl.ds(pl.multiple_of(2 * of * rows + i * STRIP, STRIP), STRIP)
                part[strip, :] = (
                    part[strip, :].astype(F32) + incoming[strip, :].astype(F32)
                ).astype(BF16)

    far = [
        copy(0, part.at[block(across_both, 0)], got.at[0], "x"),
        copy(1, part.at[block(across_both, 1)], got.at[1], "y"),
    ]
    near = [
        copy(2, part.at[block(across_x, 0)], got.at[2], "x"),
        copy(3, part.at[block(across_y, 1)], got.at[3], "y"),
    ]
    last = [copy(4, sums.at[0], got.at[4], "y"), copy(5, sums.at[1], got.at[5], "x")]
    own = [all_ref.at[block(place, 0)], all_ref.at[block(place, 1)]]
    passed = [all_ref.at[block(across_x, 0)], all_ref.at[block(across_y, 1)]]
    out_first = [copy(6, own[0], own[0], "x"), copy(7, own[1], own[1], "y")]
    out_second = [copy(8, own[0], own[0], "y"), copy(9, own[1], own[1], "x")]
    out_third = [copy(10, passed[0], passed[0], "y"), copy(11, passed[1], passed[1], "x")]

    if both_cores:
        give(0)
        give(1)
        take(0)
    for step in far:
        step.start()
    if both_cores:
        give(2)
        take(1)
        near[0].start()
        take(2)
        near[1].start()
        give(3)
        take(3)
    else:
        for step in near:
            step.start()
    gain_sum[...] = jnp.zeros_like(gain_sum)
    for half, onward in ((0, across_y), (1, across_x)):
        far[half].wait_recv()

        def add(at):
            strip = pl.ds(at, STRIP)
            mine = part[pl.ds((2 * onward + half) * rows + at, STRIP), :]
            sums[half, strip, :] = (mine.astype(F32) + got[half, strip, :].astype(F32)).astype(BF16)

        strips(add)
        last[half].start()
    for half in (0, 1):
        near[half].wait_recv()
        last[half].wait_recv()

        def finish(at):
            strip = pl.ds(at, STRIP)
            total = part[pl.ds((2 * place + half) * rows + at, STRIP), :].astype(F32)
            total = total + got[2 + half, strip, :].astype(F32)
            total = total + got[4 + half, strip, :].astype(F32)
            result = middle(total, half, strip, inputs, outs, gain_sum)
            all_ref[pl.ds((2 * place + half) * rows + at, STRIP), :] = result.astype(BF16)

        strips(finish)
        out_first[half].start()
        out_second[half].start()

    def use(of, first=False, last=False):
        if not meanwhile:
            return
        weight, left = scratch[-3], inputs[4]
        grad_left, products = outs[2], scratch[-1]
        lines = pl.ds(pl.multiple_of(2 * of * rows, rows), 2 * rows)
        grad_left[lines, :] = lax.dot_general(
            all_ref[lines, :], weight[...], NT, preferred_element_type=F32
        ).astype(BF16)

        @pl.loop(0, products.shape[1] // TILE)
        def _(i):
            tile = pl.ds(pl.multiple_of(i * TILE, TILE), TILE)
            more = lax.dot_general(
                left[lines, :], all_ref[lines, tile], TN, preferred_element_type=F32
            )
            if first:
                products[:, tile] = more
            elif last:
                outs[3][:, tile] = (products[:, tile] + more).astype(BF16)
            else:
                products[:, tile] = products[:, tile] + more

    if meanwhile:
        fetch.wait()
    use(place, first=True)
    gain = jnp.sum(gain_sum[...], axis=0, keepdims=True)
    small = []
    if small_sum:
        values, arrived = outs[-1], scratch[-1]
        first = n_in - small_sum["dummies"] - 4
        ffn_gain, out_gain, conv = inputs[first : first + 3]
        taps, width = conv.shape
        middle_lane = values.shape[1] // 2
        values[...] = jnp.zeros_like(values)
        values[0:1, :] = gain
        values[1:2, :] = ffn_gain[...]
        values[2:3, 0 : out_gain.shape[1]] = out_gain[...]
        for i in (0, 1):
            share = jnp.where(core == i, 1.0, 0.0)
            lane = i * middle_lane
            values[8 : 8 + taps, lane : lane + width] = conv[...] * share
    elif n_out > 2:
        outs[1][...] = gain

    def small_step(number):
        height = 8 if steps[number] in ("x", "y") else values.shape[0]
        step = copy(
            16 + number,
            arrived.at[number, 1, pl.ds(0, height)],
            arrived.at[number, 0, pl.ds(0, height)],
            steps[number],
        )
        arrived[number, 1, 0:height, :] = values[0:height, :]
        step.start()
        step.wait_recv()
        values[0:height, :] = values[0:height, :] + arrived[number, 0, 0:height, :]
        small.append(step)

    for half in (0, 1):
        out_first[half].wait_recv()
        out_third[half].start()
    if small_sum:
        for number in range(len(steps)):
            small_step(number)
    for step in out_second:
        step.wait_recv()
    use(across_x)
    use(across_y)
    for step in out_third:
        step.wait_recv()
    use(across_both, last=True)
    for step in relayed:
        step.wait_recv()
    for step in (*relayed, *far, *near, *last, *out_first, *out_second, *out_third, *small):
        step.wait_send()
    if both_cores:
        for step in shared:
            step.wait_send()


def normed_forward(total, half, strip, inputs, outs, gain_sum):
    residual, gain = inputs[:2]
    hidden = residual[half, strip, :].astype(F32) + total
    outs[0][half, strip, :] = hidden
    stat = lax.rsqrt(jnp.mean(hidden * hidden, axis=1, keepdims=True) + EPSILON)
    return hidden * stat * gain[...]


def normed_backward(keep, total, half, strip, inputs, outs, gain_sum):
    value, base, gain = inputs[:3]
    value = value[half, strip, :].astype(F32)
    stat = lax.rsqrt(jnp.mean(value * value, axis=1, keepdims=True) + EPSILON)
    unit = value * stat
    gain_sum[...] += jnp.sum((total * unit).reshape(2, 8, -1), axis=0)
    scaled = total * gain[...]
    grad = base[half, strip, :].astype(F32) + stat * (
        scaled - unit * jnp.mean(scaled * unit, axis=1, keepdims=True)
    )
    if keep:
        outs[0][half, strip, :] = grad
    return grad


def mp_phase(
    number,
    middle,
    part,
    inputs,
    dummies,
    outs,
    both_cores=False,
    small=None,
    passed=None,
    meanwhile=False,
):
    here, there = pl.BlockSpec(memory_space=pltpu.VMEM), pl.BlockSpec(memory_space=pl.ANY)
    count, model = part.shape
    if both_cores:
        count, depth, model = count // 2, model, inputs[3].shape[2]
    block = (count // 8, model)
    copies, scratch, small_sum = 12, [], None
    if both_cores:
        scratch += [pltpu.VMEM((count, model), BF16)] * 3
        scratch += [pltpu.VMEM((depth, model), BF16), pltpu.SemaphoreType.DMA((3,))]
    if small is not None:
        stages = lax.axis_size("row").bit_length() - 1 + 3
        copies = 16 + stages + 2
        height = 8 + small[2].shape[0]
        shape = (height + -height % 8, model)
        scratch += [pltpu.VMEM((stages, 2, *shape), F32)]
        small_sum = {"dummies": len(dummies)}
        inputs = [*inputs, *small, passed]
        outs = [
            *outs,
            jax.ShapeDtypeStruct((2 * block[0], model), BF16),
            jax.ShapeDtypeStruct(shape, F32),
        ]
    specs = [here] * len(inputs)
    if small is not None:
        specs[3] = specs[-1] = there
    if meanwhile:
        _, width, depth = inputs[3].shape
        specs[3] = there
        scratch += [
            pltpu.VMEM((width, depth), BF16),
            pltpu.SemaphoreType.DMA(()),
            pltpu.VMEM((width, model), F32),
        ]
    kernel = functools.partial(
        phase_kernel,
        middle,
        both_cores,
        small_sum,
        meanwhile,
        len(inputs) + len(dummies),
        1 + len(outs),
    )
    return pl.pallas_call(
        kernel,
        in_specs=[here, *specs] + [there] * len(dummies),
        out_specs=[here] * (1 + len(outs)),
        out_shape=[jax.ShapeDtypeStruct((count, model), BF16), *outs],
        scratch_shapes=[
            pltpu.VMEM((6, *block), BF16),
            pltpu.VMEM((2, *block), BF16),
            pltpu.VMEM((8, model), F32),
            pltpu.SemaphoreType.DMA((copies,)),
            pltpu.SemaphoreType.DMA((copies,)),
            *scratch,
        ],
        compiler_params=pltpu.CompilerParams(
            collective_id=number, has_side_effects=True, vmem_limit_bytes=50 << 20
        ),
        cost_estimate=pl.CostEstimate(flops=0, bytes_accessed=250 << 20, transcendentals=0),
    )(part, *inputs, *dummies)


def pair_kernel(product_ref, weight, hidden, left_own, left_other, gate, up, *refs):
    block_ref, gate_pair, up_pair, part_ref, got, sums, gate_in, up_in, send_sem, recv_sem = refs[-10:]
    rows = part_ref.shape[0] // 8
    place, core = lax.axis_index("mp"), lax.axis_index("seq")
    across_x = place + 1 - 2 * (place % 2)
    across_y = (place + 2) % 4
    across_both = 3 - place
    ways = {"x": {"mp": across_x}, "y": {"mp": across_y}, "core": {"seq": 1 - core}}
    barrier = pltpu.get_barrier_semaphore()
    for other in ways.values():
        pl.semaphore_signal(barrier, inc=1, device_id=other, device_id_type=MESH)
    pl.semaphore_wait(barrier, len(ways))

    def copy(index, source, target, way):
        return pltpu.make_async_remote_copy(
            src_ref=source,
            dst_ref=target,
            send_sem=send_sem.at[index],
            recv_sem=recv_sem.at[index],
            device_id=ways[way],
            device_id_type=MESH,
        )

    def block(of, half):
        return pl.ds(pl.multiple_of((2 * of + half) * rows, rows), rows)

    def strips(body):
        @pl.loop(0, rows // STRIP)
        def _(i):
            body(pl.multiple_of(i * STRIP, STRIP))

    far = [
        copy(0, part_ref.at[block(across_both, 0)], got.at[0], "x"),
        copy(1, part_ref.at[block(across_both, 1)], got.at[1], "y"),
    ]
    near = [
        copy(2, part_ref.at[block(across_x, 0)], got.at[2], "x"),
        copy(3, part_ref.at[block(across_y, 1)], got.at[3], "y"),
    ]
    last = [copy(4, sums.at[0], got.at[4], "y"), copy(5, sums.at[1], got.at[5], "x")]
    shared = [copy(6, gate, gate_in, "core"), copy(7, up, up_in, "core")]

    def produce(of):
        lines = pl.ds(pl.multiple_of(2 * of * rows, rows), 2 * rows)

        @pl.loop(0, weight.shape[1] // TILE)
        def _(i):
            tile = pl.ds(pl.multiple_of(i * TILE, TILE), TILE)
            part_ref[lines, tile] = jnp.dot(
                product_ref[lines, :], weight[:, tile], preferred_element_type=F32
            ).astype(BF16)

    for step in shared:
        step.start()
    produce(across_both)
    for step in far:
        step.start()
    produce(across_x)
    near[0].start()
    produce(across_y)
    near[1].start()
    produce(place)

    def products(own, other, target, first, count):
        @pl.loop(first, first + count)
        def _(i):
            tile = pl.ds(pl.multiple_of(i * WIDE, WIDE), WIDE)
            total = lax.dot_general(
                left_own[:, tile], own[...], TN, preferred_element_type=F32
            ) + lax.dot_general(left_other[:, tile], other[...], TN, preferred_element_type=F32)
            target[tile, :] = total.astype(BF16)

    tiles = left_own.shape[1] // WIDE
    shared[0].wait_recv()
    products(gate, gate_in, gate_pair, 0, tiles)
    for half, onward in ((0, across_y), (1, across_x)):
        far[half].wait_recv()

        def add(at):
            strip = pl.ds(at, STRIP)
            mine = part_ref[pl.ds((2 * onward + half) * rows + at, STRIP), :]
            sums[half, strip, :] = (mine.astype(F32) + got[half, strip, :].astype(F32)).astype(BF16)

        strips(add)
        last[half].start()
    shared[1].wait_recv()
    products(up, up_in, up_pair, 0, tiles)
    for half in (0, 1):
        near[half].wait_recv()
        last[half].wait_recv()

        def finish(at):
            strip = pl.ds(at, STRIP)
            total = part_ref[pl.ds((2 * place + half) * rows + at, STRIP), :].astype(F32)
            total = total + got[2 + half, strip, :].astype(F32)
            total = total + got[4 + half, strip, :].astype(F32)
            block_ref[pl.ds(half * rows + at, STRIP), :] = (hidden[half, strip, :] + total).astype(BF16)

        strips(finish)
    for step in (*shared, *far, *near, *last):
        step.wait_send()


def scattered_and_pairs(number, product, weight, hidden, left, gate, up, dummies):
    here, there = pl.BlockSpec(memory_space=pltpu.VMEM), pl.BlockSpec(memory_space=pl.ANY)
    count, model = product.shape[0], weight.shape[1]
    block = (count // 8, model)
    pair = jax.ShapeDtypeStruct((left[0].shape[1], gate.shape[1]), BF16)
    return pl.pallas_call(
        pair_kernel,
        in_specs=[here] * 7 + [there] * len(dummies),
        out_specs=[here] * 3,
        out_shape=[jax.ShapeDtypeStruct((2 * block[0], model), BF16), pair, pair],
        scratch_shapes=[
            pltpu.VMEM((count, model), BF16),
            pltpu.VMEM((6, *block), BF16),
            pltpu.VMEM((2, *block), BF16),
            pltpu.VMEM(gate.shape, BF16),
            pltpu.VMEM(up.shape, BF16),
            pltpu.SemaphoreType.DMA((8,)),
            pltpu.SemaphoreType.DMA((8,)),
        ],
        compiler_params=pltpu.CompilerParams(
            collective_id=number, has_side_effects=True, vmem_limit_bytes=54 << 20
        ),
        cost_estimate=pl.CostEstimate(flops=0, bytes_accessed=130 << 20, transcendentals=0),
    )(product, weight, hidden, *left, gate, up, *dummies)


def swapped(block):
    return lax.ppermute(block, "seq", [(0, 1), (1, 0)])


def in_order(mine, other, core, axis):
    first = jnp.where(core == 0, mine, other)
    second = jnp.where(core == 0, other, mine)
    return jnp.concatenate([first, second], axis=axis)


def after(block, *done):
    nothing = sum(part[(0,) * part.ndim].astype(F32) for part in done) * 0.0
    return block + nothing.astype(block.dtype)


def halves(block, core, axis):
    size = block.shape[axis] // 2
    pick = lambda i: lax.dynamic_slice_in_dim(block, i * size, size, axis=axis)
    return pick(core), pick(1 - core)


def both_tokens(left, right, *done):
    product = lambda a, b: lax.dot_general(
        a, b, (((0,), (0,)), ((), ())), preferred_element_type=F32
    )
    total = product(left[0], right[0]) + product(left[1], right[1])
    return (after(total, *done) if done else total).astype(BF16)


def own_columns(block, core):
    mine, other = halves(block, core, 1)
    return mine, swapped(other)


def over_row(pair, axis):
    return lax.psum_scatter(pair, "row", scatter_dimension=axis, tiled=True)


def joined_shards(
    block_in,
    doc_lengths,
    attn_gain,
    qkv_weight,
    conv_weight,
    beta_weight,
    out_gain,
    out_weight,
    ffn_gain,
    gateup_weight,
    down_weight,
    cotangent,
):
    tok_count, model = block_in.shape[1:]
    core, own = lax.axis_index("seq"), lax.axis_index("mp")
    width = conv_weight.shape[2] // 2
    own_heads = width // HDIM
    quarter = tok_count // 4

    gather = lambda weight: lax.all_gather(weight, ("seq", "row"), axis=1, tiled=True)
    mixer_full = gather(jnp.concatenate([qkv_weight, out_weight.T[None]]))
    qkv_full, out_full = mixer_full[:3], mixer_full[3]
    mixer_rows = mixer_full.transpose(0, 2, 1)
    beta_full, gateup_full, down_full = (
        gather(beta_weight),
        gather(gateup_weight),
        gather(down_weight),
    )
    qkv_own = lax.dynamic_slice_in_dim(qkv_full, core * width, width, axis=2)
    beta_own = lax.dynamic_slice_in_dim(beta_full, core * own_heads, own_heads, axis=0)
    beta_rows = jnp.pad(beta_own, ((0, HDIM - own_heads), (0, 0)))
    mix_across = jnp.concatenate([qkv_own[0].T, qkv_own[1].T, qkv_own[2].T, beta_rows])
    conv_own = lax.dynamic_slice_in_dim(conv_weight, core * width, width, axis=2)
    conv_own = conv_own.transpose(1, 0, 2).reshape(KERNEL, 3 * width)

    residual_in = block_in[0].astype(F32)
    stat_in = lax.rsqrt(jnp.mean(residual_in * residual_in, axis=-1, keepdims=True) + EPSILON)
    normed_mine = (residual_in * stat_in * attn_gain).astype(BF16)
    normed = in_order(normed_mine, swapped(normed_mine), core, 0)

    positions = jnp.arange(2 * tok_count, dtype=jnp.int32)
    doc_start, real_row = row_layout(doc_lengths[0], positions)
    keep = jnp.pad((doc_start[::BLOCK] != positions[::BLOCK]).astype(F32), (0, 1))
    count = jnp.sum(real_row.reshape(-1, BLOCK), axis=1).astype(jnp.int32)
    raw = lax.dot_general(
        normed, mix_across, (((1,), (1,)), ((), ())), preferred_element_type=F32
    ).astype(BF16)
    gain = out_gain[None, :]
    group = 4 if raw.shape[0] % (4 * CHUNK) == 0 else 1
    heads_out, *saved = forward(keep, count, raw, conv_own, gain, group)

    mine, other = halves(heads_out, core, 0)
    normed_out = in_order(mine, swapped(other), core, 1)
    branch_part = lax.dot_general(
        normed_out, out_full, (((1,), (1,)), ((), ())), preferred_element_type=F32
    )
    own_rows = lambda block: lax.dynamic_slice_in_dim(
        block[0], own * quarter, quarter, axis=0
    ).reshape(2, -1, model)
    residual_own = own_rows(block_in)
    rows_own = jax.ShapeDtypeStruct(residual_own.shape, F32)
    normed_mid, hidden = mp_phase(
        0,
        normed_forward,
        branch_part.astype(BF16),
        [residual_own, ffn_gain[None, :]],
        [],
        [rows_own],
    )

    grad_top = cotangent[0]
    gate_up = jnp.einsum("td,sdf->stf", normed_mid, gateup_full, preferred_element_type=F32)
    gate_sig = jax.nn.sigmoid(gate_up[0])
    product = (gate_up[0] * gate_sig * gate_up[1]).astype(BF16)
    normed_halves = own_columns(normed_mid, core)
    down_pair = both_tokens(
        (product, swapped(product)), own_columns(grad_top, core), normed_halves[1]
    )
    grad_product = jnp.dot(grad_top, down_full.T, preferred_element_type=F32)
    grad_product = after(grad_product, down_pair)
    grad_gate = grad_product * gate_up[1] * gate_sig * (1.0 + gate_up[0] * (1.0 - gate_sig))
    grad_up = grad_product * gate_up[0] * gate_sig
    grad_gate, grad_up = grad_gate.astype(BF16), grad_up.astype(BF16)
    grad_mid_part = jnp.einsum(
        "stf,sdf->td",
        jnp.stack([grad_gate, grad_up]),
        gateup_full,
        preferred_element_type=F32,
    ).astype(BF16)
    block_out, gate_pair, up_pair = scattered_and_pairs(
        4,
        product,
        down_full,
        hidden,
        normed_halves,
        grad_gate,
        grad_up,
        [down_pair],
    )
    down_sum, gate_sum, up_sum = over_row(down_pair, 1), over_row(gate_pair, 0), over_row(up_pair, 0)
    grad_branch, grad_hidden, ffn_gain_part, grad_normed_out, grad_out_part = mp_phase(
        1,
        partial(normed_backward, True),
        grad_mid_part,
        [hidden, own_rows(cotangent), ffn_gain[None, :], mixer_rows, normed_out],
        [block_out, down_sum, gate_pair, up_pair],
        [
            rows_own,
            jax.ShapeDtypeStruct((1, model), F32),
            jax.ShapeDtypeStruct(normed_out.shape, BF16),
            jax.ShapeDtypeStruct((normed_out.shape[1], model), BF16),
        ],
        meanwhile=True,
    )
    mine, other = halves(grad_normed_out, core, 1)
    grad_heads = in_order(mine, swapped(other), core, 0)
    mine, other = halves(grad_out_part, core, 1)
    out_pair = after(mine.astype(F32) + swapped(other).astype(F32), up_sum).astype(BF16)
    grad_raw, grad_conv_own, out_gain_part, block_out = backward(
        keep,
        count,
        raw,
        conv_own,
        gain,
        grad_heads,
        *saved,
        group,
        block_out,
        [gate_sum],
    )
    normed_mine, normed_other = halves(normed, core, 1)
    by_columns = lambda part: lax.dot_general(
        part, grad_raw, (((0,), (0,)), ((), ())), preferred_element_type=F32
    ).astype(BF16)
    qkv_other = swapped(by_columns(normed_other))
    qkv_mine = by_columns(normed_mine)
    grad_input, far_rows, small = mp_phase(
        2,
        partial(normed_backward, False),
        grad_raw,
        [residual_own, grad_hidden, attn_gain[None, :], mixer_rows, beta_rows],
        [up_sum, out_pair, qkv_mine, qkv_other],
        [],
        both_cores=True,
        small=[ffn_gain_part, out_gain_part, grad_conv_own],
        passed=block_out,
    )
    grad_input = grad_input.astype(F32)
    places = jnp.arange(4)[:, None, None]
    block_out = jnp.where(
        places == (own ^ 3),
        far_rows[None],
        block_out.reshape(4, quarter, model),
    ).reshape(tok_count, model)
    grad_attn_gain, grad_ffn_gain = small[0], small[1]
    grad_out_gain = small[2, : out_gain.shape[0]]
    conv_at = 8
    conv_of = lambda i: (
        small[conv_at : conv_at + KERNEL, i * (model // 2) : i * (model // 2) + 3 * width]
        .reshape(KERNEL, 3, width)
        .transpose(1, 0, 2)
    )
    grad_conv = jnp.concatenate([conv_of(0), conv_of(1)], axis=2)
    grad_down, grad_out = down_sum.astype(F32), over_row(out_pair, 1).astype(F32)
    grad_gateup = jnp.stack([gate_sum, up_sum]).astype(F32)
    row_sums = [over_row(part, 0) for part in (qkv_mine, qkv_other)]
    by_kind = lambda part: part[:, : 3 * width].reshape(-1, 3, width).transpose(1, 0, 2)
    grad_qkv = in_order(by_kind(row_sums[0]), by_kind(row_sums[1]), core, 2).astype(F32)
    of_heads = lambda part: part[:, 3 * width : 3 * width + own_heads].T
    grad_beta = in_order(of_heads(row_sums[0]), of_heads(row_sums[1]), core, 0).astype(F32)
    return (
        block_out[None],
        grad_input[None],
        grad_attn_gain,
        grad_qkv,
        grad_conv,
        grad_beta,
        grad_out_gain,
        grad_out,
        grad_ffn_gain,
        grad_gateup,
        grad_down,
    )


def solution(mesh):
    rows = mesh.shape["row"]
    joined = mesh.shape["seq"] == 2 and mesh.shape["mp"] == 4 and rows & (rows - 1) == 0
    return jax.shard_map(
        joined_shards if joined else spread_shards,
        mesh=mesh,
        in_specs=(
            P("row", "seq", None),
            P("row", None),
            P(),
            P(None, ("seq", "row"), "mp"),
            P(None, None, "mp"),
            P("mp", ("seq", "row")),
            P(),
            P("mp", ("seq", "row")),
            P(),
            P(None, ("seq", "row"), "mp"),
            P("mp", ("seq", "row")),
            P("row", "seq", None),
        ),
        out_specs=(
            P("row", "seq", None),
            P("row", "seq", None),
            P(),
            P(None, ("seq", "row"), "mp"),
            P(None, None, "mp"),
            P("mp", ("seq", "row")),
            P(),
            P("mp", ("seq", "row")),
            P(),
            P(None, ("seq", "row"), "mp"),
            P("mp", ("seq", "row")),
        ),
        check_vma=False,
    )
```

```python
import functools
from functools import partial

import jax
import jax.numpy as jnp
from jax import lax
from jax.experimental import pallas as pl
from jax.experimental.pallas import tpu as pltpu
from jax.sharding import PartitionSpec as P

HDIM = 128
KERNEL = 4
BLOCK = 64
CHUNK = 128
EPSILON = 1e-06
PRECISE = lax.Precision.HIGHEST
F32 = jnp.float32
BF16 = jnp.bfloat16

NT=(((1,),(1,)),((),())); NN=(((1,),(0,)),((),())); TN=(((0,),(0,)),((),()))

def mm(a,b,dims=NN):
    return lax.dot_general(a.astype(BF16), b.astype(BF16), dims, preferred_element_type=F32)

def iotas():
    return lax.broadcasted_iota(jnp.int32,(CHUNK,CHUNK),0), lax.broadcasted_iota(jnp.int32,(CHUNK,CHUNK),1)

def inverses(below):
    r,c=iotas()
    done=[jnp.where(r==c,1.0,0.0)-jnp.where(r//2==c//2,a,0.0) for a in below]
    size=2
    while size<CHUNK:
        pairs=(r//(2*size)==c//(2*size))&(r//size!=c//size)
        half=[mm(jnp.where(pairs,a,0.0),t) for a,t in zip(below,done)]
        done=[t-mm(t,x) for t,x in zip(done,half)]
        size*=2
    return done

def conv_act(ext_ref, base, lanes, cw, taps):
    total=cw[0:1]*ext_ref[pl.ds(base+8,CHUNK),lanes]
    for j in range(1,KERNEL):
        total=total+(cw[j:j+1]*taps[j-1])*ext_ref[pl.ds(base+8-j,CHUNK),lanes]
    sig=jax.nn.sigmoid(total)
    return total,sig

def layout(keep_ref, count_ref, block):
    r,_=iotas()
    inside=r%BLOCK
    first=r<BLOCK
    keep0,keep1,after=keep_ref[block],keep_ref[block+1],keep_ref[block+2]
    here=jnp.where(first,keep0,keep1)
    later=jnp.where(first,keep1,after)
    taps=[jnp.where(inside<j,here,1.0) for j in range(1,KERNEL)]
    taps_later=[jnp.where(inside>=BLOCK-j,later,1.0) for j in range(1,KERNEL)]
    real=jnp.where(inside<jnp.where(first,count_ref[block],count_ref[block+1]),1.0,0.0)
    return taps,taps_later,jnp.where(first,1.0,keep1),jnp.where(first,keep1,1.0),real,keep0,keep1

def fwd_kernel(heads, group, keep_ref, count_ref, raw_ref, cw_ref, gain_ref, normed_ref, o_ref, st_ref, wr_ref, ext, state):
    rows=group*CHUNK
    step=pl.program_id(0)
    @pl.when(step==0)
    def _():
        ext[0:8,:]=jnp.zeros((8,3*heads*HDIM),F32)
        state[...]=jnp.zeros(state.shape,F32)
    @pl.when(step>0)
    def _():
        ext[0:8,:]=ext[rows:rows+8,:]
    ext[8:,:]=raw_ref[:,0:3*heads*HDIM].astype(F32)
    r,c=iotas()
    width=heads*HDIM
    units=[]
    below=[]
    for g in range(group):
        base=g*CHUNK
        taps,_,m,m2,real,keep0,keep1=layout(keep_ref,count_ref,2*(step*group+g))
        sig_b=jax.nn.sigmoid(raw_ref[pl.ds(base,CHUNK),pl.ds(3*width,HDIM)].astype(F32))*real
        for h in range(heads):
            act=[]
            for s in range(3):
                lanes=pl.ds(s*width+h*HDIM,HDIM)
                total,sig=conv_act(ext,base,lanes,cw_ref[:,lanes],taps)
                act.append(total*sig)
            q=act[0]*(lax.rsqrt(jnp.sum(act[0]*act[0],axis=1,keepdims=True)+EPSILON)*HDIM**-0.5)
            k=act[1]*lax.rsqrt(jnp.sum(act[1]*act[1],axis=1,keepdims=True)+EPSILON)
            v=act[2]
            b=sig_b[:,h:h+1]
            gram=mm(k,k,NT)
            score=mm(q,k,NT)
            mask=jnp.where(c<BLOCK,m,1.0)
            a=jnp.where(r>c,b*gram*mask,0.0)
            l=jnp.where(r>=c,score*mask,0.0)
            below.append(a)
            units.append((g,h,q*m,k*m2,l,b*k,b*v,m,keep0,keep1))
    done=inverses(below)
    wus=[(mm(t,u[5])*u[7],mm(t,u[6])) for t,u in zip(done,units)]
    for t,(w,u),(g,h,q,k,l,_,_,_,keep0,keep1) in zip(done,wus,units):
        base=g*CHUNK
        out=(pl.ds(base,CHUNK),pl.ds(h*HDIM,HDIM))
        st_ref[g,h,1]=t.astype(BF16)
        wr_ref[out]=w.astype(BF16)
        s=state[h]*keep0
        st_ref[g,h,0]=s.astype(BF16)
        rr=u-mm(w,s)
        o=mm(q,s)+mm(l,rr)
        state[h]=s*keep1+mm(k,rr,TN)
        wr_ref[pl.ds(base,CHUNK),pl.ds(width+h*HDIM,HDIM)]=rr.astype(BF16)
        o_ref[out]=o
        stat=lax.rsqrt(jnp.mean(o*o,axis=1,keepdims=True)+EPSILON)
        normed_ref[out]=(o*stat*gain_ref[...]).astype(BF16)

def forward(keep, count, raw, cw, gain, group):
    n=raw.shape[0]; width=cw.shape[1]//3; heads=width//HDIM; rows=group*CHUNK
    nc=n//CHUNK
    row=lambda w: pl.BlockSpec((rows,w),lambda i:(i,0))
    mat=pl.BlockSpec((group,heads,2,HDIM,HDIM),lambda i:(i,0,0,0,0))
    full=lambda a: pl.BlockSpec(a.shape,lambda i:(0,0))
    return pl.pallas_call(functools.partial(fwd_kernel,heads,group),
        grid=(n//rows,),
        in_specs=[pl.BlockSpec(memory_space=pltpu.SMEM)]*2+[row(raw.shape[1]),full(cw),full(gain)],
        out_specs=[row(width),row(width),mat,row(2*width)],
        out_shape=[jax.ShapeDtypeStruct((n,width),BF16),jax.ShapeDtypeStruct((n,width),F32),
            jax.ShapeDtypeStruct((nc,heads,2,HDIM,HDIM),BF16),jax.ShapeDtypeStruct((n,2*width),BF16)],
        scratch_shapes=[pltpu.VMEM((rows+8,3*width),F32),pltpu.VMEM((heads,HDIM,HDIM),F32)],
        compiler_params=pltpu.CompilerParams(vmem_limit_bytes=24<<20),
        cost_estimate=pl.CostEstimate(flops=0,bytes_accessed=120<<20,transcendentals=0),
    )(keep,count,raw,cw,gain)

def bwd_kernel(heads, group, keep_ref, count_ref, raw_ref, prev_ref, cw_ref, gain_ref, gno_ref, o_ref, st_ref, wr_ref, *rest):
    block_ref=rest[0]
    graw_ref, gcw_ref, ggain_ref, all_ref, ext, gext, grad_state, local_sem, send_sem, recv_sem = rest[-10:]
    rows=group*CHUNK
    step=pl.program_id(0); steps=pl.num_programs(0)
    width=heads*HDIM
    @pl.when(step==0)
    def _():
        gext[rows:rows+8,:]=jnp.zeros((8,3*heads*HDIM),F32)
        grad_state[...]=jnp.zeros(grad_state.shape,F32)
        gcw_ref[...]=jnp.zeros(gcw_ref.shape,F32)
        ggain_ref[...]=jnp.zeros(ggain_ref.shape,F32)
    @pl.when(step>0)
    def _():
        gext[rows:rows+8,:]=gext[0:8,:]
    first=jnp.where(step==steps-1,0.0,1.0)
    place=lax.axis_index("mp")
    across_x=place+1-2*(place%2)
    across_y=(place+2)%4
    part=block_ref.shape[0]//2
    at=lambda of,half: all_ref.at[pl.ds(pl.multiple_of((2*of+half)*part,part),part)]
    def copy(index,source,target,other):
        return pltpu.make_async_remote_copy(src_ref=source,dst_ref=target,send_sem=send_sem.at[index],recv_sem=recv_sem.at[index],
            device_id={"mp":other},device_id_type=pl.DeviceIdType.MESH)
    top,low=block_ref.at[pl.ds(0,part)],block_ref.at[pl.ds(part,part)]
    keep_own=pltpu.make_async_copy(block_ref,all_ref.at[pl.ds(pl.multiple_of(2*place*part,2*part),2*part)],local_sem)
    sends=[copy(0,top,at(place,0),across_x),copy(1,low,at(place,1),across_y),copy(2,top,at(place,0),across_y),copy(3,low,at(place,1),across_x)]
    @pl.when(step==0)
    def _():
        barrier=pltpu.get_barrier_semaphore()
        for other in (across_x,across_y):
            pl.semaphore_signal(barrier,inc=1,device_id={"mp":other},device_id_type=pl.DeviceIdType.MESH)
        pl.semaphore_wait(barrier,2)
        keep_own.start()
        for send in sends: send.start()
    ext[0:8,:]=prev_ref[:,0:3*width].astype(F32)[8:16]*first
    ext[8:,:]=raw_ref[:,0:3*heads*HDIM].astype(F32)
    r,c=iotas()
    units=[]
    for g in range(group-1,-1,-1):
        base=g*CHUNK
        taps,taps_later,m,m2,real,keep0,keep1=layout(keep_ref,count_ref,2*((steps-1-step)*group+g))
        beta=jax.nn.sigmoid(raw_ref[pl.ds(base,CHUNK),pl.ds(3*width,HDIM)].astype(F32))
        sig_b=beta*real
        for h in range(heads):
            out=(pl.ds(base,CHUNK),pl.ds(h*HDIM,HDIM))
            act=[];tot=[];sigs=[]
            for s in range(3):
                lanes=pl.ds(s*width+h*HDIM,HDIM)
                total,sig=conv_act(ext,base,lanes,cw_ref[:,lanes],taps)
                act.append(total*sig);tot.append(total);sigs.append(sig)
            rq=lax.rsqrt(jnp.sum(act[0]*act[0],axis=1,keepdims=True)+EPSILON)
            rk=lax.rsqrt(jnp.sum(act[1]*act[1],axis=1,keepdims=True)+EPSILON)
            qu=act[0]*rq
            o=o_ref[out]
            stat=lax.rsqrt(jnp.mean(o*o,axis=1,keepdims=True)+EPSILON)
            uo=o*stat
            gno=gno_ref[out].astype(F32)
            ggain_ref[...]+=jnp.sum(gno*uo,axis=0,keepdims=True)
            gu=gno*gain_ref[...]
            do=stat*(gu-uo*jnp.mean(gu*uo,axis=1,keepdims=True))
            units.append(dict(g=g,h=h,base=base,out=out,second=(pl.ds(base,CHUNK),pl.ds(width+h*HDIM,HDIM)),taps=taps,m=m,m2=m2,keep0=keep0,keep1=keep1,tot=tot,sigs=sigs,
                rq=rq,rk=rk,qu=qu,q=qu*HDIM**-0.5,k=act[1]*rk,v=act[2],b=sig_b[:,h:h+1],do=do,
                mask=jnp.where(c<BLOCK,m,1.0)))
        for u in units[-heads:]: u.update(taps_later=taps_later,beta=beta,sig_b=sig_b)
    for u in units: u['gram']=mm(u['k'],u['k'],NT)*u['mask']
    for u in units: u['l']=jnp.where(r>=c,mm(u['q'],u['k'],NT)*u['mask'],0.0)
    for u in units: u['dr0']=mm(u['l'],u['do'],TN)
    for u in units: u['ds0']=mm(u['q']*u['m'],u['do'],TN)
    for u in units:
        dsn=grad_state[u['h']]
        u['dsn']=dsn
        u['dr']=u['dr0']+u['m2']*mm(u['k'],dsn)
        ds=u['keep1']*dsn+u['ds0']-mm(wr_ref[u['out']],u['dr'],TN)
        grad_state[u['h']]=u['keep0']*ds
    for u in units: u['df']=mm(st_ref[u['g'],u['h'],1],u['dr'],TN)
    for u in units: u['dl']=jnp.where(r>=c,mm(u['do'],wr_ref[u['second']],NT)*u['mask'],0.0)
    for u in units: u['da']=jnp.where(r>c,-mm(u['df'],wr_ref[u['second']],NT),0.0)
    for u in units:
        u['de']=u['b']*u['df']
        u['e']=u['v']-u['m']*mm(u['k'],st_ref[u['g'],u['h'],0])
        u['gb']=jnp.sum(u['df']*u['e']+u['da']*u['gram'],axis=1,keepdims=True)
        u['dkk']=u['b']*u['da']*u['mask']
    for u in units: u['dq']=u['m']*mm(u['do'],st_ref[u['g'],u['h'],0],NT)+mm(u['dl'],u['k'])
    for u in units:
        u['dk']=(mm(u['dl'],u['q'],TN)+u['m2']*mm(wr_ref[u['second']],u['dsn'],NT)-u['m']*mm(u['de'],st_ref[u['g'],u['h'],0],NT)
            +mm(u['dkk'],u['k'])+mm(u['dkk'],u['k'],TN))
    for u in units:
        gq=u['dq']*HDIM**-0.5
        gq=u['rq']*(gq-u['qu']*jnp.sum(gq*u['qu'],axis=1,keepdims=True))
        gk=u['rk']*(u['dk']-u['k']*jnp.sum(u['dk']*u['k'],axis=1,keepdims=True))
        for i,ga in enumerate((gq,gk,u['de'])):
            lanes=pl.ds(i*width+u['h']*HDIM,HDIM)
            sig,tot=u['sigs'][i],u['tot'][i]
            gc=ga*sig*(1.0+tot*(1.0-sig))
            gext[pl.ds(u['base'],CHUNK),lanes]=gc
            for j in range(KERNEL):
                win=ext[pl.ds(u['base']+8-j,CHUNK),lanes]
                prod=gc*win if j==0 else gc*win*u['taps'][j-1]
                gcw_ref[j:j+1,lanes]+=jnp.sum(prod,axis=0,keepdims=True)
    for at in range(0,len(units),heads):
        glog=jnp.zeros((CHUNK,HDIM),F32)
        for u in units[at:at+heads]:
            glog=jnp.where(c==u['h'],u['gb'],glog)
            for i in range(3):
                lanes=pl.ds(i*width+u['h']*HDIM,HDIM)
                cw=cw_ref[:,lanes]
                total=cw[0:1]*gext[pl.ds(u['base'],CHUNK),lanes]
                for j in range(1,KERNEL):
                    total=total+(cw[j:j+1]*u['taps_later'][j-1])*gext[pl.ds(u['base']+j,CHUNK),lanes]
                graw_ref[pl.ds(u['base'],CHUNK),lanes]=total.astype(BF16)
        graw_ref[pl.ds(u['base'],CHUNK),pl.ds(3*width,HDIM)]=(glog*u['sig_b']*(1.0-u['beta'])).astype(BF16)
    @pl.when(step==steps-1)
    def _():
        keep_own.wait()
        for send in sends: send.wait_recv()
        for send in sends: send.wait_send()

def backward(keep, count, raw, cw, gain, gno, o, st, wr, group, block, dummies=()):
    n=raw.shape[0]; width=cw.shape[1]//3; heads=width//HDIM; rows=group*CHUNK
    steps=n//rows
    row=lambda w: pl.BlockSpec((rows,w),lambda i:(steps-1-i,0))
    mat=pl.BlockSpec((group,heads,2,HDIM,HDIM),lambda i:(steps-1-i,0,0,0,0))
    full=lambda a: pl.BlockSpec(a.shape,lambda i:(0,0))
    prev=pl.BlockSpec((16,raw.shape[1]),lambda i:(jnp.maximum((steps-1-i)*(rows//16)-1,0),0))
    return pl.pallas_call(functools.partial(bwd_kernel,heads,group),
        grid=(steps,),
        in_specs=[pl.BlockSpec(memory_space=pltpu.SMEM)]*2+[row(raw.shape[1]),prev,full(cw),full(gain),row(width),row(width),mat,row(2*width)]+[pl.BlockSpec(memory_space=pl.ANY)]*(1+len(dummies)),
        out_specs=[row(raw.shape[1]),pl.BlockSpec((KERNEL,3*width),lambda i:(0,0)),pl.BlockSpec((1,HDIM),lambda i:(0,0)),pl.BlockSpec(memory_space=pl.ANY)],
        out_shape=[jax.ShapeDtypeStruct(raw.shape,BF16),
            jax.ShapeDtypeStruct((KERNEL,3*width),F32),jax.ShapeDtypeStruct((1,HDIM),F32),jax.ShapeDtypeStruct((4*block.shape[0],block.shape[1]),BF16)],
        scratch_shapes=[pltpu.VMEM((rows+8,3*width),F32),pltpu.VMEM((rows+8,3*width),F32),pltpu.VMEM((heads,HDIM,HDIM),F32),
            pltpu.SemaphoreType.DMA(()),pltpu.SemaphoreType.DMA((4,)),pltpu.SemaphoreType.DMA((4,))],
        compiler_params=pltpu.CompilerParams(collective_id=3,has_side_effects=True,vmem_limit_bytes=24<<20),
        cost_estimate=pl.CostEstimate(flops=0,bytes_accessed=120<<20,transcendentals=0),
    )(keep,count,raw,raw,cw,gain,gno,o,st,wr,block,*dummies)


def passed_along(block, axis, distance):
    devices = range(lax.axis_size(axis))
    route = [(i - distance, i) for i in devices if i - distance in devices]
    return lax.ppermute(block, axis, route)


def row_layout(lengths, positions):
    span_len = (lengths + BLOCK - 1) // BLOCK * BLOCK
    closing = jnp.cumsum(span_len)
    opening = closing - span_len
    bounds = jnp.concatenate([opening, closing[-1:]])
    reached = bounds[None, :] <= positions[:, None]
    doc_start = jnp.max(jnp.where(reached, bounds[None, :], 0), axis=1)
    inside = (positions[:, None] >= opening[None, :]) & (
        positions[:, None] < (opening + lengths)[None, :]
    )
    real_mask = jnp.any(inside, axis=1).astype(jnp.float32)
    return (doc_start, real_mask)


def local_span(carry_on, queries, keys_in, values, strength):
    head_count, token_count, head_width = queries.shape
    block_count = token_count // BLOCK

    def to_blocks(tensor):
        return tensor.reshape(head_count, block_count, BLOCK, -1).transpose(1, 0, 2, 3)

    def from_blocks(tensor):
        return tensor.transpose(1, 0, 2, 3).reshape(head_count, token_count, -1)

    strict_lower = jnp.tril(jnp.ones((BLOCK, BLOCK), jnp.float32), -1)
    causal = jnp.tril(jnp.ones((BLOCK, BLOCK), jnp.float32))
    identity = jnp.broadcast_to(
        jnp.eye(head_width, dtype=jnp.float32), (head_count, head_width, head_width)
    )

    def block_step(carried, block_in):
        memory, mapping = carried
        q_blk, k_blk, v_blk, s_blk, carry_flag = block_in
        write_rate = s_blk[..., 0]
        memory = memory * carry_flag
        mapping = mapping * carry_flag
        key_gram = jnp.einsum("hcp,hdp->hcd", k_blk, k_blk, precision=PRECISE)
        system = jnp.eye(BLOCK, dtype=jnp.float32) + strict_lower * (
            write_rate[:, :, None] * key_gram
        )
        right_side = jnp.concatenate(
            [write_rate[..., None] * k_blk, write_rate[..., None] * v_blk], axis=-1
        )
        solved = lax.linalg.triangular_solve(
            system, right_side, left_side=True, lower=True, unit_diagonal=True
        )
        w_mat = solved[..., :head_width]
        u_mat = solved[..., head_width:]
        corrected = u_mat - jnp.einsum("hcp,hpv->hcv", w_mat, memory, precision=PRECISE)
        scores = causal * jnp.einsum("hcp,hdp->hcd", q_blk, k_blk, precision=PRECISE)
        out_zero = jnp.einsum("hcp,hpv->hcv", q_blk, memory, precision=PRECISE)
        out_zero = out_zero + jnp.einsum("hcd,hdv->hcv", scores, corrected, precision=PRECISE)
        w_map = jnp.einsum("hcp,hpq->hcq", w_mat, mapping, precision=PRECISE)
        q_prop = jnp.einsum("hcp,hpq->hcq", q_blk, mapping, precision=PRECISE)
        q_prop = q_prop - jnp.einsum("hcd,hdq->hcq", scores, w_map, precision=PRECISE)
        memory = memory + jnp.einsum("hcp,hcv->hpv", k_blk, corrected, precision=PRECISE)
        mapping = mapping - jnp.einsum("hcp,hcq->hpq", k_blk, w_map, precision=PRECISE)
        return ((memory, mapping), (out_zero, q_prop))

    initial = (jnp.zeros((head_count, head_width, head_width), jnp.float32), identity)
    blocks = (
        to_blocks(queries),
        to_blocks(keys_in),
        to_blocks(values),
        to_blocks(strength[..., None]),
        carry_on,
    )
    (memory, mapping), (out_zero, q_prop) = lax.scan(block_step, initial, blocks)
    return (from_blocks(out_zero), from_blocks(q_prop), mapping, memory)


def spread_shards(
    block_in,
    doc_lengths,
    attn_gain,
    qkv_weight,
    conv_weight,
    beta_weight,
    out_gain,
    out_weight,
    ffn_gain,
    gateup_weight,
    down_weight,
    cotangent,
):
    tok_count = block_in.shape[1]
    seq_count = lax.axis_size("seq")
    own_index = lax.axis_index("seq")
    positions = own_index * tok_count + jnp.arange(tok_count + KERNEL - 1, dtype=jnp.int32)
    doc_start, real_ext = row_layout(doc_lengths[0], positions)
    real_mask = real_ext[:tok_count]
    taps = [(positions - shift_no >= doc_start).astype(jnp.float32) for shift_no in range(KERNEL)]
    carry_on = (doc_start[:tok_count:BLOCK] != positions[:tok_count:BLOCK]).astype(jnp.float32)
    residual_in = block_in[0].astype(jnp.float32)
    stat_in = lax.rsqrt(jnp.mean(residual_in * residual_in, axis=-1, keepdims=True) + EPSILON)
    unit_in = residual_in * stat_in
    normed = (unit_in * attn_gain).astype(jnp.bfloat16)
    qkv_full, beta_full, out_full, gateup_full, down_full = (
        lax.all_gather(qkv_weight, ("seq", "row"), axis=1, tiled=True),
        lax.all_gather(beta_weight, ("seq", "row"), axis=1, tiled=True),
        lax.all_gather(out_weight, ("seq", "row"), axis=1, tiled=True),
        lax.all_gather(gateup_weight, ("seq", "row"), axis=1, tiled=True),
        lax.all_gather(down_weight, ("seq", "row"), axis=1, tiled=True),
    )
    raw = jnp.einsum("td,sdc->stc", normed, qkv_full, preferred_element_type=jnp.float32).astype(
        jnp.bfloat16
    )
    rims = passed_along(raw[:, tok_count - KERNEL + 1 :, :], "seq", 1)
    extended = jnp.concatenate([rims, raw], axis=1).astype(jnp.float32)
    conv_sum = jnp.zeros(raw.shape, jnp.float32)
    for shift_no in range(KERNEL):
        window = extended[:, KERNEL - 1 - shift_no : KERNEL - 1 - shift_no + tok_count]
        conv_sum = (
            conv_sum
            + conv_weight[:, shift_no][:, None, :]
            * window
            * taps[shift_no][:tok_count][None, :, None]
        )
    conv_sig = jax.nn.sigmoid(conv_sum)
    head_count = conv_weight.shape[2] // HDIM
    split_heads = (
        (conv_sum * conv_sig).reshape(3, tok_count, head_count, HDIM).transpose(0, 2, 1, 3)
    )
    q_scale = lax.rsqrt(jnp.sum(split_heads[0] * split_heads[0], axis=-1, keepdims=True) + EPSILON)
    q_unit = split_heads[0] * q_scale
    queries = q_unit * HDIM ** (-0.5)
    k_scale = lax.rsqrt(jnp.sum(split_heads[1] * split_heads[1], axis=-1, keepdims=True) + EPSILON)
    keys_in = split_heads[1] * k_scale
    values = split_heads[2]
    logits = jnp.einsum("td,hd->ht", normed, beta_full, preferred_element_type=jnp.float32)
    beta_sig = jax.nn.sigmoid(logits)
    strength = beta_sig * real_mask[None, :]
    (out_zero, q_prop, span_map, span_state), span_pullback = jax.vjp(
        partial(local_span, carry_on), queries, keys_in, values, strength
    )
    empty_state = jnp.zeros_like(span_state)
    all_maps, all_states = (
        lax.all_gather(span_map[None].astype(jnp.bfloat16), "seq", axis=0, tiled=True).astype(
            jnp.float32
        ),
        lax.all_gather(span_state[None].astype(jnp.bfloat16), "seq", axis=0, tiled=True).astype(
            jnp.float32
        ),
    )

    def fold_forward(counter, incoming):
        moved = (
            jnp.einsum("hpq,hqv->hpv", all_maps[counter], incoming, precision=PRECISE)
            + all_states[counter]
        )
        return jnp.where(counter < own_index, moved, incoming)

    state_in = lax.fori_loop(0, seq_count, fold_forward, empty_state)
    mixer = out_zero + jnp.einsum("htp,hpv->htv", q_prop, state_in, precision=PRECISE)
    stat_out = lax.rsqrt(jnp.mean(mixer * mixer, axis=-1, keepdims=True) + EPSILON)
    unit_out = mixer * stat_out
    normed_out = (
        (unit_out * out_gain).transpose(1, 0, 2).reshape(tok_count, -1).astype(jnp.bfloat16)
    )
    branch_part = jnp.dot(normed_out, out_full, preferred_element_type=jnp.float32)
    hidden = residual_in + lax.psum(branch_part.astype(jnp.bfloat16), "mp").astype(jnp.float32)
    stat_mid = lax.rsqrt(jnp.mean(hidden * hidden, axis=-1, keepdims=True) + EPSILON)
    unit_mid = hidden * stat_mid
    normed_mid = (unit_mid * ffn_gain).astype(jnp.bfloat16)
    gate_up = jnp.einsum("td,sdf->stf", normed_mid, gateup_full, preferred_element_type=jnp.float32)
    gate_sig = jax.nn.sigmoid(gate_up[0])
    product = (gate_up[0] * gate_sig * gate_up[1]).astype(jnp.bfloat16)
    ffn_part = jnp.dot(product, down_full, preferred_element_type=jnp.float32)
    block_out = hidden + lax.psum(ffn_part.astype(jnp.bfloat16), "mp").astype(jnp.float32)
    qkv_full, beta_full, out_full, gateup_full, down_full = (
        lax.all_gather(qkv_weight, ("seq", "row"), axis=1, tiled=True),
        lax.all_gather(beta_weight, ("seq", "row"), axis=1, tiled=True),
        lax.all_gather(out_weight, ("seq", "row"), axis=1, tiled=True),
        lax.all_gather(gateup_weight, ("seq", "row"), axis=1, tiled=True),
        lax.all_gather(down_weight, ("seq", "row"), axis=1, tiled=True),
    )
    grad_top = cotangent[0]
    grad_down_part = jnp.dot(product.T, grad_top, preferred_element_type=jnp.float32)
    grad_product = jnp.dot(grad_top, down_full.T, preferred_element_type=jnp.float32)
    grad_gate = grad_product * gate_up[1] * gate_sig * (1.0 + gate_up[0] * (1.0 - gate_sig))
    grad_up = grad_product * gate_up[0] * gate_sig
    grad_gate_up = jnp.stack([grad_gate, grad_up]).astype(jnp.bfloat16)
    grad_gateup_part = jnp.einsum(
        "td,stf->sdf", normed_mid, grad_gate_up, preferred_element_type=jnp.float32
    )
    grad_mid_part = jnp.einsum(
        "stf,sdf->td", grad_gate_up, gateup_full, preferred_element_type=jnp.float32
    )
    grad_mid = lax.psum(grad_mid_part.astype(jnp.bfloat16), "mp").astype(jnp.float32)
    ffn_gain_part = jnp.sum(grad_mid * unit_mid, axis=0)
    grad_unit_mid = grad_mid * ffn_gain
    grad_hidden = grad_top.astype(jnp.float32) + stat_mid * (
        grad_unit_mid - unit_mid * jnp.mean(grad_unit_mid * unit_mid, axis=-1, keepdims=True)
    )
    grad_branch = grad_hidden.astype(jnp.bfloat16)
    grad_out_part = jnp.dot(normed_out.T, grad_branch, preferred_element_type=jnp.float32)
    grad_normed_out = jnp.dot(grad_branch, out_full.T, preferred_element_type=jnp.float32)
    grad_normed_out = grad_normed_out.reshape(tok_count, head_count, HDIM).transpose(1, 0, 2)
    out_gain_part = jnp.sum(grad_normed_out * unit_out, axis=(0, 1))
    grad_unit_out = grad_normed_out * out_gain
    grad_mixer = stat_out * (
        grad_unit_out - unit_out * jnp.mean(grad_unit_out * unit_out, axis=-1, keepdims=True)
    )
    local_grad = jnp.einsum("htp,htv->hpv", q_prop, grad_mixer, precision=PRECISE)
    grad_q_prop = jnp.einsum("htv,hpv->htp", grad_mixer, state_in, precision=PRECISE)
    all_grads = lax.all_gather(
        local_grad[None].astype(jnp.bfloat16), "seq", axis=0, tiled=True
    ).astype(jnp.float32)

    def fold_backward(counter, later_grad):
        source = seq_count - 1 - counter
        moved = (
            jnp.einsum("hqp,hqv->hpv", all_maps[source], later_grad, precision=PRECISE)
            + all_grads[source]
        )
        return jnp.where(source > own_index, moved, later_grad)

    grad_end = lax.fori_loop(0, seq_count, fold_backward, empty_state)
    grad_map = jnp.einsum("hpv,hqv->hpq", grad_end, state_in, precision=PRECISE)
    grad_queries, grad_keys, grad_values, grad_strength = span_pullback(
        (grad_mixer, grad_q_prop, grad_map, grad_end)
    )
    grad_logits = (grad_strength * real_mask[None, :] * beta_sig * (1.0 - beta_sig)).astype(
        jnp.bfloat16
    )
    grad_beta_part = jnp.einsum(
        "ht,td->hd", grad_logits, normed, preferred_element_type=jnp.float32
    )
    grad_q_unit = grad_queries * HDIM ** (-0.5)
    grad_q_raw = q_scale * (
        grad_q_unit - q_unit * jnp.sum(grad_q_unit * q_unit, axis=-1, keepdims=True)
    )
    grad_k_raw = k_scale * (
        grad_keys - keys_in * jnp.sum(grad_keys * keys_in, axis=-1, keepdims=True)
    )
    grad_act = (
        jnp.stack([grad_q_raw, grad_k_raw, grad_values])
        .transpose(0, 2, 1, 3)
        .reshape(3, tok_count, -1)
    )
    grad_conv_sum = grad_act * conv_sig * (1.0 + conv_sum * (1.0 - conv_sig))
    rims_back = passed_along(grad_conv_sum[:, : KERNEL - 1, :], "seq", -1)
    grad_ext = jnp.concatenate([grad_conv_sum, rims_back], axis=1)
    grad_raw = jnp.zeros(grad_conv_sum.shape, jnp.float32)
    conv_terms = []
    for shift_no in range(KERNEL):
        grad_raw = (
            grad_raw
            + conv_weight[:, shift_no][:, None, :]
            * grad_ext[:, shift_no : shift_no + tok_count]
            * taps[shift_no][shift_no : shift_no + tok_count][None, :, None]
        )
        window = extended[:, KERNEL - 1 - shift_no : KERNEL - 1 - shift_no + tok_count]
        conv_terms.append(
            jnp.sum(grad_conv_sum * window * taps[shift_no][:tok_count][None, :, None], axis=1)
        )
    grad_conv_part = jnp.stack(conv_terms, axis=1)
    grad_raw_low = grad_raw.astype(jnp.bfloat16)
    grad_qkv_part = jnp.einsum(
        "td,stc->sdc", normed, grad_raw_low, preferred_element_type=jnp.float32
    )
    grad_normed = jnp.einsum(
        "stc,sdc->td", grad_raw_low, qkv_full, preferred_element_type=jnp.float32
    )
    grad_normed = grad_normed + jnp.einsum(
        "ht,hd->td", grad_logits, beta_full, preferred_element_type=jnp.float32
    )
    grad_normed, out_gain_sum = (
        lax.psum(grad_normed.astype(jnp.bfloat16), "mp").astype(jnp.float32),
        lax.psum(out_gain_part.astype(jnp.bfloat16), "mp").astype(jnp.float32),
    )
    attn_gain_part = jnp.sum(grad_normed * unit_in, axis=0)
    grad_unit_in = grad_normed * attn_gain
    grad_input = grad_hidden + stat_in * (
        grad_unit_in - unit_in * jnp.mean(grad_unit_in * unit_in, axis=-1, keepdims=True)
    )
    weight_sums = (
        lax.psum_scatter(grad_qkv_part, ("seq", "row"), scatter_dimension=1, tiled=True),
        lax.psum_scatter(grad_beta_part, ("seq", "row"), scatter_dimension=1, tiled=True),
        lax.psum_scatter(grad_out_part, ("seq", "row"), scatter_dimension=1, tiled=True),
        lax.psum_scatter(grad_gateup_part, ("seq", "row"), scatter_dimension=1, tiled=True),
        lax.psum_scatter(grad_down_part, ("seq", "row"), scatter_dimension=1, tiled=True),
    )
    small_sums = lax.psum(
        (attn_gain_part, grad_conv_part, out_gain_sum, ffn_gain_part), ("seq", "row")
    )
    return (
        block_out.astype(jnp.bfloat16)[None],
        grad_input[None],
        small_sums[0],
        weight_sums[0],
        small_sums[1],
        weight_sums[1],
        small_sums[2],
        weight_sums[2],
        small_sums[3],
        weight_sums[3],
        weight_sums[4],
    )


MESH = pl.DeviceIdType.MESH
STRIP = 16
TILE = 512
WIDE = 256


def phase_kernel(middle, both_cores, small_sum, meanwhile, n_in, n_out, part_ref, *refs):
    inputs, all_ref = refs[:n_in], refs[n_in]
    outs, scratch = refs[n_in + 1 : n_in + n_out], refs[n_in + n_out :]
    got, sums, gain_sum, send_sem, recv_sem = scratch[:5]
    count = all_ref.shape[0]
    rows = count // 8
    place, core, row = lax.axis_index("mp"), lax.axis_index("seq"), lax.axis_index("row")
    across_x = place + 1 - 2 * (place % 2)
    across_y = (place + 2) % 4
    across_both = 3 - place
    ways = {"x": {"mp": across_x}, "y": {"mp": across_y}}
    if both_cores or small_sum:
        ways["core"] = {"seq": 1 - core}
    steps = []
    if small_sum:
        bit = 1
        while bit < lax.axis_size("row"):
            steps.append(f"row{bit}")
            ways[steps[-1]] = {"row": row + bit - 2 * bit * ((row // bit) % 2)}
            bit *= 2
        steps += ["core", "x", "y"]
    barrier = pltpu.get_barrier_semaphore()
    for other in ways.values():
        pl.semaphore_signal(barrier, inc=1, device_id=other, device_id_type=MESH)
    pl.semaphore_wait(barrier, len(ways))

    def copy(index, source, target, way):
        return pltpu.make_async_remote_copy(
            src_ref=source,
            dst_ref=target,
            send_sem=send_sem.at[index],
            recv_sem=recv_sem.at[index],
            device_id=ways[way],
            device_id_type=MESH,
        )

    def block(of, half):
        return pl.ds(pl.multiple_of((2 * of + half) * rows, rows), rows)

    def strips(body):
        @pl.loop(0, rows // STRIP)
        def _(i):
            body(pl.multiple_of(i * STRIP, STRIP))

    part, relayed, copies = part_ref, [], send_sem.shape[0]
    if meanwhile:
        fetch = pltpu.make_async_copy(inputs[3].at[3], scratch[-3], scratch[-2])
        fetch.start()
    if both_cores:
        part, outgoing, incoming, weight, weight_sem = scratch[5:10]
        mixer, beta = inputs[3:5]
        width = (weight.shape[0] - beta.shape[0]) // 3
        fetches = [
            pltpu.make_async_copy(
                mixer.at[s, pl.ds(pl.multiple_of(core * width, width), width)],
                weight.at[pl.ds(s * width, width)],
                weight_sem.at[s],
            )
            for s in range(3)
        ]
        for step in fetches:
            step.start()
        weight[3 * width :, :] = beta[...]
        order = [across_both, across_x, across_y, place]
        passed_ref, far_ref = inputs[n_in - small_sum["dummies"] - 1], outs[-2]
        relayed = [
            copy(
                copies - 2,
                passed_ref.at[block(across_x, 0)],
                far_ref.at[pl.ds(0, rows)],
                "y",
            ),
            copy(
                copies - 1,
                passed_ref.at[block(across_y, 1)],
                far_ref.at[pl.ds(rows, rows)],
                "x",
            ),
        ]
        for step in relayed:
            step.start()

        def product(whose, of, target):
            start = pl.multiple_of(whose * count + 2 * of * rows, rows)
            left = part_ref[pl.ds(start, 2 * rows), :]
            lines = pl.ds(pl.multiple_of(2 * of * rows, rows), 2 * rows)

            @pl.loop(0, weight.shape[1] // TILE)
            def _(i):
                tile = pl.ds(pl.multiple_of(i * TILE, TILE), TILE)
                target[lines, tile] = jnp.dot(
                    left, weight[:, tile], preferred_element_type=F32
                ).astype(BF16)

            return lines

        shared = []
        for number in range(4):
            lines = pl.ds(pl.multiple_of(2 * order[number] * rows, rows), 2 * rows)
            shared.append(copy(12 + number, outgoing.at[lines], incoming.at[lines], "core"))

        for step in fetches:
            step.wait()

        def give(number):
            product(1 - core, order[number], outgoing)
            shared[number].start()

        def take(number):
            of = order[number]
            product(core, of, part)
            shared[number].wait_recv()

            @pl.loop(0, 2 * rows // STRIP)
            def _(i):
                strip = pl.ds(pl.multiple_of(2 * of * rows + i * STRIP, STRIP), STRIP)
                part[strip, :] = (
                    part[strip, :].astype(F32) + incoming[strip, :].astype(F32)
                ).astype(BF16)

    far = [
        copy(0, part.at[block(across_both, 0)], got.at[0], "x"),
        copy(1, part.at[block(across_both, 1)], got.at[1], "y"),
    ]
    near = [
        copy(2, part.at[block(across_x, 0)], got.at[2], "x"),
        copy(3, part.at[block(across_y, 1)], got.at[3], "y"),
    ]
    last = [copy(4, sums.at[0], got.at[4], "y"), copy(5, sums.at[1], got.at[5], "x")]
    own = [all_ref.at[block(place, 0)], all_ref.at[block(place, 1)]]
    passed = [all_ref.at[block(across_x, 0)], all_ref.at[block(across_y, 1)]]
    out_first = [copy(6, own[0], own[0], "x"), copy(7, own[1], own[1], "y")]
    out_second = [copy(8, own[0], own[0], "y"), copy(9, own[1], own[1], "x")]
    out_third = [copy(10, passed[0], passed[0], "y"), copy(11, passed[1], passed[1], "x")]

    if both_cores:
        give(0)
        give(1)
        take(0)
    for step in far:
        step.start()
    if both_cores:
        give(2)
        take(1)
        near[0].start()
        take(2)
        near[1].start()
        give(3)
        take(3)
    else:
        for step in near:
            step.start()
    gain_sum[...] = jnp.zeros_like(gain_sum)
    for half, onward in ((0, across_y), (1, across_x)):
        far[half].wait_recv()

        def add(at):
            strip = pl.ds(at, STRIP)
            mine = part[pl.ds((2 * onward + half) * rows + at, STRIP), :]
            sums[half, strip, :] = (mine.astype(F32) + got[half, strip, :].astype(F32)).astype(BF16)

        strips(add)
        last[half].start()
    for half in (0, 1):
        near[half].wait_recv()
        last[half].wait_recv()

        def finish(at):
            strip = pl.ds(at, STRIP)
            total = part[pl.ds((2 * place + half) * rows + at, STRIP), :].astype(F32)
            total = total + got[2 + half, strip, :].astype(F32)
            total = total + got[4 + half, strip, :].astype(F32)
            result = middle(total, half, strip, inputs, outs, gain_sum)
            all_ref[pl.ds((2 * place + half) * rows + at, STRIP), :] = result.astype(BF16)

        strips(finish)
        out_first[half].start()
        out_second[half].start()

    def use(of, first=False, last=False):
        if middle is normed_forward:
            lines = pl.ds(pl.multiple_of(2 * of * rows, rows), 2 * rows)
            half = all_ref.shape[1] // 2
            for target, whose in ((outs[1], core), (outs[2], 1 - core)):
                columns = pl.ds(pl.multiple_of(whose * half, half), half)
                target[lines, :] = all_ref[lines, columns]
        if not meanwhile:
            return
        weight, left = scratch[-3], inputs[4]
        grad_left, products = outs[2], scratch[-1]
        lines = pl.ds(pl.multiple_of(2 * of * rows, rows), 2 * rows)
        grad_left[lines, :] = lax.dot_general(
            all_ref[lines, :], weight[...], NT, preferred_element_type=F32
        ).astype(BF16)

        @pl.loop(0, products.shape[1] // TILE)
        def _(i):
            tile = pl.ds(pl.multiple_of(i * TILE, TILE), TILE)
            more = lax.dot_general(
                left[lines, :], all_ref[lines, tile], TN, preferred_element_type=F32
            )
            if first:
                products[:, tile] = more
            elif last:
                outs[3][:, tile] = (products[:, tile] + more).astype(BF16)
            else:
                products[:, tile] = products[:, tile] + more

    if meanwhile:
        fetch.wait()
    use(place, first=True)
    gain = jnp.sum(gain_sum[...], axis=0, keepdims=True)
    small = []
    if small_sum:
        values, arrived = outs[-1], scratch[-1]
        first = n_in - small_sum["dummies"] - 4
        ffn_gain, out_gain, conv = inputs[first : first + 3]
        taps, width = conv.shape
        middle_lane = values.shape[1] // 2
        values[...] = jnp.zeros_like(values)
        values[0:1, :] = gain
        values[1:2, :] = ffn_gain[...]
        values[2:3, 0 : out_gain.shape[1]] = out_gain[...]
        for i in (0, 1):
            share = jnp.where(core == i, 1.0, 0.0)
            lane = i * middle_lane
            values[8 : 8 + taps, lane : lane + width] = conv[...] * share
    elif middle is not normed_forward:
        outs[1][...] = gain

    def small_step(number):
        height = 8 if steps[number] in ("x", "y") else values.shape[0]
        step = copy(
            16 + number,
            arrived.at[number, 1, pl.ds(0, height)],
            arrived.at[number, 0, pl.ds(0, height)],
            steps[number],
        )
        arrived[number, 1, 0:height, :] = values[0:height, :]
        step.start()
        step.wait_recv()
        values[0:height, :] = values[0:height, :] + arrived[number, 0, 0:height, :]
        small.append(step)

    for half in (0, 1):
        out_first[half].wait_recv()
        out_third[half].start()
    if small_sum:
        for number in range(len(steps)):
            small_step(number)
    for step in out_second:
        step.wait_recv()
    use(across_x)
    use(across_y)
    for step in out_third:
        step.wait_recv()
    use(across_both, last=True)
    for step in relayed:
        step.wait_recv()
    for step in (*relayed, *far, *near, *last, *out_first, *out_second, *out_third, *small):
        step.wait_send()
    if both_cores:
        for step in shared:
            step.wait_send()


def normed_forward(total, half, strip, inputs, outs, gain_sum):
    residual, gain = inputs[:2]
    hidden = residual[half, strip, :].astype(F32) + total
    outs[0][half, strip, :] = hidden
    stat = lax.rsqrt(jnp.mean(hidden * hidden, axis=1, keepdims=True) + EPSILON)
    return hidden * stat * gain[...]


def normed_backward(keep, total, half, strip, inputs, outs, gain_sum):
    value, base, gain = inputs[:3]
    value = value[half, strip, :].astype(F32)
    stat = lax.rsqrt(jnp.mean(value * value, axis=1, keepdims=True) + EPSILON)
    unit = value * stat
    gain_sum[...] += jnp.sum((total * unit).reshape(2, 8, -1), axis=0)
    scaled = total * gain[...]
    grad = base[half, strip, :].astype(F32) + stat * (
        scaled - unit * jnp.mean(scaled * unit, axis=1, keepdims=True)
    )
    if keep:
        outs[0][half, strip, :] = grad
    return grad


def mp_phase(
    number,
    middle,
    part,
    inputs,
    dummies,
    outs,
    both_cores=False,
    small=None,
    passed=None,
    meanwhile=False,
):
    here, there = pl.BlockSpec(memory_space=pltpu.VMEM), pl.BlockSpec(memory_space=pl.ANY)
    count, model = part.shape
    if both_cores:
        count, depth, model = count // 2, model, inputs[3].shape[2]
    block = (count // 8, model)
    copies, scratch, small_sum = 12, [], None
    if both_cores:
        scratch += [pltpu.VMEM((count, model), BF16)] * 3
        scratch += [pltpu.VMEM((depth, model), BF16), pltpu.SemaphoreType.DMA((3,))]
    if small is not None:
        stages = lax.axis_size("row").bit_length() - 1 + 3
        copies = 16 + stages + 2
        height = 8 + small[2].shape[0]
        shape = (height + -height % 8, model)
        scratch += [pltpu.VMEM((stages, 2, *shape), F32)]
        small_sum = {"dummies": len(dummies)}
        inputs = [*inputs, *small, passed]
        outs = [
            *outs,
            jax.ShapeDtypeStruct((2 * block[0], model), BF16),
            jax.ShapeDtypeStruct(shape, F32),
        ]
    specs = [here] * len(inputs)
    if small is not None:
        specs[3] = specs[-1] = there
    if meanwhile:
        _, width, depth = inputs[3].shape
        specs[3] = there
        scratch += [
            pltpu.VMEM((width, depth), BF16),
            pltpu.SemaphoreType.DMA(()),
            pltpu.VMEM((width, model), F32),
        ]
    kernel = functools.partial(
        phase_kernel,
        middle,
        both_cores,
        small_sum,
        meanwhile,
        len(inputs) + len(dummies),
        1 + len(outs),
    )
    return pl.pallas_call(
        kernel,
        in_specs=[here, *specs] + [there] * len(dummies),
        out_specs=[here] * (1 + len(outs)),
        out_shape=[jax.ShapeDtypeStruct((count, model), BF16), *outs],
        scratch_shapes=[
            pltpu.VMEM((6, *block), BF16),
            pltpu.VMEM((2, *block), BF16),
            pltpu.VMEM((8, model), F32),
            pltpu.SemaphoreType.DMA((copies,)),
            pltpu.SemaphoreType.DMA((copies,)),
            *scratch,
        ],
        compiler_params=pltpu.CompilerParams(
            collective_id=number, has_side_effects=True, vmem_limit_bytes=50 << 20
        ),
        cost_estimate=pl.CostEstimate(flops=0, bytes_accessed=250 << 20, transcendentals=0),
    )(part, *inputs, *dummies)


def pair_kernel(product_ref, weight, hidden, left_own, left_other, gate, up, *refs):
    block_ref, gate_pair, up_pair, part_ref, got, sums, gate_in, up_in, send_sem, recv_sem = refs[-10:]
    rows = part_ref.shape[0] // 8
    place, core = lax.axis_index("mp"), lax.axis_index("seq")
    across_x = place + 1 - 2 * (place % 2)
    across_y = (place + 2) % 4
    across_both = 3 - place
    ways = {"x": {"mp": across_x}, "y": {"mp": across_y}, "core": {"seq": 1 - core}}
    barrier = pltpu.get_barrier_semaphore()
    for other in ways.values():
        pl.semaphore_signal(barrier, inc=1, device_id=other, device_id_type=MESH)
    pl.semaphore_wait(barrier, len(ways))

    def copy(index, source, target, way):
        return pltpu.make_async_remote_copy(
            src_ref=source,
            dst_ref=target,
            send_sem=send_sem.at[index],
            recv_sem=recv_sem.at[index],
            device_id=ways[way],
            device_id_type=MESH,
        )

    def block(of, half):
        return pl.ds(pl.multiple_of((2 * of + half) * rows, rows), rows)

    def strips(body):
        @pl.loop(0, rows // STRIP)
        def _(i):
            body(pl.multiple_of(i * STRIP, STRIP))

    far = [
        copy(0, part_ref.at[block(across_both, 0)], got.at[0], "x"),
        copy(1, part_ref.at[block(across_both, 1)], got.at[1], "y"),
    ]
    near = [
        copy(2, part_ref.at[block(across_x, 0)], got.at[2], "x"),
        copy(3, part_ref.at[block(across_y, 1)], got.at[3], "y"),
    ]
    last = [copy(4, sums.at[0], got.at[4], "y"), copy(5, sums.at[1], got.at[5], "x")]
    shared = [copy(6, gate, gate_in, "core"), copy(7, up, up_in, "core")]

    def produce(of):
        lines = pl.ds(pl.multiple_of(2 * of * rows, rows), 2 * rows)

        @pl.loop(0, weight.shape[1] // TILE)
        def _(i):
            tile = pl.ds(pl.multiple_of(i * TILE, TILE), TILE)
            part_ref[lines, tile] = jnp.dot(
                product_ref[lines, :], weight[:, tile], preferred_element_type=F32
            ).astype(BF16)

    for step in shared:
        step.start()
    produce(across_both)
    for step in far:
        step.start()
    produce(across_x)
    near[0].start()
    produce(across_y)
    near[1].start()
    produce(place)

    def products(own, other, target, first, count):
        @pl.loop(first, first + count)
        def _(i):
            tile = pl.ds(pl.multiple_of(i * WIDE, WIDE), WIDE)
            total = lax.dot_general(
                left_own[:, tile], own[...], TN, preferred_element_type=F32
            ) + lax.dot_general(left_other[:, tile], other[...], TN, preferred_element_type=F32)
            target[tile, :] = total.astype(BF16)

    tiles = left_own.shape[1] // WIDE
    shared[0].wait_recv()
    products(gate, gate_in, gate_pair, 0, tiles)
    for half, onward in ((0, across_y), (1, across_x)):
        far[half].wait_recv()

        def add(at):
            strip = pl.ds(at, STRIP)
            mine = part_ref[pl.ds((2 * onward + half) * rows + at, STRIP), :]
            sums[half, strip, :] = (mine.astype(F32) + got[half, strip, :].astype(F32)).astype(BF16)

        strips(add)
        last[half].start()
    shared[1].wait_recv()
    products(up, up_in, up_pair, 0, tiles)
    for half in (0, 1):
        near[half].wait_recv()
        last[half].wait_recv()

        def finish(at):
            strip = pl.ds(at, STRIP)
            total = part_ref[pl.ds((2 * place + half) * rows + at, STRIP), :].astype(F32)
            total = total + got[2 + half, strip, :].astype(F32)
            total = total + got[4 + half, strip, :].astype(F32)
            block_ref[pl.ds(half * rows + at, STRIP), :] = (hidden[half, strip, :] + total).astype(BF16)

        strips(finish)
    for step in (*shared, *far, *near, *last):
        step.wait_send()


def scattered_and_pairs(number, product, weight, hidden, left, gate, up, dummies):
    here, there = pl.BlockSpec(memory_space=pltpu.VMEM), pl.BlockSpec(memory_space=pl.ANY)
    count, model = product.shape[0], weight.shape[1]
    block = (count // 8, model)
    pair = jax.ShapeDtypeStruct((left[0].shape[1], gate.shape[1]), BF16)
    return pl.pallas_call(
        pair_kernel,
        in_specs=[here] * 7 + [there] * len(dummies),
        out_specs=[here] * 3,
        out_shape=[jax.ShapeDtypeStruct((2 * block[0], model), BF16), pair, pair],
        scratch_shapes=[
            pltpu.VMEM((count, model), BF16),
            pltpu.VMEM((6, *block), BF16),
            pltpu.VMEM((2, *block), BF16),
            pltpu.VMEM(gate.shape, BF16),
            pltpu.VMEM(up.shape, BF16),
            pltpu.SemaphoreType.DMA((8,)),
            pltpu.SemaphoreType.DMA((8,)),
        ],
        compiler_params=pltpu.CompilerParams(
            collective_id=number, has_side_effects=True, vmem_limit_bytes=54 << 20
        ),
        cost_estimate=pl.CostEstimate(flops=0, bytes_accessed=130 << 20, transcendentals=0),
    )(product, weight, hidden, *left, gate, up, *dummies)


def swapped(block):
    return lax.ppermute(block, "seq", [(0, 1), (1, 0)])


def in_order(mine, other, core, axis):
    first = jnp.where(core == 0, mine, other)
    second = jnp.where(core == 0, other, mine)
    return jnp.concatenate([first, second], axis=axis)


def after(block, *done):
    nothing = sum(part[(0,) * part.ndim].astype(F32) for part in done) * 0.0
    return block + nothing.astype(block.dtype)


def halves(block, core, axis):
    size = block.shape[axis] // 2
    pick = lambda i: lax.dynamic_slice_in_dim(block, i * size, size, axis=axis)
    return pick(core), pick(1 - core)


def both_tokens(left, right, *done):
    product = lambda a, b: lax.dot_general(
        a, b, (((0,), (0,)), ((), ())), preferred_element_type=F32
    )
    total = product(left[0], right[0]) + product(left[1], right[1])
    return (after(total, *done) if done else total).astype(BF16)


def own_columns(block, core):
    mine, other = halves(block, core, 1)
    return mine, swapped(other)


def over_row(pair, axis):
    return lax.psum_scatter(pair, "row", scatter_dimension=axis, tiled=True)


def joined_shards(
    block_in,
    doc_lengths,
    attn_gain,
    qkv_weight,
    conv_weight,
    beta_weight,
    out_gain,
    out_weight,
    ffn_gain,
    gateup_weight,
    down_weight,
    cotangent,
):
    tok_count, model = block_in.shape[1:]
    core, own = lax.axis_index("seq"), lax.axis_index("mp")
    width = conv_weight.shape[2] // 2
    own_heads = width // HDIM
    quarter = tok_count // 4

    gather = lambda weight: lax.all_gather(weight, ("seq", "row"), axis=1, tiled=True)
    mixer_full = gather(jnp.concatenate([qkv_weight, out_weight.T[None]]))
    qkv_full, out_full = mixer_full[:3], mixer_full[3]
    mixer_rows = mixer_full.transpose(0, 2, 1)
    beta_full, gateup_full, down_full = (
        gather(beta_weight),
        gather(gateup_weight),
        gather(down_weight),
    )
    qkv_own = lax.dynamic_slice_in_dim(qkv_full, core * width, width, axis=2)
    beta_own = lax.dynamic_slice_in_dim(beta_full, core * own_heads, own_heads, axis=0)
    beta_rows = jnp.pad(beta_own, ((0, HDIM - own_heads), (0, 0)))
    mix_across = jnp.concatenate([qkv_own[0].T, qkv_own[1].T, qkv_own[2].T, beta_rows])
    conv_own = lax.dynamic_slice_in_dim(conv_weight, core * width, width, axis=2)
    conv_own = conv_own.transpose(1, 0, 2).reshape(KERNEL, 3 * width)

    residual_in = block_in[0].astype(F32)
    stat_in = lax.rsqrt(jnp.mean(residual_in * residual_in, axis=-1, keepdims=True) + EPSILON)
    normed_mine = (residual_in * stat_in * attn_gain).astype(BF16)
    normed = in_order(normed_mine, swapped(normed_mine), core, 0)

    positions = jnp.arange(2 * tok_count, dtype=jnp.int32)
    doc_start, real_row = row_layout(doc_lengths[0], positions)
    keep = jnp.pad((doc_start[::BLOCK] != positions[::BLOCK]).astype(F32), (0, 1))
    count = jnp.sum(real_row.reshape(-1, BLOCK), axis=1).astype(jnp.int32)
    raw = lax.dot_general(
        normed, mix_across, (((1,), (1,)), ((), ())), preferred_element_type=F32
    ).astype(BF16)
    gain = out_gain[None, :]
    group = 4 if raw.shape[0] % (4 * CHUNK) == 0 else 1
    heads_out, *saved = forward(keep, count, raw, conv_own, gain, group)

    mine, other = halves(heads_out, core, 0)
    normed_out = in_order(mine, swapped(other), core, 1)
    branch_part = lax.dot_general(
        normed_out, out_full, (((1,), (1,)), ((), ())), preferred_element_type=F32
    )
    own_rows = lambda block: lax.dynamic_slice_in_dim(
        block[0], own * quarter, quarter, axis=0
    ).reshape(2, -1, model)
    residual_own = own_rows(block_in)
    rows_own = jax.ShapeDtypeStruct(residual_own.shape, F32)
    normed_mid, hidden, normed_mine, normed_other = mp_phase(
        0,
        normed_forward,
        branch_part.astype(BF16),
        [residual_own, ffn_gain[None, :]],
        [],
        [rows_own] + [jax.ShapeDtypeStruct((tok_count, model // 2), BF16)] * 2,
    )

    grad_top = cotangent[0]
    gate_up = jnp.einsum("td,sdf->stf", normed_mid, gateup_full, preferred_element_type=F32)
    gate_sig = jax.nn.sigmoid(gate_up[0])
    product = (gate_up[0] * gate_sig * gate_up[1]).astype(BF16)
    normed_halves = normed_mine, swapped(normed_other)
    down_pair = both_tokens(
        (product, swapped(product)), own_columns(grad_top, core), normed_halves[1]
    )
    grad_product = jnp.dot(grad_top, down_full.T, preferred_element_type=F32)
    grad_product = after(grad_product, down_pair)
    grad_gate = grad_product * gate_up[1] * gate_sig * (1.0 + gate_up[0] * (1.0 - gate_sig))
    grad_up = grad_product * gate_up[0] * gate_sig
    grad_gate, grad_up = grad_gate.astype(BF16), grad_up.astype(BF16)
    grad_mid_part = jnp.einsum(
        "stf,sdf->td",
        jnp.stack([grad_gate, grad_up]),
        gateup_full,
        preferred_element_type=F32,
    ).astype(BF16)
    block_out, gate_pair, up_pair = scattered_and_pairs(
        4,
        product,
        down_full,
        hidden,
        normed_halves,
        grad_gate,
        grad_up,
        [down_pair],
    )
    down_sum, gate_sum, up_sum = over_row(down_pair, 1), over_row(gate_pair, 0), over_row(up_pair, 0)
    grad_branch, grad_hidden, ffn_gain_part, grad_normed_out, grad_out_part = mp_phase(
        1,
        partial(normed_backward, True),
        grad_mid_part,
        [hidden, own_rows(cotangent), ffn_gain[None, :], mixer_rows, normed_out],
        [block_out, down_sum, gate_pair, up_pair],
        [
            rows_own,
            jax.ShapeDtypeStruct((1, model), F32),
            jax.ShapeDtypeStruct(normed_out.shape, BF16),
            jax.ShapeDtypeStruct((normed_out.shape[1], model), BF16),
        ],
        meanwhile=True,
    )
    mine, other = halves(grad_normed_out, core, 1)
    grad_heads = in_order(mine, swapped(other), core, 0)
    mine, other = halves(grad_out_part, core, 1)
    out_pair = after(mine.astype(F32) + swapped(other).astype(F32), up_sum).astype(BF16)
    grad_raw, grad_conv_own, out_gain_part, block_out = backward(
        keep,
        count,
        raw,
        conv_own,
        gain,
        grad_heads,
        *saved,
        group,
        block_out,
        [gate_sum],
    )
    normed_mine, normed_other = halves(normed, core, 1)
    by_columns = lambda part: lax.dot_general(
        part, grad_raw, (((0,), (0,)), ((), ())), preferred_element_type=F32
    ).astype(BF16)
    qkv_other = swapped(by_columns(normed_other))
    qkv_mine = by_columns(normed_mine)
    grad_input, far_rows, small = mp_phase(
        2,
        partial(normed_backward, False),
        grad_raw,
        [residual_own, grad_hidden, attn_gain[None, :], mixer_rows, beta_rows],
        [up_sum, out_pair, qkv_mine, qkv_other],
        [],
        both_cores=True,
        small=[ffn_gain_part, out_gain_part, grad_conv_own],
        passed=block_out,
    )
    grad_input = grad_input.astype(F32)
    places = jnp.arange(4)[:, None, None]
    block_out = jnp.where(
        places == (own ^ 3),
        far_rows[None],
        block_out.reshape(4, quarter, model),
    ).reshape(tok_count, model)
    grad_attn_gain, grad_ffn_gain = small[0], small[1]
    grad_out_gain = small[2, : out_gain.shape[0]]
    conv_at = 8
    conv_of = lambda i: (
        small[conv_at : conv_at + KERNEL, i * (model // 2) : i * (model // 2) + 3 * width]
        .reshape(KERNEL, 3, width)
        .transpose(1, 0, 2)
    )
    grad_conv = jnp.concatenate([conv_of(0), conv_of(1)], axis=2)
    grad_down, grad_out = down_sum.astype(F32), over_row(out_pair, 1).astype(F32)
    grad_gateup = jnp.stack([gate_sum, up_sum]).astype(F32)
    row_sums = [over_row(part, 0) for part in (qkv_mine, qkv_other)]
    by_kind = lambda part: part[:, : 3 * width].reshape(-1, 3, width).transpose(1, 0, 2)
    grad_qkv = in_order(by_kind(row_sums[0]), by_kind(row_sums[1]), core, 2).astype(F32)
    of_heads = lambda part: part[:, 3 * width : 3 * width + own_heads].T
    grad_beta = in_order(of_heads(row_sums[0]), of_heads(row_sums[1]), core, 0).astype(F32)
    return (
        block_out[None],
        grad_input[None],
        grad_attn_gain,
        grad_qkv,
        grad_conv,
        grad_beta,
        grad_out_gain,
        grad_out,
        grad_ffn_gain,
        grad_gateup,
        grad_down,
    )


def solution(mesh):
    rows = mesh.shape["row"]
    joined = mesh.shape["seq"] == 2 and mesh.shape["mp"] == 4 and rows & (rows - 1) == 0
    return jax.shard_map(
        joined_shards if joined else spread_shards,
        mesh=mesh,
        in_specs=(
            P("row", "seq", None),
            P("row", None),
            P(),
            P(None, ("seq", "row"), "mp"),
            P(None, None, "mp"),
            P("mp", ("seq", "row")),
            P(),
            P("mp", ("seq", "row")),
            P(),
            P(None, ("seq", "row"), "mp"),
            P("mp", ("seq", "row")),
            P("row", "seq", None),
        ),
        out_specs=(
            P("row", "seq", None),
            P("row", "seq", None),
            P(),
            P(None, ("seq", "row"), "mp"),
            P(None, None, "mp"),
            P("mp", ("seq", "row")),
            P(),
            P("mp", ("seq", "row")),
            P(),
            P(None, ("seq", "row"), "mp"),
            P("mp", ("seq", "row")),
        ),
        check_vma=False,
    )
```
